32 devices in a mesh: groups: 2 (over x), space: 16 (over z, y, core).
Axes of the slice: x: 2, y: 2, z: 4, core: 2. Of those that a mesh axis runs over, the one named last changes fastest.
Arguments:
- lifted_field: float32 [64, 16, 128, 256], P('groups', 'space'), parts along dimension 0, may hold values from -6 to 6
- cotangent: bfloat16 [64, 16, 128, 256], P('groups', 'space'), parts along dimension 0, may hold values from -6 to 6
- spectral_weights: float32 [2, 32, 1024, 32, 32], P(None, None, 'space'), may hold values from -4 to 4
- point_weights: float32 [32, 32], replicated, may hold values from -1 to 1
- point_bias: float32 [32], replicated, may hold values from -3 to 3
Outputs:
- activated: bfloat16 [64, 16, 128, 256], P('groups', 'space'), parts along dimension 0
- grad_spectral: float32 [4, 32, 1024, 32, 32], P('groups', None, 'space'), parts along dimension 0
- grad_point: float32 [64, 32], P('groups'), parts along dimension 0
- grad_bias: float32 [64], P('groups'), parts along dimension 0
The draws below stay inside these ranges and needn't reach their ends.
There are 2 independent parts, one for each index of `groups`. The reference program is written for one: setup_inputs(seed, part) draws one part's arguments, and reference() takes and returns one part's arrays. A program takes and returns all parts, laid end to end along the dimension named above; an argument that names none is the same for every part. Nothing has to cross between parts.
All inputs are finite; a program needn't handle non-finite values.
Results may differ from the reference program's by a relative error of at most 0.001.
Values sent between devices are 32-bit elements; how exact they have to be, the bound alone decides.
No kernel may reach another device: no remote copies, remote signals or barrier semaphores. Data moves between devices by JAX's collectives and lax.ppermute only.
A program may use at most 192 MiB of HBM per device.

```python
import jax
import jax.numpy as jnp
from jax import lax

C = 32
MX = 32
MY = 32
MZ = 32
NY = 128
NZ = 256
NX = 16
MODES = 1024


def block_levels(own_key, shape, split, smallest, top_value):
    level = 1.0
    for axis_at, shards_of in split:
        steps = jax.random.uniform(jax.random.fold_in(jax.random.fold_in(own_key, 6), axis_at), (shards_of,), jnp.float32, smallest / len(split), top_value / len(split))
        level = level * jnp.repeat(jnp.exp(steps), shape[axis_at] // shards_of).reshape((-1,) + (1,) * (len(shape) - 1 - axis_at))
    return level


def centred(stream_key, extent, scale, most, split=(), kind=jnp.bfloat16):
    loudness = block_levels(stream_key, extent, split, -0.22, 0.18) if split else 1.0
    values = jax.random.normal(stream_key, extent, jnp.float32) * scale * loudness
    return jnp.minimum(jnp.maximum(values, -most), most).astype(kind)


def setup_inputs(seed: int = 0, part: int = 0) -> dict:
    streams_of = jax.random.split(jax.random.key(seed), 6)
    part_keys = jax.random.split(jax.random.fold_in(streams_of[5], part), 6)
    lifted_field = centred(part_keys[0], (C, NX, NY, NZ), 1.0, 6.0, ((1, 16),), jnp.float32)
    cotangent = centred(part_keys[1], (C, NX, NY, NZ), 1.0, 6.0, ((1, 16),))
    spectral_weights = centred(streams_of[2], (2, MX, MODES, C, C), (C // 16) ** -0.5, 4.0, ((2, 16),), jnp.float32)
    point_weights = centred(streams_of[3], (C, C), C ** -0.5, 1.0, (), jnp.float32)
    point_bias = centred(streams_of[4], (C,), 0.5, 3.0, (), jnp.float32)
    return {"lifted_field": lifted_field, "cotangent": cotangent, "spectral_weights": spectral_weights, "point_weights": point_weights, "point_bias": point_bias}


HIGHEST = lax.Precision.HIGHEST
INV_SQRT_TWO = 0.7071067811865476
INV_SQRT_TWO_PI = 0.3989422804014327


def trig_tables(positions, frequency, length):
    product = (positions[:, None] * frequency[None, :]) % length
    phase_angle = (2.0 * jnp.pi / length) * product.astype(jnp.float32)
    return jnp.cos(phase_angle), jnp.sin(phase_angle)


def kept_frequencies(kept_count, length):
    mode_index = jnp.arange(kept_count, dtype=jnp.int32)
    return jnp.where(mode_index < kept_count // 2, mode_index, length - kept_count + mode_index).astype(jnp.int32)


def forward_local(field_in):
    channels = field_in.shape[0]
    width_x = field_in.shape[1]
    cos_z, sin_z = trig_tables(jnp.arange(NZ, dtype=jnp.int32), jnp.arange(MZ, dtype=jnp.int32), NZ)
    table_z = jnp.concatenate([cos_z, -sin_z], axis=1)
    along_z = jnp.einsum("cxyz,zk->cxyk", field_in, table_z, precision=HIGHEST)
    z_real = along_z[..., :MZ]
    z_imag = along_z[..., MZ:]
    cos_y, sin_y = trig_tables(jnp.arange(NY, dtype=jnp.int32), kept_frequencies(MY, NY), NY)
    y_real = jnp.einsum("cxyk,yj->xcjk", z_real, cos_y, precision=HIGHEST) + jnp.einsum("cxyk,yj->xcjk", z_imag, sin_y, precision=HIGHEST)
    y_imag = jnp.einsum("cxyk,yj->xcjk", z_imag, cos_y, precision=HIGHEST) - jnp.einsum("cxyk,yj->xcjk", z_real, sin_y, precision=HIGHEST)
    stacked = jnp.stack([y_real, y_imag], axis=1)
    return stacked.reshape(width_x, 2, channels, MY * MZ)


def transform_x(x_lines):
    length_x = x_lines.shape[0]
    cos_x, sin_x = trig_tables(jnp.arange(length_x, dtype=jnp.int32), kept_frequencies(MX, length_x), length_x)
    norm_scale = 1.0 / (float(length_x * NY * NZ) ** 0.5)
    part_real = x_lines[:, 0]
    part_imag = x_lines[:, 1]
    x_real = jnp.einsum("xcm,xk->kcm", part_real, cos_x, precision=HIGHEST) + jnp.einsum("xcm,xk->kcm", part_imag, sin_x, precision=HIGHEST)
    x_imag = jnp.einsum("xcm,xk->kcm", part_imag, cos_x, precision=HIGHEST) - jnp.einsum("xcm,xk->kcm", part_real, sin_x, precision=HIGHEST)
    return norm_scale * jnp.stack([x_real, x_imag], axis=1)


def mix_modes(spectrum, weights):
    spec_real = spectrum[:, 0]
    spec_imag = spectrum[:, 1]
    out_real = jnp.einsum("kim,kmio->kom", spec_real, weights[0], precision=HIGHEST) - jnp.einsum("kim,kmio->kom", spec_imag, weights[1], precision=HIGHEST)
    out_imag = jnp.einsum("kim,kmio->kom", spec_real, weights[1], precision=HIGHEST) + jnp.einsum("kim,kmio->kom", spec_imag, weights[0], precision=HIGHEST)
    return jnp.stack([out_real, out_imag], axis=1)


def inverse_x(spectrum, positions, length_x):
    cos_x, sin_x = trig_tables(positions, kept_frequencies(MX, length_x), length_x)
    spec_real = spectrum[:, 0]
    spec_imag = spectrum[:, 1]
    a_real = jnp.einsum("kcm,xk->xcm", spec_real, cos_x, precision=HIGHEST) - jnp.einsum("kcm,xk->xcm", spec_imag, sin_x, precision=HIGHEST)
    a_imag = jnp.einsum("kcm,xk->xcm", spec_imag, cos_x, precision=HIGHEST) + jnp.einsum("kcm,xk->xcm", spec_real, sin_x, precision=HIGHEST)
    return jnp.stack([a_real, a_imag], axis=1)


def inverse_yz(x_lines, length_x):
    width_x = x_lines.shape[0]
    channels = x_lines.shape[2]
    mode_grid = x_lines.reshape(width_x, 2, channels, MY, MZ)
    cos_y, sin_y = trig_tables(jnp.arange(NY, dtype=jnp.int32), kept_frequencies(MY, NY), NY)
    b_real = jnp.einsum("xcjk,yj->cxyk", mode_grid[:, 0], cos_y, precision=HIGHEST) - jnp.einsum("xcjk,yj->cxyk", mode_grid[:, 1], sin_y, precision=HIGHEST)
    b_imag = jnp.einsum("xcjk,yj->cxyk", mode_grid[:, 1], cos_y, precision=HIGHEST) + jnp.einsum("xcjk,yj->cxyk", mode_grid[:, 0], sin_y, precision=HIGHEST)
    cos_z, sin_z = trig_tables(jnp.arange(NZ, dtype=jnp.int32), jnp.arange(MZ, dtype=jnp.int32), NZ)
    weight_z = jnp.where(jnp.arange(MZ, dtype=jnp.int32) == 0, 1.0, 2.0).astype(jnp.float32)
    table_z = jnp.concatenate([cos_z * weight_z[None, :], -sin_z * weight_z[None, :]], axis=1)
    stacked = jnp.concatenate([b_real, b_imag], axis=-1)
    result = jnp.einsum("cxyk,zk->cxyz", stacked, table_z, precision=HIGHEST)
    return result * (1.0 / (float(length_x * NY * NZ) ** 0.5))


def gelu_slope(values):
    return 0.5 * (1.0 + lax.erf(values * INV_SQRT_TWO)) + values * jnp.exp(-0.5 * values * values) * INV_SQRT_TWO_PI


def weight_gradient(spectrum, slope_modes, first_mode):
    mode_ids = first_mode + jnp.arange(spectrum.shape[3], dtype=jnp.int32)
    weight_modes = jnp.where(mode_ids % MZ == 0, 1.0, 2.0).astype(jnp.float32)
    grad_real = jnp.einsum("kim,kom->kmio", spectrum[:, 0], slope_modes[:, 0], precision=HIGHEST) + jnp.einsum("kim,kom->kmio", spectrum[:, 1], slope_modes[:, 1], precision=HIGHEST)
    grad_imag = jnp.einsum("kim,kom->kmio", spectrum[:, 0], slope_modes[:, 1], precision=HIGHEST) - jnp.einsum("kim,kom->kmio", spectrum[:, 1], slope_modes[:, 0], precision=HIGHEST)
    stacked = jnp.stack([grad_real, grad_imag], axis=0)
    return stacked * weight_modes[None, None, :, None, None]


def reference(lifted_field, cotangent, spectral_weights, point_weights, point_bias):
    length_x = lifted_field.shape[1]
    spectrum = transform_x(forward_local(lifted_field))
    mixed_modes = mix_modes(spectrum, spectral_weights)
    x_lines = inverse_x(mixed_modes, jnp.arange(length_x, dtype=jnp.int32), length_x)
    spectral = inverse_yz(x_lines, length_x)
    pointwise = jnp.einsum("ixyz,io->oxyz", lifted_field, point_weights, precision=HIGHEST) + point_bias[:, None, None, None]
    before = spectral + pointwise
    activated = jax.nn.gelu(before, approximate=False).astype(jnp.bfloat16)
    slope_field = cotangent.astype(jnp.float32) * gelu_slope(before)
    root_cells = float(length_x * NY * NZ) ** 0.5
    grad_point = jnp.einsum("ixyz,oxyz->io", lifted_field, slope_field, precision=HIGHEST) / root_cells
    grad_bias = jnp.sum(slope_field, axis=(1, 2, 3)) / root_cells
    slope_spectrum = transform_x(forward_local(slope_field))
    grad_spectral = weight_gradient(spectrum, slope_spectrum, jnp.int32(0))
    return (activated, grad_spectral, grad_point, grad_bias)
```

```python
import jax
import jax.numpy as jnp
from jax import lax
from jax.sharding import PartitionSpec as P

MX = 32
MY = 32
MZ = 32
NY = 128
NZ = 256


HIGHEST = lax.Precision.HIGH
INV_SQRT_TWO = 0.7071067811865476
INV_SQRT_TWO_PI = 0.3989422804014327


def trig_tables(positions, frequency, length):
    product = positions[:, None] * frequency[None, :] % length
    phase_angle = 2.0 * jnp.pi / length * product.astype(jnp.float32)
    return (jnp.cos(phase_angle), jnp.sin(phase_angle))


def kept_frequencies(kept_count, length):
    mode_index = jnp.arange(kept_count, dtype=jnp.int32)
    return jnp.where(mode_index < kept_count // 2, mode_index, length - kept_count + mode_index)


def forward_local(field_in):
    channels = field_in.shape[0]
    width_x = field_in.shape[1]
    cos_z, sin_z = trig_tables(jnp.arange(NZ, dtype=jnp.int32), jnp.arange(MZ, dtype=jnp.int32), NZ)
    table_z = jnp.concatenate([cos_z, -sin_z], axis=1)
    along_z = jnp.einsum("cxyz,zk->cxyk", field_in, table_z, precision=HIGHEST)
    z_real = along_z[..., :MZ]
    z_imag = along_z[..., MZ:]
    cos_y, sin_y = trig_tables(jnp.arange(NY, dtype=jnp.int32), kept_frequencies(MY, NY), NY)
    y_real = jnp.einsum("cxyk,yj->xcjk", z_real, cos_y, precision=HIGHEST) + jnp.einsum(
        "cxyk,yj->xcjk", z_imag, sin_y, precision=HIGHEST
    )
    y_imag = jnp.einsum("cxyk,yj->xcjk", z_imag, cos_y, precision=HIGHEST) - jnp.einsum(
        "cxyk,yj->xcjk", z_real, sin_y, precision=HIGHEST
    )
    stacked = jnp.stack([y_real, y_imag], axis=1)
    return stacked.reshape(width_x, 2, channels, MY * MZ)


def transform_x(x_lines):
    length_x = x_lines.shape[0]
    cos_x, sin_x = trig_tables(
        jnp.arange(length_x, dtype=jnp.int32), kept_frequencies(MX, length_x), length_x
    )
    norm_scale = 1.0 / float(length_x * NY * NZ) ** 0.5
    part_real = x_lines[:, 0]
    part_imag = x_lines[:, 1]
    x_real = jnp.einsum("xcm,xk->kcm", part_real, cos_x, precision=HIGHEST) + jnp.einsum(
        "xcm,xk->kcm", part_imag, sin_x, precision=HIGHEST
    )
    x_imag = jnp.einsum("xcm,xk->kcm", part_imag, cos_x, precision=HIGHEST) - jnp.einsum(
        "xcm,xk->kcm", part_real, sin_x, precision=HIGHEST
    )
    return norm_scale * jnp.stack([x_real, x_imag], axis=1)


def mix_modes(spectrum, weights):
    spec_real = spectrum[:, 0]
    spec_imag = spectrum[:, 1]
    out_real = jnp.einsum("kim,kmio->kom", spec_real, weights[0], precision=HIGHEST) - jnp.einsum(
        "kim,kmio->kom", spec_imag, weights[1], precision=HIGHEST
    )
    out_imag = jnp.einsum("kim,kmio->kom", spec_real, weights[1], precision=HIGHEST) + jnp.einsum(
        "kim,kmio->kom", spec_imag, weights[0], precision=HIGHEST
    )
    return jnp.stack([out_real, out_imag], axis=1)


def inverse_x(spectrum, positions, length_x):
    cos_x, sin_x = trig_tables(positions, kept_frequencies(MX, length_x), length_x)
    spec_real = spectrum[:, 0]
    spec_imag = spectrum[:, 1]
    a_real = jnp.einsum("kcm,xk->xcm", spec_real, cos_x, precision=HIGHEST) - jnp.einsum(
        "kcm,xk->xcm", spec_imag, sin_x, precision=HIGHEST
    )
    a_imag = jnp.einsum("kcm,xk->xcm", spec_imag, cos_x, precision=HIGHEST) + jnp.einsum(
        "kcm,xk->xcm", spec_real, sin_x, precision=HIGHEST
    )
    return jnp.stack([a_real, a_imag], axis=1)


def inverse_yz(x_lines, length_x):
    width_x = x_lines.shape[0]
    channels = x_lines.shape[2]
    mode_grid = x_lines.reshape(width_x, 2, channels, MY, MZ)
    cos_y, sin_y = trig_tables(jnp.arange(NY, dtype=jnp.int32), kept_frequencies(MY, NY), NY)
    b_real = jnp.einsum("xcjk,yj->cxyk", mode_grid[:, 0], cos_y, precision=HIGHEST) - jnp.einsum(
        "xcjk,yj->cxyk", mode_grid[:, 1], sin_y, precision=HIGHEST
    )
    b_imag = jnp.einsum("xcjk,yj->cxyk", mode_grid[:, 1], cos_y, precision=HIGHEST) + jnp.einsum(
        "xcjk,yj->cxyk", mode_grid[:, 0], sin_y, precision=HIGHEST
    )
    cos_z, sin_z = trig_tables(jnp.arange(NZ, dtype=jnp.int32), jnp.arange(MZ, dtype=jnp.int32), NZ)
    weight_z = jnp.where(jnp.arange(MZ, dtype=jnp.int32) == 0, 1.0, 2.0).astype(jnp.float32)
    table_z = jnp.concatenate([cos_z * weight_z[None, :], -sin_z * weight_z[None, :]], axis=1)
    stacked = jnp.concatenate([b_real, b_imag], axis=-1)
    result = jnp.einsum("cxyk,zk->cxyz", stacked, table_z, precision=HIGHEST)
    return result * (1.0 / float(length_x * NY * NZ) ** 0.5)


def gelu_slope(values):
    return (
        0.5 * (1.0 + lax.erf(values * INV_SQRT_TWO))
        + values * jnp.exp(-0.5 * values * values) * INV_SQRT_TWO_PI
    )


def weight_gradient(spectrum, slope_modes, first_mode):
    mode_ids = first_mode + jnp.arange(spectrum.shape[3], dtype=jnp.int32)
    weight_modes = jnp.where(mode_ids % MZ == 0, 1.0, 2.0).astype(jnp.float32)
    grad_real = jnp.einsum(
        "kim,kom->kmio", spectrum[:, 0], slope_modes[:, 0], precision=HIGHEST
    ) + jnp.einsum("kim,kom->kmio", spectrum[:, 1], slope_modes[:, 1], precision=HIGHEST)
    grad_imag = jnp.einsum(
        "kim,kom->kmio", spectrum[:, 0], slope_modes[:, 1], precision=HIGHEST
    ) - jnp.einsum("kim,kom->kmio", spectrum[:, 1], slope_modes[:, 0], precision=HIGHEST)
    stacked = jnp.stack([grad_real, grad_imag], axis=0)
    return stacked * weight_modes[None, None, :, None, None]


def to_modes(field_in):
    return transform_x(
        lax.all_to_all(forward_local(field_in), "space", split_axis=3, concat_axis=0, tiled=True)
    )


def body(lifted_field, cotangent, spectral_weights, point_weights, point_bias):
    devices = lax.axis_size("space")
    width_x = lifted_field.shape[1]
    length_x = width_x * devices
    spectrum = to_modes(lifted_field)
    mixed_modes = mix_modes(spectrum, spectral_weights)
    full_lines = inverse_x(mixed_modes, jnp.arange(length_x, dtype=jnp.int32), length_x)
    spectral = inverse_yz(
        lax.all_to_all(full_lines, "space", split_axis=0, concat_axis=3, tiled=True), length_x
    )
    pointwise = (
        jnp.einsum("ixyz,io->oxyz", lifted_field, point_weights, precision=HIGHEST)
        + point_bias[:, None, None, None]
    )
    before = spectral + pointwise
    activated = jax.nn.gelu(before, approximate=False).astype(jnp.bfloat16)
    slope_field = cotangent.astype(jnp.float32) * gelu_slope(before)
    local_point = jnp.einsum("ixyz,oxyz->io", lifted_field, slope_field, precision=HIGHEST)
    local_bias = jnp.sum(slope_field, axis=(1, 2, 3))
    partial = jnp.concatenate([local_point, local_bias[None, :]], axis=0)
    gathered = lax.all_gather(partial, "space", axis=0, tiled=False)
    summed = jnp.sum(gathered, axis=0)
    summed_point, summed_bias = summed[:-1], summed[-1]
    root_cells = float(length_x * NY * NZ) ** 0.5
    slope_spectrum = to_modes(slope_field)
    first_mode = lax.axis_index("space") * spectrum.shape[3]
    grad_spectral = weight_gradient(spectrum, slope_spectrum, first_mode)
    return (activated, grad_spectral, summed_point / root_cells, summed_bias / root_cells)


def solution(mesh):
    placed = (
        P("groups", "space", None, None),
        P("groups", "space", None, None),
        P(None, None, "space", None, None),
        P(),
        P(),
    )
    return jax.shard_map(
        body,
        mesh=mesh,
        in_specs=placed,
        out_specs=(
            P("groups", "space", None, None),
            P("groups", None, "space", None, None),
            P("groups", None),
            P("groups"),
        ),
        check_vma=False,
    )
```

```python
import functools

import jax
import jax.numpy as jnp
import ml_dtypes
import numpy as np
from jax import lax
from jax.experimental import pallas as pl
from jax.experimental.pallas import tpu as pltpu
from jax.sharding import PartitionSpec as P

MX = 32
MY = 32
MZ = 32
NY = 128
NZ = 256

F32 = jnp.float32
BF16 = jnp.bfloat16
INV_SQRT_TWO = 0.7071067811865476
INV_SQRT_TWO_PI = 0.3989422804014327
MIB = 1 << 20
LANES = 128
GROUP = 4


def kept(kept_count, length):
    index = np.arange(kept_count)
    return np.where(index < kept_count // 2, index, length - kept_count + index)


def angles(positions, frequency, length):
    product = positions[:, None] * frequency[None, :] % length
    return 2.0 * np.pi / length * product


def split_table(table):
    high = table.astype(ml_dtypes.bfloat16)
    return high, (table - high.astype(np.float64)).astype(ml_dtypes.bfloat16)


def lane_spread(first, second, real_table, imag_table):
    return np.concatenate(
        [real_table * first, real_table * second, imag_table * first, imag_table * second], axis=1
    )


def forward_tables():
    theta = angles(np.arange(NZ), np.arange(MZ), NZ)
    cos_z, sin_z = np.cos(theta), np.sin(theta)
    plain = [lane_spread(f, s, cos_z, -sin_z) for f, s in ((1, 0), (0, 1))]
    turned = [lane_spread(f, s, -sin_z, -cos_z) for f, s in ((1, 0), (0, 1))]
    table_z = np.concatenate([np.concatenate(plain, 0), np.concatenate(turned, 0)], axis=1)
    theta = angles(np.arange(NY), kept(MY, NY), NY)
    both = np.concatenate([np.cos(theta).T, np.sin(theta).T], axis=1)
    table_y = np.concatenate([both[0::2], both[1::2]], axis=0)
    z_high, z_low = split_table(table_z)
    y_high, y_low = split_table(table_y)
    return z_high, z_low, np.concatenate([y_high, y_low], axis=0)


def inverse_tables(norm):
    theta = angles(np.arange(NY), kept(MY, NY), NY)
    cos_y, sin_y = np.cos(theta), np.sin(theta)
    table_y = np.concatenate([cos_y[:, 0::2], cos_y[:, 1::2], sin_y[:, 0::2], sin_y[:, 1::2]], axis=1)
    y_high, y_low = split_table(table_y)
    theta = angles(np.arange(NZ), np.arange(MZ), NZ)
    weight = np.where(np.arange(MZ) == 0, 1.0, 2.0) * norm
    cos_z, sin_z = np.cos(theta) * weight, -np.sin(theta) * weight
    table_z = np.concatenate([lane_spread(f, s, cos_z, sin_z).T for f, s in ((1, 0), (0, 1))], axis=1)
    z_high, z_low = split_table(table_z)
    return (
        np.concatenate([y_high, y_high, y_low], axis=1),
        np.concatenate([z_high, z_high], axis=0),
        z_low,
    )


def dot(left, right):
    return jnp.dot(left, right, preferred_element_type=F32)


def split(values):
    high = values.astype(BF16)
    return high, (values - high.astype(F32)).astype(BF16)


def lane_index(shape):
    return lax.broadcasted_iota(jnp.int32, shape, len(shape) - 1)


def roll(values, shift):
    return pltpu.roll(values, shift % LANES, len(values.shape) - 1)


def forward_group(fields, z_high, z_low, y_both, out_ref, first, rows):
    left = jnp.concatenate(
        [jnp.concatenate([fields[q], fields[q + 1]], axis=1) for q in range(0, GROUP, 2)], axis=0
    )
    high, low = split(left)
    lines = dot(high, z_high) + dot(high, z_low) + dot(low, z_high)
    pairs = []
    for q in range(GROUP // 2):
        part = lines[q * NY : (q + 1) * NY]
        pairs.append(jnp.concatenate([part[:, :LANES], part[:, LANES:]], axis=0))
    high, low = split(jnp.concatenate(pairs, axis=1))
    wide = dot(y_both, high)
    modes = wide[:MY] + wide[MY:] + dot(y_both[:MY], low)
    half = MY // 2
    for q in range(GROUP // 2):
        even = modes[:half, q * LANES : (q + 1) * LANES]
        odd = modes[half:, q * LANES : (q + 1) * LANES]
        at_even = (lane_index(even.shape) // MZ) % 2 == 0
        out_ref[pl.ds(first + 2 * q, half, stride=rows), :] = jnp.where(at_even, even, roll(odd, MZ))
        out_ref[pl.ds(first + 2 * q + 1, half, stride=rows), :] = jnp.where(at_even, roll(even, -MZ), odd)


def inverse_y_group(modes_ref, y_table, first, rows):
    half = MY // 2
    pairs = []
    for q in range(GROUP // 2):
        c0 = modes_ref[pl.ds(first + 2 * q, half, stride=rows), :]
        c1 = modes_ref[pl.ds(first + 2 * q + 1, half, stride=rows), :]
        lane = lane_index(c0.shape)
        at_even = (lane // MZ) % 2 == 0
        even = jnp.where(at_even, c0, roll(c1, MZ))
        odd = jnp.where(at_even, roll(c0, -MZ), c1)
        both = jnp.concatenate([even, odd], axis=0)
        turned = jnp.where(lane_index(both.shape) < LANES // 2, -roll(both, 64), roll(both, 64))
        pairs.append(jnp.concatenate([both, turned], axis=0))
    high, low = split(jnp.concatenate(pairs, axis=1))
    return dot(y_table, jnp.concatenate([high, low, high], axis=0))


def full(shape):
    return pl.BlockSpec(shape, lambda *_: (0,) * len(shape))


def params(limit):
    return pltpu.CompilerParams(vmem_limit_bytes=limit * MIB)


def forward_kernel(z_high, z_low, y_both, field_ref, out_ref, *, channels, step_channels):
    step = pl.program_id(0)
    for g in range(0, step_channels, GROUP):
        fields = [field_ref[g + q] for q in range(GROUP)]
        first = step * step_channels + g
        forward_group(fields, z_high[...], z_low[...], y_both[...], out_ref, first, channels)


def forward_modes(field, tables):
    channels = field.shape[0]
    step_channels = min(channels, 8)
    z_high, z_low, y_both = tables
    owners = MY // 2
    out = pl.pallas_call(
        functools.partial(forward_kernel, channels=channels, step_channels=step_channels),
        grid=(channels // step_channels,),
        in_specs=[
            full(z_high.shape),
            full(z_low.shape),
            full(y_both.shape),
            pl.BlockSpec((step_channels, NY, NZ), lambda s: (s, 0, 0)),
        ],
        out_specs=full((owners * channels, LANES)),
        out_shape=jax.ShapeDtypeStruct((owners * channels, LANES), F32),
        compiler_params=params(24),
        cost_estimate=pl.CostEstimate(flops=2 * 10**9, bytes_accessed=8 * MIB, transcendentals=0),
        name="forward_yz",
    )(z_high, z_low, y_both, field)
    return out.reshape(owners, channels, LANES)


def fold_kernel(first_ref, *refs):
    *others, out_ref = refs
    real, imag = first_ref[0, 0], first_ref[1, 0]
    for other in others:
        real, imag = real + other[0, 0], imag + other[1, 0]
    modes = real.shape[-1]
    out_ref[0, :, :, :modes] = real
    out_ref[0, :, :, modes:] = imag


def fold_weights(weights, unique):
    _, kept_x, channels, outputs, modes = weights.shape
    block = (2, 1, channels, outputs, modes)
    copies = kept_x // unique
    return pl.pallas_call(
        fold_kernel,
        grid=(unique,),
        in_specs=[pl.BlockSpec(block, functools.partial(lambda a, r: (0, a + r, 0, 0, 0), r=r * unique)) for r in range(copies)],
        out_specs=pl.BlockSpec((1, channels, outputs, 2 * modes), lambda a: (a, 0, 0, 0)),
        out_shape=jax.ShapeDtypeStruct((unique, channels, outputs, 2 * modes), F32),
        compiler_params=params(16),
        cost_estimate=pl.CostEstimate(flops=8 * 10**6, bytes_accessed=44 * MIB, transcendentals=0),
        name="fold_weights",
    )(*([weights] * copies))


def spectrum_row(cos_ref, sin_ref, lines_ref, turned_ref, at, points):
    total = cos_ref[at, 0] * lines_ref[0] + sin_ref[at, 0] * turned_ref[0]
    for x in range(1, points):
        total += cos_ref[at, x] * lines_ref[x] + sin_ref[at, x] * turned_ref[x]
    return total


def turn_lines(lines_ref, turned_ref, points, channels):
    sign = jnp.where(lane_index((channels, LANES)) < LANES // 2, 1.0, -1.0)
    for x in range(points):
        turned_ref[x] = sign * roll(lines_ref[x, :channels], 64)


def doubled(values):
    other = roll(values, 64)
    low = lane_index(values.shape) < LANES // 2
    return jnp.where(low, values, other), jnp.where(low, other, values)


def mix_kernel(cos_ref, sin_ref, lines_ref, weights_ref, spec_ref, out_ref, turned_ref, real_ref, imag_ref, *, points, channels, per_step, norm):
    step = pl.program_id(0)

    @pl.when(step == 0)
    def _():
        turn_lines(lines_ref, turned_ref, points, channels)
        out_ref[...] = jnp.zeros_like(out_ref)

    low = lane_index((channels, LANES)) < LANES // 2

    @pl.loop(0, per_step)
    def _(q):
        at = step * per_step + q
        spec = norm * spectrum_row(cos_ref, sin_ref, lines_ref, turned_ref, at, points)
        spec_ref[q] = spec
        real_ref[...], imag_ref[...] = doubled(spec)
        by_real = jnp.zeros((channels, LANES), F32)
        by_imag = jnp.zeros((channels, LANES), F32)
        for i in range(channels):
            weight = weights_ref[q, i]
            by_real += real_ref[pl.ds(i, 1), :] * weight
            by_imag += imag_ref[pl.ds(i, 1), :] * weight
        other = roll(by_imag, 64)
        mixed = by_real + jnp.where(low, -other, other)
        other = roll(mixed, 64)
        turned = jnp.where(low, -other, other)
        for x in range(points):
            out_ref[x] += cos_ref[at, x] * mixed + sin_ref[at, x] * turned


def smem():
    return pl.BlockSpec(memory_space=pltpu.SMEM)


def mix(cos_x, sin_x, lines, weights, norm):
    points, channels, _ = lines.shape
    unique = weights.shape[0]
    per_step = min(unique, 4)
    shape = (points, channels, LANES)
    return pl.pallas_call(
        functools.partial(mix_kernel, points=points, channels=channels, per_step=per_step, norm=norm),
        grid=(unique // per_step,),
        in_specs=[
            smem(),
            smem(),
            full(shape),
            pl.BlockSpec((per_step,) + weights.shape[1:], lambda s: (s, 0, 0, 0)),
        ],
        out_specs=[
            pl.BlockSpec((per_step, channels, LANES), lambda s: (s, 0, 0)),
            full(shape),
        ],
        out_shape=[
            jax.ShapeDtypeStruct((unique, channels, LANES), F32),
            jax.ShapeDtypeStruct(shape, F32),
        ],
        scratch_shapes=[
            pltpu.VMEM(shape, F32),
            pltpu.VMEM((channels, LANES), F32),
            pltpu.VMEM((channels, LANES), F32),
        ],
        compiler_params=params(16),
        cost_estimate=pl.CostEstimate(flops=2 * 10**7, bytes_accessed=9 * MIB, transcendentals=0),
        name="mix_modes",
    )(cos_x, sin_x, lines, weights)


def pointwise_kernel(mixer_ref, bias_ref, field_ref, out_ref, *, channels, blocks):
    size = 8 * channels
    mixer = mixer_ref[...]
    bias = bias_ref[...]
    for b in range(blocks):
        high, low = split(field_ref[:, 8 * b : 8 * b + 8, :].reshape(size, NZ))
        wide = dot(mixer, high)
        values = wide[:size] + wide[size:] + dot(mixer[:size], low) + bias
        out_ref[:, 8 * b : 8 * b + 8, :] = values.reshape(channels, 8, NZ)


def pointwise(field, mixer, bias):
    channels = field.shape[0]
    blocks = 2
    block = pl.BlockSpec((channels, 8 * blocks, NZ), lambda s: (0, s, 0))
    return pl.pallas_call(
        functools.partial(pointwise_kernel, channels=channels, blocks=blocks),
        grid=(NY // (8 * blocks),),
        in_specs=[full(mixer.shape), full(bias.shape), block],
        out_specs=block,
        out_shape=jax.ShapeDtypeStruct(field.shape, F32),
        compiler_params=params(16),
        cost_estimate=pl.CostEstimate(flops=4 * 10**9, bytes_accessed=24 * MIB, transcendentals=0),
        name="pointwise",
    )(mixer, bias, field)


def cell_kernel(
    inv_y, inv_z, inv_z_low, z_high, z_low, y_both, sum_ref, modes_ref, pre_ref, cot_ref, field_hbm,
    act_ref, out_ref, field_ref, slope_high, slope_low, sem, *, channels, rows, owners,
):
    step = pl.program_id(0)
    copy = pltpu.make_async_copy(field_hbm, field_ref, sem)

    @pl.when(step == 0)
    def _():
        copy.start()

    first = step * GROUP
    lines = inverse_y_group(modes_ref, inv_y[...], first, channels)
    lines = jnp.concatenate([lines[:, q * LANES : (q + 1) * LANES] for q in range(GROUP // 2)], axis=0)
    high, low = split(lines)
    spectral = dot(jnp.concatenate([high, low], axis=1), inv_z[...]) + dot(high, inv_z_low[...])
    slopes = []
    for q in range(GROUP):
        r = q // 2 * NY
        c = q % 2 * NZ
        before = spectral[r : r + NY, c : c + NZ] + pre_ref[q]
        cdf = 0.5 + 0.5 * lax.erf(before * INV_SQRT_TWO)
        act_ref[q] = (before * cdf).astype(BF16)
        pdf = jnp.exp(-0.5 * before * before) * INV_SQRT_TWO_PI
        slope = cot_ref[q].astype(F32) * (cdf + before * pdf)
        slopes.append(slope)
        high, low = split(slope)
        slope_high[first + q] = high
        slope_low[first + q] = low
    forward_group(slopes, z_high[...], z_low[...], y_both[...], out_ref, first, rows)

    @pl.when(step == pl.num_programs(0) - 1)
    def _():
        copy.wait()
        size = 8 * channels
        total = jnp.zeros((size, size), F32)
        nt = (((1,), (1,)), ((), ()))
        for b in range(NY // 16):
            at = pl.ds(16 * b, 16)
            field_high, field_low = split(field_ref[:, at, :])
            s_high, s_low = slope_high[:, at, :], slope_low[:, at, :]
            for h in range(2):
                part = slice(8 * h, 8 * h + 8)
                f_h = field_high[:, part].reshape(size, NZ)
                f_l = field_low[:, part].reshape(size, NZ)
                s_h = s_high[:, part].reshape(size, NZ)
                s_l = s_low[:, part].reshape(size, NZ)
                total += lax.dot_general(f_h, s_h, nt, preferred_element_type=F32)
                total += lax.dot_general(f_h, s_l, nt, preferred_element_type=F32)
                total += lax.dot_general(f_l, s_h, nt, preferred_element_type=F32)
        row = lax.broadcasted_iota(jnp.int32, (size, size), 0) % 8
        total = jnp.where(row == lane_index((size, size)) % 8, total, 0.0)
        folded = jnp.sum(total.reshape(channels, 8, size), axis=1)
        point = jnp.dot(folded, sum_ref[...], precision=lax.Precision.HIGHEST, preferred_element_type=F32)
        packed = jnp.concatenate([point[8 * q : 8 * q + 8] for q in range(channels // 8)], axis=1)
        dc = jnp.broadcast_to(out_ref[0:channels, 0:1], (channels, LANES))
        eye = lax.broadcasted_iota(jnp.int32, (channels, LANES), 0) == lane_index((channels, LANES))
        bias = jnp.sum(jnp.where(eye, dc, 0.0), axis=0, keepdims=True)
        extra = jnp.where(lax.broadcasted_iota(jnp.int32, (8, LANES), 0) == 0, jnp.broadcast_to(bias, (8, LANES)), 0.0)
        for d in range(owners):
            out_ref[d * rows + channels : d * rows + channels + 8, :] = packed
            out_ref[d * rows + channels + 8 : (d + 1) * rows, :] = extra


def cell_stage(inverse, forward, summing, modes, pre, cotangent, field):
    channels = field.shape[0]
    owners = MY // 2
    rows = channels + 16
    block = pl.BlockSpec((GROUP, NY, NZ), lambda s: (s, 0, 0))
    tables = (*inverse, *forward, summing)
    act, out = pl.pallas_call(
        functools.partial(cell_kernel, channels=channels, rows=rows, owners=owners),
        grid=(channels // GROUP,),
        in_specs=[full(t.shape) for t in tables]
        + [full((owners * channels, LANES)), block, block, pl.BlockSpec(memory_space=pl.ANY)],
        out_specs=[block, full((owners * rows, LANES))],
        out_shape=[
            jax.ShapeDtypeStruct((channels, NY, NZ), BF16),
            jax.ShapeDtypeStruct((owners * rows, LANES), F32),
        ],
        scratch_shapes=[
            pltpu.VMEM((channels, NY, NZ), F32),
            pltpu.VMEM((channels, NY, NZ), BF16),
            pltpu.VMEM((channels, NY, NZ), BF16),
            pltpu.SemaphoreType.DMA,
        ],
        compiler_params=params(36),
        cost_estimate=pl.CostEstimate(flops=8 * 10**9, bytes_accessed=12 * MIB, transcendentals=2 * 10**6),
        name="cells",
    )(*tables, modes.reshape(owners * channels, LANES), pre, cotangent, field)
    return act, out.reshape(owners, rows, LANES)


def gradient_kernel(
    cos_ref, sin_ref, spec_ref, lines_ref, out_hbm, point_ref, bias_ref,
    turned_ref, slope_ref, flip_ref, real_ref, imag_ref, buffer, sems, *, points, channels, unique, copies, norm,
):
    turn_lines(lines_ref, turned_ref, points, channels)
    half = LANES // 2
    lane = lane_index((channels, LANES))
    scale = jnp.where(lane % MZ == 0, norm, 2.0 * norm)
    packed = lines_ref[0, channels : channels + 16, :]
    for x in range(1, points):
        packed += lines_ref[x, channels : channels + 16, :]
    packed = norm * packed
    for q in range(channels // 8):
        point_ref[8 * q : 8 * q + 8, :] = packed[:8, q * channels : (q + 1) * channels]
    bias_ref[...] = packed[8:9, :channels]

    def writes(at, slot):
        return [
            pltpu.make_async_copy(buffer.at[slot], out_hbm.at[:, at + r * unique], sems.at[slot, r])
            for r in range(copies)
        ]

    @pl.loop(0, unique)
    def _(at):
        slot = at % 2

        @pl.when(at >= 2)
        def _():
            for copy in writes(at - 2, slot):
                copy.wait()

        total = cos_ref[at, 0] * lines_ref[0, :channels] + sin_ref[at, 0] * turned_ref[0]
        for x in range(1, points):
            total += cos_ref[at, x] * lines_ref[x, :channels] + sin_ref[at, x] * turned_ref[x]
        slope = scale * total
        other = roll(slope, 64)
        flipped = jnp.where(lane < half, other, -other)
        real_ref[...], imag_ref[...] = doubled(spec_ref[at])
        for i in range(channels):
            both = real_ref[pl.ds(i, 1), :] * slope + imag_ref[pl.ds(i, 1), :] * flipped
            buffer[slot, 0, i] = both[:, :half]
            buffer[slot, 1, i] = both[:, half:]
        for copy in writes(at, slot):
            copy.start()

    for at in range(max(unique - 2, 0), unique):
        for copy in writes(at, at % 2):
            copy.wait()


def gradient(cos_x, sin_x, spectrum, lines, norm, kept_x):
    points, rows, _ = lines.shape
    unique, channels, _ = spectrum.shape
    half = LANES // 2
    copies = kept_x // unique
    flat = (channels, LANES)
    return pl.pallas_call(
        functools.partial(gradient_kernel, points=points, channels=channels, unique=unique, copies=copies, norm=norm),
        in_specs=[smem(), smem(), full(spectrum.shape), full(lines.shape)],
        out_specs=[pl.BlockSpec(memory_space=pl.ANY), full((channels, channels)), full((1, channels))],
        out_shape=[
            jax.ShapeDtypeStruct((2, kept_x, channels, channels, half), F32),
            jax.ShapeDtypeStruct((channels, channels), F32),
            jax.ShapeDtypeStruct((1, channels), F32),
        ],
        scratch_shapes=[
            pltpu.VMEM((points, channels, LANES), F32),
            pltpu.VMEM(flat, F32),
            pltpu.VMEM(flat, F32),
            pltpu.VMEM(flat, F32),
            pltpu.VMEM(flat, F32),
            pltpu.VMEM((2, 2, channels, channels, half), F32),
            pltpu.SemaphoreType.DMA((2, copies)),
        ],
        compiler_params=params(16),
        cost_estimate=pl.CostEstimate(flops=10**7, bytes_accessed=40 * MIB, transcendentals=0),
        name="weight_gradient",
    )(cos_x, sin_x, spectrum, lines)


def swap(lines):
    return lax.all_to_all(lines, "space", split_axis=0, concat_axis=0, tiled=True)


def suits(width_x, length_x, devices, channels, weights):
    held = weights.shape[2]
    even = np.array_equal(kept(MX, length_x) % length_x, np.arange(MX) % length_x)
    return (
        width_x == 1
        and held == 2 * MZ
        and devices * 2 == MY
        and 2 * held == LANES
        and MX % length_x == 0
        and even
        and channels == MZ
    )


def body(lifted_field, cotangent, spectral_weights, point_weights, point_bias):
    devices = lax.axis_size("space")
    channels, width_x = lifted_field.shape[:2]
    length_x = width_x * devices
    if not suits(width_x, length_x, devices, channels, spectral_weights):
        return general_body(lifted_field, cotangent, spectral_weights, point_weights, point_bias)
    norm = float(length_x * NY * NZ) ** -0.5
    theta = angles(np.arange(length_x), np.arange(length_x), length_x)
    cos_x, sin_x = jnp.asarray(np.cos(theta), F32), jnp.asarray(np.sin(theta), F32)
    forward = forward_tables()
    inverse = inverse_tables(norm)
    summing = jnp.asarray(np.repeat(np.eye(channels), 8, axis=0), F32)

    field = lifted_field.reshape(channels, NY, NZ)
    slopes_in = cotangent.reshape(channels, NY, NZ)
    weights = jnp.transpose(spectral_weights, (0, 1, 3, 4, 2))
    mixer = jnp.kron(point_weights.T, jnp.eye(8, dtype=F32))
    high = lax.reduce_precision(mixer, 8, 7)
    mixer = jnp.concatenate([high, mixer - high], axis=0).astype(BF16)
    bias = jnp.repeat(point_bias, 8)[:, None]

    lines = swap(forward_modes(field, forward))
    folded = fold_weights(weights, length_x)
    spectrum, mixed = mix(cos_x, sin_x, lines, folded, norm)
    modes = swap(mixed)
    pre = pointwise(field, mixer, bias)
    activated, slope_lines = cell_stage(inverse, forward, summing, modes, pre, slopes_in, field)
    slope_lines = swap(slope_lines)
    grad, grad_point, grad_bias = gradient(cos_x, sin_x, spectrum, slope_lines, norm, MX)
    return (
        activated.reshape(cotangent.shape),
        jnp.transpose(grad, (0, 1, 4, 2, 3)),
        grad_point,
        grad_bias.reshape(channels),
    )


HIGHEST = lax.Precision.HIGHEST


def trig_tables(positions, frequency, length):
    product = positions[:, None] * frequency[None, :] % length
    phase_angle = 2.0 * jnp.pi / length * product.astype(jnp.float32)
    return (jnp.cos(phase_angle), jnp.sin(phase_angle))


def kept_frequencies(kept_count, length):
    mode_index = jnp.arange(kept_count, dtype=jnp.int32)
    return jnp.where(mode_index < kept_count // 2, mode_index, length - kept_count + mode_index)


def forward_local(field_in):
    channels = field_in.shape[0]
    width_x = field_in.shape[1]
    cos_z, sin_z = trig_tables(jnp.arange(NZ, dtype=jnp.int32), jnp.arange(MZ, dtype=jnp.int32), NZ)
    table_z = jnp.concatenate([cos_z, -sin_z], axis=1)
    along_z = jnp.einsum("cxyz,zk->cxyk", field_in, table_z, precision=HIGHEST)
    z_real = along_z[..., :MZ]
    z_imag = along_z[..., MZ:]
    cos_y, sin_y = trig_tables(jnp.arange(NY, dtype=jnp.int32), kept_frequencies(MY, NY), NY)
    y_real = jnp.einsum("cxyk,yj->xcjk", z_real, cos_y, precision=HIGHEST) + jnp.einsum(
        "cxyk,yj->xcjk", z_imag, sin_y, precision=HIGHEST
    )
    y_imag = jnp.einsum("cxyk,yj->xcjk", z_imag, cos_y, precision=HIGHEST) - jnp.einsum(
        "cxyk,yj->xcjk", z_real, sin_y, precision=HIGHEST
    )
    stacked = jnp.stack([y_real, y_imag], axis=1)
    return stacked.reshape(width_x, 2, channels, MY * MZ)


def transform_x(x_lines):
    length_x = x_lines.shape[0]
    cos_x, sin_x = trig_tables(
        jnp.arange(length_x, dtype=jnp.int32), kept_frequencies(MX, length_x), length_x
    )
    norm_scale = 1.0 / float(length_x * NY * NZ) ** 0.5
    part_real = x_lines[:, 0]
    part_imag = x_lines[:, 1]
    x_real = jnp.einsum("xcm,xk->kcm", part_real, cos_x, precision=HIGHEST) + jnp.einsum(
        "xcm,xk->kcm", part_imag, sin_x, precision=HIGHEST
    )
    x_imag = jnp.einsum("xcm,xk->kcm", part_imag, cos_x, precision=HIGHEST) - jnp.einsum(
        "xcm,xk->kcm", part_real, sin_x, precision=HIGHEST
    )
    return norm_scale * jnp.stack([x_real, x_imag], axis=1)


def mix_modes(spectrum, weights):
    spec_real = spectrum[:, 0]
    spec_imag = spectrum[:, 1]
    out_real = jnp.einsum("kim,kmio->kom", spec_real, weights[0], precision=HIGHEST) - jnp.einsum(
        "kim,kmio->kom", spec_imag, weights[1], precision=HIGHEST
    )
    out_imag = jnp.einsum("kim,kmio->kom", spec_real, weights[1], precision=HIGHEST) + jnp.einsum(
        "kim,kmio->kom", spec_imag, weights[0], precision=HIGHEST
    )
    return jnp.stack([out_real, out_imag], axis=1)


def inverse_x(spectrum, positions, length_x):
    cos_x, sin_x = trig_tables(positions, kept_frequencies(MX, length_x), length_x)
    spec_real = spectrum[:, 0]
    spec_imag = spectrum[:, 1]
    a_real = jnp.einsum("kcm,xk->xcm", spec_real, cos_x, precision=HIGHEST) - jnp.einsum(
        "kcm,xk->xcm", spec_imag, sin_x, precision=HIGHEST
    )
    a_imag = jnp.einsum("kcm,xk->xcm", spec_imag, cos_x, precision=HIGHEST) + jnp.einsum(
        "kcm,xk->xcm", spec_real, sin_x, precision=HIGHEST
    )
    return jnp.stack([a_real, a_imag], axis=1)


def inverse_yz(x_lines, length_x):
    width_x = x_lines.shape[0]
    channels = x_lines.shape[2]
    mode_grid = x_lines.reshape(width_x, 2, channels, MY, MZ)
    cos_y, sin_y = trig_tables(jnp.arange(NY, dtype=jnp.int32), kept_frequencies(MY, NY), NY)
    b_real = jnp.einsum("xcjk,yj->cxyk", mode_grid[:, 0], cos_y, precision=HIGHEST) - jnp.einsum(
        "xcjk,yj->cxyk", mode_grid[:, 1], sin_y, precision=HIGHEST
    )
    b_imag = jnp.einsum("xcjk,yj->cxyk", mode_grid[:, 1], cos_y, precision=HIGHEST) + jnp.einsum(
        "xcjk,yj->cxyk", mode_grid[:, 0], sin_y, precision=HIGHEST
    )
    cos_z, sin_z = trig_tables(jnp.arange(NZ, dtype=jnp.int32), jnp.arange(MZ, dtype=jnp.int32), NZ)
    weight_z = jnp.where(jnp.arange(MZ, dtype=jnp.int32) == 0, 1.0, 2.0).astype(jnp.float32)
    table_z = jnp.concatenate([cos_z * weight_z[None, :], -sin_z * weight_z[None, :]], axis=1)
    stacked = jnp.concatenate([b_real, b_imag], axis=-1)
    result = jnp.einsum("cxyk,zk->cxyz", stacked, table_z, precision=HIGHEST)
    return result * (1.0 / float(length_x * NY * NZ) ** 0.5)


def gelu_slope(values):
    return (
        0.5 * (1.0 + lax.erf(values * INV_SQRT_TWO))
        + values * jnp.exp(-0.5 * values * values) * INV_SQRT_TWO_PI
    )


def weight_gradient(spectrum, slope_modes, first_mode):
    mode_ids = first_mode + jnp.arange(spectrum.shape[3], dtype=jnp.int32)
    weight_modes = jnp.where(mode_ids % MZ == 0, 1.0, 2.0).astype(jnp.float32)
    grad_real = jnp.einsum(
        "kim,kom->kmio", spectrum[:, 0], slope_modes[:, 0], precision=HIGHEST
    ) + jnp.einsum("kim,kom->kmio", spectrum[:, 1], slope_modes[:, 1], precision=HIGHEST)
    grad_imag = jnp.einsum(
        "kim,kom->kmio", spectrum[:, 0], slope_modes[:, 1], precision=HIGHEST
    ) - jnp.einsum("kim,kom->kmio", spectrum[:, 1], slope_modes[:, 0], precision=HIGHEST)
    stacked = jnp.stack([grad_real, grad_imag], axis=0)
    return stacked * weight_modes[None, None, :, None, None]


def to_modes(field_in):
    return transform_x(
        lax.all_to_all(forward_local(field_in), "space", split_axis=3, concat_axis=0, tiled=True)
    )


def general_body(lifted_field, cotangent, spectral_weights, point_weights, point_bias):
    devices = lax.axis_size("space")
    width_x = lifted_field.shape[1]
    length_x = width_x * devices
    spectrum = to_modes(lifted_field)
    mixed_modes = mix_modes(spectrum, spectral_weights)
    full_lines = inverse_x(mixed_modes, jnp.arange(length_x, dtype=jnp.int32), length_x)
    spectral = inverse_yz(
        lax.all_to_all(full_lines, "space", split_axis=0, concat_axis=3, tiled=True), length_x
    )
    pointwise = (
        jnp.einsum("ixyz,io->oxyz", lifted_field, point_weights, precision=HIGHEST)
        + point_bias[:, None, None, None]
    )
    before = spectral + pointwise
    activated = jax.nn.gelu(before, approximate=False).astype(jnp.bfloat16)
    slope_field = cotangent.astype(jnp.float32) * gelu_slope(before)
    local_point = jnp.einsum("ixyz,oxyz->io", lifted_field, slope_field, precision=HIGHEST)
    local_bias = jnp.sum(slope_field, axis=(1, 2, 3))
    partial = jnp.concatenate([local_point, local_bias[None, :]], axis=0)
    gathered = lax.all_gather(partial, "space", axis=0, tiled=False)
    summed = jnp.sum(gathered, axis=0)
    summed_point, summed_bias = summed[:-1], summed[-1]
    root_cells = float(length_x * NY * NZ) ** 0.5
    slope_spectrum = to_modes(slope_field)
    first_mode = lax.axis_index("space") * spectrum.shape[3]
    grad_spectral = weight_gradient(spectrum, slope_spectrum, first_mode)
    return (activated, grad_spectral, summed_point / root_cells, summed_bias / root_cells)


def solution(mesh):
    placed = (
        P("groups", "space", None, None),
        P("groups", "space", None, None),
        P(None, None, "space", None, None),
        P(),
        P(),
    )
    return jax.shard_map(
        body,
        mesh=mesh,
        in_specs=placed,
        out_specs=(
            P("groups", "space", None, None),
            P("groups", None, "space", None, None),
            P("groups", None),
            P("groups"),
        ),
        check_vma=False,
    )
```

```python
import functools

import jax
import jax.numpy as jnp
import ml_dtypes
import numpy as np
from jax import lax
from jax.experimental import pallas as pl
from jax.experimental.pallas import tpu as pltpu
from jax.sharding import PartitionSpec as P

MX = 32
MY = 32
MZ = 32
NY = 128
NZ = 256

F32 = jnp.float32
BF16 = jnp.bfloat16
INV_SQRT_TWO = 0.7071067811865476
INV_SQRT_TWO_PI = 0.3989422804014327
MIB = 1 << 20
LANES = 128
GROUP = 4


def kept(kept_count, length):
    index = np.arange(kept_count)
    return np.where(index < kept_count // 2, index, length - kept_count + index)


def angles(positions, frequency, length):
    product = positions[:, None] * frequency[None, :] % length
    return 2.0 * np.pi / length * product


def split_table(table):
    high = table.astype(ml_dtypes.bfloat16)
    return high, (table - high.astype(np.float64)).astype(ml_dtypes.bfloat16)


def lane_spread(first, second, real_table, imag_table):
    return np.concatenate(
        [real_table * first, real_table * second, imag_table * first, imag_table * second], axis=1
    )


def forward_tables():
    theta = angles(np.arange(NZ), np.arange(MZ), NZ)
    cos_z, sin_z = np.cos(theta), np.sin(theta)
    plain = [lane_spread(f, s, cos_z, -sin_z) for f, s in ((1, 0), (0, 1))]
    turned = [lane_spread(f, s, -sin_z, -cos_z) for f, s in ((1, 0), (0, 1))]
    table_z = np.concatenate([np.concatenate(plain, 0), np.concatenate(turned, 0)], axis=1)
    theta = angles(np.arange(NY), kept(MY, NY), NY)
    both = np.concatenate([np.cos(theta).T, np.sin(theta).T], axis=1)
    table_y = np.concatenate([both[0::2], both[1::2]], axis=0)
    z_high, z_low = split_table(table_z)
    y_high, y_low = split_table(table_y)
    return z_high, z_low, np.concatenate([y_high, y_low], axis=0)


def inverse_tables(norm):
    theta = angles(np.arange(NY), kept(MY, NY), NY)
    cos_y, sin_y = np.cos(theta), np.sin(theta)
    table_y = np.concatenate([cos_y[:, 0::2], cos_y[:, 1::2], sin_y[:, 0::2], sin_y[:, 1::2]], axis=1)
    y_high, y_low = split_table(table_y)
    theta = angles(np.arange(NZ), np.arange(MZ), NZ)
    weight = np.where(np.arange(MZ) == 0, 1.0, 2.0) * norm
    cos_z, sin_z = np.cos(theta) * weight, -np.sin(theta) * weight
    table_z = np.concatenate([lane_spread(f, s, cos_z, sin_z).T for f, s in ((1, 0), (0, 1))], axis=1)
    z_high, z_low = split_table(table_z)
    return (
        np.concatenate([y_high, y_high, y_low], axis=1),
        np.concatenate([z_high, z_high], axis=0),
        z_low,
    )


def dot(left, right):
    return jnp.dot(left, right, preferred_element_type=F32)


def split(values):
    high = values.astype(BF16)
    return high, (values - high.astype(F32)).astype(BF16)


def lane_index(shape):
    return lax.broadcasted_iota(jnp.int32, shape, len(shape) - 1)


def roll(values, shift):
    return pltpu.roll(values, shift % LANES, len(values.shape) - 1)


def forward_group(fields, z_high, z_low, y_both, out_ref, first, rows):
    left = jnp.concatenate(
        [jnp.concatenate([fields[q], fields[q + 1]], axis=1) for q in range(0, GROUP, 2)], axis=0
    )
    high, low = split(left)
    lines = dot(high, z_high) + dot(high, z_low) + dot(low, z_high)
    pairs = []
    for q in range(GROUP // 2):
        part = lines[q * NY : (q + 1) * NY]
        pairs.append(jnp.concatenate([part[:, :LANES], part[:, LANES:]], axis=0))
    high, low = split(jnp.concatenate(pairs, axis=1))
    wide = dot(y_both, high)
    modes = wide[:MY] + wide[MY:] + dot(y_both[:MY], low)
    half = MY // 2
    for q in range(GROUP // 2):
        even = modes[:half, q * LANES : (q + 1) * LANES]
        odd = modes[half:, q * LANES : (q + 1) * LANES]
        at_even = (lane_index(even.shape) // MZ) % 2 == 0
        out_ref[pl.ds(first + 2 * q, half, stride=rows), :] = jnp.where(at_even, even, roll(odd, MZ))
        out_ref[pl.ds(first + 2 * q + 1, half, stride=rows), :] = jnp.where(at_even, roll(even, -MZ), odd)


def inverse_y_group(modes_ref, y_table, first, rows):
    half = MY // 2
    pairs = []
    for q in range(GROUP // 2):
        c0 = modes_ref[pl.ds(first + 2 * q, half, stride=rows), :]
        c1 = modes_ref[pl.ds(first + 2 * q + 1, half, stride=rows), :]
        lane = lane_index(c0.shape)
        at_even = (lane // MZ) % 2 == 0
        even = jnp.where(at_even, c0, roll(c1, MZ))
        odd = jnp.where(at_even, roll(c0, -MZ), c1)
        both = jnp.concatenate([even, odd], axis=0)
        turned = jnp.where(lane_index(both.shape) < LANES // 2, -roll(both, 64), roll(both, 64))
        pairs.append(jnp.concatenate([both, turned], axis=0))
    high, low = split(jnp.concatenate(pairs, axis=1))
    return dot(y_table, jnp.concatenate([high, low, high], axis=0))


def full(shape):
    return pl.BlockSpec(shape, lambda *_: (0,) * len(shape))


def params(limit):
    return pltpu.CompilerParams(vmem_limit_bytes=limit * MIB)


def fold_block(pieces, out_ref, at):
    real, imag = pieces[0][0, at], pieces[0][1, at]
    for piece in pieces[1:]:
        real, imag = real + piece[0, at], imag + piece[1, at]
    modes = real.shape[-1]
    out_ref[at, :, :, :modes] = real
    out_ref[at, :, :, modes:] = imag


def fold_specs(weights, unique, per_step, first):
    block = (2, per_step) + weights.shape[2:]
    pieces = [
        pl.BlockSpec(block, functools.partial(lambda s, r: (0, first + s + r, 0, 0, 0), r=r * (unique // per_step)))
        for r in range(weights.shape[1] // unique)
    ]
    shape = (unique,) + weights.shape[2:4] + (2 * weights.shape[4],)
    out = pl.BlockSpec((per_step,) + shape[1:], lambda s: (first + s, 0, 0, 0))
    return pieces, out, jax.ShapeDtypeStruct(shape, F32)


def forward_kernel(z_high, z_low, y_both, field_ref, *refs, channels, step_channels, per_step):
    *pieces, out_ref, folded_ref = refs
    step = pl.program_id(0)
    for at in range(per_step):
        fold_block(pieces, folded_ref, at)
    for g in range(0, step_channels, GROUP):
        fields = [field_ref[g + q] for q in range(GROUP)]
        first = step * step_channels + g
        forward_group(fields, z_high[...], z_low[...], y_both[...], out_ref, first, channels)


def forward_modes(field, tables, weights, unique):
    channels = field.shape[0]
    step_channels = 8
    steps = channels // step_channels
    per_step = unique // 2 // steps
    pieces, folded, folded_shape = fold_specs(weights, unique, per_step, 0)
    owners = MY // 2
    out, half = pl.pallas_call(
        functools.partial(forward_kernel, channels=channels, step_channels=step_channels, per_step=per_step),
        grid=(steps,),
        in_specs=[full(t.shape) for t in tables]
        + [pl.BlockSpec((step_channels, NY, NZ), lambda s: (s, 0, 0))]
        + pieces,
        out_specs=[full((owners * channels, LANES)), folded],
        out_shape=[jax.ShapeDtypeStruct((owners * channels, LANES), F32), folded_shape],
        compiler_params=params(60),
        cost_estimate=pl.CostEstimate(flops=2 * 10**9, bytes_accessed=26 * MIB, transcendentals=0),
        name="forward_yz",
    )(*tables, field, *([weights] * len(pieces)))
    return out.reshape(owners, channels, LANES), half


def fold_kernel(*refs):
    *pieces, _, out_ref = refs
    fold_block(pieces, out_ref, 0)


def fold_rest(weights, half, unique):
    first = unique // 2
    pieces, folded, folded_shape = fold_specs(weights, unique, 1, first)
    return pl.pallas_call(
        fold_kernel,
        grid=(unique - first,),
        in_specs=pieces + [pl.BlockSpec(memory_space=pl.ANY)],
        out_specs=folded,
        out_shape=folded_shape,
        input_output_aliases={len(pieces): 0},
        compiler_params=params(60),
        cost_estimate=pl.CostEstimate(flops=4 * 10**6, bytes_accessed=20 * MIB, transcendentals=0),
        name="fold_weights",
    )(*([weights] * len(pieces)), half)


def spectrum_row(cos_ref, sin_ref, lines_ref, turned_ref, at, points):
    total = cos_ref[at, 0] * lines_ref[0] + sin_ref[at, 0] * turned_ref[0]
    for x in range(1, points):
        total += cos_ref[at, x] * lines_ref[x] + sin_ref[at, x] * turned_ref[x]
    return total


def turn_lines(lines_ref, turned_ref, points, channels):
    sign = jnp.where(lane_index((channels, LANES)) < LANES // 2, 1.0, -1.0)
    for x in range(points):
        turned_ref[x] = sign * roll(lines_ref[x, :channels], 64)


def doubled(values):
    other = roll(values, 64)
    low = lane_index(values.shape) < LANES // 2
    return jnp.where(low, values, other), jnp.where(low, other, values)


def mix_kernel(cos_ref, sin_ref, lines_ref, weights_ref, spec_ref, out_ref, turned_ref, real_ref, imag_ref, *, points, channels, per_step, norm):
    step = pl.program_id(0)

    @pl.when(step == 0)
    def _():
        turn_lines(lines_ref, turned_ref, points, channels)
        out_ref[...] = jnp.zeros_like(out_ref)

    low = lane_index((channels, LANES)) < LANES // 2

    @pl.loop(0, per_step)
    def _(q):
        at = step * per_step + q
        spec = norm * spectrum_row(cos_ref, sin_ref, lines_ref, turned_ref, at, points)
        spec_ref[q] = spec
        real_ref[...], imag_ref[...] = doubled(spec)
        by_real = jnp.zeros((channels, LANES), F32)
        by_imag = jnp.zeros((channels, LANES), F32)
        for i in range(channels):
            weight = weights_ref[q, i]
            by_real += real_ref[pl.ds(i, 1), :] * weight
            by_imag += imag_ref[pl.ds(i, 1), :] * weight
        other = roll(by_imag, 64)
        mixed = by_real + jnp.where(low, -other, other)
        other = roll(mixed, 64)
        turned = jnp.where(low, -other, other)
        for x in range(points):
            out_ref[x] += cos_ref[at, x] * mixed + sin_ref[at, x] * turned


def smem():
    return pl.BlockSpec(memory_space=pltpu.SMEM)


def mix(cos_x, sin_x, lines, weights, norm):
    points, channels, _ = lines.shape
    unique = weights.shape[0]
    per_step = min(unique, 4)
    shape = (points, channels, LANES)
    return pl.pallas_call(
        functools.partial(mix_kernel, points=points, channels=channels, per_step=per_step, norm=norm),
        grid=(unique // per_step,),
        in_specs=[
            smem(),
            smem(),
            full(shape),
            pl.BlockSpec((per_step,) + weights.shape[1:], lambda s: (s, 0, 0, 0)),
        ],
        out_specs=[
            pl.BlockSpec((per_step, channels, LANES), lambda s: (s, 0, 0)),
            full(shape),
        ],
        out_shape=[
            jax.ShapeDtypeStruct((unique, channels, LANES), F32),
            jax.ShapeDtypeStruct(shape, F32),
        ],
        scratch_shapes=[
            pltpu.VMEM(shape, F32),
            pltpu.VMEM((channels, LANES), F32),
            pltpu.VMEM((channels, LANES), F32),
        ],
        compiler_params=params(60),
        cost_estimate=pl.CostEstimate(flops=2 * 10**7, bytes_accessed=9 * MIB, transcendentals=0),
        name="mix_modes",
    )(cos_x, sin_x, lines, weights)


def exact_dot(left, right):
    return jnp.dot(left, right, precision=lax.Precision.HIGHEST, preferred_element_type=F32)


def pointwise_kernel(sum_ref, turned_ref, bias_in_ref, field_ref, out_ref, mixer_ref, bias_ref, *, channels, blocks):
    size = 8 * channels

    @pl.when(pl.program_id(0) == 0)
    def _():
        wide = exact_dot(sum_ref[...], turned_ref[...])
        wide = lax.dot_general(
            wide, sum_ref[...], (((1,), (1,)), ((), ())), precision=lax.Precision.HIGHEST, preferred_element_type=F32
        )
        row = lax.broadcasted_iota(jnp.int32, (size, size), 0) % 8
        high, low = split(jnp.where(row == lane_index((size, size)) % 8, wide, 0.0))
        mixer_ref[:size] = high
        mixer_ref[size:] = low
        bias_ref[...] = exact_dot(sum_ref[...], bias_in_ref[...])

    for b in range(blocks):
        high, low = split(field_ref[:, 8 * b : 8 * b + 8, :].reshape(size, NZ))
        wide = dot(mixer_ref[...], high)
        values = wide[:size] + wide[size:] + dot(mixer_ref[:size], low) + bias_ref[...]
        out_ref[:, 8 * b : 8 * b + 8, :] = values.reshape(channels, 8, NZ)


def pointwise(field, summing, point_weights, point_bias):
    channels = field.shape[0]
    blocks = 2
    turned = point_weights.T
    bias = point_bias[:, None]
    size = 8 * channels
    block = pl.BlockSpec((channels, 8 * blocks, NZ), lambda s: (0, s, 0))
    return pl.pallas_call(
        functools.partial(pointwise_kernel, channels=channels, blocks=blocks),
        grid=(NY // (8 * blocks),),
        in_specs=[full(summing.shape), full(turned.shape), full(bias.shape), block],
        out_specs=block,
        out_shape=jax.ShapeDtypeStruct(field.shape, F32),
        scratch_shapes=[pltpu.VMEM((2 * size, size), BF16), pltpu.VMEM((size, 1), F32)],
        compiler_params=params(60),
        cost_estimate=pl.CostEstimate(flops=4 * 10**9, bytes_accessed=24 * MIB, transcendentals=0),
        name="pointwise",
    )(summing, turned, bias, field)


def cell_kernel(
    inv_y, inv_z, inv_z_low, z_high, z_low, y_both, sum_ref, modes_ref, pre_ref, cot_ref, field_hbm,
    act_ref, out_ref, field_ref, slope_high, slope_low, sem, *, channels, rows, owners,
):
    step = pl.program_id(0)
    copy = pltpu.make_async_copy(field_hbm, field_ref, sem)

    @pl.when(step == 0)
    def _():
        copy.start()

    first = step * GROUP
    lines = inverse_y_group(modes_ref, inv_y[...], first, channels)
    lines = jnp.concatenate([lines[:, q * LANES : (q + 1) * LANES] for q in range(GROUP // 2)], axis=0)
    high, low = split(lines)
    spectral = dot(jnp.concatenate([high, low], axis=1), inv_z[...]) + dot(high, inv_z_low[...])
    slopes = []
    for q in range(GROUP):
        r = q // 2 * NY
        c = q % 2 * NZ
        before = spectral[r : r + NY, c : c + NZ] + pre_ref[q]
        cdf = 0.5 + 0.5 * lax.erf(before * INV_SQRT_TWO)
        act_ref[q] = (before * cdf).astype(BF16)
        pdf = jnp.exp(-0.5 * before * before) * INV_SQRT_TWO_PI
        slope = cot_ref[q].astype(F32) * (cdf + before * pdf)
        slopes.append(slope)
        high, low = split(slope)
        slope_high[first + q] = high
        slope_low[first + q] = low
    forward_group(slopes, z_high[...], z_low[...], y_both[...], out_ref, first, rows)

    @pl.when(step == pl.num_programs(0) - 1)
    def _():
        copy.wait()
        size = 8 * channels
        total = jnp.zeros((size, size), F32)
        nt = (((1,), (1,)), ((), ()))
        for b in range(NY // 16):
            at = pl.ds(16 * b, 16)
            field_high, field_low = split(field_ref[:, at, :])
            s_high, s_low = slope_high[:, at, :], slope_low[:, at, :]
            for h in range(2):
                part = slice(8 * h, 8 * h + 8)
                f_h = field_high[:, part].reshape(size, NZ)
                f_l = field_low[:, part].reshape(size, NZ)
                s_h = s_high[:, part].reshape(size, NZ)
                s_l = s_low[:, part].reshape(size, NZ)
                total += lax.dot_general(f_h, s_h, nt, preferred_element_type=F32)
                total += lax.dot_general(f_h, s_l, nt, preferred_element_type=F32)
                total += lax.dot_general(f_l, s_h, nt, preferred_element_type=F32)
        row = lax.broadcasted_iota(jnp.int32, (size, size), 0) % 8
        total = jnp.where(row == lane_index((size, size)) % 8, total, 0.0)
        folded = jnp.sum(total.reshape(channels, 8, size), axis=1)
        point = exact_dot(folded, sum_ref[...])
        packed = jnp.concatenate([point[8 * q : 8 * q + 8] for q in range(channels // 8)], axis=1)
        dc = jnp.broadcast_to(out_ref[0:channels, 0:1], (channels, LANES))
        eye = lax.broadcasted_iota(jnp.int32, (channels, LANES), 0) == lane_index((channels, LANES))
        bias = jnp.sum(jnp.where(eye, dc, 0.0), axis=0, keepdims=True)
        extra = jnp.where(lax.broadcasted_iota(jnp.int32, (8, LANES), 0) == 0, jnp.broadcast_to(bias, (8, LANES)), 0.0)
        for d in range(owners):
            out_ref[d * rows + channels : d * rows + channels + 8, :] = packed
            out_ref[d * rows + channels + 8 : (d + 1) * rows, :] = extra


def cell_stage(inverse, forward, summing, modes, pre, cotangent, field):
    channels = field.shape[0]
    owners = MY // 2
    rows = channels + 16
    block = pl.BlockSpec((GROUP, NY, NZ), lambda s: (s, 0, 0))
    tables = (*inverse, *forward, summing)
    act, out = pl.pallas_call(
        functools.partial(cell_kernel, channels=channels, rows=rows, owners=owners),
        grid=(channels // GROUP,),
        in_specs=[full(t.shape) for t in tables]
        + [full((owners * channels, LANES)), block, block, pl.BlockSpec(memory_space=pl.ANY)],
        out_specs=[block, full((owners * rows, LANES))],
        out_shape=[
            jax.ShapeDtypeStruct((channels, NY, NZ), BF16),
            jax.ShapeDtypeStruct((owners * rows, LANES), F32),
        ],
        scratch_shapes=[
            pltpu.VMEM((channels, NY, NZ), F32),
            pltpu.VMEM((channels, NY, NZ), BF16),
            pltpu.VMEM((channels, NY, NZ), BF16),
            pltpu.SemaphoreType.DMA,
        ],
        compiler_params=params(60),
        cost_estimate=pl.CostEstimate(flops=8 * 10**9, bytes_accessed=12 * MIB, transcendentals=2 * 10**6),
        name="cells",
    )(*tables, modes.reshape(owners * channels, LANES), pre, cotangent, field)
    return act, out.reshape(owners, rows, LANES)


def gradient_kernel(
    cos_ref, sin_ref, spec_ref, lines_ref, out_hbm, point_ref, bias_ref,
    turned_ref, slope_ref, flip_ref, real_ref, imag_ref, buffer, sems, *, points, channels, unique, copies, norm,
):
    turn_lines(lines_ref, turned_ref, points, channels)
    half = LANES // 2
    lane = lane_index((channels, LANES))
    scale = jnp.where(lane % MZ == 0, norm, 2.0 * norm)
    packed = lines_ref[0, channels : channels + 16, :]
    for x in range(1, points):
        packed += lines_ref[x, channels : channels + 16, :]
    packed = norm * packed
    for q in range(channels // 8):
        point_ref[8 * q : 8 * q + 8, :] = packed[:8, q * channels : (q + 1) * channels]
    bias_ref[...] = packed[8:9, :channels]

    def writes(at, slot):
        return [
            pltpu.make_async_copy(buffer.at[slot], out_hbm.at[:, at + r * unique], sems.at[slot, r])
            for r in range(copies)
        ]

    @pl.loop(0, unique)
    def _(at):
        slot = at % 2

        @pl.when(at >= 2)
        def _():
            for copy in writes(at - 2, slot):
                copy.wait()

        total = cos_ref[at, 0] * lines_ref[0, :channels] + sin_ref[at, 0] * turned_ref[0]
        for x in range(1, points):
            total += cos_ref[at, x] * lines_ref[x, :channels] + sin_ref[at, x] * turned_ref[x]
        slope = scale * total
        other = roll(slope, 64)
        flipped = jnp.where(lane < half, other, -other)
        real_ref[...], imag_ref[...] = doubled(spec_ref[at])
        for i in range(channels):
            both = real_ref[pl.ds(i, 1), :] * slope + imag_ref[pl.ds(i, 1), :] * flipped
            buffer[slot, 0, i] = both[:, :half]
            buffer[slot, 1, i] = both[:, half:]
        for copy in writes(at, slot):
            copy.start()

    for at in range(max(unique - 2, 0), unique):
        for copy in writes(at, at % 2):
            copy.wait()


def gradient(cos_x, sin_x, spectrum, lines, norm, kept_x):
    points, rows, _ = lines.shape
    unique, channels, _ = spectrum.shape
    half = LANES // 2
    copies = kept_x // unique
    flat = (channels, LANES)
    return pl.pallas_call(
        functools.partial(gradient_kernel, points=points, channels=channels, unique=unique, copies=copies, norm=norm),
        in_specs=[smem(), smem(), full(spectrum.shape), full(lines.shape)],
        out_specs=[pl.BlockSpec(memory_space=pl.ANY), full((channels, channels)), full((1, channels))],
        out_shape=[
            jax.ShapeDtypeStruct((2, kept_x, channels, channels, half), F32),
            jax.ShapeDtypeStruct((channels, channels), F32),
            jax.ShapeDtypeStruct((1, channels), F32),
        ],
        scratch_shapes=[
            pltpu.VMEM((points, channels, LANES), F32),
            pltpu.VMEM(flat, F32),
            pltpu.VMEM(flat, F32),
            pltpu.VMEM(flat, F32),
            pltpu.VMEM(flat, F32),
            pltpu.VMEM((2, 2, channels, channels, half), F32),
            pltpu.SemaphoreType.DMA((2, copies)),
        ],
        compiler_params=params(60),
        cost_estimate=pl.CostEstimate(flops=10**7, bytes_accessed=40 * MIB, transcendentals=0),
        name="weight_gradient",
    )(cos_x, sin_x, spectrum, lines)


def swap(lines):
    return lax.all_to_all(lines, "space", split_axis=0, concat_axis=0, tiled=True)


def suits(width_x, length_x, devices, channels, weights):
    held = weights.shape[2]
    even = np.array_equal(kept(MX, length_x) % length_x, np.arange(MX) % length_x)
    return (
        width_x == 1
        and held == 2 * MZ
        and devices * 2 == MY
        and 2 * held == LANES
        and MX % length_x == 0
        and even
        and channels == MZ
    )


def body(lifted_field, cotangent, spectral_weights, point_weights, point_bias):
    devices = lax.axis_size("space")
    channels, width_x = lifted_field.shape[:2]
    length_x = width_x * devices
    if not suits(width_x, length_x, devices, channels, spectral_weights):
        return general_body(lifted_field, cotangent, spectral_weights, point_weights, point_bias)
    norm = float(length_x * NY * NZ) ** -0.5
    theta = angles(np.arange(length_x), np.arange(length_x), length_x)
    cos_x, sin_x = jnp.asarray(np.cos(theta), F32), jnp.asarray(np.sin(theta), F32)
    forward = forward_tables()
    inverse = inverse_tables(norm)
    summing = jnp.asarray(np.repeat(np.eye(channels), 8, axis=0), F32)

    field = lifted_field.reshape(channels, NY, NZ)
    slopes_in = cotangent.reshape(channels, NY, NZ)
    weights = jnp.transpose(spectral_weights, (0, 1, 3, 4, 2))

    lines, half = forward_modes(field, forward, weights, length_x)
    lines = swap(lines)
    folded = fold_rest(weights, half, length_x)
    spectrum, mixed = mix(cos_x, sin_x, lines, folded, norm)
    field_late, mixed = lax.optimization_barrier((field, mixed))
    modes = swap(mixed)
    pre = pointwise(field_late, summing, point_weights, point_bias)
    activated, slope_lines = cell_stage(inverse, forward, summing, modes, pre, slopes_in, field)
    slope_lines = swap(slope_lines)
    grad, grad_point, grad_bias = gradient(cos_x, sin_x, spectrum, slope_lines, norm, MX)
    return (
        activated.reshape(cotangent.shape),
        jnp.transpose(grad, (0, 1, 4, 2, 3)),
        grad_point,
        grad_bias.reshape(channels),
    )


HIGHEST = lax.Precision.HIGHEST


def trig_tables(positions, frequency, length):
    product = positions[:, None] * frequency[None, :] % length
    phase_angle = 2.0 * jnp.pi / length * product.astype(jnp.float32)
    return (jnp.cos(phase_angle), jnp.sin(phase_angle))


def kept_frequencies(kept_count, length):
    mode_index = jnp.arange(kept_count, dtype=jnp.int32)
    return jnp.where(mode_index < kept_count // 2, mode_index, length - kept_count + mode_index)


def forward_local(field_in):
    channels = field_in.shape[0]
    width_x = field_in.shape[1]
    cos_z, sin_z = trig_tables(jnp.arange(NZ, dtype=jnp.int32), jnp.arange(MZ, dtype=jnp.int32), NZ)
    table_z = jnp.concatenate([cos_z, -sin_z], axis=1)
    along_z = jnp.einsum("cxyz,zk->cxyk", field_in, table_z, precision=HIGHEST)
    z_real = along_z[..., :MZ]
    z_imag = along_z[..., MZ:]
    cos_y, sin_y = trig_tables(jnp.arange(NY, dtype=jnp.int32), kept_frequencies(MY, NY), NY)
    y_real = jnp.einsum("cxyk,yj->xcjk", z_real, cos_y, precision=HIGHEST) + jnp.einsum(
        "cxyk,yj->xcjk", z_imag, sin_y, precision=HIGHEST
    )
    y_imag = jnp.einsum("cxyk,yj->xcjk", z_imag, cos_y, precision=HIGHEST) - jnp.einsum(
        "cxyk,yj->xcjk", z_real, sin_y, precision=HIGHEST
    )
    stacked = jnp.stack([y_real, y_imag], axis=1)
    return stacked.reshape(width_x, 2, channels, MY * MZ)


def transform_x(x_lines):
    length_x = x_lines.shape[0]
    cos_x, sin_x = trig_tables(
        jnp.arange(length_x, dtype=jnp.int32), kept_frequencies(MX, length_x), length_x
    )
    norm_scale = 1.0 / float(length_x * NY * NZ) ** 0.5
    part_real = x_lines[:, 0]
    part_imag = x_lines[:, 1]
    x_real = jnp.einsum("xcm,xk->kcm", part_real, cos_x, precision=HIGHEST) + jnp.einsum(
        "xcm,xk->kcm", part_imag, sin_x, precision=HIGHEST
    )
    x_imag = jnp.einsum("xcm,xk->kcm", part_imag, cos_x, precision=HIGHEST) - jnp.einsum(
        "xcm,xk->kcm", part_real, sin_x, precision=HIGHEST
    )
    return norm_scale * jnp.stack([x_real, x_imag], axis=1)


def mix_modes(spectrum, weights):
    spec_real = spectrum[:, 0]
    spec_imag = spectrum[:, 1]
    out_real = jnp.einsum("kim,kmio->kom", spec_real, weights[0], precision=HIGHEST) - jnp.einsum(
        "kim,kmio->kom", spec_imag, weights[1], precision=HIGHEST
    )
    out_imag = jnp.einsum("kim,kmio->kom", spec_real, weights[1], precision=HIGHEST) + jnp.einsum(
        "kim,kmio->kom", spec_imag, weights[0], precision=HIGHEST
    )
    return jnp.stack([out_real, out_imag], axis=1)


def inverse_x(spectrum, positions, length_x):
    cos_x, sin_x = trig_tables(positions, kept_frequencies(MX, length_x), length_x)
    spec_real = spectrum[:, 0]
    spec_imag = spectrum[:, 1]
    a_real = jnp.einsum("kcm,xk->xcm", spec_real, cos_x, precision=HIGHEST) - jnp.einsum(
        "kcm,xk->xcm", spec_imag, sin_x, precision=HIGHEST
    )
    a_imag = jnp.einsum("kcm,xk->xcm", spec_imag, cos_x, precision=HIGHEST) + jnp.einsum(
        "kcm,xk->xcm", spec_real, sin_x, precision=HIGHEST
    )
    return jnp.stack([a_real, a_imag], axis=1)


def inverse_yz(x_lines, length_x):
    width_x = x_lines.shape[0]
    channels = x_lines.shape[2]
    mode_grid = x_lines.reshape(width_x, 2, channels, MY, MZ)
    cos_y, sin_y = trig_tables(jnp.arange(NY, dtype=jnp.int32), kept_frequencies(MY, NY), NY)
    b_real = jnp.einsum("xcjk,yj->cxyk", mode_grid[:, 0], cos_y, precision=HIGHEST) - jnp.einsum(
        "xcjk,yj->cxyk", mode_grid[:, 1], sin_y, precision=HIGHEST
    )
    b_imag = jnp.einsum("xcjk,yj->cxyk", mode_grid[:, 1], cos_y, precision=HIGHEST) + jnp.einsum(
        "xcjk,yj->cxyk", mode_grid[:, 0], sin_y, precision=HIGHEST
    )
    cos_z, sin_z = trig_tables(jnp.arange(NZ, dtype=jnp.int32), jnp.arange(MZ, dtype=jnp.int32), NZ)
    weight_z = jnp.where(jnp.arange(MZ, dtype=jnp.int32) == 0, 1.0, 2.0).astype(jnp.float32)
    table_z = jnp.concatenate([cos_z * weight_z[None, :], -sin_z * weight_z[None, :]], axis=1)
    stacked = jnp.concatenate([b_real, b_imag], axis=-1)
    result = jnp.einsum("cxyk,zk->cxyz", stacked, table_z, precision=HIGHEST)
    return result * (1.0 / float(length_x * NY * NZ) ** 0.5)


def gelu_slope(values):
    return (
        0.5 * (1.0 + lax.erf(values * INV_SQRT_TWO))
        + values * jnp.exp(-0.5 * values * values) * INV_SQRT_TWO_PI
    )


def weight_gradient(spectrum, slope_modes, first_mode):
    mode_ids = first_mode + jnp.arange(spectrum.shape[3], dtype=jnp.int32)
    weight_modes = jnp.where(mode_ids % MZ == 0, 1.0, 2.0).astype(jnp.float32)
    grad_real = jnp.einsum(
        "kim,kom->kmio", spectrum[:, 0], slope_modes[:, 0], precision=HIGHEST
    ) + jnp.einsum("kim,kom->kmio", spectrum[:, 1], slope_modes[:, 1], precision=HIGHEST)
    grad_imag = jnp.einsum(
        "kim,kom->kmio", spectrum[:, 0], slope_modes[:, 1], precision=HIGHEST
    ) - jnp.einsum("kim,kom->kmio", spectrum[:, 1], slope_modes[:, 0], precision=HIGHEST)
    stacked = jnp.stack([grad_real, grad_imag], axis=0)
    return stacked * weight_modes[None, None, :, None, None]


def to_modes(field_in):
    return transform_x(
        lax.all_to_all(forward_local(field_in), "space", split_axis=3, concat_axis=0, tiled=True)
    )


def general_body(lifted_field, cotangent, spectral_weights, point_weights, point_bias):
    devices = lax.axis_size("space")
    width_x = lifted_field.shape[1]
    length_x = width_x * devices
    spectrum = to_modes(lifted_field)
    mixed_modes = mix_modes(spectrum, spectral_weights)
    full_lines = inverse_x(mixed_modes, jnp.arange(length_x, dtype=jnp.int32), length_x)
    spectral = inverse_yz(
        lax.all_to_all(full_lines, "space", split_axis=0, concat_axis=3, tiled=True), length_x
    )
    pointwise = (
        jnp.einsum("ixyz,io->oxyz", lifted_field, point_weights, precision=HIGHEST)
        + point_bias[:, None, None, None]
    )
    before = spectral + pointwise
    activated = jax.nn.gelu(before, approximate=False).astype(jnp.bfloat16)
    slope_field = cotangent.astype(jnp.float32) * gelu_slope(before)
    local_point = jnp.einsum("ixyz,oxyz->io", lifted_field, slope_field, precision=HIGHEST)
    local_bias = jnp.sum(slope_field, axis=(1, 2, 3))
    partial = jnp.concatenate([local_point, local_bias[None, :]], axis=0)
    gathered = lax.all_gather(partial, "space", axis=0, tiled=False)
    summed = jnp.sum(gathered, axis=0)
    summed_point, summed_bias = summed[:-1], summed[-1]
    root_cells = float(length_x * NY * NZ) ** 0.5
    slope_spectrum = to_modes(slope_field)
    first_mode = lax.axis_index("space") * spectrum.shape[3]
    grad_spectral = weight_gradient(spectrum, slope_spectrum, first_mode)
    return (activated, grad_spectral, summed_point / root_cells, summed_bias / root_cells)


def solution(mesh):
    placed = (
        P("groups", "space", None, None),
        P("groups", "space", None, None),
        P(None, None, "space", None, None),
        P(),
        P(),
    )
    return jax.shard_map(
        body,
        mesh=mesh,
        in_specs=placed,
        out_specs=(
            P("groups", "space", None, None),
            P("groups", None, "space", None, None),
            P("groups", None),
            P("groups"),
        ),
        check_vma=False,
    )
```

```python
import functools

import jax
import jax.numpy as jnp
import ml_dtypes
import numpy as np
from jax import lax
from jax.experimental import pallas as pl
from jax.experimental.pallas import tpu as pltpu
from jax.sharding import PartitionSpec as P

MX = 32
MY = 32
MZ = 32
NY = 128
NZ = 256

F32 = jnp.float32
BF16 = jnp.bfloat16
INV_SQRT_TWO = 0.7071067811865476
INV_SQRT_TWO_PI = 0.3989422804014327
MIB = 1 << 20
LANES = 128
GROUP = 4
STEP = 16


def kept(kept_count, length):
    index = np.arange(kept_count)
    return np.where(index < kept_count // 2, index, length - kept_count + index)


def angles(positions, frequency, length):
    product = positions[:, None] * frequency[None, :] % length
    return 2.0 * np.pi / length * product


def split_table(table):
    high = table.astype(ml_dtypes.bfloat16)
    return high, (table - high.astype(np.float64)).astype(ml_dtypes.bfloat16)


def lane_spread(first, second, real_table, imag_table):
    return np.concatenate(
        [real_table * first, real_table * second, imag_table * first, imag_table * second], axis=1
    )


def forward_tables():
    theta = angles(np.arange(NZ), np.arange(MZ), NZ)
    cos_z, sin_z = np.cos(theta), np.sin(theta)
    plain = [lane_spread(f, s, cos_z, -sin_z) for f, s in ((1, 0), (0, 1))]
    turned = [lane_spread(f, s, -sin_z, -cos_z) for f, s in ((1, 0), (0, 1))]
    table_z = np.concatenate([np.concatenate(plain, 0), np.concatenate(turned, 0)], axis=1)
    theta = angles(np.arange(NY), kept(MY, NY), NY)
    both = np.concatenate([np.cos(theta).T, np.sin(theta).T], axis=1)
    table_y = np.concatenate([both[0::2], both[1::2]], axis=0)
    z_high, z_low = split_table(table_z)
    y_high, y_low = split_table(table_y)
    return z_high, z_low, np.concatenate([y_high, y_low], axis=0)


def inverse_tables(norm):
    theta = angles(np.arange(NY), kept(MY, NY), NY)
    cos_y, sin_y = np.cos(theta), np.sin(theta)
    table_y = np.concatenate([cos_y[:, 0::2], cos_y[:, 1::2], sin_y[:, 0::2], sin_y[:, 1::2]], axis=1)
    y_high, y_low = split_table(table_y)
    theta = angles(np.arange(NZ), np.arange(MZ), NZ)
    weight = np.where(np.arange(MZ) == 0, 1.0, 2.0) * norm
    cos_z, sin_z = np.cos(theta) * weight, -np.sin(theta) * weight
    table_z = np.concatenate([lane_spread(f, s, cos_z, sin_z).T for f, s in ((1, 0), (0, 1))], axis=1)
    z_high, z_low = split_table(table_z)
    return (
        np.concatenate([y_high, y_high, y_low], axis=1),
        np.concatenate([z_high, z_high], axis=0),
        z_low,
    )


def dot(left, right):
    return jnp.dot(left, right, preferred_element_type=F32)


def split(values):
    high = values.astype(BF16)
    return high, (values - high.astype(F32)).astype(BF16)


def lane_index(shape):
    return lax.broadcasted_iota(jnp.int32, shape, len(shape) - 1)


def roll(values, shift):
    return pltpu.roll(values, shift % LANES, len(values.shape) - 1)


def forward_group(fields, z_high, z_low, y_both, out_ref, first, rows):
    left = jnp.concatenate(
        [jnp.concatenate([fields[q], fields[q + 1]], axis=1) for q in range(0, len(fields), 2)], axis=0
    )
    high, low = split(left)
    lines = dot(high, z_high) + dot(high, z_low) + dot(low, z_high)
    half = MY // 2
    for g in range(0, len(fields) // 2, GROUP // 2):
        pairs = []
        for q in range(g, g + GROUP // 2):
            part = lines[q * NY : (q + 1) * NY]
            pairs.append(jnp.concatenate([part[:, :LANES], part[:, LANES:]], axis=0))
        high, low = split(jnp.concatenate(pairs, axis=1))
        wide = dot(y_both, high)
        modes = wide[:MY] + wide[MY:] + dot(y_both[:MY], low)
        for q in range(GROUP // 2):
            even = modes[:half, q * LANES : (q + 1) * LANES]
            odd = modes[half:, q * LANES : (q + 1) * LANES]
            at_even = (lane_index(even.shape) // MZ) % 2 == 0
            at = first + 2 * (g + q)
            out_ref[pl.ds(at, half, stride=rows), :] = jnp.where(at_even, even, roll(odd, MZ))
            out_ref[pl.ds(at + 1, half, stride=rows), :] = jnp.where(at_even, roll(even, -MZ), odd)


def inverse_y_group(modes_ref, y_table, first, rows):
    half = MY // 2
    pairs = []
    for q in range(GROUP // 2):
        c0 = modes_ref[pl.ds(first + 2 * q, half, stride=rows), :]
        c1 = modes_ref[pl.ds(first + 2 * q + 1, half, stride=rows), :]
        at_even = (lane_index(c0.shape) // MZ) % 2 == 0
        even = jnp.where(at_even, c0, roll(c1, MZ))
        odd = jnp.where(at_even, roll(c0, -MZ), c1)
        both = jnp.concatenate([even, odd], axis=0)
        other = roll(both, 64)
        turned = jnp.where(lane_index(both.shape) < LANES // 2, -other, other)
        pairs.append(jnp.concatenate([both, turned], axis=0))
    high, low = split(jnp.concatenate(pairs, axis=1))
    lines = dot(y_table, jnp.concatenate([high, low, high], axis=0))
    return [lines[:, q * LANES : (q + 1) * LANES] for q in range(GROUP // 2)]


def full(shape):
    return pl.BlockSpec(shape, lambda *_: (0,) * len(shape))


def params(limit):
    return pltpu.CompilerParams(vmem_limit_bytes=limit * MIB)


def fold_block(pieces, out_ref, at):
    real, imag = pieces[0][0, at], pieces[0][1, at]
    for piece in pieces[1:]:
        real, imag = real + piece[0, at], imag + piece[1, at]
    modes = real.shape[-1]
    out_ref[at, :, :, :modes] = real
    out_ref[at, :, :, modes:] = imag


def fold_specs(weights, unique, per_step, first):
    block = (2, per_step) + weights.shape[2:]
    pieces = [
        pl.BlockSpec(block, functools.partial(lambda s, r: (0, first + s + r, 0, 0, 0), r=r * (unique // per_step)))
        for r in range(weights.shape[1] // unique)
    ]
    shape = (unique,) + weights.shape[2:4] + (2 * weights.shape[4],)
    out = pl.BlockSpec((per_step,) + shape[1:], lambda s: (first + s, 0, 0, 0))
    return pieces, out, jax.ShapeDtypeStruct(shape, F32)


def forward_kernel(z_high, z_low, y_both, field_ref, *refs, channels, step_channels, per_step):
    *pieces, out_ref, folded_ref = refs
    step = pl.program_id(0)
    for at in range(per_step):
        fold_block(pieces, folded_ref, at)
    fields = [field_ref[q] for q in range(step_channels)]
    forward_group(fields, z_high[...], z_low[...], y_both[...], out_ref, step * step_channels, channels)


def forward_modes(field, tables, weights, unique):
    channels = field.shape[0]
    step_channels = 8
    steps = channels // step_channels
    per_step = unique // 2 // steps
    pieces, folded, folded_shape = fold_specs(weights, unique, per_step, 0)
    owners = MY // 2
    out, half = pl.pallas_call(
        functools.partial(forward_kernel, channels=channels, step_channels=step_channels, per_step=per_step),
        grid=(steps,),
        in_specs=[full(t.shape) for t in tables]
        + [pl.BlockSpec((step_channels, NY, NZ), lambda s: (s, 0, 0))]
        + pieces,
        out_specs=[full((owners * channels, LANES)), folded],
        out_shape=[jax.ShapeDtypeStruct((owners * channels, LANES), F32), folded_shape],
        compiler_params=params(60),
        cost_estimate=pl.CostEstimate(flops=2 * 10**9, bytes_accessed=26 * MIB, transcendentals=0),
        name="forward_yz",
    )(*tables, field, *([weights] * len(pieces)))
    return out.reshape(owners, channels, LANES), half


def fold_kernel(*refs):
    *pieces, _, out_ref = refs
    fold_block(pieces, out_ref, 0)


def fold_rest(weights, half, unique):
    first = unique // 2
    pieces, folded, folded_shape = fold_specs(weights, unique, 1, first)
    return pl.pallas_call(
        fold_kernel,
        grid=(unique - first,),
        in_specs=pieces + [pl.BlockSpec(memory_space=pl.ANY)],
        out_specs=folded,
        out_shape=folded_shape,
        input_output_aliases={len(pieces): 0},
        compiler_params=params(60),
        cost_estimate=pl.CostEstimate(flops=4 * 10**6, bytes_accessed=20 * MIB, transcendentals=0),
        name="fold_weights",
    )(*([weights] * len(pieces)), half)


def halve_lines(lines_ref, sums_ref, points, channels):
    half = points // 2
    sign = jnp.where(lane_index((channels, LANES)) < LANES // 2, 1.0, -1.0)
    for x in range(half):
        near, far = lines_ref[x, :channels], lines_ref[x + half, :channels]
        for parity, value in enumerate((near + far, near - far)):
            sums_ref[parity, 0, x] = value
            sums_ref[parity, 1, x] = sign * roll(value, 64)


def spectrum_row(cos_ref, sin_ref, sums_ref, at, parity, half):
    total = cos_ref[at, 0] * sums_ref[parity, 0, 0] + sin_ref[at, 0] * sums_ref[parity, 1, 0]
    for x in range(1, half):
        total += cos_ref[at, x] * sums_ref[parity, 0, x] + sin_ref[at, x] * sums_ref[parity, 1, x]
    return total


def doubled(values):
    other = roll(values, 64)
    low = lane_index(values.shape) < LANES // 2
    return jnp.where(low, values, other), jnp.where(low, other, values)


def mix_kernel(
    cos_ref, sin_ref, lines_ref, weights_ref, spec_ref, out_ref, sums_ref, total_ref, real_ref, imag_ref,
    *, points, channels, per_step, norm,
):
    step = pl.program_id(0)
    half = points // 2

    @pl.when(step == 0)
    def _():
        halve_lines(lines_ref, sums_ref, points, channels)
        total_ref[...] = jnp.zeros_like(total_ref)

    low = lane_index((channels, LANES)) < LANES // 2
    for q in range(per_step):
        at = step * per_step + q
        parity = q % 2
        spec = norm * spectrum_row(cos_ref, sin_ref, sums_ref, at, parity, half)
        spec_ref[q] = spec
        real_ref[q], imag_ref[q] = doubled(spec)
        by_real = jnp.zeros((channels, LANES), F32)
        by_imag = jnp.zeros((channels, LANES), F32)
        for i in range(channels):
            weight = weights_ref[q, i]
            by_real += real_ref[q, pl.ds(i, 1), :] * weight
            by_imag += imag_ref[q, pl.ds(i, 1), :] * weight
        other = roll(by_imag, 64)
        mixed = by_real + jnp.where(low, -other, other)
        other = roll(mixed, 64)
        turned = jnp.where(low, -other, other)
        for x in range(half):
            total_ref[parity, x] += cos_ref[at, x] * mixed + sin_ref[at, x] * turned

    @pl.when(step == pl.num_programs(0) - 1)
    def _():
        for x in range(half):
            out_ref[x] = total_ref[0, x] + total_ref[1, x]
            out_ref[x + half] = total_ref[0, x] - total_ref[1, x]


def smem():
    return pl.BlockSpec(memory_space=pltpu.SMEM)


def mix(cos_x, sin_x, lines, weights, norm):
    points, channels, _ = lines.shape
    unique = weights.shape[0]
    per_step = min(unique, 4)
    shape = (points, channels, LANES)
    return pl.pallas_call(
        functools.partial(mix_kernel, points=points, channels=channels, per_step=per_step, norm=norm),
        grid=(unique // per_step,),
        in_specs=[
            smem(),
            smem(),
            full(shape),
            pl.BlockSpec((per_step,) + weights.shape[1:], lambda s: (s, 0, 0, 0)),
        ],
        out_specs=[
            pl.BlockSpec((per_step, channels, LANES), lambda s: (s, 0, 0)),
            full(shape),
        ],
        out_shape=[
            jax.ShapeDtypeStruct((unique, channels, LANES), F32),
            jax.ShapeDtypeStruct(shape, F32),
        ],
        scratch_shapes=[
            pltpu.VMEM((2, 2, points // 2, channels, LANES), F32),
            pltpu.VMEM((2, points // 2, channels, LANES), F32),
            pltpu.VMEM((per_step, channels, LANES), F32),
            pltpu.VMEM((per_step, channels, LANES), F32),
        ],
        compiler_params=params(60),
        cost_estimate=pl.CostEstimate(flops=2 * 10**7, bytes_accessed=9 * MIB, transcendentals=0),
        name="mix_modes",
    )(cos_x, sin_x, lines, weights)


def exact_dot(left, right):
    return jnp.dot(left, right, precision=lax.Precision.HIGHEST, preferred_element_type=F32)


def pointwise_kernel(sum_ref, turned_ref, bias_in_ref, field_ref, out_ref, mixer_ref, bias_ref, *, channels, blocks):
    size = 8 * channels

    @pl.when(pl.program_id(0) == 0)
    def _():
        wide = exact_dot(sum_ref[...], turned_ref[...])
        wide = lax.dot_general(
            wide, sum_ref[...], (((1,), (1,)), ((), ())), precision=lax.Precision.HIGHEST, preferred_element_type=F32
        )
        row = lax.broadcasted_iota(jnp.int32, (size, size), 0) % 8
        high, low = split(jnp.where(row == lane_index((size, size)) % 8, wide, 0.0))
        mixer_ref[:size] = high
        mixer_ref[size:] = low
        bias_ref[...] = exact_dot(sum_ref[...], bias_in_ref[...])

    for b in range(blocks):
        high, low = split(field_ref[:, 8 * b : 8 * b + 8, :].reshape(size, NZ))
        wide = dot(mixer_ref[...], high)
        values = wide[:size] + wide[size:] + dot(mixer_ref[:size], low) + bias_ref[...]
        out_ref[:, 8 * b : 8 * b + 8, :] = values.reshape(channels, 8, NZ)


def pointwise(field, summing, point_weights, point_bias):
    channels = field.shape[0]
    blocks = 2
    turned = point_weights.T
    bias = point_bias[:, None]
    size = 8 * channels
    block = pl.BlockSpec((channels, 8 * blocks, NZ), lambda s: (0, s, 0))
    return pl.pallas_call(
        functools.partial(pointwise_kernel, channels=channels, blocks=blocks),
        grid=(NY // (8 * blocks),),
        in_specs=[full(summing.shape), full(turned.shape), full(bias.shape), block],
        out_specs=block,
        out_shape=jax.ShapeDtypeStruct(field.shape, F32),
        scratch_shapes=[pltpu.VMEM((2 * size, size), BF16), pltpu.VMEM((size, 1), F32)],
        compiler_params=params(60),
        cost_estimate=pl.CostEstimate(flops=4 * 10**9, bytes_accessed=24 * MIB, transcendentals=0),
        name="pointwise",
    )(summing, turned, bias, field)


def cell_kernel(
    inv_y, inv_z, inv_z_low, z_high, z_low, y_both, sum_ref, modes_ref, pre_ref, cot_ref, field_hbm,
    act_ref, out_ref, field_ref, slope_ref, sem, *, channels, step_channels, rows, owners,
):
    step = pl.program_id(0)
    copy = pltpu.make_async_copy(field_hbm, field_ref, sem)

    @pl.when(step == 0)
    def _():
        copy.start()

    first = step * step_channels
    lines = []
    for g in range(0, step_channels, GROUP):
        lines += inverse_y_group(modes_ref, inv_y[...], first + g, channels)
    high, low = split(jnp.concatenate(lines, axis=0))
    spectral = dot(jnp.concatenate([high, low], axis=1), inv_z[...]) + dot(high, inv_z_low[...])
    slopes = []
    for q in range(step_channels):
        r = q // 2 * NY
        c = q % 2 * NZ
        before = spectral[r : r + NY, c : c + NZ] + pre_ref[q]
        cdf = 0.5 + 0.5 * lax.erf(before * INV_SQRT_TWO)
        act_ref[q] = (before * cdf).astype(BF16)
        pdf = jnp.exp(-0.5 * before * before) * INV_SQRT_TWO_PI
        slope = cot_ref[q].astype(F32) * (cdf + before * pdf)
        slopes.append(slope)
        slope_ref[first + q] = slope
    forward_group(slopes, z_high[...], z_low[...], y_both[...], out_ref, first, rows)

    @pl.when(step == pl.num_programs(0) - 1)
    def _():
        copy.wait()
        size = 8 * channels
        total = jnp.zeros((size, size), F32)
        for b in range(NY // 8):
            at = slice(8 * b, 8 * b + 8)
            f_h, f_l = split(field_ref[:, at, :].reshape(size, NZ))
            s_h, s_l = split(slope_ref[:, at, :].reshape(size, NZ))
            total += lax.dot_general(
                jnp.concatenate([f_h, f_h, f_l], axis=1),
                jnp.concatenate([s_h, s_l, s_h], axis=1),
                (((1,), (1,)), ((), ())),
                preferred_element_type=F32,
            )
        row = lax.broadcasted_iota(jnp.int32, (size, size), 0) % 8
        total = jnp.where(row == lane_index((size, size)) % 8, total, 0.0)
        folded = jnp.sum(total.reshape(channels, 8, size), axis=1)
        point = exact_dot(folded, sum_ref[...])
        packed = jnp.concatenate([point[8 * q : 8 * q + 8] for q in range(channels // 8)], axis=1)
        dc = jnp.broadcast_to(out_ref[0:channels, 0:1], (channels, LANES))
        eye = lax.broadcasted_iota(jnp.int32, (channels, LANES), 0) == lane_index((channels, LANES))
        bias = jnp.sum(jnp.where(eye, dc, 0.0), axis=0, keepdims=True)
        extra = jnp.where(lax.broadcasted_iota(jnp.int32, (8, LANES), 0) == 0, jnp.broadcast_to(bias, (8, LANES)), 0.0)
        for d in range(owners):
            out_ref[d * rows + channels : d * rows + channels + 8, :] = packed
            out_ref[d * rows + channels + 8 : (d + 1) * rows, :] = extra


def cell_stage(inverse, forward, summing, modes, pre, cotangent, field):
    channels = field.shape[0]
    owners = MY // 2
    rows = channels + 16
    step_channels = STEP
    block = pl.BlockSpec((step_channels, NY, NZ), lambda s: (s, 0, 0))
    tables = (*inverse, *forward, summing)
    act, out = pl.pallas_call(
        functools.partial(cell_kernel, channels=channels, step_channels=step_channels, rows=rows, owners=owners),
        grid=(channels // step_channels,),
        in_specs=[full(t.shape) for t in tables]
        + [full((owners * channels, LANES)), block, block, pl.BlockSpec(memory_space=pl.ANY)],
        out_specs=[block, full((owners * rows, LANES))],
        out_shape=[
            jax.ShapeDtypeStruct((channels, NY, NZ), BF16),
            jax.ShapeDtypeStruct((owners * rows, LANES), F32),
        ],
        scratch_shapes=[
            pltpu.VMEM((channels, NY, NZ), F32),
            pltpu.VMEM((channels, NY, NZ), F32),
            pltpu.SemaphoreType.DMA,
        ],
        compiler_params=params(60),
        cost_estimate=pl.CostEstimate(flops=8 * 10**9, bytes_accessed=12 * MIB, transcendentals=2 * 10**6),
        name="cells",
    )(*tables, modes.reshape(owners * channels, LANES), pre, cotangent, field)
    return act, out.reshape(owners, rows, LANES)


def gradient_kernel(
    cos_ref, sin_ref, spec_ref, lines_ref, out_hbm, point_ref, bias_ref,
    sums_ref, real_ref, imag_ref, buffer, sems, *, points, channels, unique, copies, norm,
):
    halve_lines(lines_ref, sums_ref, points, channels)
    half = LANES // 2
    lane = lane_index((channels, LANES))
    scale = jnp.where(lane % MZ == 0, norm, 2.0 * norm)
    packed = lines_ref[0, channels : channels + 16, :]
    for x in range(1, points):
        packed += lines_ref[x, channels : channels + 16, :]
    packed = norm * packed
    for q in range(channels // 8):
        point_ref[8 * q : 8 * q + 8, :] = packed[:8, q * channels : (q + 1) * channels]
    bias_ref[...] = packed[8:9, :channels]

    def writes(at, slot):
        return [
            pltpu.make_async_copy(buffer.at[slot], out_hbm.at[:, at + r * unique], sems.at[slot, r])
            for r in range(copies)
        ]

    @pl.loop(0, unique // 2)
    def _(pair):
        for slot in range(2):
            at = 2 * pair + slot

            @pl.when(pair > 0)
            def _():
                for copy in writes(at - 2, slot):
                    copy.wait()

            slope = scale * spectrum_row(cos_ref, sin_ref, sums_ref, at, slot, points // 2)
            other = roll(slope, 64)
            flipped = jnp.where(lane < half, other, -other)
            real_ref[slot], imag_ref[slot] = doubled(spec_ref[at])
            for i in range(channels):
                both = real_ref[slot, pl.ds(i, 1), :] * slope + imag_ref[slot, pl.ds(i, 1), :] * flipped
                buffer[slot, 0, i] = both[:, :half]
                buffer[slot, 1, i] = both[:, half:]
            for copy in writes(at, slot):
                copy.start()

    for at in range(unique - 2, unique):
        for copy in writes(at, at % 2):
            copy.wait()


def gradient(cos_x, sin_x, spectrum, lines, norm, kept_x):
    points, rows, _ = lines.shape
    unique, channels, _ = spectrum.shape
    half = LANES // 2
    copies = kept_x // unique
    flat = (channels, LANES)
    return pl.pallas_call(
        functools.partial(gradient_kernel, points=points, channels=channels, unique=unique, copies=copies, norm=norm),
        in_specs=[smem(), smem(), full(spectrum.shape), full(lines.shape)],
        out_specs=[pl.BlockSpec(memory_space=pl.ANY), full((channels, channels)), full((1, channels))],
        out_shape=[
            jax.ShapeDtypeStruct((2, kept_x, channels, channels, half), F32),
            jax.ShapeDtypeStruct((channels, channels), F32),
            jax.ShapeDtypeStruct((1, channels), F32),
        ],
        scratch_shapes=[
            pltpu.VMEM((2, 2, points // 2, channels, LANES), F32),
            pltpu.VMEM((2,) + flat, F32),
            pltpu.VMEM((2,) + flat, F32),
            pltpu.VMEM((2, 2, channels, channels, half), F32),
            pltpu.SemaphoreType.DMA((2, copies)),
        ],
        compiler_params=params(60),
        cost_estimate=pl.CostEstimate(flops=10**7, bytes_accessed=40 * MIB, transcendentals=0),
        name="weight_gradient",
    )(cos_x, sin_x, spectrum, lines)


def swap(lines):
    return lax.all_to_all(lines, "space", split_axis=0, concat_axis=0, tiled=True)


def suits(width_x, length_x, devices, channels, weights):
    held = weights.shape[2]
    even = np.array_equal(kept(MX, length_x) % length_x, np.arange(MX) % length_x)
    return (
        width_x == 1
        and held == 2 * MZ
        and devices * 2 == MY
        and 2 * held == LANES
        and MX % length_x == 0
        and length_x % 8 == 0
        and even
        and channels == MZ
    )


def body(lifted_field, cotangent, spectral_weights, point_weights, point_bias):
    devices = lax.axis_size("space")
    channels, width_x = lifted_field.shape[:2]
    length_x = width_x * devices
    if not suits(width_x, length_x, devices, channels, spectral_weights):
        return general_body(lifted_field, cotangent, spectral_weights, point_weights, point_bias)
    norm = float(length_x * NY * NZ) ** -0.5
    theta = angles(np.arange(length_x), np.arange(length_x), length_x)
    cos_x, sin_x = jnp.asarray(np.cos(theta), F32), jnp.asarray(np.sin(theta), F32)
    forward = forward_tables()
    inverse = inverse_tables(norm)
    summing = jnp.asarray(np.repeat(np.eye(channels), 8, axis=0), F32)

    field = lifted_field.reshape(channels, NY, NZ)
    slopes_in = cotangent.reshape(channels, NY, NZ)
    weights = jnp.transpose(spectral_weights, (0, 1, 3, 4, 2))

    lines, half = forward_modes(field, forward, weights, length_x)
    lines = swap(lines)
    folded = fold_rest(weights, half, length_x)
    spectrum, mixed = mix(cos_x, sin_x, lines, folded, norm)
    field_late, mixed = lax.optimization_barrier((field, mixed))
    modes = swap(mixed)
    pre = pointwise(field_late, summing, point_weights, point_bias)
    activated, slope_lines = cell_stage(inverse, forward, summing, modes, pre, slopes_in, field)
    slope_lines = swap(slope_lines)
    grad, grad_point, grad_bias = gradient(cos_x, sin_x, spectrum, slope_lines, norm, MX)
    return (
        activated.reshape(cotangent.shape),
        jnp.transpose(grad, (0, 1, 4, 2, 3)),
        grad_point,
        grad_bias.reshape(channels),
    )


HIGHEST = lax.Precision.HIGHEST


def trig_tables(positions, frequency, length):
    product = positions[:, None] * frequency[None, :] % length
    phase_angle = 2.0 * jnp.pi / length * product.astype(jnp.float32)
    return (jnp.cos(phase_angle), jnp.sin(phase_angle))


def kept_frequencies(kept_count, length):
    mode_index = jnp.arange(kept_count, dtype=jnp.int32)
    return jnp.where(mode_index < kept_count // 2, mode_index, length - kept_count + mode_index)


def forward_local(field_in):
    channels = field_in.shape[0]
    width_x = field_in.shape[1]
    cos_z, sin_z = trig_tables(jnp.arange(NZ, dtype=jnp.int32), jnp.arange(MZ, dtype=jnp.int32), NZ)
    table_z = jnp.concatenate([cos_z, -sin_z], axis=1)
    along_z = jnp.einsum("cxyz,zk->cxyk", field_in, table_z, precision=HIGHEST)
    z_real = along_z[..., :MZ]
    z_imag = along_z[..., MZ:]
    cos_y, sin_y = trig_tables(jnp.arange(NY, dtype=jnp.int32), kept_frequencies(MY, NY), NY)
    y_real = jnp.einsum("cxyk,yj->xcjk", z_real, cos_y, precision=HIGHEST) + jnp.einsum(
        "cxyk,yj->xcjk", z_imag, sin_y, precision=HIGHEST
    )
    y_imag = jnp.einsum("cxyk,yj->xcjk", z_imag, cos_y, precision=HIGHEST) - jnp.einsum(
        "cxyk,yj->xcjk", z_real, sin_y, precision=HIGHEST
    )
    stacked = jnp.stack([y_real, y_imag], axis=1)
    return stacked.reshape(width_x, 2, channels, MY * MZ)


def transform_x(x_lines):
    length_x = x_lines.shape[0]
    cos_x, sin_x = trig_tables(
        jnp.arange(length_x, dtype=jnp.int32), kept_frequencies(MX, length_x), length_x
    )
    norm_scale = 1.0 / float(length_x * NY * NZ) ** 0.5
    part_real = x_lines[:, 0]
    part_imag = x_lines[:, 1]
    x_real = jnp.einsum("xcm,xk->kcm", part_real, cos_x, precision=HIGHEST) + jnp.einsum(
        "xcm,xk->kcm", part_imag, sin_x, precision=HIGHEST
    )
    x_imag = jnp.einsum("xcm,xk->kcm", part_imag, cos_x, precision=HIGHEST) - jnp.einsum(
        "xcm,xk->kcm", part_real, sin_x, precision=HIGHEST
    )
    return norm_scale * jnp.stack([x_real, x_imag], axis=1)


def mix_modes(spectrum, weights):
    spec_real = spectrum[:, 0]
    spec_imag = spectrum[:, 1]
    out_real = jnp.einsum("kim,kmio->kom", spec_real, weights[0], precision=HIGHEST) - jnp.einsum(
        "kim,kmio->kom", spec_imag, weights[1], precision=HIGHEST
    )
    out_imag = jnp.einsum("kim,kmio->kom", spec_real, weights[1], precision=HIGHEST) + jnp.einsum(
        "kim,kmio->kom", spec_imag, weights[0], precision=HIGHEST
    )
    return jnp.stack([out_real, out_imag], axis=1)


def inverse_x(spectrum, positions, length_x):
    cos_x, sin_x = trig_tables(positions, kept_frequencies(MX, length_x), length_x)
    spec_real = spectrum[:, 0]
    spec_imag = spectrum[:, 1]
    a_real = jnp.einsum("kcm,xk->xcm", spec_real, cos_x, precision=HIGHEST) - jnp.einsum(
        "kcm,xk->xcm", spec_imag, sin_x, precision=HIGHEST
    )
    a_imag = jnp.einsum("kcm,xk->xcm", spec_imag, cos_x, precision=HIGHEST) + jnp.einsum(
        "kcm,xk->xcm", spec_real, sin_x, precision=HIGHEST
    )
    return jnp.stack([a_real, a_imag], axis=1)


def inverse_yz(x_lines, length_x):
    width_x = x_lines.shape[0]
    channels = x_lines.shape[2]
    mode_grid = x_lines.reshape(width_x, 2, channels, MY, MZ)
    cos_y, sin_y = trig_tables(jnp.arange(NY, dtype=jnp.int32), kept_frequencies(MY, NY), NY)
    b_real = jnp.einsum("xcjk,yj->cxyk", mode_grid[:, 0], cos_y, precision=HIGHEST) - jnp.einsum(
        "xcjk,yj->cxyk", mode_grid[:, 1], sin_y, precision=HIGHEST
    )
    b_imag = jnp.einsum("xcjk,yj->cxyk", mode_grid[:, 1], cos_y, precision=HIGHEST) + jnp.einsum(
        "xcjk,yj->cxyk", mode_grid[:, 0], sin_y, precision=HIGHEST
    )
    cos_z, sin_z = trig_tables(jnp.arange(NZ, dtype=jnp.int32), jnp.arange(MZ, dtype=jnp.int32), NZ)
    weight_z = jnp.where(jnp.arange(MZ, dtype=jnp.int32) == 0, 1.0, 2.0).astype(jnp.float32)
    table_z = jnp.concatenate([cos_z * weight_z[None, :], -sin_z * weight_z[None, :]], axis=1)
    stacked = jnp.concatenate([b_real, b_imag], axis=-1)
    result = jnp.einsum("cxyk,zk->cxyz", stacked, table_z, precision=HIGHEST)
    return result * (1.0 / float(length_x * NY * NZ) ** 0.5)


def gelu_slope(values):
    return (
        0.5 * (1.0 + lax.erf(values * INV_SQRT_TWO))
        + values * jnp.exp(-0.5 * values * values) * INV_SQRT_TWO_PI
    )


def weight_gradient(spectrum, slope_modes, first_mode):
    mode_ids = first_mode + jnp.arange(spectrum.shape[3], dtype=jnp.int32)
    weight_modes = jnp.where(mode_ids % MZ == 0, 1.0, 2.0).astype(jnp.float32)
    grad_real = jnp.einsum(
        "kim,kom->kmio", spectrum[:, 0], slope_modes[:, 0], precision=HIGHEST
    ) + jnp.einsum("kim,kom->kmio", spectrum[:, 1], slope_modes[:, 1], precision=HIGHEST)
    grad_imag = jnp.einsum(
        "kim,kom->kmio", spectrum[:, 0], slope_modes[:, 1], precision=HIGHEST
    ) - jnp.einsum("kim,kom->kmio", spectrum[:, 1], slope_modes[:, 0], precision=HIGHEST)
    stacked = jnp.stack([grad_real, grad_imag], axis=0)
    return stacked * weight_modes[None, None, :, None, None]


def to_modes(field_in):
    return transform_x(
        lax.all_to_all(forward_local(field_in), "space", split_axis=3, concat_axis=0, tiled=True)
    )


def general_body(lifted_field, cotangent, spectral_weights, point_weights, point_bias):
    devices = lax.axis_size("space")
    width_x = lifted_field.shape[1]
    length_x = width_x * devices
    spectrum = to_modes(lifted_field)
    mixed_modes = mix_modes(spectrum, spectral_weights)
    full_lines = inverse_x(mixed_modes, jnp.arange(length_x, dtype=jnp.int32), length_x)
    spectral = inverse_yz(
        lax.all_to_all(full_lines, "space", split_axis=0, concat_axis=3, tiled=True), length_x
    )
    pointwise = (
        jnp.einsum("ixyz,io->oxyz", lifted_field, point_weights, precision=HIGHEST)
        + point_bias[:, None, None, None]
    )
    before = spectral + pointwise
    activated = jax.nn.gelu(before, approximate=False).astype(jnp.bfloat16)
    slope_field = cotangent.astype(jnp.float32) * gelu_slope(before)
    local_point = jnp.einsum("ixyz,oxyz->io", lifted_field, slope_field, precision=HIGHEST)
    local_bias = jnp.sum(slope_field, axis=(1, 2, 3))
    partial = jnp.concatenate([local_point, local_bias[None, :]], axis=0)
    gathered = lax.all_gather(partial, "space", axis=0, tiled=False)
    summed = jnp.sum(gathered, axis=0)
    summed_point, summed_bias = summed[:-1], summed[-1]
    root_cells = float(length_x * NY * NZ) ** 0.5
    slope_spectrum = to_modes(slope_field)
    first_mode = lax.axis_index("space") * spectrum.shape[3]
    grad_spectral = weight_gradient(spectrum, slope_spectrum, first_mode)
    return (activated, grad_spectral, summed_point / root_cells, summed_bias / root_cells)


def solution(mesh):
    placed = (
        P("groups", "space", None, None),
        P("groups", "space", None, None),
        P(None, None, "space", None, None),
        P(),
        P(),
    )
    return jax.shard_map(
        body,
        mesh=mesh,
        in_specs=placed,
        out_specs=(
            P("groups", "space", None, None),
            P("groups", None, "space", None, None),
            P("groups", None),
            P("groups"),
        ),
        check_vma=False,
    )
```

```python
import functools

import jax
import jax.numpy as jnp
import ml_dtypes
import numpy as np
from jax import lax
from jax.experimental import pallas as pl
from jax.experimental.pallas import tpu as pltpu
from jax.sharding import PartitionSpec as P

MX = 32
MY = 32
MZ = 32
NY = 128
NZ = 256

F32 = jnp.float32
BF16 = jnp.bfloat16
INV_SQRT_TWO = 0.7071067811865476
INV_SQRT_TWO_PI = 0.3989422804014327
MIB = 1 << 20
LANES = 128
GROUP = 4
STEP = 16


def kept(kept_count, length):
    index = np.arange(kept_count)
    return np.where(index < kept_count // 2, index, length - kept_count + index)


def angles(positions, frequency, length):
    product = positions[:, None] * frequency[None, :] % length
    return 2.0 * np.pi / length * product


def split_table(table):
    high = table.astype(ml_dtypes.bfloat16)
    return high, (table - high.astype(np.float64)).astype(ml_dtypes.bfloat16)


def lane_spread(first, second, real_table, imag_table):
    return np.concatenate(
        [real_table * first, real_table * second, imag_table * first, imag_table * second], axis=1
    )


def forward_tables():
    theta = angles(np.arange(NZ), np.arange(MZ), NZ)
    cos_z, sin_z = np.cos(theta), np.sin(theta)
    plain = [lane_spread(f, s, cos_z, -sin_z) for f, s in ((1, 0), (0, 1))]
    turned = [lane_spread(f, s, -sin_z, -cos_z) for f, s in ((1, 0), (0, 1))]
    table_z = np.concatenate([np.concatenate(plain, 0), np.concatenate(turned, 0)], axis=1)
    theta = angles(np.arange(NY), kept(MY, NY), NY)
    both = np.concatenate([np.cos(theta).T, np.sin(theta).T], axis=1)
    table_y = np.concatenate([both[0::2], both[1::2]], axis=0)
    z_high, z_low = split_table(table_z)
    y_high, y_low = split_table(table_y)
    return z_high, z_low, np.concatenate([y_high, y_low], axis=0)


def inverse_tables(norm):
    theta = angles(np.arange(NY), kept(MY, NY), NY)
    cos_y, sin_y = np.cos(theta), np.sin(theta)
    table_y = np.concatenate([cos_y[:, 0::2], cos_y[:, 1::2], sin_y[:, 0::2], sin_y[:, 1::2]], axis=1)
    y_high, y_low = split_table(table_y)
    theta = angles(np.arange(NZ), np.arange(MZ), NZ)
    weight = np.where(np.arange(MZ) == 0, 1.0, 2.0) * norm
    cos_z, sin_z = np.cos(theta) * weight, -np.sin(theta) * weight
    table_z = np.concatenate([lane_spread(f, s, cos_z, sin_z).T for f, s in ((1, 0), (0, 1))], axis=1)
    z_high, z_low = split_table(table_z)
    return (
        np.concatenate([y_high, y_high, y_low], axis=1),
        np.concatenate([z_high, z_high], axis=0),
        z_low,
    )


def dot(left, right):
    return jnp.dot(left, right, preferred_element_type=F32)


def split(values):
    high = values.astype(BF16)
    return high, (values - high.astype(F32)).astype(BF16)


def lane_index(shape):
    return lax.broadcasted_iota(jnp.int32, shape, len(shape) - 1)


def roll(values, shift):
    return pltpu.roll(values, shift % LANES, len(values.shape) - 1)


def forward_group(fields, z_high, z_low, y_both, out_ref, first, rows):
    left = jnp.concatenate(
        [jnp.concatenate([fields[q], fields[q + 1]], axis=1) for q in range(0, len(fields), 2)], axis=0
    )
    high, low = split(left)
    lines = dot(high, z_high) + dot(high, z_low) + dot(low, z_high)
    half = MY // 2
    for g in range(0, len(fields) // 2, GROUP // 2):
        pairs = []
        for q in range(g, g + GROUP // 2):
            part = lines[q * NY : (q + 1) * NY]
            pairs.append(jnp.concatenate([part[:, :LANES], part[:, LANES:]], axis=0))
        high, low = split(jnp.concatenate(pairs, axis=1))
        wide = dot(y_both, high)
        modes = wide[:MY] + wide[MY:] + dot(y_both[:MY], low)
        for q in range(GROUP // 2):
            even = modes[:half, q * LANES : (q + 1) * LANES]
            odd = modes[half:, q * LANES : (q + 1) * LANES]
            at_even = (lane_index(even.shape) // MZ) % 2 == 0
            at = first + 2 * (g + q)
            out_ref[pl.ds(at, half, stride=rows), :] = jnp.where(at_even, even, roll(odd, MZ))
            out_ref[pl.ds(at + 1, half, stride=rows), :] = jnp.where(at_even, roll(even, -MZ), odd)


def inverse_y_group(modes_ref, y_table, first, rows):
    half = MY // 2
    pairs = []
    for q in range(GROUP // 2):
        c0 = modes_ref[pl.ds(first + 2 * q, half, stride=rows), :]
        c1 = modes_ref[pl.ds(first + 2 * q + 1, half, stride=rows), :]
        at_even = (lane_index(c0.shape) // MZ) % 2 == 0
        even = jnp.where(at_even, c0, roll(c1, MZ))
        odd = jnp.where(at_even, roll(c0, -MZ), c1)
        both = jnp.concatenate([even, odd], axis=0)
        other = roll(both, 64)
        turned = jnp.where(lane_index(both.shape) < LANES // 2, -other, other)
        pairs.append(jnp.concatenate([both, turned], axis=0))
    high, low = split(jnp.concatenate(pairs, axis=1))
    lines = dot(y_table, jnp.concatenate([high, low, high], axis=0))
    return [lines[:, q * LANES : (q + 1) * LANES] for q in range(GROUP // 2)]


def full(shape):
    return pl.BlockSpec(shape, lambda *_: (0,) * len(shape))


def params(limit):
    return pltpu.CompilerParams(vmem_limit_bytes=limit * MIB)


def fold_block(pieces, out_ref, at):
    real, imag = pieces[0][0, at], pieces[0][1, at]
    for piece in pieces[1:]:
        real, imag = real + piece[0, at], imag + piece[1, at]
    modes = real.shape[-1]
    out_ref[at, :, :, :modes] = real
    out_ref[at, :, :, modes:] = imag


def fold_specs(weights, unique, per_step, first):
    block = (2, per_step) + weights.shape[2:]
    pieces = [
        pl.BlockSpec(block, functools.partial(lambda s, r: (0, first + s + r, 0, 0, 0), r=r * (unique // per_step)))
        for r in range(weights.shape[1] // unique)
    ]
    shape = (unique,) + weights.shape[2:4] + (2 * weights.shape[4],)
    out = pl.BlockSpec((per_step,) + shape[1:], lambda s: (first + s, 0, 0, 0))
    return pieces, out, jax.ShapeDtypeStruct(shape, F32)


def forward_kernel(z_high, z_low, y_both, field_ref, *refs, channels, step_channels, per_step):
    *pieces, out_ref, folded_ref = refs
    step = pl.program_id(0)
    for at in range(per_step):
        fold_block(pieces, folded_ref, at)
    fields = [field_ref[q] for q in range(step_channels)]
    forward_group(fields, z_high[...], z_low[...], y_both[...], out_ref, step * step_channels, channels)


def forward_modes(field, tables, weights, unique):
    channels = field.shape[0]
    step_channels = 8
    steps = channels // step_channels
    per_step = unique // 2 // steps
    pieces, folded, folded_shape = fold_specs(weights, unique, per_step, 0)
    owners = MY // 2
    out, half = pl.pallas_call(
        functools.partial(forward_kernel, channels=channels, step_channels=step_channels, per_step=per_step),
        grid=(steps,),
        in_specs=[full(t.shape) for t in tables]
        + [pl.BlockSpec((step_channels, NY, NZ), lambda s: (s, 0, 0))]
        + pieces,
        out_specs=[full((owners * channels, LANES)), folded],
        out_shape=[jax.ShapeDtypeStruct((owners * channels, LANES), F32), folded_shape],
        compiler_params=params(60),
        cost_estimate=pl.CostEstimate(flops=2 * 10**9, bytes_accessed=26 * MIB, transcendentals=0),
        name="forward_yz",
    )(*tables, field, *([weights] * len(pieces)))
    return out.reshape(owners, channels, LANES), half


def fold_kernel(*refs):
    *pieces, _, out_ref = refs
    fold_block(pieces, out_ref, 0)


def fold_rest(weights, half, unique):
    first = unique // 2
    pieces, folded, folded_shape = fold_specs(weights, unique, 1, first)
    return pl.pallas_call(
        fold_kernel,
        grid=(unique - first,),
        in_specs=pieces + [pl.BlockSpec(memory_space=pl.ANY)],
        out_specs=folded,
        out_shape=folded_shape,
        input_output_aliases={len(pieces): 0},
        compiler_params=params(60),
        cost_estimate=pl.CostEstimate(flops=4 * 10**6, bytes_accessed=20 * MIB, transcendentals=0),
        name="fold_weights",
    )(*([weights] * len(pieces)), half)


def halve_lines(lines_ref, sums_ref, points, channels):
    half = points // 2
    sign = jnp.where(lane_index((channels, LANES)) < LANES // 2, 1.0, -1.0)
    for x in range(half):
        near, far = lines_ref[x, :channels], lines_ref[x + half, :channels]
        for parity, value in enumerate((near + far, near - far)):
            sums_ref[parity, 0, x] = value
            sums_ref[parity, 1, x] = sign * roll(value, 64)


def spectrum_row(cos_ref, sin_ref, sums_ref, at, parity, half):
    total = cos_ref[at, 0] * sums_ref[parity, 0, 0] + sin_ref[at, 0] * sums_ref[parity, 1, 0]
    for x in range(1, half):
        total += cos_ref[at, x] * sums_ref[parity, 0, x] + sin_ref[at, x] * sums_ref[parity, 1, x]
    return total


def doubled(values):
    other = roll(values, 64)
    low = lane_index(values.shape) < LANES // 2
    return jnp.where(low, values, other), jnp.where(low, other, values)


def mix_kernel(
    core_ref, cos_ref, sin_ref, near_ref, far_ref, weights_ref, spec_ref, out_ref,
    lines_ref, sums_ref, total_ref, real_ref, imag_ref,
    *, points, channels, per_step, norm,
):
    step = pl.program_id(0)
    half = points // 2

    @pl.when(step == 0)
    def _():
        join(core_ref[0], near_ref, far_ref, lines_ref)
        halve_lines(lines_ref, sums_ref, points, channels)
        total_ref[...] = jnp.zeros_like(total_ref)

    low = lane_index((channels, LANES)) < LANES // 2
    for q in range(per_step):
        at = step * per_step + q
        parity = q % 2
        spec = norm * spectrum_row(cos_ref, sin_ref, sums_ref, at, parity, half)
        spec_ref[q] = spec
        real_ref[q], imag_ref[q] = doubled(spec)
        by_real = jnp.zeros((channels, LANES), F32)
        by_imag = jnp.zeros((channels, LANES), F32)
        for i in range(channels):
            weight = weights_ref[q, i]
            by_real += real_ref[q, pl.ds(i, 1), :] * weight
            by_imag += imag_ref[q, pl.ds(i, 1), :] * weight
        other = roll(by_imag, 64)
        mixed = by_real + jnp.where(low, -other, other)
        other = roll(mixed, 64)
        turned = jnp.where(low, -other, other)
        for x in range(half):
            total_ref[parity, x] += cos_ref[at, x] * mixed + sin_ref[at, x] * turned

    @pl.when(step == pl.num_programs(0) - 1)
    def _():
        for x in range(half):
            out_ref[x] = total_ref[0, x] + total_ref[1, x]
            out_ref[x + half] = total_ref[0, x] - total_ref[1, x]


def smem():
    return pl.BlockSpec(memory_space=pltpu.SMEM)


def mix(core, cos_x, sin_x, lines, weights, norm):
    near, far = lines
    chips, cores, channels, _ = near.shape
    points = chips * cores
    unique = weights.shape[0]
    per_step = min(unique, 4)
    shape = (points, channels, LANES)
    return pl.pallas_call(
        functools.partial(mix_kernel, points=points, channels=channels, per_step=per_step, norm=norm),
        grid=(unique // per_step,),
        in_specs=[
            smem(),
            smem(),
            smem(),
            full(near.shape),
            full(far.shape),
            pl.BlockSpec((per_step,) + weights.shape[1:], lambda s: (s, 0, 0, 0)),
        ],
        out_specs=[
            pl.BlockSpec((per_step, channels, LANES), lambda s: (s, 0, 0)),
            full(shape),
        ],
        out_shape=[
            jax.ShapeDtypeStruct((unique, channels, LANES), F32),
            jax.ShapeDtypeStruct(shape, F32),
        ],
        scratch_shapes=[
            pltpu.VMEM(shape, F32),
            pltpu.VMEM((2, 2, points // 2, channels, LANES), F32),
            pltpu.VMEM((2, points // 2, channels, LANES), F32),
            pltpu.VMEM((per_step, channels, LANES), F32),
            pltpu.VMEM((per_step, channels, LANES), F32),
        ],
        compiler_params=params(60),
        cost_estimate=pl.CostEstimate(flops=2 * 10**7, bytes_accessed=9 * MIB, transcendentals=0),
        name="mix_modes",
    )(core, cos_x, sin_x, near, far, weights)


def exact_dot(left, right):
    return jnp.dot(left, right, precision=lax.Precision.HIGHEST, preferred_element_type=F32)


def pointwise_kernel(sum_ref, turned_ref, bias_in_ref, field_ref, out_ref, mixer_ref, bias_ref, *, channels, blocks):
    size = 8 * channels

    @pl.when(pl.program_id(0) == 0)
    def _():
        wide = exact_dot(sum_ref[...], turned_ref[...])
        wide = lax.dot_general(
            wide, sum_ref[...], (((1,), (1,)), ((), ())), precision=lax.Precision.HIGHEST, preferred_element_type=F32
        )
        row = lax.broadcasted_iota(jnp.int32, (size, size), 0) % 8
        high, low = split(jnp.where(row == lane_index((size, size)) % 8, wide, 0.0))
        mixer_ref[:size] = high
        mixer_ref[size:] = low
        bias_ref[...] = exact_dot(sum_ref[...], bias_in_ref[...])

    for b in range(blocks):
        high, low = split(field_ref[:, 8 * b : 8 * b + 8, :].reshape(size, NZ))
        wide = dot(mixer_ref[...], high)
        values = wide[:size] + wide[size:] + dot(mixer_ref[:size], low) + bias_ref[...]
        out_ref[:, 8 * b : 8 * b + 8, :] = values.reshape(channels, 8, NZ)


def pointwise(field, summing, point_weights, point_bias):
    channels = field.shape[0]
    blocks = 2
    turned = point_weights.T
    bias = point_bias[:, None]
    size = 8 * channels
    block = pl.BlockSpec((channels, 8 * blocks, NZ), lambda s: (0, s, 0))
    return pl.pallas_call(
        functools.partial(pointwise_kernel, channels=channels, blocks=blocks),
        grid=(NY // (8 * blocks),),
        in_specs=[full(summing.shape), full(turned.shape), full(bias.shape), block],
        out_specs=block,
        out_shape=jax.ShapeDtypeStruct(field.shape, F32),
        scratch_shapes=[pltpu.VMEM((2 * size, size), BF16), pltpu.VMEM((size, 1), F32)],
        compiler_params=params(60),
        cost_estimate=pl.CostEstimate(flops=4 * 10**9, bytes_accessed=24 * MIB, transcendentals=0),
        name="pointwise",
    )(summing, turned, bias, field)


def cell_kernel(
    core_ref, inv_y, inv_z, inv_z_low, z_high, z_low, y_both, sum_ref, near_ref, far_ref, pre_ref, cot_ref, field_hbm,
    act_ref, out_ref, field_ref, slope_ref, lines_ref, sem, *, channels, step_channels, rows, owners,
):
    step = pl.program_id(0)
    copy = pltpu.make_async_copy(field_hbm, field_ref, sem)

    @pl.when(step == 0)
    def _():
        copy.start()
        join(core_ref[0], near_ref, far_ref, lines_ref)

    modes_ref = lines_ref.reshape(owners * channels, LANES)
    first = step * step_channels
    lines = []
    for g in range(0, step_channels, GROUP):
        lines += inverse_y_group(modes_ref, inv_y[...], first + g, channels)
    high, low = split(jnp.concatenate(lines, axis=0))
    spectral = dot(jnp.concatenate([high, low], axis=1), inv_z[...]) + dot(high, inv_z_low[...])
    slopes = []
    for q in range(step_channels):
        r = q // 2 * NY
        c = q % 2 * NZ
        before = spectral[r : r + NY, c : c + NZ] + pre_ref[q]
        cdf = 0.5 + 0.5 * lax.erf(before * INV_SQRT_TWO)
        act_ref[q] = (before * cdf).astype(BF16)
        pdf = jnp.exp(-0.5 * before * before) * INV_SQRT_TWO_PI
        slope = cot_ref[q].astype(F32) * (cdf + before * pdf)
        slopes.append(slope)
        slope_ref[first + q] = slope
    forward_group(slopes, z_high[...], z_low[...], y_both[...], out_ref, first, rows)

    @pl.when(step == pl.num_programs(0) - 1)
    def _():
        copy.wait()
        size = 8 * channels
        total = jnp.zeros((size, size), F32)
        for b in range(NY // 8):
            at = slice(8 * b, 8 * b + 8)
            f_h, f_l = split(field_ref[:, at, :].reshape(size, NZ))
            s_h, s_l = split(slope_ref[:, at, :].reshape(size, NZ))
            total += lax.dot_general(
                jnp.concatenate([f_h, f_h, f_l], axis=1),
                jnp.concatenate([s_h, s_l, s_h], axis=1),
                (((1,), (1,)), ((), ())),
                preferred_element_type=F32,
            )
        row = lax.broadcasted_iota(jnp.int32, (size, size), 0) % 8
        total = jnp.where(row == lane_index((size, size)) % 8, total, 0.0)
        folded = jnp.sum(total.reshape(channels, 8, size), axis=1)
        point = exact_dot(folded, sum_ref[...])
        packed = jnp.concatenate([point[8 * q : 8 * q + 8] for q in range(channels // 8)], axis=1)
        dc = jnp.broadcast_to(out_ref[0:channels, 0:1], (channels, LANES))
        eye = lax.broadcasted_iota(jnp.int32, (channels, LANES), 0) == lane_index((channels, LANES))
        bias = jnp.sum(jnp.where(eye, dc, 0.0), axis=0, keepdims=True)
        extra = jnp.where(lax.broadcasted_iota(jnp.int32, (8, LANES), 0) == 0, jnp.broadcast_to(bias, (8, LANES)), 0.0)
        for d in range(owners):
            out_ref[d * rows + channels : d * rows + channels + 8, :] = packed
            out_ref[d * rows + channels + 8 : (d + 1) * rows, :] = extra


def cell_stage(core, inverse, forward, summing, modes, pre, cotangent, field):
    channels = field.shape[0]
    owners = MY // 2
    rows = channels + 16
    step_channels = STEP
    near, far = modes
    block = pl.BlockSpec((step_channels, NY, NZ), lambda s: (s, 0, 0))
    tables = (*inverse, *forward, summing)
    act, out = pl.pallas_call(
        functools.partial(cell_kernel, channels=channels, step_channels=step_channels, rows=rows, owners=owners),
        grid=(channels // step_channels,),
        in_specs=[smem()]
        + [full(t.shape) for t in tables]
        + [full(near.shape), full(far.shape), block, block, pl.BlockSpec(memory_space=pl.ANY)],
        out_specs=[block, full((owners * rows, LANES))],
        out_shape=[
            jax.ShapeDtypeStruct((channels, NY, NZ), BF16),
            jax.ShapeDtypeStruct((owners * rows, LANES), F32),
        ],
        scratch_shapes=[
            pltpu.VMEM((channels, NY, NZ), F32),
            pltpu.VMEM((channels, NY, NZ), F32),
            pltpu.VMEM((owners, channels, LANES), F32),
            pltpu.SemaphoreType.DMA,
        ],
        compiler_params=params(60),
        cost_estimate=pl.CostEstimate(flops=8 * 10**9, bytes_accessed=12 * MIB, transcendentals=2 * 10**6),
        name="cells",
    )(core, *tables, near, far, pre, cotangent, field)
    return act, out.reshape(owners, rows, LANES)


def gradient_kernel(
    core_ref, cos_ref, sin_ref, spec_ref, near_ref, far_ref, out_hbm, point_ref, bias_ref,
    lines_ref, sums_ref, real_ref, imag_ref, buffer, sems, *, points, channels, unique, copies, norm,
):
    join(core_ref[0], near_ref, far_ref, lines_ref)
    halve_lines(lines_ref, sums_ref, points, channels)
    half = LANES // 2
    lane = lane_index((channels, LANES))
    scale = jnp.where(lane % MZ == 0, norm, 2.0 * norm)
    packed = lines_ref[0, channels : channels + 16, :]
    for x in range(1, points):
        packed += lines_ref[x, channels : channels + 16, :]
    packed = norm * packed
    for q in range(channels // 8):
        point_ref[8 * q : 8 * q + 8, :] = packed[:8, q * channels : (q + 1) * channels]
    bias_ref[...] = packed[8:9, :channels]

    def writes(at, slot):
        return [
            pltpu.make_async_copy(buffer.at[slot], out_hbm.at[:, at + r * unique], sems.at[slot, r])
            for r in range(copies)
        ]

    @pl.loop(0, unique // 2)
    def _(pair):
        for slot in range(2):
            at = 2 * pair + slot

            @pl.when(pair > 0)
            def _():
                for copy in writes(at - 2, slot):
                    copy.wait()

            slope = scale * spectrum_row(cos_ref, sin_ref, sums_ref, at, slot, points // 2)
            other = roll(slope, 64)
            flipped = jnp.where(lane < half, other, -other)
            real_ref[slot], imag_ref[slot] = doubled(spec_ref[at])
            for i in range(channels):
                both = real_ref[slot, pl.ds(i, 1), :] * slope + imag_ref[slot, pl.ds(i, 1), :] * flipped
                buffer[slot, 0, i] = both[:, :half]
                buffer[slot, 1, i] = both[:, half:]
            for copy in writes(at, slot):
                copy.start()

    for at in range(unique - 2, unique):
        for copy in writes(at, at % 2):
            copy.wait()


def gradient(core, cos_x, sin_x, spectrum, lines, norm, kept_x):
    near, far = lines
    chips, cores, rows, _ = near.shape
    points = chips * cores
    unique, channels, _ = spectrum.shape
    half = LANES // 2
    copies = kept_x // unique
    flat = (channels, LANES)
    return pl.pallas_call(
        functools.partial(gradient_kernel, points=points, channels=channels, unique=unique, copies=copies, norm=norm),
        in_specs=[smem(), smem(), smem(), full(spectrum.shape), full(near.shape), full(far.shape)],
        out_specs=[pl.BlockSpec(memory_space=pl.ANY), full((channels, channels)), full((1, channels))],
        out_shape=[
            jax.ShapeDtypeStruct((2, kept_x, channels, channels, half), F32),
            jax.ShapeDtypeStruct((channels, channels), F32),
            jax.ShapeDtypeStruct((1, channels), F32),
        ],
        scratch_shapes=[
            pltpu.VMEM((points, rows, LANES), F32),
            pltpu.VMEM((2, 2, points // 2, channels, LANES), F32),
            pltpu.VMEM((2,) + flat, F32),
            pltpu.VMEM((2,) + flat, F32),
            pltpu.VMEM((2, 2, channels, channels, half), F32),
            pltpu.SemaphoreType.DMA((2, copies)),
        ],
        compiler_params=params(60),
        cost_estimate=pl.CostEstimate(flops=10**7, bytes_accessed=40 * MIB, transcendentals=0),
        name="weight_gradient",
    )(core, cos_x, sin_x, spectrum, near, far)


CORES = 2


def swap(lines, core):
    devices, rows, lanes = lines.shape
    chips = devices // CORES
    groups = [[p * CORES + q for p in range(chips)] for q in range(CORES)]
    near = lax.all_to_all(
        lines.reshape(chips, CORES * rows, lanes), "space", split_axis=0, concat_axis=0, tiled=True, axis_index_groups=groups
    ).reshape(chips, CORES, rows, lanes)
    give = lax.dynamic_index_in_dim(near, 1 - core, axis=1, keepdims=False)
    far = lax.ppermute(give, "space", [(d, d ^ 1) for d in range(devices)])
    return near, far


def join(core, near_ref, far_ref, lines_ref):
    chips, _, rows, _ = near_ref.shape
    for p in range(chips):
        lines_ref[CORES * p + core] = near_ref[p, core]
        lines_ref[CORES * p + 1 - core] = far_ref[p]


def suits(width_x, length_x, devices, channels, weights):
    held = weights.shape[2]
    even = np.array_equal(kept(MX, length_x) % length_x, np.arange(MX) % length_x)
    return (
        width_x == 1
        and held == 2 * MZ
        and devices * 2 == MY
        and 2 * held == LANES
        and MX % length_x == 0
        and length_x % 8 == 0
        and even
        and channels == MZ
    )


def body(lifted_field, cotangent, spectral_weights, point_weights, point_bias):
    devices = lax.axis_size("space")
    channels, width_x = lifted_field.shape[:2]
    length_x = width_x * devices
    if not suits(width_x, length_x, devices, channels, spectral_weights):
        return general_body(lifted_field, cotangent, spectral_weights, point_weights, point_bias)
    norm = float(length_x * NY * NZ) ** -0.5
    core = lax.axis_index("space") % CORES
    theta = angles(np.arange(length_x), np.arange(length_x), length_x)
    cos_x, sin_x = jnp.asarray(np.cos(theta), F32), jnp.asarray(np.sin(theta), F32)
    forward = forward_tables()
    inverse = inverse_tables(norm)
    summing = jnp.asarray(np.repeat(np.eye(channels), 8, axis=0), F32)

    field = lifted_field.reshape(channels, NY, NZ)
    slopes_in = cotangent.reshape(channels, NY, NZ)
    weights = jnp.transpose(spectral_weights, (0, 1, 3, 4, 2))

    lines, half = forward_modes(field, forward, weights, length_x)
    lines = swap(lines, core)
    folded = fold_rest(weights, half, length_x)
    spectrum, mixed = mix(core[None], cos_x, sin_x, lines, folded, norm)
    field_late, mixed = lax.optimization_barrier((field, mixed))
    modes = swap(mixed, core)
    pre = pointwise(field_late, summing, point_weights, point_bias)
    activated, slope_lines = cell_stage(core[None], inverse, forward, summing, modes, pre, slopes_in, field)
    slope_lines = swap(slope_lines, core)
    grad, grad_point, grad_bias = gradient(core[None], cos_x, sin_x, spectrum, slope_lines, norm, MX)
    return (
        activated.reshape(cotangent.shape),
        jnp.transpose(grad, (0, 1, 4, 2, 3)),
        grad_point,
        grad_bias.reshape(channels),
    )


HIGHEST = lax.Precision.HIGHEST


def trig_tables(positions, frequency, length):
    product = positions[:, None] * frequency[None, :] % length
    phase_angle = 2.0 * jnp.pi / length * product.astype(jnp.float32)
    return (jnp.cos(phase_angle), jnp.sin(phase_angle))


def kept_frequencies(kept_count, length):
    mode_index = jnp.arange(kept_count, dtype=jnp.int32)
    return jnp.where(mode_index < kept_count // 2, mode_index, length - kept_count + mode_index)


def forward_local(field_in):
    channels = field_in.shape[0]
    width_x = field_in.shape[1]
    cos_z, sin_z = trig_tables(jnp.arange(NZ, dtype=jnp.int32), jnp.arange(MZ, dtype=jnp.int32), NZ)
    table_z = jnp.concatenate([cos_z, -sin_z], axis=1)
    along_z = jnp.einsum("cxyz,zk->cxyk", field_in, table_z, precision=HIGHEST)
    z_real = along_z[..., :MZ]
    z_imag = along_z[..., MZ:]
    cos_y, sin_y = trig_tables(jnp.arange(NY, dtype=jnp.int32), kept_frequencies(MY, NY), NY)
    y_real = jnp.einsum("cxyk,yj->xcjk", z_real, cos_y, precision=HIGHEST) + jnp.einsum(
        "cxyk,yj->xcjk", z_imag, sin_y, precision=HIGHEST
    )
    y_imag = jnp.einsum("cxyk,yj->xcjk", z_imag, cos_y, precision=HIGHEST) - jnp.einsum(
        "cxyk,yj->xcjk", z_real, sin_y, precision=HIGHEST
    )
    stacked = jnp.stack([y_real, y_imag], axis=1)
    return stacked.reshape(width_x, 2, channels, MY * MZ)


def transform_x(x_lines):
    length_x = x_lines.shape[0]
    cos_x, sin_x = trig_tables(
        jnp.arange(length_x, dtype=jnp.int32), kept_frequencies(MX, length_x), length_x
    )
    norm_scale = 1.0 / float(length_x * NY * NZ) ** 0.5
    part_real = x_lines[:, 0]
    part_imag = x_lines[:, 1]
    x_real = jnp.einsum("xcm,xk->kcm", part_real, cos_x, precision=HIGHEST) + jnp.einsum(
        "xcm,xk->kcm", part_imag, sin_x, precision=HIGHEST
    )
    x_imag = jnp.einsum("xcm,xk->kcm", part_imag, cos_x, precision=HIGHEST) - jnp.einsum(
        "xcm,xk->kcm", part_real, sin_x, precision=HIGHEST
    )
    return norm_scale * jnp.stack([x_real, x_imag], axis=1)


def mix_modes(spectrum, weights):
    spec_real = spectrum[:, 0]
    spec_imag = spectrum[:, 1]
    out_real = jnp.einsum("kim,kmio->kom", spec_real, weights[0], precision=HIGHEST) - jnp.einsum(
        "kim,kmio->kom", spec_imag, weights[1], precision=HIGHEST
    )
    out_imag = jnp.einsum("kim,kmio->kom", spec_real, weights[1], precision=HIGHEST) + jnp.einsum(
        "kim,kmio->kom", spec_imag, weights[0], precision=HIGHEST
    )
    return jnp.stack([out_real, out_imag], axis=1)


def inverse_x(spectrum, positions, length_x):
    cos_x, sin_x = trig_tables(positions, kept_frequencies(MX, length_x), length_x)
    spec_real = spectrum[:, 0]
    spec_imag = spectrum[:, 1]
    a_real = jnp.einsum("kcm,xk->xcm", spec_real, cos_x, precision=HIGHEST) - jnp.einsum(
        "kcm,xk->xcm", spec_imag, sin_x, precision=HIGHEST
    )
    a_imag = jnp.einsum("kcm,xk->xcm", spec_imag, cos_x, precision=HIGHEST) + jnp.einsum(
        "kcm,xk->xcm", spec_real, sin_x, precision=HIGHEST
    )
    return jnp.stack([a_real, a_imag], axis=1)


def inverse_yz(x_lines, length_x):
    width_x = x_lines.shape[0]
    channels = x_lines.shape[2]
    mode_grid = x_lines.reshape(width_x, 2, channels, MY, MZ)
    cos_y, sin_y = trig_tables(jnp.arange(NY, dtype=jnp.int32), kept_frequencies(MY, NY), NY)
    b_real = jnp.einsum("xcjk,yj->cxyk", mode_grid[:, 0], cos_y, precision=HIGHEST) - jnp.einsum(
        "xcjk,yj->cxyk", mode_grid[:, 1], sin_y, precision=HIGHEST
    )
    b_imag = jnp.einsum("xcjk,yj->cxyk", mode_grid[:, 1], cos_y, precision=HIGHEST) + jnp.einsum(
        "xcjk,yj->cxyk", mode_grid[:, 0], sin_y, precision=HIGHEST
    )
    cos_z, sin_z = trig_tables(jnp.arange(NZ, dtype=jnp.int32), jnp.arange(MZ, dtype=jnp.int32), NZ)
    weight_z = jnp.where(jnp.arange(MZ, dtype=jnp.int32) == 0, 1.0, 2.0).astype(jnp.float32)
    table_z = jnp.concatenate([cos_z * weight_z[None, :], -sin_z * weight_z[None, :]], axis=1)
    stacked = jnp.concatenate([b_real, b_imag], axis=-1)
    result = jnp.einsum("cxyk,zk->cxyz", stacked, table_z, precision=HIGHEST)
    return result * (1.0 / float(length_x * NY * NZ) ** 0.5)


def gelu_slope(values):
    return (
        0.5 * (1.0 + lax.erf(values * INV_SQRT_TWO))
        + values * jnp.exp(-0.5 * values * values) * INV_SQRT_TWO_PI
    )


def weight_gradient(spectrum, slope_modes, first_mode):
    mode_ids = first_mode + jnp.arange(spectrum.shape[3], dtype=jnp.int32)
    weight_modes = jnp.where(mode_ids % MZ == 0, 1.0, 2.0).astype(jnp.float32)
    grad_real = jnp.einsum(
        "kim,kom->kmio", spectrum[:, 0], slope_modes[:, 0], precision=HIGHEST
    ) + jnp.einsum("kim,kom->kmio", spectrum[:, 1], slope_modes[:, 1], precision=HIGHEST)
    grad_imag = jnp.einsum(
        "kim,kom->kmio", spectrum[:, 0], slope_modes[:, 1], precision=HIGHEST
    ) - jnp.einsum("kim,kom->kmio", spectrum[:, 1], slope_modes[:, 0], precision=HIGHEST)
    stacked = jnp.stack([grad_real, grad_imag], axis=0)
    return stacked * weight_modes[None, None, :, None, None]


def to_modes(field_in):
    return transform_x(
        lax.all_to_all(forward_local(field_in), "space", split_axis=3, concat_axis=0, tiled=True)
    )


def general_body(lifted_field, cotangent, spectral_weights, point_weights, point_bias):
    devices = lax.axis_size("space")
    width_x = lifted_field.shape[1]
    length_x = width_x * devices
    spectrum = to_modes(lifted_field)
    mixed_modes = mix_modes(spectrum, spectral_weights)
    full_lines = inverse_x(mixed_modes, jnp.arange(length_x, dtype=jnp.int32), length_x)
    spectral = inverse_yz(
        lax.all_to_all(full_lines, "space", split_axis=0, concat_axis=3, tiled=True), length_x
    )
    pointwise = (
        jnp.einsum("ixyz,io->oxyz", lifted_field, point_weights, precision=HIGHEST)
        + point_bias[:, None, None, None]
    )
    before = spectral + pointwise
    activated = jax.nn.gelu(before, approximate=False).astype(jnp.bfloat16)
    slope_field = cotangent.astype(jnp.float32) * gelu_slope(before)
    local_point = jnp.einsum("ixyz,oxyz->io", lifted_field, slope_field, precision=HIGHEST)
    local_bias = jnp.sum(slope_field, axis=(1, 2, 3))
    partial = jnp.concatenate([local_point, local_bias[None, :]], axis=0)
    gathered = lax.all_gather(partial, "space", axis=0, tiled=False)
    summed = jnp.sum(gathered, axis=0)
    summed_point, summed_bias = summed[:-1], summed[-1]
    root_cells = float(length_x * NY * NZ) ** 0.5
    slope_spectrum = to_modes(slope_field)
    first_mode = lax.axis_index("space") * spectrum.shape[3]
    grad_spectral = weight_gradient(spectrum, slope_spectrum, first_mode)
    return (activated, grad_spectral, summed_point / root_cells, summed_bias / root_cells)


def solution(mesh):
    placed = (
        P("groups", "space", None, None),
        P("groups", "space", None, None),
        P(None, None, "space", None, None),
        P(),
        P(),
    )
    return jax.shard_map(
        body,
        mesh=mesh,
        in_specs=placed,
        out_specs=(
            P("groups", "space", None, None),
            P("groups", None, "space", None, None),
            P("groups", None),
            P("groups"),
        ),
        check_vma=False,
    )
```

```python
import functools

import jax
import jax.numpy as jnp
import ml_dtypes
import numpy as np
from jax import lax
from jax.experimental import pallas as pl
from jax.experimental.pallas import tpu as pltpu
from jax.sharding import PartitionSpec as P

MX = 32
MY = 32
MZ = 32
NY = 128
NZ = 256

F32 = jnp.float32
BF16 = jnp.bfloat16
INV_SQRT_TWO = 0.7071067811865476
INV_SQRT_TWO_PI = 0.3989422804014327
MIB = 1 << 20
LANES = 128
GROUP = 4
STEP = 16


def kept(kept_count, length):
    index = np.arange(kept_count)
    return np.where(index < kept_count // 2, index, length - kept_count + index)


def angles(positions, frequency, length):
    product = positions[:, None] * frequency[None, :] % length
    return 2.0 * np.pi / length * product


def split_table(table):
    high = table.astype(ml_dtypes.bfloat16)
    return high, (table - high.astype(np.float64)).astype(ml_dtypes.bfloat16)


def lane_spread(first, second, real_table, imag_table):
    return np.concatenate(
        [real_table * first, real_table * second, imag_table * first, imag_table * second], axis=1
    )


def forward_tables():
    theta = angles(np.arange(NZ), np.arange(MZ), NZ)
    cos_z, sin_z = np.cos(theta), np.sin(theta)
    plain = [lane_spread(f, s, cos_z, -sin_z) for f, s in ((1, 0), (0, 1))]
    turned = [lane_spread(f, s, -sin_z, -cos_z) for f, s in ((1, 0), (0, 1))]
    table_z = np.concatenate([np.concatenate(plain, 0), np.concatenate(turned, 0)], axis=1)
    theta = angles(np.arange(NY), kept(MY, NY), NY)
    both = np.concatenate([np.cos(theta).T, np.sin(theta).T], axis=1)
    table_y = np.concatenate([both[0::2], both[1::2]], axis=0)
    z_high, z_low = split_table(table_z)
    y_high, y_low = split_table(table_y)
    return z_high, z_low, np.concatenate([y_high, y_low], axis=0)


def inverse_tables(norm):
    theta = angles(np.arange(NY), kept(MY, NY), NY)
    cos_y, sin_y = np.cos(theta), np.sin(theta)
    table_y = np.concatenate([cos_y[:, 0::2], cos_y[:, 1::2], sin_y[:, 0::2], sin_y[:, 1::2]], axis=1)
    y_high, y_low = split_table(table_y)
    theta = angles(np.arange(NZ), np.arange(MZ), NZ)
    weight = np.where(np.arange(MZ) == 0, 1.0, 2.0) * norm
    cos_z, sin_z = np.cos(theta) * weight, -np.sin(theta) * weight
    table_z = np.concatenate([lane_spread(f, s, cos_z, sin_z).T for f, s in ((1, 0), (0, 1))], axis=1)
    z_high, z_low = split_table(table_z)
    return (
        np.concatenate([y_high, y_high, y_low], axis=1),
        np.concatenate([z_high, z_high], axis=0),
        z_low,
    )


def dot(left, right):
    return jnp.dot(left, right, preferred_element_type=F32)


def split(values):
    high = values.astype(BF16)
    return high, (values - high.astype(F32)).astype(BF16)


def lane_index(shape):
    return lax.broadcasted_iota(jnp.int32, shape, len(shape) - 1)


def roll(values, shift):
    return pltpu.roll(values, shift % LANES, len(values.shape) - 1)


def forward_group(fields, z_high, z_low, y_both, out_ref, first, rows):
    left = jnp.concatenate(
        [jnp.concatenate([fields[q], fields[q + 1]], axis=1) for q in range(0, len(fields), 2)], axis=0
    )
    high, low = split(left)
    lines = dot(high, z_high) + dot(high, z_low) + dot(low, z_high)
    half = MY // 2
    for g in range(0, len(fields) // 2, GROUP // 2):
        pairs = []
        for q in range(g, g + GROUP // 2):
            part = lines[q * NY : (q + 1) * NY]
            pairs.append(jnp.concatenate([part[:, :LANES], part[:, LANES:]], axis=0))
        high, low = split(jnp.concatenate(pairs, axis=1))
        wide = dot(y_both, high)
        modes = wide[:MY] + wide[MY:] + dot(y_both[:MY], low)
        for q in range(GROUP // 2):
            even = modes[:half, q * LANES : (q + 1) * LANES]
            odd = modes[half:, q * LANES : (q + 1) * LANES]
            at_even = (lane_index(even.shape) // MZ) % 2 == 0
            at = first + 2 * (g + q)
            out_ref[pl.ds(at, half, stride=rows), :] = jnp.where(at_even, even, roll(odd, MZ))
            out_ref[pl.ds(at + 1, half, stride=rows), :] = jnp.where(at_even, roll(even, -MZ), odd)


def inverse_y_group(modes_ref, y_table, first, rows):
    half = MY // 2
    pairs = []
    for q in range(GROUP // 2):
        c0 = modes_ref[pl.ds(first + 2 * q, half, stride=rows), :]
        c1 = modes_ref[pl.ds(first + 2 * q + 1, half, stride=rows), :]
        at_even = (lane_index(c0.shape) // MZ) % 2 == 0
        even = jnp.where(at_even, c0, roll(c1, MZ))
        odd = jnp.where(at_even, roll(c0, -MZ), c1)
        both = jnp.concatenate([even, odd], axis=0)
        other = roll(both, 64)
        turned = jnp.where(lane_index(both.shape) < LANES // 2, -other, other)
        pairs.append(jnp.concatenate([both, turned], axis=0))
    high, low = split(jnp.concatenate(pairs, axis=1))
    lines = dot(y_table, jnp.concatenate([high, low, high], axis=0))
    return [lines[:, q * LANES : (q + 1) * LANES] for q in range(GROUP // 2)]


def join(me, piece_refs, lines_ref):
    for s, piece in enumerate(piece_refs):
        lines_ref[me ^ s] = piece[...]


def part(me, s, lines_ref, rows):
    return lines_ref[pl.ds(pl.multiple_of((me ^ s) * rows, 8), rows), :]


def full(shape):
    return pl.BlockSpec(shape, lambda *_: (0,) * len(shape))


def params(limit):
    return pltpu.CompilerParams(vmem_limit_bytes=limit * MIB)


def fold_block(pieces, out_ref, at):
    real, imag = pieces[0][0, at], pieces[0][1, at]
    for piece in pieces[1:]:
        real, imag = real + piece[0, at], imag + piece[1, at]
    modes = real.shape[-1]
    out_ref[at, :, :, :modes] = real
    out_ref[at, :, :, modes:] = imag


def fold_specs(weights, unique, per_step, first):
    block = (2, per_step) + weights.shape[2:]
    pieces = [
        pl.BlockSpec(block, functools.partial(lambda s, r: (0, first + s + r, 0, 0, 0), r=r * (unique // per_step)))
        for r in range(weights.shape[1] // unique)
    ]
    shape = (unique,) + weights.shape[2:4] + (2 * weights.shape[4],)
    out = pl.BlockSpec((per_step,) + shape[1:], lambda s: (first + s, 0, 0, 0))
    return pieces, out, jax.ShapeDtypeStruct(shape, F32)


def forward_kernel(me_ref, z_high, z_low, y_both, field_ref, *refs, channels, step_channels, per_step, copies):
    pieces, (folded_ref, *out_refs, out_ref) = refs[:copies], refs[copies:]
    step = pl.program_id(0)
    for at in range(per_step):
        fold_block(pieces, folded_ref, at)
    fields = [field_ref[q] for q in range(step_channels)]
    forward_group(fields, z_high[...], z_low[...], y_both[...], out_ref, step * step_channels, channels)

    @pl.when(step == pl.num_programs(0) - 1)
    def _():
        for s, ref in enumerate(out_refs):
            ref[...] = part(me_ref[0], s, out_ref, channels)


def forward_modes(me, field, tables, weights, unique):
    channels = field.shape[0]
    step_channels = 8
    steps = channels // step_channels
    per_step = unique // 2 // steps
    pieces, folded, folded_shape = fold_specs(weights, unique, per_step, 0)
    owners = MY // 2
    half, *out = pl.pallas_call(
        functools.partial(
            forward_kernel, channels=channels, step_channels=step_channels, per_step=per_step, copies=len(pieces)
        ),
        grid=(steps,),
        in_specs=[smem()]
        + [full(t.shape) for t in tables]
        + [pl.BlockSpec((step_channels, NY, NZ), lambda s: (s, 0, 0))]
        + pieces,
        out_specs=[folded] + [full((channels, LANES))] * owners,
        out_shape=[folded_shape] + [jax.ShapeDtypeStruct((channels, LANES), F32)] * owners,
        scratch_shapes=[pltpu.VMEM((owners * channels, LANES), F32)],
        compiler_params=params(60),
        cost_estimate=pl.CostEstimate(flops=2 * 10**9, bytes_accessed=26 * MIB, transcendentals=0),
        name="forward_yz",
    )(me, *tables, field, *([weights] * len(pieces)))
    return out, half


def fold_kernel(*refs):
    *pieces, _, out_ref = refs
    fold_block(pieces, out_ref, 0)


def fold_rest(weights, half, unique):
    first = unique // 2
    pieces, folded, folded_shape = fold_specs(weights, unique, 1, first)
    return pl.pallas_call(
        fold_kernel,
        grid=(unique - first,),
        in_specs=pieces + [pl.BlockSpec(memory_space=pl.ANY)],
        out_specs=folded,
        out_shape=folded_shape,
        input_output_aliases={len(pieces): 0},
        compiler_params=params(60),
        cost_estimate=pl.CostEstimate(flops=4 * 10**6, bytes_accessed=20 * MIB, transcendentals=0),
        name="fold_weights",
    )(*([weights] * len(pieces)), half)


def halve_lines(lines_ref, sums_ref, points, channels):
    half = points // 2
    sign = jnp.where(lane_index((channels, LANES)) < LANES // 2, 1.0, -1.0)
    for x in range(half):
        near, far = lines_ref[x, :channels], lines_ref[x + half, :channels]
        for parity, value in enumerate((near + far, near - far)):
            sums_ref[parity, 0, x] = value
            sums_ref[parity, 1, x] = sign * roll(value, 64)


def spectrum_row(cos_ref, sin_ref, sums_ref, at, parity, half):
    total = cos_ref[at, 0] * sums_ref[parity, 0, 0] + sin_ref[at, 0] * sums_ref[parity, 1, 0]
    for x in range(1, half):
        total += cos_ref[at, x] * sums_ref[parity, 0, x] + sin_ref[at, x] * sums_ref[parity, 1, x]
    return total


def doubled(values):
    other = roll(values, 64)
    low = lane_index(values.shape) < LANES // 2
    return jnp.where(low, values, other), jnp.where(low, other, values)


def mix_kernel(
    me_ref, cos_ref, sin_ref, weights_ref, *refs, points, channels, per_step, norm,
):
    piece_refs, spec_ref, out_refs = refs[:points], refs[points], refs[points + 1 : 2 * points + 1]
    lines_ref, sums_ref, total_ref, real_ref, imag_ref = refs[2 * points + 1 :]
    step = pl.program_id(0)
    half = points // 2

    @pl.when(step == 0)
    def _():
        join(me_ref[0], piece_refs, lines_ref)
        halve_lines(lines_ref, sums_ref, points, channels)
        total_ref[...] = jnp.zeros_like(total_ref)

    low = lane_index((channels, LANES)) < LANES // 2
    for q in range(per_step):
        at = step * per_step + q
        parity = q % 2
        spec = norm * spectrum_row(cos_ref, sin_ref, sums_ref, at, parity, half)
        spec_ref[q] = spec
        real_ref[q], imag_ref[q] = doubled(spec)
        by_real = jnp.zeros((channels, LANES), F32)
        by_imag = jnp.zeros((channels, LANES), F32)
        for i in range(channels):
            weight = weights_ref[q, i]
            by_real += real_ref[q, pl.ds(i, 1), :] * weight
            by_imag += imag_ref[q, pl.ds(i, 1), :] * weight
        other = roll(by_imag, 64)
        mixed = by_real + jnp.where(low, -other, other)
        other = roll(mixed, 64)
        turned = jnp.where(low, -other, other)
        for x in range(half):
            total_ref[parity, x] += cos_ref[at, x] * mixed + sin_ref[at, x] * turned

    @pl.when(step == pl.num_programs(0) - 1)
    def _():
        for x in range(half):
            lines_ref[x] = total_ref[0, x] + total_ref[1, x]
            lines_ref[x + half] = total_ref[0, x] - total_ref[1, x]
        for s, ref in enumerate(out_refs):
            ref[...] = lines_ref[me_ref[0] ^ s]


def smem():
    return pl.BlockSpec(memory_space=pltpu.SMEM)


def mix(me, cos_x, sin_x, pieces, weights, norm):
    points = len(pieces)
    channels = pieces[0].shape[0]
    unique = weights.shape[0]
    per_step = min(unique, 4)
    flat = (channels, LANES)
    spectrum, *out = pl.pallas_call(
        functools.partial(mix_kernel, points=points, channels=channels, per_step=per_step, norm=norm),
        grid=(unique // per_step,),
        in_specs=[smem(), smem(), smem(), pl.BlockSpec((per_step,) + weights.shape[1:], lambda s: (s, 0, 0, 0))]
        + [full(flat)] * points,
        out_specs=[pl.BlockSpec((per_step,) + flat, lambda s: (s, 0, 0))] + [full(flat)] * points,
        out_shape=[jax.ShapeDtypeStruct((unique,) + flat, F32)] + [jax.ShapeDtypeStruct(flat, F32)] * points,
        scratch_shapes=[
            pltpu.VMEM((points,) + flat, F32),
            pltpu.VMEM((2, 2, points // 2) + flat, F32),
            pltpu.VMEM((2, points // 2) + flat, F32),
            pltpu.VMEM((per_step,) + flat, F32),
            pltpu.VMEM((per_step,) + flat, F32),
        ],
        compiler_params=params(60),
        cost_estimate=pl.CostEstimate(flops=2 * 10**7, bytes_accessed=9 * MIB, transcendentals=0),
        name="mix_modes",
    )(me, cos_x, sin_x, weights, *pieces)
    return spectrum, out


def exact_dot(left, right):
    return jnp.dot(left, right, precision=lax.Precision.HIGHEST, preferred_element_type=F32)


def pointwise_kernel(sum_ref, turned_ref, bias_in_ref, field_ref, out_ref, mixer_ref, bias_ref, *, channels, blocks):
    size = 8 * channels

    @pl.when(pl.program_id(0) == 0)
    def _():
        wide = exact_dot(sum_ref[...], turned_ref[...])
        wide = lax.dot_general(
            wide, sum_ref[...], (((1,), (1,)), ((), ())), precision=lax.Precision.HIGHEST, preferred_element_type=F32
        )
        row = lax.broadcasted_iota(jnp.int32, (size, size), 0) % 8
        high, low = split(jnp.where(row == lane_index((size, size)) % 8, wide, 0.0))
        mixer_ref[:size] = high
        mixer_ref[size:] = low
        bias_ref[...] = exact_dot(sum_ref[...], bias_in_ref[...])

    for b in range(blocks):
        high, low = split(field_ref[:, 8 * b : 8 * b + 8, :].reshape(size, NZ))
        wide = dot(mixer_ref[...], high)
        values = wide[:size] + wide[size:] + dot(mixer_ref[:size], low) + bias_ref[...]
        out_ref[:, 8 * b : 8 * b + 8, :] = values.reshape(channels, 8, NZ)


def pointwise(field, summing, point_weights, point_bias):
    channels = field.shape[0]
    blocks = 2
    turned = point_weights.T
    bias = point_bias[:, None]
    size = 8 * channels
    block = pl.BlockSpec((channels, 8 * blocks, NZ), lambda s: (0, s, 0))
    return pl.pallas_call(
        functools.partial(pointwise_kernel, channels=channels, blocks=blocks),
        grid=(NY // (8 * blocks),),
        in_specs=[full(summing.shape), full(turned.shape), full(bias.shape), block],
        out_specs=block,
        out_shape=jax.ShapeDtypeStruct(field.shape, F32),
        scratch_shapes=[pltpu.VMEM((2 * size, size), BF16), pltpu.VMEM((size, 1), F32)],
        compiler_params=params(60),
        cost_estimate=pl.CostEstimate(flops=4 * 10**9, bytes_accessed=24 * MIB, transcendentals=0),
        name="pointwise",
    )(summing, turned, bias, field)


def cell_kernel(
    me_ref, inv_y, inv_z, inv_z_low, z_high, z_low, y_both, sum_ref, pre_ref, cot_ref, field_hbm, *refs,
    channels, step_channels, owners,
):
    piece_refs, act_ref, out_refs = refs[:owners], refs[owners], refs[owners + 1 : 2 * owners + 1]
    lines_ref, out_ref, field_ref, slope_ref, sem = refs[2 * owners + 1 :]
    step = pl.program_id(0)
    copy = pltpu.make_async_copy(field_hbm, field_ref, sem)

    @pl.when(step == 0)
    def _():
        copy.start()
        join(me_ref[0], piece_refs, lines_ref)

    modes_ref = lines_ref.reshape(owners * channels, LANES)
    first = step * step_channels
    lines = []
    for g in range(0, step_channels, GROUP):
        lines += inverse_y_group(modes_ref, inv_y[...], first + g, channels)
    high, low = split(jnp.concatenate(lines, axis=0))
    spectral = dot(jnp.concatenate([high, low], axis=1), inv_z[...]) + dot(high, inv_z_low[...])
    slopes = []
    for q in range(step_channels):
        r = q // 2 * NY
        c = q % 2 * NZ
        before = spectral[r : r + NY, c : c + NZ] + pre_ref[q]
        cdf = 0.5 + 0.5 * lax.erf(before * INV_SQRT_TWO)
        act_ref[q] = (before * cdf).astype(BF16)
        pdf = jnp.exp(-0.5 * before * before) * INV_SQRT_TWO_PI
        slope = cot_ref[q].astype(F32) * (cdf + before * pdf)
        slopes.append(slope)
        slope_ref[first + q] = slope
    forward_group(slopes, z_high[...], z_low[...], y_both[...], out_ref, first, channels)

    @pl.when(step == pl.num_programs(0) - 1)
    def _():
        copy.wait()
        size = 8 * channels
        total = jnp.zeros((size, size), F32)
        for b in range(NY // 8):
            at = slice(8 * b, 8 * b + 8)
            f_h, f_l = split(field_ref[:, at, :].reshape(size, NZ))
            s_h, s_l = split(slope_ref[:, at, :].reshape(size, NZ))
            total += lax.dot_general(
                jnp.concatenate([f_h, f_h, f_l], axis=1),
                jnp.concatenate([s_h, s_l, s_h], axis=1),
                (((1,), (1,)), ((), ())),
                preferred_element_type=F32,
            )
        row = lax.broadcasted_iota(jnp.int32, (size, size), 0) % 8
        total = jnp.where(row == lane_index((size, size)) % 8, total, 0.0)
        folded = jnp.sum(total.reshape(channels, 8, size), axis=1)
        point = exact_dot(folded, sum_ref[...])
        packed = jnp.concatenate([point[8 * q : 8 * q + 8] for q in range(channels // 8)], axis=1)
        dc = jnp.broadcast_to(out_ref[0:channels, 0:1], (channels, LANES))
        eye = lax.broadcasted_iota(jnp.int32, (channels, LANES), 0) == lane_index((channels, LANES))
        bias = jnp.sum(jnp.where(eye, dc, 0.0), axis=0, keepdims=True)
        extra = jnp.where(lax.broadcasted_iota(jnp.int32, (8, LANES), 0) == 0, jnp.broadcast_to(bias, (8, LANES)), 0.0)
        for s, ref in enumerate(out_refs):
            ref[:channels, :] = part(me_ref[0], s, out_ref, channels)
            ref[channels : channels + 8, :] = packed
            ref[channels + 8 :, :] = extra


def cell_stage(me, inverse, forward, summing, pieces, pre, cotangent, field):
    channels = field.shape[0]
    owners = len(pieces)
    step_channels = STEP
    rows = channels + 16
    block = pl.BlockSpec((step_channels, NY, NZ), lambda s: (s, 0, 0))
    tables = (*inverse, *forward, summing)
    act, *out = pl.pallas_call(
        functools.partial(cell_kernel, channels=channels, step_channels=step_channels, owners=owners),
        grid=(channels // step_channels,),
        in_specs=[smem()]
        + [full(t.shape) for t in tables]
        + [block, block, pl.BlockSpec(memory_space=pl.ANY)]
        + [full((channels, LANES))] * owners,
        out_specs=[block] + [full((rows, LANES))] * owners,
        out_shape=[jax.ShapeDtypeStruct((channels, NY, NZ), BF16)]
        + [jax.ShapeDtypeStruct((rows, LANES), F32)] * owners,
        scratch_shapes=[
            pltpu.VMEM((owners, channels, LANES), F32),
            pltpu.VMEM((owners * channels, LANES), F32),
            pltpu.VMEM((channels, NY, NZ), F32),
            pltpu.VMEM((channels, NY, NZ), F32),
            pltpu.SemaphoreType.DMA,
        ],
        compiler_params=params(60),
        cost_estimate=pl.CostEstimate(flops=8 * 10**9, bytes_accessed=12 * MIB, transcendentals=2 * 10**6),
        name="cells",
    )(me, *tables, pre, cotangent, field, *pieces)
    return act, out


def gradient_kernel(
    me_ref, cos_ref, sin_ref, spec_ref, *refs, points, channels, unique, copies, norm,
):
    piece_refs, (out_hbm, point_ref, bias_ref) = refs[:points], refs[points : points + 3]
    lines_ref, sums_ref, real_ref, imag_ref, buffer, sems = refs[points + 3 :]
    join(me_ref[0], piece_refs, lines_ref)
    halve_lines(lines_ref, sums_ref, points, channels)
    half = LANES // 2
    lane = lane_index((channels, LANES))
    scale = jnp.where(lane % MZ == 0, norm, 2.0 * norm)
    packed = lines_ref[0, channels : channels + 16, :]
    for x in range(1, points):
        packed += lines_ref[x, channels : channels + 16, :]
    packed = norm * packed
    for q in range(channels // 8):
        point_ref[8 * q : 8 * q + 8, :] = packed[:8, q * channels : (q + 1) * channels]
    bias_ref[...] = packed[8:9, :channels]

    def writes(at, slot):
        return [
            pltpu.make_async_copy(buffer.at[slot], out_hbm.at[:, at + r * unique], sems.at[slot, r])
            for r in range(copies)
        ]

    @pl.loop(0, unique // 2)
    def _(pair):
        for slot in range(2):
            at = 2 * pair + slot

            @pl.when(pair > 0)
            def _():
                for copy in writes(at - 2, slot):
                    copy.wait()

            slope = scale * spectrum_row(cos_ref, sin_ref, sums_ref, at, slot, points // 2)
            other = roll(slope, 64)
            flipped = jnp.where(lane < half, other, -other)
            real_ref[slot], imag_ref[slot] = doubled(spec_ref[at])
            for i in range(channels):
                both = real_ref[slot, pl.ds(i, 1), :] * slope + imag_ref[slot, pl.ds(i, 1), :] * flipped
                buffer[slot, 0, i] = both[:, :half]
                buffer[slot, 1, i] = both[:, half:]
            for copy in writes(at, slot):
                copy.start()

    for at in range(unique - 2, unique):
        for copy in writes(at, at % 2):
            copy.wait()


def gradient(me, cos_x, sin_x, spectrum, pieces, norm, kept_x):
    points = len(pieces)
    rows = pieces[0].shape[0]
    unique, channels, _ = spectrum.shape
    half = LANES // 2
    copies = kept_x // unique
    flat = (channels, LANES)
    return pl.pallas_call(
        functools.partial(gradient_kernel, points=points, channels=channels, unique=unique, copies=copies, norm=norm),
        in_specs=[smem(), smem(), smem(), full(spectrum.shape)] + [full((rows, LANES))] * points,
        out_specs=[pl.BlockSpec(memory_space=pl.ANY), full((channels, channels)), full((1, channels))],
        out_shape=[
            jax.ShapeDtypeStruct((2, kept_x, channels, channels, half), F32),
            jax.ShapeDtypeStruct((channels, channels), F32),
            jax.ShapeDtypeStruct((1, channels), F32),
        ],
        scratch_shapes=[
            pltpu.VMEM((points, rows, LANES), F32),
            pltpu.VMEM((2, 2, points // 2, channels, LANES), F32),
            pltpu.VMEM((2,) + flat, F32),
            pltpu.VMEM((2,) + flat, F32),
            pltpu.VMEM((2, 2, channels, channels, half), F32),
            pltpu.SemaphoreType.DMA((2, copies)),
        ],
        compiler_params=params(60),
        cost_estimate=pl.CostEstimate(flops=10**7, bytes_accessed=40 * MIB, transcendentals=0),
        name="weight_gradient",
    )(me, cos_x, sin_x, spectrum, *pieces)


def swap(pieces):
    count = len(pieces)
    return pieces[:1] + [
        lax.ppermute(pieces[s], "space", [(d, d ^ s) for d in range(count)]) for s in range(1, count)
    ]


def suits(width_x, length_x, devices, channels, weights):
    held = weights.shape[2]
    even = np.array_equal(kept(MX, length_x) % length_x, np.arange(MX) % length_x)
    return (
        width_x == 1
        and held == 2 * MZ
        and devices * 2 == MY
        and 2 * held == LANES
        and MX % length_x == 0
        and length_x % 8 == 0
        and devices & (devices - 1) == 0
        and even
        and channels == MZ
    )


def body(lifted_field, cotangent, spectral_weights, point_weights, point_bias):
    devices = lax.axis_size("space")
    channels, width_x = lifted_field.shape[:2]
    length_x = width_x * devices
    if not suits(width_x, length_x, devices, channels, spectral_weights):
        return general_body(lifted_field, cotangent, spectral_weights, point_weights, point_bias)
    norm = float(length_x * NY * NZ) ** -0.5
    theta = angles(np.arange(length_x), np.arange(length_x), length_x)
    cos_x, sin_x = jnp.asarray(np.cos(theta), F32), jnp.asarray(np.sin(theta), F32)
    forward = forward_tables()
    inverse = inverse_tables(norm)
    summing = jnp.asarray(np.repeat(np.eye(channels), 8, axis=0), F32)

    field = lifted_field.reshape(channels, NY, NZ)
    slopes_in = cotangent.reshape(channels, NY, NZ)
    weights = jnp.transpose(spectral_weights, (0, 1, 3, 4, 2))

    me = lax.axis_index("space")[None]
    lines, half = forward_modes(me, field, forward, weights, length_x)
    lines = swap(lines)
    folded = fold_rest(weights, half, length_x)
    spectrum, mixed = mix(me, cos_x, sin_x, lines, folded, norm)
    field_late, *mixed = lax.optimization_barrier((field, *mixed))
    modes = swap(mixed)
    pre = pointwise(field_late, summing, point_weights, point_bias)
    activated, slope_lines = cell_stage(me, inverse, forward, summing, modes, pre, slopes_in, field)
    slope_lines = swap(slope_lines)
    grad, grad_point, grad_bias = gradient(me, cos_x, sin_x, spectrum, slope_lines, norm, MX)
    return (
        activated.reshape(cotangent.shape),
        jnp.transpose(grad, (0, 1, 4, 2, 3)),
        grad_point,
        grad_bias.reshape(channels),
    )


HIGHEST = lax.Precision.HIGHEST


def trig_tables(positions, frequency, length):
    product = positions[:, None] * frequency[None, :] % length
    phase_angle = 2.0 * jnp.pi / length * product.astype(jnp.float32)
    return (jnp.cos(phase_angle), jnp.sin(phase_angle))


def kept_frequencies(kept_count, length):
    mode_index = jnp.arange(kept_count, dtype=jnp.int32)
    return jnp.where(mode_index < kept_count // 2, mode_index, length - kept_count + mode_index)


def forward_local(field_in):
    channels = field_in.shape[0]
    width_x = field_in.shape[1]
    cos_z, sin_z = trig_tables(jnp.arange(NZ, dtype=jnp.int32), jnp.arange(MZ, dtype=jnp.int32), NZ)
    table_z = jnp.concatenate([cos_z, -sin_z], axis=1)
    along_z = jnp.einsum("cxyz,zk->cxyk", field_in, table_z, precision=HIGHEST)
    z_real = along_z[..., :MZ]
    z_imag = along_z[..., MZ:]
    cos_y, sin_y = trig_tables(jnp.arange(NY, dtype=jnp.int32), kept_frequencies(MY, NY), NY)
    y_real = jnp.einsum("cxyk,yj->xcjk", z_real, cos_y, precision=HIGHEST) + jnp.einsum(
        "cxyk,yj->xcjk", z_imag, sin_y, precision=HIGHEST
    )
    y_imag = jnp.einsum("cxyk,yj->xcjk", z_imag, cos_y, precision=HIGHEST) - jnp.einsum(
        "cxyk,yj->xcjk", z_real, sin_y, precision=HIGHEST
    )
    stacked = jnp.stack([y_real, y_imag], axis=1)
    return stacked.reshape(width_x, 2, channels, MY * MZ)


def transform_x(x_lines):
    length_x = x_lines.shape[0]
    cos_x, sin_x = trig_tables(
        jnp.arange(length_x, dtype=jnp.int32), kept_frequencies(MX, length_x), length_x
    )
    norm_scale = 1.0 / float(length_x * NY * NZ) ** 0.5
    part_real = x_lines[:, 0]
    part_imag = x_lines[:, 1]
    x_real = jnp.einsum("xcm,xk->kcm", part_real, cos_x, precision=HIGHEST) + jnp.einsum(
        "xcm,xk->kcm", part_imag, sin_x, precision=HIGHEST
    )
    x_imag = jnp.einsum("xcm,xk->kcm", part_imag, cos_x, precision=HIGHEST) - jnp.einsum(
        "xcm,xk->kcm", part_real, sin_x, precision=HIGHEST
    )
    return norm_scale * jnp.stack([x_real, x_imag], axis=1)


def mix_modes(spectrum, weights):
    spec_real = spectrum[:, 0]
    spec_imag = spectrum[:, 1]
    out_real = jnp.einsum("kim,kmio->kom", spec_real, weights[0], precision=HIGHEST) - jnp.einsum(
        "kim,kmio->kom", spec_imag, weights[1], precision=HIGHEST
    )
    out_imag = jnp.einsum("kim,kmio->kom", spec_real, weights[1], precision=HIGHEST) + jnp.einsum(
        "kim,kmio->kom", spec_imag, weights[0], precision=HIGHEST
    )
    return jnp.stack([out_real, out_imag], axis=1)


def inverse_x(spectrum, positions, length_x):
    cos_x, sin_x = trig_tables(positions, kept_frequencies(MX, length_x), length_x)
    spec_real = spectrum[:, 0]
    spec_imag = spectrum[:, 1]
    a_real = jnp.einsum("kcm,xk->xcm", spec_real, cos_x, precision=HIGHEST) - jnp.einsum(
        "kcm,xk->xcm", spec_imag, sin_x, precision=HIGHEST
    )
    a_imag = jnp.einsum("kcm,xk->xcm", spec_imag, cos_x, precision=HIGHEST) + jnp.einsum(
        "kcm,xk->xcm", spec_real, sin_x, precision=HIGHEST
    )
    return jnp.stack([a_real, a_imag], axis=1)


def inverse_yz(x_lines, length_x):
    width_x = x_lines.shape[0]
    channels = x_lines.shape[2]
    mode_grid = x_lines.reshape(width_x, 2, channels, MY, MZ)
    cos_y, sin_y = trig_tables(jnp.arange(NY, dtype=jnp.int32), kept_frequencies(MY, NY), NY)
    b_real = jnp.einsum("xcjk,yj->cxyk", mode_grid[:, 0], cos_y, precision=HIGHEST) - jnp.einsum(
        "xcjk,yj->cxyk", mode_grid[:, 1], sin_y, precision=HIGHEST
    )
    b_imag = jnp.einsum("xcjk,yj->cxyk", mode_grid[:, 1], cos_y, precision=HIGHEST) + jnp.einsum(
        "xcjk,yj->cxyk", mode_grid[:, 0], sin_y, precision=HIGHEST
    )
    cos_z, sin_z = trig_tables(jnp.arange(NZ, dtype=jnp.int32), jnp.arange(MZ, dtype=jnp.int32), NZ)
    weight_z = jnp.where(jnp.arange(MZ, dtype=jnp.int32) == 0, 1.0, 2.0).astype(jnp.float32)
    table_z = jnp.concatenate([cos_z * weight_z[None, :], -sin_z * weight_z[None, :]], axis=1)
    stacked = jnp.concatenate([b_real, b_imag], axis=-1)
    result = jnp.einsum("cxyk,zk->cxyz", stacked, table_z, precision=HIGHEST)
    return result * (1.0 / float(length_x * NY * NZ) ** 0.5)


def gelu_slope(values):
    return (
        0.5 * (1.0 + lax.erf(values * INV_SQRT_TWO))
        + values * jnp.exp(-0.5 * values * values) * INV_SQRT_TWO_PI
    )


def weight_gradient(spectrum, slope_modes, first_mode):
    mode_ids = first_mode + jnp.arange(spectrum.shape[3], dtype=jnp.int32)
    weight_modes = jnp.where(mode_ids % MZ == 0, 1.0, 2.0).astype(jnp.float32)
    grad_real = jnp.einsum(
        "kim,kom->kmio", spectrum[:, 0], slope_modes[:, 0], precision=HIGHEST
    ) + jnp.einsum("kim,kom->kmio", spectrum[:, 1], slope_modes[:, 1], precision=HIGHEST)
    grad_imag = jnp.einsum(
        "kim,kom->kmio", spectrum[:, 0], slope_modes[:, 1], precision=HIGHEST
    ) - jnp.einsum("kim,kom->kmio", spectrum[:, 1], slope_modes[:, 0], precision=HIGHEST)
    stacked = jnp.stack([grad_real, grad_imag], axis=0)
    return stacked * weight_modes[None, None, :, None, None]


def to_modes(field_in):
    return transform_x(
        lax.all_to_all(forward_local(field_in), "space", split_axis=3, concat_axis=0, tiled=True)
    )


def general_body(lifted_field, cotangent, spectral_weights, point_weights, point_bias):
    devices = lax.axis_size("space")
    width_x = lifted_field.shape[1]
    length_x = width_x * devices
    spectrum = to_modes(lifted_field)
    mixed_modes = mix_modes(spectrum, spectral_weights)
    full_lines = inverse_x(mixed_modes, jnp.arange(length_x, dtype=jnp.int32), length_x)
    spectral = inverse_yz(
        lax.all_to_all(full_lines, "space", split_axis=0, concat_axis=3, tiled=True), length_x
    )
    pointwise = (
        jnp.einsum("ixyz,io->oxyz", lifted_field, point_weights, precision=HIGHEST)
        + point_bias[:, None, None, None]
    )
    before = spectral + pointwise
    activated = jax.nn.gelu(before, approximate=False).astype(jnp.bfloat16)
    slope_field = cotangent.astype(jnp.float32) * gelu_slope(before)
    local_point = jnp.einsum("ixyz,oxyz->io", lifted_field, slope_field, precision=HIGHEST)
    local_bias = jnp.sum(slope_field, axis=(1, 2, 3))
    partial = jnp.concatenate([local_point, local_bias[None, :]], axis=0)
    gathered = lax.all_gather(partial, "space", axis=0, tiled=False)
    summed = jnp.sum(gathered, axis=0)
    summed_point, summed_bias = summed[:-1], summed[-1]
    root_cells = float(length_x * NY * NZ) ** 0.5
    slope_spectrum = to_modes(slope_field)
    first_mode = lax.axis_index("space") * spectrum.shape[3]
    grad_spectral = weight_gradient(spectrum, slope_spectrum, first_mode)
    return (activated, grad_spectral, summed_point / root_cells, summed_bias / root_cells)


def solution(mesh):
    placed = (
        P("groups", "space", None, None),
        P("groups", "space", None, None),
        P(None, None, "space", None, None),
        P(),
        P(),
    )
    return jax.shard_map(
        body,
        mesh=mesh,
        in_specs=placed,
        out_specs=(
            P("groups", "space", None, None),
            P("groups", None, "space", None, None),
            P("groups", None),
            P("groups"),
        ),
        check_vma=False,
    )
```

```python
import functools

import jax
import jax.numpy as jnp
import ml_dtypes
import numpy as np
from jax import lax
from jax.experimental import pallas as pl
from jax.experimental.pallas import tpu as pltpu
from jax.sharding import PartitionSpec as P

MX = 32
MY = 32
MZ = 32
NY = 128
NZ = 256

F32 = jnp.float32
BF16 = jnp.bfloat16
INV_SQRT_TWO = 0.7071067811865476
INV_SQRT_TWO_PI = 0.3989422804014327
MIB = 1 << 20
LANES = 128
GROUP = 4
STEP = 8


def kept(kept_count, length):
    index = np.arange(kept_count)
    return np.where(index < kept_count // 2, index, length - kept_count + index)


def angles(positions, frequency, length):
    product = positions[:, None] * frequency[None, :] % length
    return 2.0 * np.pi / length * product


def split_table(table):
    high = table.astype(ml_dtypes.bfloat16)
    return high, (table - high.astype(np.float64)).astype(ml_dtypes.bfloat16)


def lane_spread(first, second, real_table, imag_table):
    return np.concatenate(
        [real_table * first, real_table * second, imag_table * first, imag_table * second], axis=1
    )


def forward_tables():
    theta = angles(np.arange(NZ), np.arange(MZ), NZ)
    cos_z, sin_z = np.cos(theta), np.sin(theta)
    plain = [lane_spread(f, s, cos_z, -sin_z) for f, s in ((1, 0), (0, 1))]
    turned = [lane_spread(f, s, -sin_z, -cos_z) for f, s in ((1, 0), (0, 1))]
    table_z = np.concatenate([np.concatenate(plain, 0), np.concatenate(turned, 0)], axis=1)
    theta = angles(np.arange(NY), kept(MY, NY), NY)
    both = np.concatenate([np.cos(theta).T, np.sin(theta).T], axis=1)
    table_y = np.concatenate([both[0::2], both[1::2]], axis=0)
    z_high, z_low = split_table(table_z)
    y_high, y_low = split_table(table_y)
    return z_high, z_low, np.concatenate([y_high, y_low], axis=0)


def inverse_tables(norm):
    theta = angles(np.arange(NY), kept(MY, NY), NY)
    cos_y, sin_y = np.cos(theta), np.sin(theta)
    table_y = np.concatenate([cos_y[:, 0::2], cos_y[:, 1::2], sin_y[:, 0::2], sin_y[:, 1::2]], axis=1)
    y_high, y_low = split_table(table_y)
    theta = angles(np.arange(NZ), np.arange(MZ), NZ)
    weight = np.where(np.arange(MZ) == 0, 1.0, 2.0) * norm
    cos_z, sin_z = np.cos(theta) * weight, -np.sin(theta) * weight
    table_z = np.concatenate([lane_spread(f, s, cos_z, sin_z).T for f, s in ((1, 0), (0, 1))], axis=1)
    z_high, z_low = split_table(table_z)
    return (
        np.concatenate([y_high, y_high, y_low], axis=1),
        np.concatenate([z_high, z_high], axis=0),
        z_low,
    )


def dot(left, right):
    return jnp.dot(left, right, preferred_element_type=F32)


def split(values):
    high = values.astype(BF16)
    return high, (values - high.astype(F32)).astype(BF16)


def lane_index(shape):
    return lax.broadcasted_iota(jnp.int32, shape, len(shape) - 1)


def roll(values, shift):
    return pltpu.roll(values, shift % LANES, len(values.shape) - 1)


def forward_group(fields, z_high, z_low, y_both, out_ref, first, rows):
    left = jnp.concatenate(
        [jnp.concatenate([fields[q], fields[q + 1]], axis=1) for q in range(0, len(fields), 2)], axis=0
    )
    high, low = split(left)
    lines = dot(high, z_high) + dot(high, z_low) + dot(low, z_high)
    half = MY // 2
    for g in range(0, len(fields) // 2, GROUP // 2):
        pairs = []
        for q in range(g, g + GROUP // 2):
            part = lines[q * NY : (q + 1) * NY]
            pairs.append(jnp.concatenate([part[:, :LANES], part[:, LANES:]], axis=0))
        high, low = split(jnp.concatenate(pairs, axis=1))
        wide = dot(y_both, high)
        modes = wide[:MY] + wide[MY:] + dot(y_both[:MY], low)
        for q in range(GROUP // 2):
            even = modes[:half, q * LANES : (q + 1) * LANES]
            odd = modes[half:, q * LANES : (q + 1) * LANES]
            at_even = (lane_index(even.shape) // MZ) % 2 == 0
            at = first + 2 * (g + q)
            out_ref[pl.ds(at, half, stride=rows), :] = jnp.where(at_even, even, roll(odd, MZ))
            out_ref[pl.ds(at + 1, half, stride=rows), :] = jnp.where(at_even, roll(even, -MZ), odd)


def inverse_y_group(modes_ref, y_table, first, rows):
    half = MY // 2
    pairs = []
    for q in range(GROUP // 2):
        c0 = modes_ref[pl.ds(first + 2 * q, half, stride=rows), :]
        c1 = modes_ref[pl.ds(first + 2 * q + 1, half, stride=rows), :]
        at_even = (lane_index(c0.shape) // MZ) % 2 == 0
        even = jnp.where(at_even, c0, roll(c1, MZ))
        odd = jnp.where(at_even, roll(c0, -MZ), c1)
        both = jnp.concatenate([even, odd], axis=0)
        other = roll(both, 64)
        turned = jnp.where(lane_index(both.shape) < LANES // 2, -other, other)
        pairs.append(jnp.concatenate([both, turned], axis=0))
    high, low = split(jnp.concatenate(pairs, axis=1))
    lines = dot(y_table, jnp.concatenate([high, low, high], axis=0))
    return [lines[:, q * LANES : (q + 1) * LANES] for q in range(GROUP // 2)]


def full(shape):
    return pl.BlockSpec(shape, lambda *_: (0,) * len(shape))


def params(limit):
    return pltpu.CompilerParams(vmem_limit_bytes=limit * MIB)


def fold_block(pieces, out_ref, at):
    real, imag = pieces[0][0, at], pieces[0][1, at]
    for piece in pieces[1:]:
        real, imag = real + piece[0, at], imag + piece[1, at]
    modes = real.shape[-1]
    out_ref[at, :, :, :modes] = real
    out_ref[at, :, :, modes:] = imag


def fold_specs(weights, unique, per_step, first):
    block = (2, per_step) + weights.shape[2:]
    pieces = [
        pl.BlockSpec(block, functools.partial(lambda s, r: (0, first + s + r, 0, 0, 0), r=r * (unique // per_step)))
        for r in range(weights.shape[1] // unique)
    ]
    shape = (unique,) + weights.shape[2:4] + (2 * weights.shape[4],)
    out = pl.BlockSpec((per_step,) + shape[1:], lambda s: (first + s, 0, 0, 0))
    return pieces, out, jax.ShapeDtypeStruct(shape, F32)


def forward_kernel(z_high, z_low, y_both, field_ref, *refs, channels, step_channels, per_step):
    *pieces, out_ref, folded_ref = refs
    step = pl.program_id(0)
    for at in range(per_step):
        fold_block(pieces, folded_ref, at)
    fields = [field_ref[q] for q in range(step_channels)]
    forward_group(fields, z_high[...], z_low[...], y_both[...], out_ref, step * step_channels, channels)


def forward_modes(field, tables, weights, unique):
    channels = field.shape[0]
    step_channels = 8
    steps = channels // step_channels
    per_step = unique // 2 // steps
    pieces, folded, folded_shape = fold_specs(weights, unique, per_step, 0)
    owners = MY // 2
    out, half = pl.pallas_call(
        functools.partial(forward_kernel, channels=channels, step_channels=step_channels, per_step=per_step),
        grid=(steps,),
        in_specs=[full(t.shape) for t in tables]
        + [pl.BlockSpec((step_channels, NY, NZ), lambda s: (s, 0, 0))]
        + pieces,
        out_specs=[full((owners * channels, LANES)), folded],
        out_shape=[jax.ShapeDtypeStruct((owners * channels, LANES), F32), folded_shape],
        compiler_params=params(60),
        cost_estimate=pl.CostEstimate(flops=2 * 10**9, bytes_accessed=26 * MIB, transcendentals=0),
        name="forward_yz",
    )(*tables, field, *([weights] * len(pieces)))
    return out.reshape(owners, channels, LANES), half


def fold_kernel(*refs):
    *pieces, _, out_ref = refs
    fold_block(pieces, out_ref, 0)


def fold_rest(weights, half, unique):
    first = unique // 2
    pieces, folded, folded_shape = fold_specs(weights, unique, 1, first)
    return pl.pallas_call(
        fold_kernel,
        grid=(unique - first,),
        in_specs=pieces + [pl.BlockSpec(memory_space=pl.ANY)],
        out_specs=folded,
        out_shape=folded_shape,
        input_output_aliases={len(pieces): 0},
        compiler_params=params(60),
        cost_estimate=pl.CostEstimate(flops=4 * 10**6, bytes_accessed=20 * MIB, transcendentals=0),
        name="fold_weights",
    )(*([weights] * len(pieces)), half)


def halve_lines(lines_ref, sums_ref, points, channels):
    half = points // 2
    sign = jnp.where(lane_index((channels, LANES)) < LANES // 2, 1.0, -1.0)
    for x in range(half):
        near, far = lines_ref[x, :channels], lines_ref[x + half, :channels]
        for parity, value in enumerate((near + far, near - far)):
            sums_ref[parity, 0, x] = value
            sums_ref[parity, 1, x] = sign * roll(value, 64)


def spectrum_row(cos_ref, sin_ref, sums_ref, at, parity, half):
    total = cos_ref[at, 0] * sums_ref[parity, 0, 0] + sin_ref[at, 0] * sums_ref[parity, 1, 0]
    for x in range(1, half):
        total += cos_ref[at, x] * sums_ref[parity, 0, x] + sin_ref[at, x] * sums_ref[parity, 1, x]
    return total


def doubled(values):
    other = roll(values, 64)
    low = lane_index(values.shape) < LANES // 2
    return jnp.where(low, values, other), jnp.where(low, other, values)


def mix_kernel(
    cos_ref, sin_ref, lines_ref, weights_ref, spec_ref, out_ref, sums_ref, total_ref, real_ref, imag_ref,
    *, points, channels, per_step, norm,
):
    step = pl.program_id(0)
    half = points // 2

    @pl.when(step == 0)
    def _():
        halve_lines(lines_ref, sums_ref, points, channels)
        total_ref[...] = jnp.zeros_like(total_ref)

    low = lane_index((channels, LANES)) < LANES // 2
    for q in range(per_step):
        at = step * per_step + q
        parity = q % 2
        spec = norm * spectrum_row(cos_ref, sin_ref, sums_ref, at, parity, half)
        spec_ref[q] = spec
        real_ref[q], imag_ref[q] = doubled(spec)
        by_real = jnp.zeros((channels, LANES), F32)
        by_imag = jnp.zeros((channels, LANES), F32)
        for i in range(channels):
            weight = weights_ref[q, i]
            by_real += real_ref[q, pl.ds(i, 1), :] * weight
            by_imag += imag_ref[q, pl.ds(i, 1), :] * weight
        other = roll(by_imag, 64)
        mixed = by_real + jnp.where(low, -other, other)
        other = roll(mixed, 64)
        turned = jnp.where(low, -other, other)
        for x in range(half):
            total_ref[parity, x] += cos_ref[at, x] * mixed + sin_ref[at, x] * turned

    @pl.when(step == pl.num_programs(0) - 1)
    def _():
        for x in range(half):
            out_ref[x] = total_ref[0, x] + total_ref[1, x]
            out_ref[x + half] = total_ref[0, x] - total_ref[1, x]


def smem():
    return pl.BlockSpec(memory_space=pltpu.SMEM)


def mix(cos_x, sin_x, lines, weights, norm):
    points, channels, _ = lines.shape
    unique = weights.shape[0]
    per_step = min(unique, 4)
    shape = (points, channels, LANES)
    return pl.pallas_call(
        functools.partial(mix_kernel, points=points, channels=channels, per_step=per_step, norm=norm),
        grid=(unique // per_step,),
        in_specs=[
            smem(),
            smem(),
            full(shape),
            pl.BlockSpec((per_step,) + weights.shape[1:], lambda s: (s, 0, 0, 0)),
        ],
        out_specs=[
            pl.BlockSpec((per_step, channels, LANES), lambda s: (s, 0, 0)),
            full(shape),
        ],
        out_shape=[
            jax.ShapeDtypeStruct((unique, channels, LANES), F32),
            jax.ShapeDtypeStruct(shape, F32),
        ],
        scratch_shapes=[
            pltpu.VMEM((2, 2, points // 2, channels, LANES), F32),
            pltpu.VMEM((2, points // 2, channels, LANES), F32),
            pltpu.VMEM((per_step, channels, LANES), F32),
            pltpu.VMEM((per_step, channels, LANES), F32),
        ],
        compiler_params=params(60),
        cost_estimate=pl.CostEstimate(flops=2 * 10**7, bytes_accessed=9 * MIB, transcendentals=0),
        name="mix_modes",
    )(cos_x, sin_x, lines, weights)


def exact_dot(left, right):
    return jnp.dot(left, right, precision=lax.Precision.HIGHEST, preferred_element_type=F32)


def pointwise_kernel(sum_ref, turned_ref, bias_in_ref, field_ref, out_ref, mixer_ref, bias_ref, *, channels, blocks):
    size = 8 * channels

    @pl.when(pl.program_id(0) == 0)
    def _():
        wide = exact_dot(sum_ref[...], turned_ref[...])
        wide = lax.dot_general(
            wide, sum_ref[...], (((1,), (1,)), ((), ())), precision=lax.Precision.HIGHEST, preferred_element_type=F32
        )
        row = lax.broadcasted_iota(jnp.int32, (size, size), 0) % 8
        high, low = split(jnp.where(row == lane_index((size, size)) % 8, wide, 0.0))
        mixer_ref[:size] = high
        mixer_ref[size:] = low
        bias_ref[...] = exact_dot(sum_ref[...], bias_in_ref[...])

    for b in range(blocks):
        high, low = split(field_ref[:, 8 * b : 8 * b + 8, :].reshape(size, NZ))
        wide = dot(mixer_ref[...], high)
        values = wide[:size] + wide[size:] + dot(mixer_ref[:size], low) + bias_ref[...]
        out_ref[:, 8 * b : 8 * b + 8, :] = values.reshape(channels, 8, NZ)


def pointwise(field, summing, point_weights, point_bias):
    channels = field.shape[0]
    blocks = 2
    turned = point_weights.T
    bias = point_bias[:, None]
    size = 8 * channels
    block = pl.BlockSpec((channels, 8 * blocks, NZ), lambda s: (0, s, 0))
    return pl.pallas_call(
        functools.partial(pointwise_kernel, channels=channels, blocks=blocks),
        grid=(NY // (8 * blocks),),
        in_specs=[full(summing.shape), full(turned.shape), full(bias.shape), block],
        out_specs=block,
        out_shape=jax.ShapeDtypeStruct(field.shape, F32),
        scratch_shapes=[pltpu.VMEM((2 * size, size), BF16), pltpu.VMEM((size, 1), F32)],
        compiler_params=params(60),
        cost_estimate=pl.CostEstimate(flops=4 * 10**9, bytes_accessed=24 * MIB, transcendentals=0),
        name="pointwise",
    )(summing, turned, bias, field)


def cell_group(inv_y, inv_z, inv_z_low, modes_ref, pre_ref, cot_ref, act_ref, first, count, channels):
    lines = []
    for g in range(0, count, GROUP):
        lines += inverse_y_group(modes_ref, inv_y, first + g, channels)
    high, low = split(jnp.concatenate(lines, axis=0))
    spectral = dot(jnp.concatenate([high, low], axis=1), inv_z) + dot(high, inv_z_low)
    slopes = []
    for q in range(count):
        r = q // 2 * NY
        c = q % 2 * NZ
        before = spectral[r : r + NY, c : c + NZ] + pre_ref[q]
        cdf = 0.5 + 0.5 * lax.erf(before * INV_SQRT_TWO)
        act_ref[q] = (before * cdf).astype(BF16)
        pdf = jnp.exp(-0.5 * before * before) * INV_SQRT_TWO_PI
        slopes.append(cot_ref[q].astype(F32) * (cdf + before * pdf))
    return slopes


def early_cell_kernel(
    inv_y, inv_z, inv_z_low, z_high, z_low, y_both, modes_ref, pre_ref, cot_ref, act_ref, slope_ref, out_ref,
    *, channels, count, rows,
):
    step = pl.program_id(0)
    slopes = cell_group(
        inv_y[...], inv_z[...], inv_z_low[...], modes_ref, pre_ref, cot_ref, act_ref, step * count, count, channels
    )
    for q in range(count):
        slope_ref[q] = slopes[q]
    forward_group(slopes, z_high[...], z_low[...], y_both[...], out_ref, step * count, rows)


def point_gradient(field_ref, slope_ref, sum_ref, channels):
    size = 8 * channels
    total = jnp.zeros((size, size), F32)
    for b in range(NY // 8):
        at = slice(8 * b, 8 * b + 8)
        f_h, f_l = split(field_ref[:, at, :].reshape(size, NZ))
        s_h, s_l = split(slope_ref[:, at, :].reshape(size, NZ))
        total += lax.dot_general(
            jnp.concatenate([f_h, f_h, f_l], axis=1),
            jnp.concatenate([s_h, s_l, s_h], axis=1),
            (((1,), (1,)), ((), ())),
            preferred_element_type=F32,
        )
    row = lax.broadcasted_iota(jnp.int32, (size, size), 0) % 8
    total = jnp.where(row == lane_index((size, size)) % 8, total, 0.0)
    return exact_dot(jnp.sum(total.reshape(channels, 8, size), axis=1), sum_ref[...])


def late_cell_kernel(
    inv_y, inv_z, inv_z_low, z_high, z_low, y_both, sum_ref, modes_ref, pre_ref, cot_ref, early_ref,
    slope_hbm, field_hbm, _, act_ref, out_ref, field_ref, slope_ref, sems, *, channels, count, rows, owners,
):
    step = pl.program_id(0)
    half = channels // 2
    copies = [
        pltpu.make_async_copy(field_hbm, field_ref, sems.at[0]),
        pltpu.make_async_copy(slope_hbm, slope_ref.at[pl.ds(0, half)], sems.at[1]),
    ]

    @pl.when(step == 0)
    def _():
        for copy in copies:
            copy.start()

    first = half + step * count
    slopes = cell_group(
        inv_y[...], inv_z[...], inv_z_low[...], modes_ref, pre_ref, cot_ref, act_ref, first, count, channels
    )
    for q in range(count):
        slope_ref[first + q] = slopes[q]
    forward_group(slopes, z_high[...], z_low[...], y_both[...], out_ref, step * count, rows)

    @pl.when(step == pl.num_programs(0) - 1)
    def _():
        for copy in copies:
            copy.wait()
        point = point_gradient(field_ref, slope_ref, sum_ref, channels)
        packed = jnp.concatenate([point[8 * q : 8 * q + 8] for q in range(channels // 8)], axis=1)
        zero_mode = jnp.concatenate([early_ref[0:half, 0:1], out_ref[0:half, 0:1]], axis=0)
        eye = lax.broadcasted_iota(jnp.int32, (channels, LANES), 0) == lane_index((channels, LANES))
        bias = jnp.sum(jnp.where(eye, jnp.broadcast_to(zero_mode, (channels, LANES)), 0.0), axis=0, keepdims=True)
        extra = jnp.where(lax.broadcasted_iota(jnp.int32, (8, LANES), 0) == 0, jnp.broadcast_to(bias, (8, LANES)), 0.0)
        for d in range(owners):
            out_ref[d * rows + half : d * rows + half + 8, :] = packed
            out_ref[d * rows + half + 8 : (d + 1) * rows, :] = extra


def early_cells(inverse, forward, modes, pre, cotangent):
    channels = pre.shape[0]
    owners = MY // 2
    half = channels // 2
    block = pl.BlockSpec((STEP, NY, NZ), lambda s: (s, 0, 0))
    tables = (*inverse, *forward)
    act, slope, out = pl.pallas_call(
        functools.partial(early_cell_kernel, channels=channels, count=STEP, rows=half),
        grid=(half // STEP,),
        in_specs=[full(t.shape) for t in tables] + [full((owners * channels, LANES)), block, block],
        out_specs=[block, block, full((owners * half, LANES))],
        out_shape=[
            jax.ShapeDtypeStruct((channels, NY, NZ), BF16),
            jax.ShapeDtypeStruct((half, NY, NZ), F32),
            jax.ShapeDtypeStruct((owners * half, LANES), F32),
        ],
        compiler_params=params(60),
        cost_estimate=pl.CostEstimate(flops=3 * 10**9, bytes_accessed=7 * MIB, transcendentals=10**6),
        name="early_cells",
    )(*tables, modes.reshape(owners * channels, LANES), pre, cotangent)
    return act, slope, out.reshape(owners, half, LANES)


def late_cells(inverse, forward, summing, modes, pre, cotangent, field, early, slope, act):
    channels = field.shape[0]
    owners = MY // 2
    half = channels // 2
    rows = half + 16
    start = half // STEP
    block = pl.BlockSpec((STEP, NY, NZ), lambda s: (start + s, 0, 0))
    anywhere = pl.BlockSpec(memory_space=pl.ANY)
    tables = (*inverse, *forward, summing)
    act, out = pl.pallas_call(
        functools.partial(late_cell_kernel, channels=channels, count=STEP, rows=rows, owners=owners),
        grid=(start,),
        in_specs=[full(t.shape) for t in tables]
        + [full((owners * channels, LANES)), block, block, full((owners * half, LANES))]
        + [anywhere] * 3,
        out_specs=[block, full((owners * rows, LANES))],
        out_shape=[
            jax.ShapeDtypeStruct((channels, NY, NZ), BF16),
            jax.ShapeDtypeStruct((owners * rows, LANES), F32),
        ],
        scratch_shapes=[
            pltpu.VMEM((channels, NY, NZ), F32),
            pltpu.VMEM((channels, NY, NZ), F32),
            pltpu.SemaphoreType.DMA((2,)),
        ],
        input_output_aliases={len(tables) + 6: 0},
        compiler_params=params(60),
        cost_estimate=pl.CostEstimate(flops=6 * 10**9, bytes_accessed=11 * MIB, transcendentals=10**6),
        name="late_cells",
    )(
        *tables, modes.reshape(owners * channels, LANES), pre, cotangent, early.reshape(owners * half, LANES),
        slope, field, act,
    )
    return act, out.reshape(owners, rows, LANES)


def gradient_kernel(cos_ref, sin_ref, spec_ref, lines_ref, *refs, points, channels, unique, copies, norm, part):
    if part == 1:
        _, out_hbm, point_ref, bias_ref, sums_ref, real_ref, imag_ref, buffer, sems = refs
    else:
        out_hbm, sums_ref, real_ref, imag_ref, buffer, sems = refs
    outputs = channels // 2
    halve_lines(lines_ref, sums_ref, points, outputs)
    half = LANES // 2
    lane = lane_index((outputs, LANES))
    scale = jnp.where(lane % MZ == 0, norm, 2.0 * norm)

    def writes(at, slot):
        return [
            pltpu.make_async_copy(
                buffer.at[slot],
                out_hbm.at[:, at + r * unique, :, pl.ds(part * outputs, outputs), :],
                sems.at[slot, r],
            )
            for r in range(copies)
        ]

    @pl.loop(0, unique // 2)
    def _(pair):
        for slot in range(2):
            at = 2 * pair + slot

            @pl.when(pair > 0)
            def _():
                for copy in writes(at - 2, slot):
                    copy.wait()

            slope = scale * spectrum_row(cos_ref, sin_ref, sums_ref, at, slot, points // 2)
            other = roll(slope, 64)
            flipped = jnp.where(lane < half, other, -other)
            real_ref[slot], imag_ref[slot] = doubled(spec_ref[at])
            for i in range(channels):
                both = real_ref[slot, pl.ds(i, 1), :] * slope + imag_ref[slot, pl.ds(i, 1), :] * flipped
                buffer[slot, 0, i] = both[:, :half]
                buffer[slot, 1, i] = both[:, half:]
            for copy in writes(at, slot):
                copy.start()

    if part == 1:
        packed = lines_ref[0, outputs : outputs + 16, :]
        for x in range(1, points):
            packed += lines_ref[x, outputs : outputs + 16, :]
        packed = norm * packed
        for q in range(channels // 8):
            point_ref[8 * q : 8 * q + 8, :] = packed[:8, q * channels : (q + 1) * channels]
        bias_ref[...] = packed[8:9, :channels]

    for at in range(unique - 2, unique):
        for copy in writes(at, at % 2):
            copy.wait()


def gradient(cos_x, sin_x, spectrum, lines, norm, kept_x, part, before=()):
    points, rows, _ = lines.shape
    unique, channels, _ = spectrum.shape
    half = LANES // 2
    copies = kept_x // unique
    anywhere = pl.BlockSpec(memory_space=pl.ANY)
    shape = jax.ShapeDtypeStruct((2, kept_x, channels, channels, half), F32)
    sums = [(channels, channels), (1, channels)] if part == 1 else []
    return pl.pallas_call(
        functools.partial(
            gradient_kernel, points=points, channels=channels, unique=unique, copies=copies, norm=norm, part=part
        ),
        in_specs=[smem(), smem(), full(spectrum.shape), full(lines.shape)] + [anywhere] * len(before),
        out_specs=[anywhere] + [full(each) for each in sums],
        out_shape=[shape] + [jax.ShapeDtypeStruct(each, F32) for each in sums],
        scratch_shapes=[
            pltpu.VMEM((2, 2, points // 2, channels // 2, LANES), F32),
            pltpu.VMEM((2, channels, LANES), F32),
            pltpu.VMEM((2, channels, LANES), F32),
            pltpu.VMEM((2, 2, channels, channels // 2, half), F32),
            pltpu.SemaphoreType.DMA((2, copies)),
        ],
        input_output_aliases={4: 0} if before else {},
        compiler_params=params(60),
        cost_estimate=pl.CostEstimate(flops=5 * 10**6, bytes_accessed=32 * MIB, transcendentals=0),
        name="weight_gradient",
    )(cos_x, sin_x, spectrum, lines, *before)


def swap(lines):
    return lax.all_to_all(lines, "space", split_axis=0, concat_axis=0, tiled=True)


def suits(width_x, length_x, devices, channels, weights):
    held = weights.shape[2]
    even = np.array_equal(kept(MX, length_x) % length_x, np.arange(MX) % length_x)
    return (
        width_x == 1
        and held == 2 * MZ
        and devices * 2 == MY
        and 2 * held == LANES
        and MX % length_x == 0
        and length_x % 8 == 0
        and even
        and channels == MZ
    )


def body(lifted_field, cotangent, spectral_weights, point_weights, point_bias):
    devices = lax.axis_size("space")
    channels, width_x = lifted_field.shape[:2]
    length_x = width_x * devices
    if not suits(width_x, length_x, devices, channels, spectral_weights):
        return general_body(lifted_field, cotangent, spectral_weights, point_weights, point_bias)
    norm = float(length_x * NY * NZ) ** -0.5
    theta = angles(np.arange(length_x), np.arange(length_x), length_x)
    cos_x, sin_x = jnp.asarray(np.cos(theta), F32), jnp.asarray(np.sin(theta), F32)
    forward = forward_tables()
    inverse = inverse_tables(norm)
    summing = jnp.asarray(np.repeat(np.eye(channels), 8, axis=0), F32)

    field = lifted_field.reshape(channels, NY, NZ)
    slopes_in = cotangent.reshape(channels, NY, NZ)
    weights = jnp.transpose(spectral_weights, (0, 1, 3, 4, 2))

    lines, half = forward_modes(field, forward, weights, length_x)
    lines = swap(lines)
    folded = fold_rest(weights, half, length_x)
    spectrum, mixed = mix(cos_x, sin_x, lines, folded, norm)
    field_late, mixed = lax.optimization_barrier((field, mixed))
    modes = swap(mixed)
    pre = pointwise(field_late, summing, point_weights, point_bias)
    act, slope, early = early_cells(inverse, forward, modes, pre, slopes_in)
    early_lines = swap(early)
    activated, late = late_cells(inverse, forward, summing, modes, pre, slopes_in, field, early, slope, act)
    late_lines = swap(late)
    (grad,) = gradient(cos_x, sin_x, spectrum, early_lines, norm, MX, 0)
    grad, grad_point, grad_bias = gradient(cos_x, sin_x, spectrum, late_lines, norm, MX, 1, (grad,))
    return (
        activated.reshape(cotangent.shape),
        jnp.transpose(grad, (0, 1, 4, 2, 3)),
        grad_point,
        grad_bias.reshape(channels),
    )


HIGHEST = lax.Precision.HIGHEST


def trig_tables(positions, frequency, length):
    product = positions[:, None] * frequency[None, :] % length
    phase_angle = 2.0 * jnp.pi / length * product.astype(jnp.float32)
    return (jnp.cos(phase_angle), jnp.sin(phase_angle))


def kept_frequencies(kept_count, length):
    mode_index = jnp.arange(kept_count, dtype=jnp.int32)
    return jnp.where(mode_index < kept_count // 2, mode_index, length - kept_count + mode_index)


def forward_local(field_in):
    channels = field_in.shape[0]
    width_x = field_in.shape[1]
    cos_z, sin_z = trig_tables(jnp.arange(NZ, dtype=jnp.int32), jnp.arange(MZ, dtype=jnp.int32), NZ)
    table_z = jnp.concatenate([cos_z, -sin_z], axis=1)
    along_z = jnp.einsum("cxyz,zk->cxyk", field_in, table_z, precision=HIGHEST)
    z_real = along_z[..., :MZ]
    z_imag = along_z[..., MZ:]
    cos_y, sin_y = trig_tables(jnp.arange(NY, dtype=jnp.int32), kept_frequencies(MY, NY), NY)
    y_real = jnp.einsum("cxyk,yj->xcjk", z_real, cos_y, precision=HIGHEST) + jnp.einsum(
        "cxyk,yj->xcjk", z_imag, sin_y, precision=HIGHEST
    )
    y_imag = jnp.einsum("cxyk,yj->xcjk", z_imag, cos_y, precision=HIGHEST) - jnp.einsum(
        "cxyk,yj->xcjk", z_real, sin_y, precision=HIGHEST
    )
    stacked = jnp.stack([y_real, y_imag], axis=1)
    return stacked.reshape(width_x, 2, channels, MY * MZ)


def transform_x(x_lines):
    length_x = x_lines.shape[0]
    cos_x, sin_x = trig_tables(
        jnp.arange(length_x, dtype=jnp.int32), kept_frequencies(MX, length_x), length_x
    )
    norm_scale = 1.0 / float(length_x * NY * NZ) ** 0.5
    part_real = x_lines[:, 0]
    part_imag = x_lines[:, 1]
    x_real = jnp.einsum("xcm,xk->kcm", part_real, cos_x, precision=HIGHEST) + jnp.einsum(
        "xcm,xk->kcm", part_imag, sin_x, precision=HIGHEST
    )
    x_imag = jnp.einsum("xcm,xk->kcm", part_imag, cos_x, precision=HIGHEST) - jnp.einsum(
        "xcm,xk->kcm", part_real, sin_x, precision=HIGHEST
    )
    return norm_scale * jnp.stack([x_real, x_imag], axis=1)


def mix_modes(spectrum, weights):
    spec_real = spectrum[:, 0]
    spec_imag = spectrum[:, 1]
    out_real = jnp.einsum("kim,kmio->kom", spec_real, weights[0], precision=HIGHEST) - jnp.einsum(
        "kim,kmio->kom", spec_imag, weights[1], precision=HIGHEST
    )
    out_imag = jnp.einsum("kim,kmio->kom", spec_real, weights[1], precision=HIGHEST) + jnp.einsum(
        "kim,kmio->kom", spec_imag, weights[0], precision=HIGHEST
    )
    return jnp.stack([out_real, out_imag], axis=1)


def inverse_x(spectrum, positions, length_x):
    cos_x, sin_x = trig_tables(positions, kept_frequencies(MX, length_x), length_x)
    spec_real = spectrum[:, 0]
    spec_imag = spectrum[:, 1]
    a_real = jnp.einsum("kcm,xk->xcm", spec_real, cos_x, precision=HIGHEST) - jnp.einsum(
        "kcm,xk->xcm", spec_imag, sin_x, precision=HIGHEST
    )
    a_imag = jnp.einsum("kcm,xk->xcm", spec_imag, cos_x, precision=HIGHEST) + jnp.einsum(
        "kcm,xk->xcm", spec_real, sin_x, precision=HIGHEST
    )
    return jnp.stack([a_real, a_imag], axis=1)


def inverse_yz(x_lines, length_x):
    width_x = x_lines.shape[0]
    channels = x_lines.shape[2]
    mode_grid = x_lines.reshape(width_x, 2, channels, MY, MZ)
    cos_y, sin_y = trig_tables(jnp.arange(NY, dtype=jnp.int32), kept_frequencies(MY, NY), NY)
    b_real = jnp.einsum("xcjk,yj->cxyk", mode_grid[:, 0], cos_y, precision=HIGHEST) - jnp.einsum(
        "xcjk,yj->cxyk", mode_grid[:, 1], sin_y, precision=HIGHEST
    )
    b_imag = jnp.einsum("xcjk,yj->cxyk", mode_grid[:, 1], cos_y, precision=HIGHEST) + jnp.einsum(
        "xcjk,yj->cxyk", mode_grid[:, 0], sin_y, precision=HIGHEST
    )
    cos_z, sin_z = trig_tables(jnp.arange(NZ, dtype=jnp.int32), jnp.arange(MZ, dtype=jnp.int32), NZ)
    weight_z = jnp.where(jnp.arange(MZ, dtype=jnp.int32) == 0, 1.0, 2.0).astype(jnp.float32)
    table_z = jnp.concatenate([cos_z * weight_z[None, :], -sin_z * weight_z[None, :]], axis=1)
    stacked = jnp.concatenate([b_real, b_imag], axis=-1)
    result = jnp.einsum("cxyk,zk->cxyz", stacked, table_z, precision=HIGHEST)
    return result * (1.0 / float(length_x * NY * NZ) ** 0.5)


def gelu_slope(values):
    return (
        0.5 * (1.0 + lax.erf(values * INV_SQRT_TWO))
        + values * jnp.exp(-0.5 * values * values) * INV_SQRT_TWO_PI
    )


def weight_gradient(spectrum, slope_modes, first_mode):
    mode_ids = first_mode + jnp.arange(spectrum.shape[3], dtype=jnp.int32)
    weight_modes = jnp.where(mode_ids % MZ == 0, 1.0, 2.0).astype(jnp.float32)
    grad_real = jnp.einsum(
        "kim,kom->kmio", spectrum[:, 0], slope_modes[:, 0], precision=HIGHEST
    ) + jnp.einsum("kim,kom->kmio", spectrum[:, 1], slope_modes[:, 1], precision=HIGHEST)
    grad_imag = jnp.einsum(
        "kim,kom->kmio", spectrum[:, 0], slope_modes[:, 1], precision=HIGHEST
    ) - jnp.einsum("kim,kom->kmio", spectrum[:, 1], slope_modes[:, 0], precision=HIGHEST)
    stacked = jnp.stack([grad_real, grad_imag], axis=0)
    return stacked * weight_modes[None, None, :, None, None]


def to_modes(field_in):
    return transform_x(
        lax.all_to_all(forward_local(field_in), "space", split_axis=3, concat_axis=0, tiled=True)
    )


def general_body(lifted_field, cotangent, spectral_weights, point_weights, point_bias):
    devices = lax.axis_size("space")
    width_x = lifted_field.shape[1]
    length_x = width_x * devices
    spectrum = to_modes(lifted_field)
    mixed_modes = mix_modes(spectrum, spectral_weights)
    full_lines = inverse_x(mixed_modes, jnp.arange(length_x, dtype=jnp.int32), length_x)
    spectral = inverse_yz(
        lax.all_to_all(full_lines, "space", split_axis=0, concat_axis=3, tiled=True), length_x
    )
    pointwise = (
        jnp.einsum("ixyz,io->oxyz", lifted_field, point_weights, precision=HIGHEST)
        + point_bias[:, None, None, None]
    )
    before = spectral + pointwise
    activated = jax.nn.gelu(before, approximate=False).astype(jnp.bfloat16)
    slope_field = cotangent.astype(jnp.float32) * gelu_slope(before)
    local_point = jnp.einsum("ixyz,oxyz->io", lifted_field, slope_field, precision=HIGHEST)
    local_bias = jnp.sum(slope_field, axis=(1, 2, 3))
    partial = jnp.concatenate([local_point, local_bias[None, :]], axis=0)
    gathered = lax.all_gather(partial, "space", axis=0, tiled=False)
    summed = jnp.sum(gathered, axis=0)
    summed_point, summed_bias = summed[:-1], summed[-1]
    root_cells = float(length_x * NY * NZ) ** 0.5
    slope_spectrum = to_modes(slope_field)
    first_mode = lax.axis_index("space") * spectrum.shape[3]
    grad_spectral = weight_gradient(spectrum, slope_spectrum, first_mode)
    return (activated, grad_spectral, summed_point / root_cells, summed_bias / root_cells)


def solution(mesh):
    placed = (
        P("groups", "space", None, None),
        P("groups", "space", None, None),
        P(None, None, "space", None, None),
        P(),
        P(),
    )
    return jax.shard_map(
        body,
        mesh=mesh,
        in_specs=placed,
        out_specs=(
            P("groups", "space", None, None),
            P("groups", None, "space", None, None),
            P("groups", None),
            P("groups"),
        ),
        check_vma=False,
    )
```

```python
import functools

import jax
import jax.numpy as jnp
import ml_dtypes
import numpy as np
from jax import lax
from jax.experimental import pallas as pl
from jax.experimental.pallas import tpu as pltpu
from jax.sharding import PartitionSpec as P

MX = 32
MY = 32
MZ = 32
NY = 128
NZ = 256

F32 = jnp.float32
BF16 = jnp.bfloat16
INV_SQRT_TWO = 0.7071067811865476
INV_SQRT_TWO_PI = 0.3989422804014327
MIB = 1 << 20
LIMIT = 48
LANES = 128
GROUP = 4
SLOTS = 4
STEP = 8


def kept(kept_count, length):
    index = np.arange(kept_count)
    return np.where(index < kept_count // 2, index, length - kept_count + index)


def angles(positions, frequency, length):
    product = positions[:, None] * frequency[None, :] % length
    return 2.0 * np.pi / length * product


def split_table(table):
    high = table.astype(ml_dtypes.bfloat16)
    return high, (table - high.astype(np.float64)).astype(ml_dtypes.bfloat16)


def lane_spread(first, second, real_table, imag_table):
    return np.concatenate(
        [real_table * first, real_table * second, imag_table * first, imag_table * second], axis=1
    )


def forward_tables():
    theta = angles(np.arange(NZ), np.arange(MZ), NZ)
    cos_z, sin_z = np.cos(theta), np.sin(theta)
    plain = [lane_spread(f, s, cos_z, -sin_z) for f, s in ((1, 0), (0, 1))]
    turned = [lane_spread(f, s, -sin_z, -cos_z) for f, s in ((1, 0), (0, 1))]
    table_z = np.concatenate([np.concatenate(plain, 0), np.concatenate(turned, 0)], axis=1)
    theta = angles(np.arange(NY), kept(MY, NY), NY)
    both = np.concatenate([np.cos(theta).T, np.sin(theta).T], axis=1)
    table_y = np.concatenate([both[0::2], both[1::2]], axis=0)
    z_high, z_low = split_table(table_z)
    y_high, y_low = split_table(table_y)
    return z_high, z_low, np.concatenate([y_high, y_low], axis=0)


def inverse_tables(norm):
    theta = angles(np.arange(NY), kept(MY, NY), NY)
    cos_y, sin_y = np.cos(theta), np.sin(theta)
    table_y = np.concatenate([cos_y[:, 0::2], cos_y[:, 1::2], sin_y[:, 0::2], sin_y[:, 1::2]], axis=1)
    y_high, y_low = split_table(table_y)
    theta = angles(np.arange(NZ), np.arange(MZ), NZ)
    weight = np.where(np.arange(MZ) == 0, 1.0, 2.0) * norm
    cos_z, sin_z = np.cos(theta) * weight, -np.sin(theta) * weight
    table_z = np.concatenate([lane_spread(f, s, cos_z, sin_z).T for f, s in ((1, 0), (0, 1))], axis=1)
    z_high, z_low = split_table(table_z)
    return (
        np.concatenate([y_high, y_high, y_low], axis=1),
        np.concatenate([z_high, z_high], axis=0),
        z_low,
    )


def dot(left, right):
    return jnp.dot(left, right, preferred_element_type=F32)


def split(values):
    high = values.astype(BF16)
    return high, (values - high.astype(F32)).astype(BF16)


def lane_index(shape):
    return lax.broadcasted_iota(jnp.int32, shape, len(shape) - 1)


def roll(values, shift):
    return pltpu.roll(values, shift % LANES, len(values.shape) - 1)


def forward_group(fields, z_high, z_low, y_both, out_ref, first, rows):
    left = jnp.concatenate(
        [jnp.concatenate([fields[q], fields[q + 1]], axis=1) for q in range(0, len(fields), 2)], axis=0
    )
    high, low = split(left)
    lines = dot(high, z_high) + dot(high, z_low) + dot(low, z_high)
    half = MY // 2
    for g in range(0, len(fields) // 2, GROUP // 2):
        pairs = []
        for q in range(g, g + GROUP // 2):
            part = lines[q * NY : (q + 1) * NY]
            pairs.append(jnp.concatenate([part[:, :LANES], part[:, LANES:]], axis=0))
        high, low = split(jnp.concatenate(pairs, axis=1))
        wide = dot(y_both, high)
        modes = wide[:MY] + wide[MY:] + dot(y_both[:MY], low)
        for q in range(GROUP // 2):
            even = modes[:half, q * LANES : (q + 1) * LANES]
            odd = modes[half:, q * LANES : (q + 1) * LANES]
            at_even = (lane_index(even.shape) // MZ) % 2 == 0
            at = first + 2 * (g + q)
            out_ref[pl.ds(at, half, stride=rows), :] = jnp.where(at_even, even, roll(odd, MZ))
            out_ref[pl.ds(at + 1, half, stride=rows), :] = jnp.where(at_even, roll(even, -MZ), odd)


def inverse_y_group(modes_ref, y_table, first, rows):
    half = MY // 2
    pairs = []
    for q in range(GROUP // 2):
        c0 = modes_ref[pl.ds(first + 2 * q, half, stride=rows), :]
        c1 = modes_ref[pl.ds(first + 2 * q + 1, half, stride=rows), :]
        at_even = (lane_index(c0.shape) // MZ) % 2 == 0
        even = jnp.where(at_even, c0, roll(c1, MZ))
        odd = jnp.where(at_even, roll(c0, -MZ), c1)
        both = jnp.concatenate([even, odd], axis=0)
        other = roll(both, 64)
        turned = jnp.where(lane_index(both.shape) < LANES // 2, -other, other)
        pairs.append(jnp.concatenate([both, turned], axis=0))
    high, low = split(jnp.concatenate(pairs, axis=1))
    lines = dot(y_table, jnp.concatenate([high, low, high], axis=0))
    return [lines[:, q * LANES : (q + 1) * LANES] for q in range(GROUP // 2)]


def in_hbm(*arrays):
    return [pltpu.with_memory_space_constraint(each, pltpu.HBM) for each in arrays]


def in_vmem(*arrays):
    return [pltpu.with_memory_space_constraint(each, pltpu.VMEM) for each in arrays]


def full(shape):
    return pl.BlockSpec(shape, lambda *_: (0,) * len(shape))


def params(limit):
    return pltpu.CompilerParams(vmem_limit_bytes=limit * MIB)


def fold_block(pieces, out_ref, at):
    real, imag = pieces[0][0, at], pieces[0][1, at]
    for piece in pieces[1:]:
        real, imag = real + piece[0, at], imag + piece[1, at]
    modes = real.shape[-1]
    out_ref[at, :, :, :modes] = real
    out_ref[at, :, :, modes:] = imag


def fold_specs(weights, unique, per_step, first):
    block = (2, per_step) + weights.shape[2:]
    pieces = [
        pl.BlockSpec(
            block,
            functools.partial(lambda s, r: (0, first + s + r, 0, 0, 0), r=r * (unique // per_step)),
        )
        for r in range(weights.shape[1] // unique)
    ]
    shape = (unique,) + weights.shape[2:4] + (2 * weights.shape[4],)
    out = pl.BlockSpec((per_step,) + shape[1:], lambda s: (first + s, 0, 0, 0))
    return pieces, out, pltpu.HBM(shape, F32)


def forward_kernel(z_high, z_low, y_both, field_ref, *refs, channels, step_channels, per_step):
    *pieces, out_ref, folded_ref = refs
    step = pl.program_id(0)
    for at in range(per_step):
        fold_block(pieces, folded_ref, at)
    fields = [field_ref[q] for q in range(step_channels)]
    forward_group(fields, z_high[...], z_low[...], y_both[...], out_ref, step * step_channels, channels)


def forward_modes(field, tables, weights, unique):
    channels = field.shape[0]
    step_channels = 8
    steps = channels // step_channels
    per_step = unique // 2 // steps
    pieces, folded, folded_shape = fold_specs(weights, unique, per_step, 0)
    owners = MY // 2
    out, half = pl.pallas_call(
        functools.partial(forward_kernel, channels=channels, step_channels=step_channels, per_step=per_step),
        grid=(steps,),
        in_specs=[full(t.shape) for t in tables]
        + [pl.BlockSpec((step_channels, NY, NZ), lambda s: (s, 0, 0))]
        + pieces,
        out_specs=[full((owners * channels, LANES)), folded],
        out_shape=[pltpu.VMEM((owners * channels, LANES), F32), folded_shape],
        compiler_params=params(LIMIT),
        cost_estimate=pl.CostEstimate(flops=2 * 10**9, bytes_accessed=26 * MIB, transcendentals=0),
        name="forward_yz",
    )(*in_hbm(*tables, field, *([weights] * len(pieces))))
    return out.reshape(owners, channels, LANES), half


def fold_kernel(*refs):
    *pieces, _, out_ref = refs
    fold_block(pieces, out_ref, 0)


def fold_rest(weights, half, unique):
    first = unique // 2
    pieces, folded, folded_shape = fold_specs(weights, unique, 1, first)
    return pl.pallas_call(
        fold_kernel,
        grid=(unique - first,),
        in_specs=pieces + [pl.BlockSpec(memory_space=pl.ANY)],
        out_specs=folded,
        out_shape=folded_shape,
        input_output_aliases={len(pieces): 0},
        compiler_params=params(LIMIT),
        cost_estimate=pl.CostEstimate(flops=4 * 10**6, bytes_accessed=20 * MIB, transcendentals=0),
        name="fold_weights",
    )(*in_hbm(*([weights] * len(pieces)), half))


def halve_lines(lines_ref, sums_ref, points, channels):
    half = points // 2
    sign = jnp.where(lane_index((channels, LANES)) < LANES // 2, 1.0, -1.0)
    for x in range(half):
        near, far = lines_ref[x, :channels], lines_ref[x + half, :channels]
        for parity, value in enumerate((near + far, near - far)):
            sums_ref[parity, 0, x] = value
            sums_ref[parity, 1, x] = sign * roll(value, 64)


def spectrum_row(cos_ref, sin_ref, sums_ref, at, parity, half):
    total = cos_ref[at, 0] * sums_ref[parity, 0, 0] + sin_ref[at, 0] * sums_ref[parity, 1, 0]
    for x in range(1, half):
        total += cos_ref[at, x] * sums_ref[parity, 0, x] + sin_ref[at, x] * sums_ref[parity, 1, x]
    return total


def doubled(values):
    other = roll(values, 64)
    low = lane_index(values.shape) < LANES // 2
    return jnp.where(low, values, other), jnp.where(low, other, values)


def mix_kernel(
    cos_ref, sin_ref, lines_ref, weights_ref, spec_ref, out_ref, sums_ref, total_ref, real_ref, imag_ref,
    *, points, channels, per_step, norm,
):
    step = pl.program_id(0)
    half = points // 2

    @pl.when(step == 0)
    def _():
        halve_lines(lines_ref, sums_ref, points, channels)
        total_ref[...] = jnp.zeros_like(total_ref)

    low = lane_index((channels, LANES)) < LANES // 2
    for q in range(per_step):
        at = step * per_step + q
        parity = q % 2
        spec = norm * spectrum_row(cos_ref, sin_ref, sums_ref, at, parity, half)
        spec_ref[q] = spec
        real_ref[q], imag_ref[q] = doubled(spec)
        by_real = jnp.zeros((channels, LANES), F32)
        by_imag = jnp.zeros((channels, LANES), F32)
        for i in range(channels):
            weight = weights_ref[q, i]
            by_real += real_ref[q, pl.ds(i, 1), :] * weight
            by_imag += imag_ref[q, pl.ds(i, 1), :] * weight
        other = roll(by_imag, 64)
        mixed = by_real + jnp.where(low, -other, other)
        other = roll(mixed, 64)
        turned = jnp.where(low, -other, other)
        for x in range(half):
            total_ref[parity, x] += cos_ref[at, x] * mixed + sin_ref[at, x] * turned

    @pl.when(step == pl.num_programs(0) - 1)
    def _():
        for x in range(half):
            out_ref[x] = total_ref[0, x] + total_ref[1, x]
            out_ref[x + half] = total_ref[0, x] - total_ref[1, x]


def smem():
    return pl.BlockSpec(memory_space=pltpu.SMEM)


def mix(cos_x, sin_x, lines, weights, norm):
    points, channels, _ = lines.shape
    unique = weights.shape[0]
    per_step = min(unique, 4)
    shape = (points, channels, LANES)
    return pl.pallas_call(
        functools.partial(mix_kernel, points=points, channels=channels, per_step=per_step, norm=norm),
        grid=(unique // per_step,),
        in_specs=[
            smem(),
            smem(),
            full(shape),
            pl.BlockSpec((per_step,) + weights.shape[1:], lambda s: (s, 0, 0, 0)),
        ],
        out_specs=[
            pl.BlockSpec((per_step, channels, LANES), lambda s: (s, 0, 0)),
            full(shape),
        ],
        out_shape=[
            pltpu.VMEM((unique, channels, LANES), F32),
            pltpu.VMEM(shape, F32),
        ],
        scratch_shapes=[
            pltpu.VMEM((2, 2, points // 2, channels, LANES), F32),
            pltpu.VMEM((2, points // 2, channels, LANES), F32),
            pltpu.VMEM((per_step, channels, LANES), F32),
            pltpu.VMEM((per_step, channels, LANES), F32),
        ],
        compiler_params=params(LIMIT),
        cost_estimate=pl.CostEstimate(flops=2 * 10**7, bytes_accessed=9 * MIB, transcendentals=0),
        name="mix_modes",
    )(cos_x, sin_x, *in_vmem(lines), *in_hbm(weights))


def exact_dot(left, right):
    return jnp.dot(left, right, precision=lax.Precision.HIGHEST, preferred_element_type=F32)


def pointwise_kernel(sum_ref, turned_ref, bias_in_ref, field_ref, out_ref, mixer_ref, bias_ref, *, channels, blocks):
    size = 8 * channels

    @pl.when(pl.program_id(0) == 0)
    def _():
        wide = exact_dot(sum_ref[...], turned_ref[...])
        wide = lax.dot_general(
            wide, sum_ref[...], (((1,), (1,)), ((), ())), precision=lax.Precision.HIGHEST, preferred_element_type=F32
        )
        row = lax.broadcasted_iota(jnp.int32, (size, size), 0) % 8
        high, low = split(jnp.where(row == lane_index((size, size)) % 8, wide, 0.0))
        mixer_ref[:size] = high
        mixer_ref[size:] = low
        bias_ref[...] = exact_dot(sum_ref[...], bias_in_ref[...])

    for b in range(blocks):
        high, low = split(field_ref[:, 8 * b : 8 * b + 8, :].reshape(size, NZ))
        wide = dot(mixer_ref[...], high)
        values = wide[:size] + wide[size:] + dot(mixer_ref[:size], low) + bias_ref[...]
        out_ref[:, 8 * b : 8 * b + 8, :] = values.reshape(channels, 8, NZ)


def pointwise(field, summing, point_weights, point_bias):
    channels = field.shape[0]
    blocks = 2
    turned = point_weights.T
    bias = point_bias[:, None]
    size = 8 * channels
    block = pl.BlockSpec((channels, 8 * blocks, NZ), lambda s: (0, s, 0))
    return pl.pallas_call(
        functools.partial(pointwise_kernel, channels=channels, blocks=blocks),
        grid=(NY // (8 * blocks),),
        in_specs=[full(summing.shape), full(turned.shape), full(bias.shape), block],
        out_specs=block,
        out_shape=pltpu.HBM(field.shape, F32),
        scratch_shapes=[pltpu.VMEM((2 * size, size), BF16), pltpu.VMEM((size, 1), F32)],
        compiler_params=params(LIMIT),
        cost_estimate=pl.CostEstimate(flops=4 * 10**9, bytes_accessed=24 * MIB, transcendentals=0),
        name="pointwise",
    )(*in_hbm(summing, turned, bias, field))


def cell_group(inv_y, inv_z, inv_z_low, modes_ref, pre_ref, cot_ref, act_ref, first, count, channels):
    lines = []
    for g in range(0, count, GROUP):
        lines += inverse_y_group(modes_ref, inv_y, first + g, channels)
    high, low = split(jnp.concatenate(lines, axis=0))
    spectral = dot(jnp.concatenate([high, low], axis=1), inv_z) + dot(high, inv_z_low)
    slopes = []
    for q in range(count):
        r = q // 2 * NY
        c = q % 2 * NZ
        before = spectral[r : r + NY, c : c + NZ] + pre_ref[q]
        cdf = 0.5 + 0.5 * lax.erf(before * INV_SQRT_TWO)
        act_ref[q] = (before * cdf).astype(BF16)
        pdf = jnp.exp(-0.5 * before * before) * INV_SQRT_TWO_PI
        slopes.append(cot_ref[q].astype(F32) * (cdf + before * pdf))
    return slopes


def early_cell_kernel(
    inv_y, inv_z, inv_z_low, z_high, z_low, y_both, modes_ref, pre_ref, cot_ref, act_ref, slope_ref, out_ref,
    *, channels, count, rows,
):
    step = pl.program_id(0)
    slopes = cell_group(
        inv_y[...], inv_z[...], inv_z_low[...], modes_ref, pre_ref, cot_ref, act_ref, step * count, count, channels
    )
    for q in range(count):
        slope_ref[q] = slopes[q]
    forward_group(slopes, z_high[...], z_low[...], y_both[...], out_ref, step * count, rows)


def point_gradient(field_ref, slope_ref, sum_ref, channels):
    size = 8 * channels
    total = jnp.zeros((size, size), F32)
    for b in range(NY // 8):
        at = slice(8 * b, 8 * b + 8)
        f_h, f_l = split(field_ref[:, at, :].reshape(size, NZ))
        s_h, s_l = split(slope_ref[:, at, :].reshape(size, NZ))
        total += lax.dot_general(
            jnp.concatenate([f_h, f_h, f_l], axis=1),
            jnp.concatenate([s_h, s_l, s_h], axis=1),
            (((1,), (1,)), ((), ())),
            preferred_element_type=F32,
        )
    row = lax.broadcasted_iota(jnp.int32, (size, size), 0) % 8
    total = jnp.where(row == lane_index((size, size)) % 8, total, 0.0)
    return exact_dot(jnp.sum(total.reshape(channels, 8, size), axis=1), sum_ref[...])


def late_cell_kernel(
    inv_y, inv_z, inv_z_low, z_high, z_low, y_both, sum_ref, modes_ref, pre_ref, cot_ref, early_ref,
    slope_hbm, field_hbm, _, act_ref, out_ref, field_ref, slope_ref, sems, *, channels, count, rows, owners,
):
    step = pl.program_id(0)
    half = channels // 2
    copies = [
        pltpu.make_async_copy(field_hbm, field_ref, sems.at[0]),
        pltpu.make_async_copy(slope_hbm, slope_ref.at[pl.ds(0, half)], sems.at[1]),
    ]

    @pl.when(step == 0)
    def _():
        for copy in copies:
            copy.start()

    first = half + step * count
    slopes = cell_group(
        inv_y[...], inv_z[...], inv_z_low[...], modes_ref, pre_ref, cot_ref, act_ref, first, count, channels
    )
    for q in range(count):
        slope_ref[first + q] = slopes[q]
    forward_group(slopes, z_high[...], z_low[...], y_both[...], out_ref, step * count, rows)

    @pl.when(step == pl.num_programs(0) - 1)
    def _():
        for copy in copies:
            copy.wait()
        point = point_gradient(field_ref, slope_ref, sum_ref, channels)
        packed = jnp.concatenate([point[8 * q : 8 * q + 8] for q in range(channels // 8)], axis=1)
        zero_mode = jnp.concatenate([early_ref[0:half, 0:1], out_ref[0:half, 0:1]], axis=0)
        eye = lax.broadcasted_iota(jnp.int32, (channels, LANES), 0) == lane_index((channels, LANES))
        bias = jnp.sum(jnp.where(eye, jnp.broadcast_to(zero_mode, (channels, LANES)), 0.0), axis=0, keepdims=True)
        extra = jnp.where(lax.broadcasted_iota(jnp.int32, (8, LANES), 0) == 0, jnp.broadcast_to(bias, (8, LANES)), 0.0)
        for d in range(owners):
            out_ref[d * rows + half : d * rows + half + 8, :] = packed
            out_ref[d * rows + half + 8 : (d + 1) * rows, :] = extra


def early_cells(inverse, forward, modes, pre, cotangent):
    channels = pre.shape[0]
    owners = MY // 2
    half = channels // 2
    block = pl.BlockSpec((STEP, NY, NZ), lambda s: (s, 0, 0))
    tables = (*inverse, *forward)
    act, slope, out = pl.pallas_call(
        functools.partial(early_cell_kernel, channels=channels, count=STEP, rows=half),
        grid=(half // STEP,),
        in_specs=[full(t.shape) for t in tables] + [full((owners * channels, LANES)), block, block],
        out_specs=[block, block, full((owners * half, LANES))],
        out_shape=[
            pltpu.HBM((channels, NY, NZ), BF16),
            pltpu.HBM((half, NY, NZ), F32),
            pltpu.VMEM((owners * half, LANES), F32),
        ],
        compiler_params=params(LIMIT),
        cost_estimate=pl.CostEstimate(flops=3 * 10**9, bytes_accessed=7 * MIB, transcendentals=10**6),
        name="early_cells",
    )(*in_hbm(*tables), *in_vmem(modes.reshape(owners * channels, LANES)), *in_hbm(pre, cotangent))
    return act, slope, out.reshape(owners, half, LANES)


def late_cells(inverse, forward, summing, modes, pre, cotangent, field, early, slope, act):
    channels = field.shape[0]
    owners = MY // 2
    half = channels // 2
    rows = half + 16
    start = half // STEP
    block = pl.BlockSpec((STEP, NY, NZ), lambda s: (start + s, 0, 0))
    anywhere = pl.BlockSpec(memory_space=pl.ANY)
    tables = (*inverse, *forward, summing)
    act, out = pl.pallas_call(
        functools.partial(late_cell_kernel, channels=channels, count=STEP, rows=rows, owners=owners),
        grid=(start,),
        in_specs=[full(t.shape) for t in tables]
        + [full((owners * channels, LANES)), block, block, full((owners * half, LANES))]
        + [anywhere] * 3,
        out_specs=[block, full((owners * rows, LANES))],
        out_shape=[
            pltpu.HBM((channels, NY, NZ), BF16),
            pltpu.VMEM((owners * rows, LANES), F32),
        ],
        scratch_shapes=[
            pltpu.VMEM((channels, NY, NZ), F32),
            pltpu.VMEM((channels, NY, NZ), F32),
            pltpu.SemaphoreType.DMA((2,)),
        ],
        input_output_aliases={len(tables) + 6: 0},
        compiler_params=params(LIMIT),
        cost_estimate=pl.CostEstimate(flops=6 * 10**9, bytes_accessed=11 * MIB, transcendentals=10**6),
        name="late_cells",
    )(
        *in_hbm(*tables),
        *in_vmem(modes.reshape(owners * channels, LANES)),
        *in_hbm(pre, cotangent),
        *in_vmem(early.reshape(owners * half, LANES)),
        *in_hbm(slope, field, act),
    )
    return act, out.reshape(owners, rows, LANES)


def gradient_kernel(cos_ref, sin_ref, spec_ref, lines_ref, *refs, points, channels, unique, copies, norm, part):
    if part == 1:
        _, out_hbm, point_ref, bias_ref, sums_ref, real_ref, imag_ref, buffer, sems = refs
    else:
        out_hbm, sums_ref, real_ref, imag_ref, buffer, sems = refs
    outputs = channels // 2
    halve_lines(lines_ref, sums_ref, points, outputs)
    half = LANES // 2
    lane = lane_index((outputs, LANES))
    scale = jnp.where(lane % MZ == 0, norm, 2.0 * norm)

    def writes(at, slot):
        return [
            pltpu.make_async_copy(
                buffer.at[slot, c],
                out_hbm.at[c, at + r * unique, :, pl.ds(part * outputs, outputs), :],
                sems.at[slot, c, r],
            )
            for r in range(copies)
            for c in range(2)
        ]

    @pl.loop(0, unique // SLOTS)
    def _(turn):
        for slot in range(SLOTS):
            at = SLOTS * turn + slot

            @pl.when(turn > 0)
            def _():
                for copy in writes(at - SLOTS, slot):
                    copy.wait()

            slope = scale * spectrum_row(cos_ref, sin_ref, sums_ref, at, slot % 2, points // 2)
            other = roll(slope, 64)
            flipped = jnp.where(lane < half, other, -other)
            real_ref[slot], imag_ref[slot] = doubled(spec_ref[at])
            for i in range(channels):
                both = real_ref[slot, pl.ds(i, 1), :] * slope + imag_ref[slot, pl.ds(i, 1), :] * flipped
                buffer[slot, 0, i] = both[:, :half]
                buffer[slot, 1, i] = both[:, half:]
            for copy in writes(at, slot):
                copy.start()

    if part == 1:
        packed = lines_ref[0, outputs : outputs + 16, :]
        for x in range(1, points):
            packed += lines_ref[x, outputs : outputs + 16, :]
        packed = norm * packed
        for q in range(channels // 8):
            point_ref[8 * q : 8 * q + 8, :] = packed[:8, q * channels : (q + 1) * channels]
        bias_ref[...] = packed[8:9, :channels]

    for at in range(unique - SLOTS, unique):
        for copy in writes(at, at % SLOTS):
            copy.wait()


def gradient(cos_x, sin_x, spectrum, lines, norm, kept_x, part, before=()):
    points, rows, _ = lines.shape
    unique, channels, _ = spectrum.shape
    half = LANES // 2
    copies = kept_x // unique
    anywhere = pl.BlockSpec(memory_space=pl.ANY)
    shape = jax.ShapeDtypeStruct((2, kept_x, channels, channels, half), F32)
    sums = [(channels, channels), (1, channels)] if part == 1 else []
    return pl.pallas_call(
        functools.partial(
            gradient_kernel, points=points, channels=channels, unique=unique, copies=copies, norm=norm, part=part
        ),
        in_specs=[smem(), smem(), full(spectrum.shape), full(lines.shape)] + [anywhere] * len(before),
        out_specs=[anywhere] + [full(each) for each in sums],
        out_shape=[shape] + [jax.ShapeDtypeStruct(each, F32) for each in sums],
        scratch_shapes=[
            pltpu.VMEM((2, 2, points // 2, channels // 2, LANES), F32),
            pltpu.VMEM((SLOTS, channels, LANES), F32),
            pltpu.VMEM((SLOTS, channels, LANES), F32),
            pltpu.VMEM((SLOTS, 2, channels, channels // 2, half), F32),
            pltpu.SemaphoreType.DMA((SLOTS, 2, copies)),
        ],
        input_output_aliases={4: 0} if before else {},
        compiler_params=params(LIMIT),
        cost_estimate=pl.CostEstimate(flops=5 * 10**6, bytes_accessed=32 * MIB, transcendentals=0),
        name="weight_gradient",
    )(cos_x, sin_x, *in_vmem(spectrum, lines), *before)


def swap(lines):
    return lax.all_to_all(lines, "space", split_axis=0, concat_axis=0, tiled=True)


def suits(width_x, length_x, devices, channels, weights):
    held = weights.shape[2]
    even = np.array_equal(kept(MX, length_x) % length_x, np.arange(MX) % length_x)
    return (
        width_x == 1
        and held == 2 * MZ
        and devices * 2 == MY
        and 2 * held == LANES
        and MX % length_x == 0
        and length_x % 8 == 0
        and even
        and channels == MZ
    )


def body(lifted_field, cotangent, spectral_weights, point_weights, point_bias):
    devices = lax.axis_size("space")
    channels, width_x = lifted_field.shape[:2]
    length_x = width_x * devices
    if not suits(width_x, length_x, devices, channels, spectral_weights):
        return general_body(lifted_field, cotangent, spectral_weights, point_weights, point_bias)
    norm = float(length_x * NY * NZ) ** -0.5
    theta = angles(np.arange(length_x), np.arange(length_x), length_x)
    cos_x, sin_x = jnp.asarray(np.cos(theta), F32), jnp.asarray(np.sin(theta), F32)
    forward = forward_tables()
    inverse = inverse_tables(norm)
    summing = jnp.asarray(np.repeat(np.eye(channels), 8, axis=0), F32)

    field = lifted_field.reshape(channels, NY, NZ)
    slopes_in = cotangent.reshape(channels, NY, NZ)
    weights = jnp.transpose(spectral_weights, (0, 1, 3, 4, 2))

    lines, half = forward_modes(field, forward, weights, length_x)
    lines = swap(lines)
    folded = fold_rest(weights, half, length_x)
    spectrum, mixed = mix(cos_x, sin_x, lines, folded, norm)
    field_late, mixed = lax.optimization_barrier((field, mixed))
    modes = swap(mixed)
    pre = pointwise(field_late, summing, point_weights, point_bias)
    act, slope, early = early_cells(inverse, forward, modes, pre, slopes_in)
    early_lines = swap(early)
    activated, late = late_cells(inverse, forward, summing, modes, pre, slopes_in, field, early, slope, act)
    late_lines = swap(late)
    (grad,) = gradient(cos_x, sin_x, spectrum, early_lines, norm, MX, 0)
    grad, grad_point, grad_bias = gradient(cos_x, sin_x, spectrum, late_lines, norm, MX, 1, (grad,))
    return (
        activated.reshape(cotangent.shape),
        jnp.transpose(grad, (0, 1, 4, 2, 3)),
        grad_point,
        grad_bias.reshape(channels),
    )


HIGHEST = lax.Precision.HIGHEST


def trig_tables(positions, frequency, length):
    product = positions[:, None] * frequency[None, :] % length
    phase_angle = 2.0 * jnp.pi / length * product.astype(jnp.float32)
    return (jnp.cos(phase_angle), jnp.sin(phase_angle))


def kept_frequencies(kept_count, length):
    mode_index = jnp.arange(kept_count, dtype=jnp.int32)
    return jnp.where(mode_index < kept_count // 2, mode_index, length - kept_count + mode_index)


def forward_local(field_in):
    channels = field_in.shape[0]
    width_x = field_in.shape[1]
    cos_z, sin_z = trig_tables(jnp.arange(NZ, dtype=jnp.int32), jnp.arange(MZ, dtype=jnp.int32), NZ)
    table_z = jnp.concatenate([cos_z, -sin_z], axis=1)
    along_z = jnp.einsum("cxyz,zk->cxyk", field_in, table_z, precision=HIGHEST)
    z_real = along_z[..., :MZ]
    z_imag = along_z[..., MZ:]
    cos_y, sin_y = trig_tables(jnp.arange(NY, dtype=jnp.int32), kept_frequencies(MY, NY), NY)
    y_real = jnp.einsum("cxyk,yj->xcjk", z_real, cos_y, precision=HIGHEST) + jnp.einsum(
        "cxyk,yj->xcjk", z_imag, sin_y, precision=HIGHEST
    )
    y_imag = jnp.einsum("cxyk,yj->xcjk", z_imag, cos_y, precision=HIGHEST) - jnp.einsum(
        "cxyk,yj->xcjk", z_real, sin_y, precision=HIGHEST
    )
    stacked = jnp.stack([y_real, y_imag], axis=1)
    return stacked.reshape(width_x, 2, channels, MY * MZ)


def transform_x(x_lines):
    length_x = x_lines.shape[0]
    cos_x, sin_x = trig_tables(
        jnp.arange(length_x, dtype=jnp.int32), kept_frequencies(MX, length_x), length_x
    )
    norm_scale = 1.0 / float(length_x * NY * NZ) ** 0.5
    part_real = x_lines[:, 0]
    part_imag = x_lines[:, 1]
    x_real = jnp.einsum("xcm,xk->kcm", part_real, cos_x, precision=HIGHEST) + jnp.einsum(
        "xcm,xk->kcm", part_imag, sin_x, precision=HIGHEST
    )
    x_imag = jnp.einsum("xcm,xk->kcm", part_imag, cos_x, precision=HIGHEST) - jnp.einsum(
        "xcm,xk->kcm", part_real, sin_x, precision=HIGHEST
    )
    return norm_scale * jnp.stack([x_real, x_imag], axis=1)


def mix_modes(spectrum, weights):
    spec_real = spectrum[:, 0]
    spec_imag = spectrum[:, 1]
    out_real = jnp.einsum("kim,kmio->kom", spec_real, weights[0], precision=HIGHEST) - jnp.einsum(
        "kim,kmio->kom", spec_imag, weights[1], precision=HIGHEST
    )
    out_imag = jnp.einsum("kim,kmio->kom", spec_real, weights[1], precision=HIGHEST) + jnp.einsum(
        "kim,kmio->kom", spec_imag, weights[0], precision=HIGHEST
    )
    return jnp.stack([out_real, out_imag], axis=1)


def inverse_x(spectrum, positions, length_x):
    cos_x, sin_x = trig_tables(positions, kept_frequencies(MX, length_x), length_x)
    spec_real = spectrum[:, 0]
    spec_imag = spectrum[:, 1]
    a_real = jnp.einsum("kcm,xk->xcm", spec_real, cos_x, precision=HIGHEST) - jnp.einsum(
        "kcm,xk->xcm", spec_imag, sin_x, precision=HIGHEST
    )
    a_imag = jnp.einsum("kcm,xk->xcm", spec_imag, cos_x, precision=HIGHEST) + jnp.einsum(
        "kcm,xk->xcm", spec_real, sin_x, precision=HIGHEST
    )
    return jnp.stack([a_real, a_imag], axis=1)


def inverse_yz(x_lines, length_x):
    width_x = x_lines.shape[0]
    channels = x_lines.shape[2]
    mode_grid = x_lines.reshape(width_x, 2, channels, MY, MZ)
    cos_y, sin_y = trig_tables(jnp.arange(NY, dtype=jnp.int32), kept_frequencies(MY, NY), NY)
    b_real = jnp.einsum("xcjk,yj->cxyk", mode_grid[:, 0], cos_y, precision=HIGHEST) - jnp.einsum(
        "xcjk,yj->cxyk", mode_grid[:, 1], sin_y, precision=HIGHEST
    )
    b_imag = jnp.einsum("xcjk,yj->cxyk", mode_grid[:, 1], cos_y, precision=HIGHEST) + jnp.einsum(
        "xcjk,yj->cxyk", mode_grid[:, 0], sin_y, precision=HIGHEST
    )
    cos_z, sin_z = trig_tables(jnp.arange(NZ, dtype=jnp.int32), jnp.arange(MZ, dtype=jnp.int32), NZ)
    weight_z = jnp.where(jnp.arange(MZ, dtype=jnp.int32) == 0, 1.0, 2.0).astype(jnp.float32)
    table_z = jnp.concatenate([cos_z * weight_z[None, :], -sin_z * weight_z[None, :]], axis=1)
    stacked = jnp.concatenate([b_real, b_imag], axis=-1)
    result = jnp.einsum("cxyk,zk->cxyz", stacked, table_z, precision=HIGHEST)
    return result * (1.0 / float(length_x * NY * NZ) ** 0.5)


def gelu_slope(values):
    return (
        0.5 * (1.0 + lax.erf(values * INV_SQRT_TWO))
        + values * jnp.exp(-0.5 * values * values) * INV_SQRT_TWO_PI
    )


def weight_gradient(spectrum, slope_modes, first_mode):
    mode_ids = first_mode + jnp.arange(spectrum.shape[3], dtype=jnp.int32)
    weight_modes = jnp.where(mode_ids % MZ == 0, 1.0, 2.0).astype(jnp.float32)
    grad_real = jnp.einsum(
        "kim,kom->kmio", spectrum[:, 0], slope_modes[:, 0], precision=HIGHEST
    ) + jnp.einsum("kim,kom->kmio", spectrum[:, 1], slope_modes[:, 1], precision=HIGHEST)
    grad_imag = jnp.einsum(
        "kim,kom->kmio", spectrum[:, 0], slope_modes[:, 1], precision=HIGHEST
    ) - jnp.einsum("kim,kom->kmio", spectrum[:, 1], slope_modes[:, 0], precision=HIGHEST)
    stacked = jnp.stack([grad_real, grad_imag], axis=0)
    return stacked * weight_modes[None, None, :, None, None]


def to_modes(field_in):
    return transform_x(
        lax.all_to_all(forward_local(field_in), "space", split_axis=3, concat_axis=0, tiled=True)
    )


def general_body(lifted_field, cotangent, spectral_weights, point_weights, point_bias):
    devices = lax.axis_size("space")
    width_x = lifted_field.shape[1]
    length_x = width_x * devices
    spectrum = to_modes(lifted_field)
    mixed_modes = mix_modes(spectrum, spectral_weights)
    full_lines = inverse_x(mixed_modes, jnp.arange(length_x, dtype=jnp.int32), length_x)
    spectral = inverse_yz(
        lax.all_to_all(full_lines, "space", split_axis=0, concat_axis=3, tiled=True), length_x
    )
    pointwise = (
        jnp.einsum("ixyz,io->oxyz", lifted_field, point_weights, precision=HIGHEST)
        + point_bias[:, None, None, None]
    )
    before = spectral + pointwise
    activated = jax.nn.gelu(before, approximate=False).astype(jnp.bfloat16)
    slope_field = cotangent.astype(jnp.float32) * gelu_slope(before)
    local_point = jnp.einsum("ixyz,oxyz->io", lifted_field, slope_field, precision=HIGHEST)
    local_bias = jnp.sum(slope_field, axis=(1, 2, 3))
    partial = jnp.concatenate([local_point, local_bias[None, :]], axis=0)
    gathered = lax.all_gather(partial, "space", axis=0, tiled=False)
    summed = jnp.sum(gathered, axis=0)
    summed_point, summed_bias = summed[:-1], summed[-1]
    root_cells = float(length_x * NY * NZ) ** 0.5
    slope_spectrum = to_modes(slope_field)
    first_mode = lax.axis_index("space") * spectrum.shape[3]
    grad_spectral = weight_gradient(spectrum, slope_spectrum, first_mode)
    return (activated, grad_spectral, summed_point / root_cells, summed_bias / root_cells)


def solution(mesh):
    placed = (
        P("groups", "space", None, None),
        P("groups", "space", None, None),
        P(None, None, "space", None, None),
        P(),
        P(),
    )
    return jax.shard_map(
        body,
        mesh=mesh,
        in_specs=placed,
        out_specs=(
            P("groups", "space", None, None),
            P("groups", None, "space", None, None),
            P("groups", None),
            P("groups"),
        ),
        check_vma=False,
    )
```

```python
import functools

import jax
import jax.numpy as jnp
import ml_dtypes
import numpy as np
from jax import lax
from jax.experimental import pallas as pl
from jax.experimental.pallas import tpu as pltpu
from jax.sharding import PartitionSpec as P

MX = 32
MY = 32
MZ = 32
NY = 128
NZ = 256

F32 = jnp.float32
BF16 = jnp.bfloat16
INV_SQRT_TWO = 0.7071067811865476
INV_SQRT_TWO_PI = 0.3989422804014327
MIB = 1 << 20
LIMIT = 48
LANES = 128
GROUP = 4
STEP = 8


def kept(kept_count, length):
    index = np.arange(kept_count)
    return np.where(index < kept_count // 2, index, length - kept_count + index)


def angles(positions, frequency, length):
    product = positions[:, None] * frequency[None, :] % length
    return 2.0 * np.pi / length * product


def split_table(table):
    high = table.astype(ml_dtypes.bfloat16)
    return high, (table - high.astype(np.float64)).astype(ml_dtypes.bfloat16)


def lane_spread(first, second, real_table, imag_table):
    return np.concatenate(
        [real_table * first, real_table * second, imag_table * first, imag_table * second], axis=1
    )


def forward_tables():
    theta = angles(np.arange(NZ), np.arange(MZ), NZ)
    cos_z, sin_z = np.cos(theta), np.sin(theta)
    plain = [lane_spread(f, s, cos_z, -sin_z) for f, s in ((1, 0), (0, 1))]
    turned = [lane_spread(f, s, -sin_z, -cos_z) for f, s in ((1, 0), (0, 1))]
    table_z = np.concatenate([np.concatenate(plain, 0), np.concatenate(turned, 0)], axis=1)
    theta = angles(np.arange(NY), kept(MY, NY), NY)
    both = np.concatenate([np.cos(theta).T, np.sin(theta).T], axis=1)
    table_y = np.concatenate([both[0::2], both[1::2]], axis=0)
    z_high, z_low = split_table(table_z)
    y_high, y_low = split_table(table_y)
    return z_high, z_low, np.concatenate([y_high, y_low], axis=0)


def inverse_tables(norm):
    theta = angles(np.arange(NY), kept(MY, NY), NY)
    cos_y, sin_y = np.cos(theta), np.sin(theta)
    table_y = np.concatenate([cos_y[:, 0::2], cos_y[:, 1::2], sin_y[:, 0::2], sin_y[:, 1::2]], axis=1)
    y_high, y_low = split_table(table_y)
    theta = angles(np.arange(NZ), np.arange(MZ), NZ)
    weight = np.where(np.arange(MZ) == 0, 1.0, 2.0) * norm
    cos_z, sin_z = np.cos(theta) * weight, -np.sin(theta) * weight
    table_z = np.concatenate([lane_spread(f, s, cos_z, sin_z).T for f, s in ((1, 0), (0, 1))], axis=1)
    z_high, z_low = split_table(table_z)
    return (
        np.concatenate([y_high, y_high, y_low], axis=1),
        np.concatenate([z_high, z_high], axis=0),
        z_low,
    )


def dot(left, right):
    return jnp.dot(left, right, preferred_element_type=F32)


def split(values):
    high = values.astype(BF16)
    return high, (values - high.astype(F32)).astype(BF16)


def lane_index(shape):
    return lax.broadcasted_iota(jnp.int32, shape, len(shape) - 1)


def roll(values, shift):
    return pltpu.roll(values, shift % LANES, len(values.shape) - 1)


def forward_group(fields, z_high, z_low, y_both, out_ref, first, rows):
    left = jnp.concatenate(
        [jnp.concatenate([fields[q], fields[q + 1]], axis=1) for q in range(0, len(fields), 2)], axis=0
    )
    high, low = split(left)
    lines = dot(high, z_high) + dot(high, z_low) + dot(low, z_high)
    half = MY // 2
    for g in range(0, len(fields) // 2, GROUP // 2):
        pairs = []
        for q in range(g, g + GROUP // 2):
            part = lines[q * NY : (q + 1) * NY]
            pairs.append(jnp.concatenate([part[:, :LANES], part[:, LANES:]], axis=0))
        high, low = split(jnp.concatenate(pairs, axis=1))
        wide = dot(y_both, high)
        modes = wide[:MY] + wide[MY:] + dot(y_both[:MY], low)
        for q in range(GROUP // 2):
            even = modes[:half, q * LANES : (q + 1) * LANES]
            odd = modes[half:, q * LANES : (q + 1) * LANES]
            at_even = (lane_index(even.shape) // MZ) % 2 == 0
            at = first + 2 * (g + q)
            out_ref[pl.ds(at, half, stride=rows), :] = jnp.where(at_even, even, roll(odd, MZ))
            out_ref[pl.ds(at + 1, half, stride=rows), :] = jnp.where(at_even, roll(even, -MZ), odd)


def inverse_y_group(modes_ref, y_table, first, rows):
    half = MY // 2
    pairs = []
    for q in range(GROUP // 2):
        c0 = modes_ref[pl.ds(first + 2 * q, half, stride=rows), :]
        c1 = modes_ref[pl.ds(first + 2 * q + 1, half, stride=rows), :]
        at_even = (lane_index(c0.shape) // MZ) % 2 == 0
        even = jnp.where(at_even, c0, roll(c1, MZ))
        odd = jnp.where(at_even, roll(c0, -MZ), c1)
        both = jnp.concatenate([even, odd], axis=0)
        other = roll(both, 64)
        turned = jnp.where(lane_index(both.shape) < LANES // 2, -other, other)
        pairs.append(jnp.concatenate([both, turned], axis=0))
    high, low = split(jnp.concatenate(pairs, axis=1))
    lines = dot(y_table, jnp.concatenate([high, low, high], axis=0))
    return [lines[:, q * LANES : (q + 1) * LANES] for q in range(GROUP // 2)]


def in_hbm(*arrays):
    return [pltpu.with_memory_space_constraint(each, pltpu.HBM) for each in arrays]


def in_vmem(*arrays):
    return [pltpu.with_memory_space_constraint(each, pltpu.VMEM) for each in arrays]


def full(shape):
    return pl.BlockSpec(shape, lambda *_: (0,) * len(shape))


def params(limit):
    return pltpu.CompilerParams(vmem_limit_bytes=limit * MIB)


def fold_block(pieces, out_ref, at):
    copies = pieces.shape[0]
    real, imag = pieces[0, 0], pieces[0, 1]
    for r in range(1, copies):
        real, imag = real + pieces[r, 0], imag + pieces[r, 1]
    modes = real.shape[-1]
    out_ref[at, :, :, :modes] = real
    out_ref[at, :, :, modes:] = imag


def fetches(weights_hbm, ring_ref, sems, at, slot, unique):
    copies = ring_ref.shape[1]
    return [
        pltpu.make_async_copy(weights_hbm.at[c, at + r * unique], ring_ref.at[slot, r, c], sems.at[slot, r, c])
        for r in range(copies)
        for c in range(2)
    ]


def fold_shapes(weights, unique, slots):
    copies = weights.shape[1] // unique
    shape = (unique,) + weights.shape[2:4] + (2 * weights.shape[4],)
    ring = [pltpu.VMEM((slots, copies, 2) + weights.shape[2:], F32), pltpu.SemaphoreType.DMA((slots, copies, 2))]
    return pltpu.HBM(shape, F32), ring


def forward_kernel(
    z_high, z_low, y_both, field_ref, weights_hbm, out_ref, folded_ref, ring_ref, sems,
    *, channels, step_channels, per_step, unique, slots,
):
    step = pl.program_id(0)

    def transform():
        fields = [field_ref[q] for q in range(step_channels)]
        forward_group(fields, z_high[...], z_low[...], y_both[...], out_ref, step * step_channels, channels)

    @pl.when(step == 0)
    def _():
        for at in range(slots):
            for copy in fetches(weights_hbm, ring_ref, sems, at, at, unique):
                copy.start()
        transform()

    @pl.when(step > 0)
    def _():
        for q in range(per_step):
            at = (step - 1) * per_step + q
            for copy in fetches(weights_hbm, ring_ref, sems, at, at, unique):
                copy.wait()
            fold_block(ring_ref.at[at], folded_ref, q)
        transform()


FOLD_STEP = 2
FIELD_STEP = 8


def folded_early(channels):
    return (channels // FIELD_STEP - 1) * FOLD_STEP


def forward_modes(field, tables, weights, unique):
    channels = field.shape[0]
    slots = folded_early(channels)
    folded_shape, ring = fold_shapes(weights, unique, slots)
    owners = MY // 2
    out, some = pl.pallas_call(
        functools.partial(
            forward_kernel, channels=channels, step_channels=FIELD_STEP, per_step=FOLD_STEP, unique=unique, slots=slots
        ),
        grid=(channels // FIELD_STEP,),
        in_specs=[full(t.shape) for t in tables]
        + [pl.BlockSpec((FIELD_STEP, NY, NZ), lambda s: (s, 0, 0)), pl.BlockSpec(memory_space=pl.ANY)],
        out_specs=[
            full((owners * channels, LANES)),
            pl.BlockSpec((FOLD_STEP,) + folded_shape.shape[1:], lambda s: (jnp.maximum(s - 1, 0), 0, 0, 0)),
        ],
        out_shape=[pltpu.VMEM((owners * channels, LANES), F32), folded_shape],
        scratch_shapes=ring,
        compiler_params=params(LIMIT),
        cost_estimate=pl.CostEstimate(flops=2 * 10**9, bytes_accessed=22 * MIB, transcendentals=0),
        name="forward_yz",
    )(*in_hbm(*tables, field, weights))
    return out.reshape(owners, channels, LANES), some


def fold_kernel(weights_hbm, _, out_ref, ring_ref, sems, *, first, unique, slots):
    step = pl.program_id(0)
    slot = step % slots

    @pl.when(step == 0)
    def _():
        for ahead in range(slots):
            for copy in fetches(weights_hbm, ring_ref, sems, first + ahead, ahead, unique):
                copy.start()

    for copy in fetches(weights_hbm, ring_ref, sems, first + step, slot, unique):
        copy.wait()
    fold_block(ring_ref.at[slot], out_ref, 0)

    @pl.when(step + slots < pl.num_programs(0))
    def _():
        for copy in fetches(weights_hbm, ring_ref, sems, first + step + slots, slot, unique):
            copy.start()


def fold_rest(weights, some, unique):
    first = folded_early(weights.shape[2])
    slots = min(4, unique - first)
    folded_shape, ring = fold_shapes(weights, unique, slots)
    anywhere = pl.BlockSpec(memory_space=pl.ANY)
    return pl.pallas_call(
        functools.partial(fold_kernel, first=first, unique=unique, slots=slots),
        grid=(unique - first,),
        in_specs=[anywhere, anywhere],
        out_specs=pl.BlockSpec((1,) + folded_shape.shape[1:], lambda s: (first + s, 0, 0, 0)),
        out_shape=folded_shape,
        scratch_shapes=ring,
        input_output_aliases={1: 0},
        compiler_params=params(LIMIT),
        cost_estimate=pl.CostEstimate(flops=4 * 10**6, bytes_accessed=25 * MIB, transcendentals=0),
        name="fold_weights",
    )(*in_hbm(weights, some))


def halve_lines(lines_ref, sums_ref, points, channels):
    half = points // 2
    sign = jnp.where(lane_index((channels, LANES)) < LANES // 2, 1.0, -1.0)
    for x in range(half):
        near, far = lines_ref[x, :channels], lines_ref[x + half, :channels]
        for parity, value in enumerate((near + far, near - far)):
            sums_ref[parity, 0, x] = value
            sums_ref[parity, 1, x] = sign * roll(value, 64)


def spectrum_row(cos_ref, sin_ref, sums_ref, at, parity, half):
    total = cos_ref[at, 0] * sums_ref[parity, 0, 0] + sin_ref[at, 0] * sums_ref[parity, 1, 0]
    for x in range(1, half):
        total += cos_ref[at, x] * sums_ref[parity, 0, x] + sin_ref[at, x] * sums_ref[parity, 1, x]
    return total


def doubled(values):
    other = roll(values, 64)
    low = lane_index(values.shape) < LANES // 2
    return jnp.where(low, values, other), jnp.where(low, other, values)


def mix_kernel(
    cos_ref, sin_ref, lines_ref, weights_hbm, spec_ref, out_ref,
    sums_ref, total_ref, real_ref, imag_ref, weights_ref, sems, *, points, channels, per_step, norm,
):
    step = pl.program_id(0)
    half = points // 2

    def fetch(at):
        return pltpu.make_async_copy(weights_hbm.at[at], weights_ref.at[at], sems.at[at])

    @pl.when(step == 0)
    def _():
        for at in range(points):
            fetch(at).start()
        halve_lines(lines_ref, sums_ref, points, channels)
        total_ref[...] = jnp.zeros_like(total_ref)

    low = lane_index((channels, LANES)) < LANES // 2
    for q in range(per_step):
        at = step * per_step + q
        parity = q % 2
        spec = norm * spectrum_row(cos_ref, sin_ref, sums_ref, at, parity, half)
        spec_ref[q] = spec
        real_ref[q], imag_ref[q] = doubled(spec)
        by_real = jnp.zeros((channels, LANES), F32)
        by_imag = jnp.zeros((channels, LANES), F32)
        fetch(at).wait()
        for i in range(channels):
            weight = weights_ref[at, i]
            by_real += real_ref[q, pl.ds(i, 1), :] * weight
            by_imag += imag_ref[q, pl.ds(i, 1), :] * weight
        other = roll(by_imag, 64)
        mixed = by_real + jnp.where(low, -other, other)
        other = roll(mixed, 64)
        turned = jnp.where(low, -other, other)
        for x in range(half):
            total_ref[parity, x] += cos_ref[at, x] * mixed + sin_ref[at, x] * turned

    @pl.when(step == pl.num_programs(0) - 1)
    def _():
        for x in range(half):
            out_ref[x] = total_ref[0, x] + total_ref[1, x]
            out_ref[x + half] = total_ref[0, x] - total_ref[1, x]


def smem():
    return pl.BlockSpec(memory_space=pltpu.SMEM)


def mix(cos_x, sin_x, lines, weights, norm):
    points, channels, _ = lines.shape
    unique = weights.shape[0]
    per_step = min(unique, 4)
    shape = (points, channels, LANES)
    return pl.pallas_call(
        functools.partial(mix_kernel, points=points, channels=channels, per_step=per_step, norm=norm),
        grid=(unique // per_step,),
        in_specs=[
            smem(),
            smem(),
            full(shape),
            pl.BlockSpec(memory_space=pl.ANY),
        ],
        out_specs=[
            pl.BlockSpec((per_step, channels, LANES), lambda s: (s, 0, 0)),
            full(shape),
        ],
        out_shape=[
            pltpu.VMEM((unique, channels, LANES), F32),
            pltpu.VMEM(shape, F32),
        ],
        scratch_shapes=[
            pltpu.VMEM((2, 2, points // 2, channels, LANES), F32),
            pltpu.VMEM((2, points // 2, channels, LANES), F32),
            pltpu.VMEM((per_step, channels, LANES), F32),
            pltpu.VMEM((per_step, channels, LANES), F32),
            pltpu.VMEM(weights.shape, F32),
            pltpu.SemaphoreType.DMA((unique,)),
        ],
        compiler_params=params(LIMIT),
        cost_estimate=pl.CostEstimate(flops=2 * 10**7, bytes_accessed=9 * MIB, transcendentals=0),
        name="mix_modes",
    )(cos_x, sin_x, *in_vmem(lines), *in_hbm(weights))


def exact_dot(left, right):
    return jnp.dot(left, right, precision=lax.Precision.HIGHEST, preferred_element_type=F32)


def pointwise_kernel(sum_ref, turned_ref, bias_in_ref, field_ref, out_ref, mixer_ref, bias_ref, *, channels, blocks):
    size = 8 * channels

    @pl.when(pl.program_id(0) == 0)
    def _():
        wide = exact_dot(sum_ref[...], turned_ref[...])
        wide = lax.dot_general(
            wide, sum_ref[...], (((1,), (1,)), ((), ())), precision=lax.Precision.HIGHEST, preferred_element_type=F32
        )
        row = lax.broadcasted_iota(jnp.int32, (size, size), 0) % 8
        high, low = split(jnp.where(row == lane_index((size, size)) % 8, wide, 0.0))
        mixer_ref[:size] = high
        mixer_ref[size:] = low
        bias_ref[...] = exact_dot(sum_ref[...], bias_in_ref[...])

    for b in range(blocks):
        high, low = split(field_ref[:, 8 * b : 8 * b + 8, :].reshape(size, NZ))
        wide = dot(mixer_ref[...], high)
        values = wide[:size] + wide[size:] + dot(mixer_ref[:size], low) + bias_ref[...]
        out_ref[:, 8 * b : 8 * b + 8, :] = values.reshape(channels, 8, NZ)


def pointwise(field, summing, point_weights, point_bias):
    channels = field.shape[0]
    blocks = 2
    turned = point_weights.T
    bias = point_bias[:, None]
    size = 8 * channels
    block = pl.BlockSpec((channels, 8 * blocks, NZ), lambda s: (0, s, 0))
    return pl.pallas_call(
        functools.partial(pointwise_kernel, channels=channels, blocks=blocks),
        grid=(NY // (8 * blocks),),
        in_specs=[full(summing.shape), full(turned.shape), full(bias.shape), block],
        out_specs=block,
        out_shape=pltpu.HBM(field.shape, F32),
        scratch_shapes=[pltpu.VMEM((2 * size, size), BF16), pltpu.VMEM((size, 1), F32)],
        compiler_params=params(LIMIT),
        cost_estimate=pl.CostEstimate(flops=4 * 10**9, bytes_accessed=24 * MIB, transcendentals=0),
        name="pointwise",
    )(*in_hbm(summing, turned, bias, field))


def cell_group(inv_y, inv_z, inv_z_low, modes_ref, pre_ref, cot_ref, act_ref, first, count, channels):
    lines = []
    for g in range(0, count, GROUP):
        lines += inverse_y_group(modes_ref, inv_y, first + g, channels)
    high, low = split(jnp.concatenate(lines, axis=0))
    spectral = dot(jnp.concatenate([high, low], axis=1), inv_z) + dot(high, inv_z_low)
    slopes = []
    for q in range(count):
        r = q // 2 * NY
        c = q % 2 * NZ
        before = spectral[r : r + NY, c : c + NZ] + pre_ref[q]
        cdf = 0.5 + 0.5 * lax.erf(before * INV_SQRT_TWO)
        act_ref[q] = (before * cdf).astype(BF16)
        pdf = jnp.exp(-0.5 * before * before) * INV_SQRT_TWO_PI
        slopes.append(cot_ref[q].astype(F32) * (cdf + before * pdf))
    return slopes


def early_cell_kernel(
    inv_y, inv_z, inv_z_low, z_high, z_low, y_both, modes_ref, pre_ref, cot_ref, act_ref, slope_ref, out_ref,
    *, channels, count, rows,
):
    step = pl.program_id(0)
    slopes = cell_group(
        inv_y[...], inv_z[...], inv_z_low[...], modes_ref, pre_ref, cot_ref, act_ref, step * count, count, channels
    )
    for q in range(count):
        slope_ref[q] = slopes[q]
    forward_group(slopes, z_high[...], z_low[...], y_both[...], out_ref, step * count, rows)


def point_gradient(field_ref, slope_ref, sum_ref, channels):
    size = 8 * channels
    total = jnp.zeros((size, size), F32)
    for b in range(NY // 8):
        at = slice(8 * b, 8 * b + 8)
        f_h, f_l = split(field_ref[:, at, :].reshape(size, NZ))
        s_h, s_l = split(slope_ref[:, at, :].reshape(size, NZ))
        total += lax.dot_general(
            jnp.concatenate([f_h, f_h, f_l], axis=1),
            jnp.concatenate([s_h, s_l, s_h], axis=1),
            (((1,), (1,)), ((), ())),
            preferred_element_type=F32,
        )
    row = lax.broadcasted_iota(jnp.int32, (size, size), 0) % 8
    total = jnp.where(row == lane_index((size, size)) % 8, total, 0.0)
    return exact_dot(jnp.sum(total.reshape(channels, 8, size), axis=1), sum_ref[...])


def late_cell_kernel(
    inv_y, inv_z, inv_z_low, z_high, z_low, y_both, sum_ref, modes_ref, pre_ref, cot_ref, early_ref,
    slope_hbm, field_hbm, _, act_ref, out_ref, field_ref, slope_ref, sems, *, channels, count, rows, owners,
):
    step = pl.program_id(0)
    early = early_count(channels)
    late = channels - early
    copies = [
        pltpu.make_async_copy(field_hbm, field_ref, sems.at[0]),
        pltpu.make_async_copy(slope_hbm, slope_ref.at[pl.ds(0, early)], sems.at[1]),
    ]

    @pl.when(step == 0)
    def _():
        for copy in copies:
            copy.start()

    first = early + step * count
    slopes = cell_group(
        inv_y[...], inv_z[...], inv_z_low[...], modes_ref, pre_ref, cot_ref, act_ref, first, count, channels
    )
    for q in range(count):
        slope_ref[first + q] = slopes[q]
    forward_group(slopes, z_high[...], z_low[...], y_both[...], out_ref, step * count, rows)

    @pl.when(step == pl.num_programs(0) - 1)
    def _():
        for copy in copies:
            copy.wait()
        point = point_gradient(field_ref, slope_ref, sum_ref, channels)
        packed = jnp.concatenate([point[8 * q : 8 * q + 8] for q in range(channels // 8)], axis=1)
        zero_mode = jnp.concatenate([early_ref[0:early, 0:1], out_ref[0:late, 0:1]], axis=0)
        eye = lax.broadcasted_iota(jnp.int32, (channels, LANES), 0) == lane_index((channels, LANES))
        bias = jnp.sum(jnp.where(eye, jnp.broadcast_to(zero_mode, (channels, LANES)), 0.0), axis=0, keepdims=True)
        extra = jnp.where(lax.broadcasted_iota(jnp.int32, (8, LANES), 0) == 0, jnp.broadcast_to(bias, (8, LANES)), 0.0)
        for d in range(owners):
            out_ref[d * rows + late : d * rows + late + 8, :] = packed
            out_ref[d * rows + late + 8 : (d + 1) * rows, :] = extra


def early_count(channels):
    return channels * 3 // 4


def early_cells(inverse, forward, modes, pre, cotangent):
    channels = pre.shape[0]
    owners = MY // 2
    early = early_count(channels)
    block = pl.BlockSpec((STEP, NY, NZ), lambda s: (s, 0, 0))
    tables = (*inverse, *forward)
    act, slope, out = pl.pallas_call(
        functools.partial(early_cell_kernel, channels=channels, count=STEP, rows=early),
        grid=(early // STEP,),
        in_specs=[full(t.shape) for t in tables] + [full((owners * channels, LANES)), block, block],
        out_specs=[block, block, full((owners * early, LANES))],
        out_shape=[
            pltpu.HBM((channels, NY, NZ), BF16),
            pltpu.HBM((early, NY, NZ), F32),
            pltpu.VMEM((owners * early, LANES), F32),
        ],
        compiler_params=params(LIMIT),
        cost_estimate=pl.CostEstimate(flops=3 * 10**9, bytes_accessed=7 * MIB, transcendentals=10**6),
        name="early_cells",
    )(*in_hbm(*tables), *in_vmem(modes.reshape(owners * channels, LANES)), *in_hbm(pre, cotangent))
    return act, slope, out.reshape(owners, early, LANES)


def late_cells(inverse, forward, summing, modes, pre, cotangent, field, early, slope, act):
    channels = field.shape[0]
    owners = MY // 2
    first = early_count(channels)
    rows = channels - first + 16
    start = first // STEP
    block = pl.BlockSpec((STEP, NY, NZ), lambda s: (start + s, 0, 0))
    anywhere = pl.BlockSpec(memory_space=pl.ANY)
    tables = (*inverse, *forward, summing)
    act, out = pl.pallas_call(
        functools.partial(late_cell_kernel, channels=channels, count=STEP, rows=rows, owners=owners),
        grid=((channels - first) // STEP,),
        in_specs=[full(t.shape) for t in tables]
        + [full((owners * channels, LANES)), block, block, full((owners * first, LANES))]
        + [anywhere] * 3,
        out_specs=[block, full((owners * rows, LANES))],
        out_shape=[
            pltpu.HBM((channels, NY, NZ), BF16),
            pltpu.VMEM((owners * rows, LANES), F32),
        ],
        scratch_shapes=[
            pltpu.VMEM((channels, NY, NZ), F32),
            pltpu.VMEM((channels, NY, NZ), F32),
            pltpu.SemaphoreType.DMA((2,)),
        ],
        input_output_aliases={len(tables) + 6: 0},
        compiler_params=params(LIMIT),
        cost_estimate=pl.CostEstimate(flops=6 * 10**9, bytes_accessed=11 * MIB, transcendentals=10**6),
        name="late_cells",
    )(
        *in_hbm(*tables),
        *in_vmem(modes.reshape(owners * channels, LANES)),
        *in_hbm(pre, cotangent),
        *in_vmem(early.reshape(owners * first, LANES)),
        *in_hbm(slope, field, act),
    )
    return act, out.reshape(owners, rows, LANES)


def gradient_kernel(cos_ref, sin_ref, spec_ref, lines_ref, *refs, points, channels, unique, copies, norm, first, outputs, slots):
    last = first > 0
    if last:
        _, out_hbm, point_ref, bias_ref, sums_ref, real_ref, imag_ref, buffer, sems = refs
    else:
        out_hbm, sums_ref, real_ref, imag_ref, buffer, sems = refs
    halve_lines(lines_ref, sums_ref, points, outputs)
    half = LANES // 2
    lane = lane_index((outputs, LANES))
    scale = jnp.where(lane % MZ == 0, norm, 2.0 * norm)

    def writes(at, slot):
        return [
            pltpu.make_async_copy(
                buffer.at[slot, c],
                out_hbm.at[c, at + r * unique, :, pl.ds(first, outputs), :],
                sems.at[slot, c, r],
            )
            for r in range(copies)
            for c in range(2)
        ]

    @pl.loop(0, unique // slots)
    def _(turn):
        for slot in range(slots):
            at = slots * turn + slot

            @pl.when(turn > 0)
            def _():
                for copy in writes(at - slots, slot):
                    copy.wait()

            slope = scale * spectrum_row(cos_ref, sin_ref, sums_ref, at, slot % 2, points // 2)
            other = roll(slope, 64)
            flipped = jnp.where(lane < half, other, -other)
            real_ref[slot], imag_ref[slot] = doubled(spec_ref[at])
            for i in range(channels):
                both = real_ref[slot, pl.ds(i, 1), :] * slope + imag_ref[slot, pl.ds(i, 1), :] * flipped
                buffer[slot, 0, i] = both[:, :half]
                buffer[slot, 1, i] = both[:, half:]
            for copy in writes(at, slot):
                copy.start()

    if last:
        packed = lines_ref[0, outputs : outputs + 16, :]
        for x in range(1, points):
            packed += lines_ref[x, outputs : outputs + 16, :]
        packed = norm * packed
        for q in range(channels // 8):
            point_ref[8 * q : 8 * q + 8, :] = packed[:8, q * channels : (q + 1) * channels]
        bias_ref[...] = packed[8:9, :channels]

    for at in range(unique - slots, unique):
        for copy in writes(at, at % slots):
            copy.wait()


def gradient(cos_x, sin_x, spectrum, lines, norm, kept_x, before=()):
    points, rows, _ = lines.shape
    unique, channels, _ = spectrum.shape
    half = LANES // 2
    copies = kept_x // unique
    first = early_count(channels) if before else 0
    outputs = channels - first if before else early_count(channels)
    slots = 8 if before else 4
    anywhere = pl.BlockSpec(memory_space=pl.ANY)
    shape = jax.ShapeDtypeStruct((2, kept_x, channels, channels, half), F32)
    sums = [(channels, channels), (1, channels)] if before else []
    return pl.pallas_call(
        functools.partial(
            gradient_kernel, points=points, channels=channels, unique=unique, copies=copies, norm=norm,
            first=first, outputs=outputs, slots=slots,
        ),
        in_specs=[smem(), smem(), full(spectrum.shape), full(lines.shape)] + [anywhere] * len(before),
        out_specs=[anywhere] + [full(each) for each in sums],
        out_shape=[shape] + [jax.ShapeDtypeStruct(each, F32) for each in sums],
        scratch_shapes=[
            pltpu.VMEM((2, 2, points // 2, outputs, LANES), F32),
            pltpu.VMEM((slots, channels, LANES), F32),
            pltpu.VMEM((slots, channels, LANES), F32),
            pltpu.VMEM((slots, 2, channels, outputs, half), F32),
            pltpu.SemaphoreType.DMA((slots, 2, copies)),
        ],
        input_output_aliases={4: 0} if before else {},
        compiler_params=params(LIMIT),
        cost_estimate=pl.CostEstimate(flops=5 * 10**6, bytes_accessed=32 * MIB, transcendentals=0),
        name="weight_gradient",
    )(cos_x, sin_x, *in_vmem(spectrum, lines), *before)


def swap(lines):
    return lax.all_to_all(lines, "space", split_axis=0, concat_axis=0, tiled=True)


def suits(width_x, length_x, devices, channels, weights):
    held = weights.shape[2]
    even = np.array_equal(kept(MX, length_x) % length_x, np.arange(MX) % length_x)
    return (
        width_x == 1
        and held == 2 * MZ
        and devices * 2 == MY
        and 2 * held == LANES
        and MX % length_x == 0
        and length_x % 8 == 0
        and even
        and channels == MZ
    )


def body(lifted_field, cotangent, spectral_weights, point_weights, point_bias):
    devices = lax.axis_size("space")
    channels, width_x = lifted_field.shape[:2]
    length_x = width_x * devices
    if not suits(width_x, length_x, devices, channels, spectral_weights):
        return general_body(lifted_field, cotangent, spectral_weights, point_weights, point_bias)
    norm = float(length_x * NY * NZ) ** -0.5
    theta = angles(np.arange(length_x), np.arange(length_x), length_x)
    cos_x, sin_x = jnp.asarray(np.cos(theta), F32), jnp.asarray(np.sin(theta), F32)
    forward = forward_tables()
    inverse = inverse_tables(norm)
    summing = jnp.asarray(np.repeat(np.eye(channels), 8, axis=0), F32)

    field = lifted_field.reshape(channels, NY, NZ)
    slopes_in = cotangent.reshape(channels, NY, NZ)
    weights = jnp.transpose(spectral_weights, (0, 1, 3, 4, 2))

    lines, some = forward_modes(field, forward, weights, length_x)
    lines = swap(lines)
    folded = fold_rest(weights, some, length_x)
    spectrum, mixed = mix(cos_x, sin_x, lines, folded, norm)
    field_late, mixed = lax.optimization_barrier((field, mixed))
    modes = swap(mixed)
    pre = pointwise(field_late, summing, point_weights, point_bias)
    act, slope, early = early_cells(inverse, forward, modes, pre, slopes_in)
    early_lines = swap(early)
    activated, late = late_cells(inverse, forward, summing, modes, pre, slopes_in, field, early, slope, act)
    late_lines = swap(late)
    (grad,) = gradient(cos_x, sin_x, spectrum, early_lines, norm, MX)
    grad, grad_point, grad_bias = gradient(cos_x, sin_x, spectrum, late_lines, norm, MX, (grad,))
    return (
        activated.reshape(cotangent.shape),
        jnp.transpose(grad, (0, 1, 4, 2, 3)),
        grad_point,
        grad_bias.reshape(channels),
    )


HIGHEST = lax.Precision.HIGHEST


def trig_tables(positions, frequency, length):
    product = positions[:, None] * frequency[None, :] % length
    phase_angle = 2.0 * jnp.pi / length * product.astype(jnp.float32)
    return (jnp.cos(phase_angle), jnp.sin(phase_angle))


def kept_frequencies(kept_count, length):
    mode_index = jnp.arange(kept_count, dtype=jnp.int32)
    return jnp.where(mode_index < kept_count // 2, mode_index, length - kept_count + mode_index)


def forward_local(field_in):
    channels = field_in.shape[0]
    width_x = field_in.shape[1]
    cos_z, sin_z = trig_tables(jnp.arange(NZ, dtype=jnp.int32), jnp.arange(MZ, dtype=jnp.int32), NZ)
    table_z = jnp.concatenate([cos_z, -sin_z], axis=1)
    along_z = jnp.einsum("cxyz,zk->cxyk", field_in, table_z, precision=HIGHEST)
    z_real = along_z[..., :MZ]
    z_imag = along_z[..., MZ:]
    cos_y, sin_y = trig_tables(jnp.arange(NY, dtype=jnp.int32), kept_frequencies(MY, NY), NY)
    y_real = jnp.einsum("cxyk,yj->xcjk", z_real, cos_y, precision=HIGHEST) + jnp.einsum(
        "cxyk,yj->xcjk", z_imag, sin_y, precision=HIGHEST
    )
    y_imag = jnp.einsum("cxyk,yj->xcjk", z_imag, cos_y, precision=HIGHEST) - jnp.einsum(
        "cxyk,yj->xcjk", z_real, sin_y, precision=HIGHEST
    )
    stacked = jnp.stack([y_real, y_imag], axis=1)
    return stacked.reshape(width_x, 2, channels, MY * MZ)


def transform_x(x_lines):
    length_x = x_lines.shape[0]
    cos_x, sin_x = trig_tables(
        jnp.arange(length_x, dtype=jnp.int32), kept_frequencies(MX, length_x), length_x
    )
    norm_scale = 1.0 / float(length_x * NY * NZ) ** 0.5
    part_real = x_lines[:, 0]
    part_imag = x_lines[:, 1]
    x_real = jnp.einsum("xcm,xk->kcm", part_real, cos_x, precision=HIGHEST) + jnp.einsum(
        "xcm,xk->kcm", part_imag, sin_x, precision=HIGHEST
    )
    x_imag = jnp.einsum("xcm,xk->kcm", part_imag, cos_x, precision=HIGHEST) - jnp.einsum(
        "xcm,xk->kcm", part_real, sin_x, precision=HIGHEST
    )
    return norm_scale * jnp.stack([x_real, x_imag], axis=1)


def mix_modes(spectrum, weights):
    spec_real = spectrum[:, 0]
    spec_imag = spectrum[:, 1]
    out_real = jnp.einsum("kim,kmio->kom", spec_real, weights[0], precision=HIGHEST) - jnp.einsum(
        "kim,kmio->kom", spec_imag, weights[1], precision=HIGHEST
    )
    out_imag = jnp.einsum("kim,kmio->kom", spec_real, weights[1], precision=HIGHEST) + jnp.einsum(
        "kim,kmio->kom", spec_imag, weights[0], precision=HIGHEST
    )
    return jnp.stack([out_real, out_imag], axis=1)


def inverse_x(spectrum, positions, length_x):
    cos_x, sin_x = trig_tables(positions, kept_frequencies(MX, length_x), length_x)
    spec_real = spectrum[:, 0]
    spec_imag = spectrum[:, 1]
    a_real = jnp.einsum("kcm,xk->xcm", spec_real, cos_x, precision=HIGHEST) - jnp.einsum(
        "kcm,xk->xcm", spec_imag, sin_x, precision=HIGHEST
    )
    a_imag = jnp.einsum("kcm,xk->xcm", spec_imag, cos_x, precision=HIGHEST) + jnp.einsum(
        "kcm,xk->xcm", spec_real, sin_x, precision=HIGHEST
    )
    return jnp.stack([a_real, a_imag], axis=1)


def inverse_yz(x_lines, length_x):
    width_x = x_lines.shape[0]
    channels = x_lines.shape[2]
    mode_grid = x_lines.reshape(width_x, 2, channels, MY, MZ)
    cos_y, sin_y = trig_tables(jnp.arange(NY, dtype=jnp.int32), kept_frequencies(MY, NY), NY)
    b_real = jnp.einsum("xcjk,yj->cxyk", mode_grid[:, 0], cos_y, precision=HIGHEST) - jnp.einsum(
        "xcjk,yj->cxyk", mode_grid[:, 1], sin_y, precision=HIGHEST
    )
    b_imag = jnp.einsum("xcjk,yj->cxyk", mode_grid[:, 1], cos_y, precision=HIGHEST) + jnp.einsum(
        "xcjk,yj->cxyk", mode_grid[:, 0], sin_y, precision=HIGHEST
    )
    cos_z, sin_z = trig_tables(jnp.arange(NZ, dtype=jnp.int32), jnp.arange(MZ, dtype=jnp.int32), NZ)
    weight_z = jnp.where(jnp.arange(MZ, dtype=jnp.int32) == 0, 1.0, 2.0).astype(jnp.float32)
    table_z = jnp.concatenate([cos_z * weight_z[None, :], -sin_z * weight_z[None, :]], axis=1)
    stacked = jnp.concatenate([b_real, b_imag], axis=-1)
    result = jnp.einsum("cxyk,zk->cxyz", stacked, table_z, precision=HIGHEST)
    return result * (1.0 / float(length_x * NY * NZ) ** 0.5)


def gelu_slope(values):
    return (
        0.5 * (1.0 + lax.erf(values * INV_SQRT_TWO))
        + values * jnp.exp(-0.5 * values * values) * INV_SQRT_TWO_PI
    )


def weight_gradient(spectrum, slope_modes, first_mode):
    mode_ids = first_mode + jnp.arange(spectrum.shape[3], dtype=jnp.int32)
    weight_modes = jnp.where(mode_ids % MZ == 0, 1.0, 2.0).astype(jnp.float32)
    grad_real = jnp.einsum(
        "kim,kom->kmio", spectrum[:, 0], slope_modes[:, 0], precision=HIGHEST
    ) + jnp.einsum("kim,kom->kmio", spectrum[:, 1], slope_modes[:, 1], precision=HIGHEST)
    grad_imag = jnp.einsum(
        "kim,kom->kmio", spectrum[:, 0], slope_modes[:, 1], precision=HIGHEST
    ) - jnp.einsum("kim,kom->kmio", spectrum[:, 1], slope_modes[:, 0], precision=HIGHEST)
    stacked = jnp.stack([grad_real, grad_imag], axis=0)
    return stacked * weight_modes[None, None, :, None, None]


def to_modes(field_in):
    return transform_x(
        lax.all_to_all(forward_local(field_in), "space", split_axis=3, concat_axis=0, tiled=True)
    )


def general_body(lifted_field, cotangent, spectral_weights, point_weights, point_bias):
    devices = lax.axis_size("space")
    width_x = lifted_field.shape[1]
    length_x = width_x * devices
    spectrum = to_modes(lifted_field)
    mixed_modes = mix_modes(spectrum, spectral_weights)
    full_lines = inverse_x(mixed_modes, jnp.arange(length_x, dtype=jnp.int32), length_x)
    spectral = inverse_yz(
        lax.all_to_all(full_lines, "space", split_axis=0, concat_axis=3, tiled=True), length_x
    )
    pointwise = (
        jnp.einsum("ixyz,io->oxyz", lifted_field, point_weights, precision=HIGHEST)
        + point_bias[:, None, None, None]
    )
    before = spectral + pointwise
    activated = jax.nn.gelu(before, approximate=False).astype(jnp.bfloat16)
    slope_field = cotangent.astype(jnp.float32) * gelu_slope(before)
    local_point = jnp.einsum("ixyz,oxyz->io", lifted_field, slope_field, precision=HIGHEST)
    local_bias = jnp.sum(slope_field, axis=(1, 2, 3))
    partial = jnp.concatenate([local_point, local_bias[None, :]], axis=0)
    gathered = lax.all_gather(partial, "space", axis=0, tiled=False)
    summed = jnp.sum(gathered, axis=0)
    summed_point, summed_bias = summed[:-1], summed[-1]
    root_cells = float(length_x * NY * NZ) ** 0.5
    slope_spectrum = to_modes(slope_field)
    first_mode = lax.axis_index("space") * spectrum.shape[3]
    grad_spectral = weight_gradient(spectrum, slope_spectrum, first_mode)
    return (activated, grad_spectral, summed_point / root_cells, summed_bias / root_cells)


def solution(mesh):
    placed = (
        P("groups", "space", None, None),
        P("groups", "space", None, None),
        P(None, None, "space", None, None),
        P(),
        P(),
    )
    return jax.shard_map(
        body,
        mesh=mesh,
        in_specs=placed,
        out_specs=(
            P("groups", "space", None, None),
            P("groups", None, "space", None, None),
            P("groups", None),
            P("groups"),
        ),
        check_vma=False,
    )
```

```python
import functools

import jax
import jax.numpy as jnp
import ml_dtypes
import numpy as np
from jax import lax
from jax.experimental import pallas as pl
from jax.experimental.pallas import tpu as pltpu
from jax.sharding import PartitionSpec as P

MX = 32
MY = 32
MZ = 32
NY = 128
NZ = 256

F32 = jnp.float32
BF16 = jnp.bfloat16
INV_SQRT_TWO = 0.7071067811865476
INV_SQRT_TWO_PI = 0.3989422804014327
MIB = 1 << 20
LIMIT = 48
LANES = 128
GROUP = 4
STEP = 8


def kept(kept_count, length):
    index = np.arange(kept_count)
    return np.where(index < kept_count // 2, index, length - kept_count + index)


def angles(positions, frequency, length):
    product = positions[:, None] * frequency[None, :] % length
    return 2.0 * np.pi / length * product


def split_table(table):
    high = table.astype(ml_dtypes.bfloat16)
    return high, (table - high.astype(np.float64)).astype(ml_dtypes.bfloat16)


def lane_spread(first, second, real_table, imag_table):
    return np.concatenate(
        [real_table * first, real_table * second, imag_table * first, imag_table * second], axis=1
    )


def forward_tables():
    theta = angles(np.arange(NZ), np.arange(MZ), NZ)
    table = np.concatenate([lane_spread(f, s, np.cos(theta), -np.sin(theta)) for f, s in ((1, 0), (0, 1))], axis=0)
    high, low = split_table(table)
    table_z = np.concatenate(
        [np.concatenate([high, low], axis=1), np.concatenate([high, np.zeros_like(low)], axis=1)], axis=0
    )
    theta = angles(np.arange(NY), kept(MY, NY), NY).T
    table = np.concatenate([np.cos(theta)[0::2], np.cos(theta)[1::2], np.sin(theta)[0::2], np.sin(theta)[1::2]], axis=0)
    high, low = split_table(table)
    table_y = np.concatenate(
        [np.concatenate([high, high], axis=1), np.concatenate([low, np.zeros_like(low)], axis=1)], axis=0
    )
    return table_z, table_y


def inverse_tables(norm):
    theta = angles(np.arange(NY), kept(MY, NY), NY)
    cos_y, sin_y = np.cos(theta), np.sin(theta)
    table_y = np.concatenate([cos_y[:, 0::2], cos_y[:, 1::2], sin_y[:, 0::2], sin_y[:, 1::2]], axis=1)
    y_high, y_low = split_table(table_y)
    theta = angles(np.arange(NZ), np.arange(MZ), NZ)
    weight = np.where(np.arange(MZ) == 0, 1.0, 2.0) * norm
    parts = (np.cos(theta) * weight, -np.sin(theta) * weight)
    own, other = lane_spread(1, 0, *parts).T, lane_spread(0, 1, *parts).T
    tables_z = []
    for mine, theirs in ((own, other), (other, own)):
        high = split_table(mine)[0]
        tables_z.append(np.concatenate([high, high + split_table(theirs)[1]], axis=0))
    return np.concatenate([y_high, y_high, y_low], axis=1), *tables_z


def dot(left, right):
    return jnp.dot(left, right, preferred_element_type=F32)


def split(values):
    high = values.astype(BF16)
    return high, (values - high.astype(F32)).astype(BF16)


def lane_index(shape):
    return lax.broadcasted_iota(jnp.int32, shape, len(shape) - 1)


def roll(values, shift):
    return pltpu.roll(values, shift % LANES, len(values.shape) - 1)


def forward_group(fields, table_z, table_y, out_ref, first, rows):
    left = jnp.concatenate(
        [jnp.concatenate([fields[q], fields[q + 1]], axis=1) for q in range(0, len(fields), 2)], axis=0
    )
    lines = dot(jnp.concatenate(split(left), axis=1), table_z)
    lines = lines[:, :LANES] + lines[:, LANES:]
    half = MY // 2
    for g in range(0, len(fields) // 2, GROUP // 2):
        quad = jnp.concatenate([lines[q * NY : (q + 1) * NY] for q in range(g, g + GROUP // 2)], axis=1)
        wide = dot(table_y, jnp.concatenate(split(quad), axis=0))
        wide = wide[: 2 * MY] + wide[2 * MY :]
        for q in range(GROUP // 2):
            by_cos = wide[:MY, q * LANES : (q + 1) * LANES]
            by_sin = roll(wide[MY:, q * LANES : (q + 1) * LANES], 64)
            modes = by_cos + jnp.where(lane_index(by_sin.shape) < LANES // 2, by_sin, -by_sin)
            even, odd = modes[:half], modes[half:]
            at_even = (lane_index(even.shape) // MZ) % 2 == 0
            at = first + 2 * (g + q)
            out_ref[pl.ds(at, half, stride=rows), :] = jnp.where(at_even, even, roll(odd, MZ))
            out_ref[pl.ds(at + 1, half, stride=rows), :] = jnp.where(at_even, roll(even, -MZ), odd)


def inverse_y_group(modes_ref, y_table, first, rows):
    half = MY // 2
    pairs = []
    for q in range(GROUP // 2):
        c0 = modes_ref[pl.ds(first + 2 * q, half, stride=rows), :]
        c1 = modes_ref[pl.ds(first + 2 * q + 1, half, stride=rows), :]
        at_even = (lane_index(c0.shape) // MZ) % 2 == 0
        even = jnp.where(at_even, c0, roll(c1, MZ))
        odd = jnp.where(at_even, roll(c0, -MZ), c1)
        both = jnp.concatenate([even, odd], axis=0)
        other = roll(both, 64)
        turned = jnp.where(lane_index(both.shape) < LANES // 2, -other, other)
        pairs.append(jnp.concatenate([both, turned], axis=0))
    high, low = split(jnp.concatenate(pairs, axis=1))
    lines = dot(y_table, jnp.concatenate([high, low, high], axis=0))
    return [lines[:, q * LANES : (q + 1) * LANES] for q in range(GROUP // 2)]


def in_hbm(*arrays):
    return [pltpu.with_memory_space_constraint(each, pltpu.HBM) for each in arrays]


def in_vmem(*arrays):
    return [pltpu.with_memory_space_constraint(each, pltpu.VMEM) for each in arrays]


def full(shape):
    return pl.BlockSpec(shape, lambda *_: (0,) * len(shape))


def params(limit):
    return pltpu.CompilerParams(vmem_limit_bytes=limit * MIB)


def fold_block(pieces, out_ref, at):
    copies = pieces.shape[0]
    real, imag = pieces[0, 0], pieces[0, 1]
    for r in range(1, copies):
        real, imag = real + pieces[r, 0], imag + pieces[r, 1]
    modes = real.shape[-1]
    out_ref[at, :, :, :modes] = real
    out_ref[at, :, :, modes:] = imag


def fetches(weights_hbm, ring_ref, sems, at, slot, unique):
    copies = ring_ref.shape[1]
    return [
        pltpu.make_async_copy(weights_hbm.at[c, at + r * unique], ring_ref.at[slot, r, c], sems.at[slot, r, c])
        for r in range(copies)
        for c in range(2)
    ]


def fold_shapes(weights, unique, slots):
    copies = weights.shape[1] // unique
    shape = (unique,) + weights.shape[2:4] + (2 * weights.shape[4],)
    ring = [pltpu.VMEM((slots, copies, 2) + weights.shape[2:], F32), pltpu.SemaphoreType.DMA((slots, copies, 2))]
    return pltpu.HBM(shape, F32), ring


def forward_kernel(
    table_z, table_y, field_ref, weights_hbm, out_ref, folded_ref, ring_ref, sems,
    *, channels, step_channels, per_step, unique, slots,
):
    step = pl.program_id(0)

    def transform():
        fields = [field_ref[q] for q in range(step_channels)]
        forward_group(fields, table_z[...], table_y[...], out_ref, step * step_channels, channels)

    @pl.when(step == 0)
    def _():
        for at in range(slots):
            for copy in fetches(weights_hbm, ring_ref, sems, at, at, unique):
                copy.start()
        transform()

    @pl.when(step > 0)
    def _():
        for q in range(per_step):
            at = (step - 1) * per_step + q
            for copy in fetches(weights_hbm, ring_ref, sems, at, at, unique):
                copy.wait()
            fold_block(ring_ref.at[at], folded_ref, q)
        transform()


FOLD_STEP = 2
FIELD_STEP = 8


def folded_early(channels):
    return (channels // FIELD_STEP - 1) * FOLD_STEP


def forward_modes(field, tables, weights, unique):
    channels = field.shape[0]
    slots = folded_early(channels)
    folded_shape, ring = fold_shapes(weights, unique, slots)
    owners = MY // 2
    out, some = pl.pallas_call(
        functools.partial(
            forward_kernel, channels=channels, step_channels=FIELD_STEP, per_step=FOLD_STEP, unique=unique, slots=slots
        ),
        grid=(channels // FIELD_STEP,),
        in_specs=[full(t.shape) for t in tables]
        + [pl.BlockSpec((FIELD_STEP, NY, NZ), lambda s: (s, 0, 0)), pl.BlockSpec(memory_space=pl.ANY)],
        out_specs=[
            full((owners * channels, LANES)),
            pl.BlockSpec((FOLD_STEP,) + folded_shape.shape[1:], lambda s: (jnp.maximum(s - 1, 0), 0, 0, 0)),
        ],
        out_shape=[pltpu.VMEM((owners * channels, LANES), F32), folded_shape],
        scratch_shapes=ring,
        compiler_params=params(LIMIT),
        cost_estimate=pl.CostEstimate(flops=2 * 10**9, bytes_accessed=22 * MIB, transcendentals=0),
        name="forward_yz",
    )(*in_hbm(*tables, field, weights))
    return out.reshape(owners, channels, LANES), some


def fold_kernel(weights_hbm, _, out_ref, ring_ref, sems, *, first, unique, slots):
    step = pl.program_id(0)
    slot = step % slots

    @pl.when(step == 0)
    def _():
        for ahead in range(slots):
            for copy in fetches(weights_hbm, ring_ref, sems, first + ahead, ahead, unique):
                copy.start()

    for copy in fetches(weights_hbm, ring_ref, sems, first + step, slot, unique):
        copy.wait()
    fold_block(ring_ref.at[slot], out_ref, 0)

    @pl.when(step + slots < pl.num_programs(0))
    def _():
        for copy in fetches(weights_hbm, ring_ref, sems, first + step + slots, slot, unique):
            copy.start()


def fold_rest(weights, some, unique):
    first = folded_early(weights.shape[2])
    slots = min(4, unique - first)
    folded_shape, ring = fold_shapes(weights, unique, slots)
    anywhere = pl.BlockSpec(memory_space=pl.ANY)
    return pl.pallas_call(
        functools.partial(fold_kernel, first=first, unique=unique, slots=slots),
        grid=(unique - first,),
        in_specs=[anywhere, anywhere],
        out_specs=pl.BlockSpec((1,) + folded_shape.shape[1:], lambda s: (first + s, 0, 0, 0)),
        out_shape=folded_shape,
        scratch_shapes=ring,
        input_output_aliases={1: 0},
        compiler_params=params(LIMIT),
        cost_estimate=pl.CostEstimate(flops=4 * 10**6, bytes_accessed=25 * MIB, transcendentals=0),
        name="fold_weights",
    )(*in_hbm(weights, some))


def halve_lines(lines_ref, sums_ref, points, channels):
    half = points // 2
    sign = jnp.where(lane_index((channels, LANES)) < LANES // 2, 1.0, -1.0)
    for x in range(half):
        near, far = lines_ref[x, :channels], lines_ref[x + half, :channels]
        for parity, value in enumerate((near + far, near - far)):
            sums_ref[parity, 0, x] = value
            sums_ref[parity, 1, x] = sign * roll(value, 64)


def spectrum_row(cos_ref, sin_ref, sums_ref, at, parity, half):
    total = cos_ref[at, 0] * sums_ref[parity, 0, 0] + sin_ref[at, 0] * sums_ref[parity, 1, 0]
    for x in range(1, half):
        total += cos_ref[at, x] * sums_ref[parity, 0, x] + sin_ref[at, x] * sums_ref[parity, 1, x]
    return total


def doubled(values):
    other = roll(values, 64)
    low = lane_index(values.shape) < LANES // 2
    return jnp.where(low, values, other), jnp.where(low, other, values)


def mix_kernel(
    cos_ref, sin_ref, lines_ref, weights_ref, spec_ref, out_ref, sums_ref, total_ref, real_ref, imag_ref,
    *, points, channels, per_step, norm,
):
    step = pl.program_id(0)
    half = points // 2

    @pl.when(step == 0)
    def _():
        halve_lines(lines_ref, sums_ref, points, channels)
        total_ref[...] = jnp.zeros_like(total_ref)

    low = lane_index((channels, LANES)) < LANES // 2
    for q in range(per_step):
        at = step * per_step + q
        parity = q % 2
        spec = norm * spectrum_row(cos_ref, sin_ref, sums_ref, at, parity, half)
        spec_ref[q] = spec
        real_ref[q], imag_ref[q] = doubled(spec)
        by_real = jnp.zeros((channels, LANES), F32)
        by_imag = jnp.zeros((channels, LANES), F32)
        for i in range(channels):
            weight = weights_ref[q, i]
            by_real += real_ref[q, pl.ds(i, 1), :] * weight
            by_imag += imag_ref[q, pl.ds(i, 1), :] * weight
        other = roll(by_imag, 64)
        mixed = by_real + jnp.where(low, -other, other)
        other = roll(mixed, 64)
        turned = jnp.where(low, -other, other)
        for x in range(half):
            total_ref[parity, x] += cos_ref[at, x] * mixed + sin_ref[at, x] * turned

    @pl.when(step == pl.num_programs(0) - 1)
    def _():
        for x in range(half):
            out_ref[x] = total_ref[0, x] + total_ref[1, x]
            out_ref[x + half] = total_ref[0, x] - total_ref[1, x]


def smem():
    return pl.BlockSpec(memory_space=pltpu.SMEM)


def mix(cos_x, sin_x, lines, weights, norm):
    points, channels, _ = lines.shape
    unique = weights.shape[0]
    per_step = min(unique, 4)
    shape = (points, channels, LANES)
    return pl.pallas_call(
        functools.partial(mix_kernel, points=points, channels=channels, per_step=per_step, norm=norm),
        grid=(unique // per_step,),
        in_specs=[
            smem(),
            smem(),
            full(shape),
            pl.BlockSpec((per_step,) + weights.shape[1:], lambda s: (s, 0, 0, 0)),
        ],
        out_specs=[
            pl.BlockSpec((per_step, channels, LANES), lambda s: (s, 0, 0)),
            full(shape),
        ],
        out_shape=[
            pltpu.VMEM((unique, channels, LANES), F32),
            pltpu.VMEM(shape, F32),
        ],
        scratch_shapes=[
            pltpu.VMEM((2, 2, points // 2, channels, LANES), F32),
            pltpu.VMEM((2, points // 2, channels, LANES), F32),
            pltpu.VMEM((per_step, channels, LANES), F32),
            pltpu.VMEM((per_step, channels, LANES), F32),
        ],
        compiler_params=params(LIMIT),
        cost_estimate=pl.CostEstimate(flops=2 * 10**7, bytes_accessed=9 * MIB, transcendentals=0),
        name="mix_modes",
    )(cos_x, sin_x, *in_vmem(lines), *in_hbm(weights))


def exact_dot(left, right):
    return jnp.dot(left, right, precision=lax.Precision.HIGHEST, preferred_element_type=F32)


def pointwise_kernel(sum_ref, turned_ref, bias_in_ref, field_ref, out_ref, mixer_ref, bias_ref, *, channels, blocks):
    size = 8 * channels

    @pl.when(pl.program_id(0) == 0)
    def _():
        wide = exact_dot(sum_ref[...], turned_ref[...])
        wide = lax.dot_general(
            wide, sum_ref[...], (((1,), (1,)), ((), ())), precision=lax.Precision.HIGHEST, preferred_element_type=F32
        )
        row = lax.broadcasted_iota(jnp.int32, (size, size), 0) % 8
        high, low = split(jnp.where(row == lane_index((size, size)) % 8, wide, 0.0))
        mixer_ref[:size] = high
        mixer_ref[size:] = low
        bias_ref[...] = exact_dot(sum_ref[...], bias_in_ref[...])

    for b in range(blocks):
        high, low = split(field_ref[:, 8 * b : 8 * b + 8, :].reshape(size, NZ))
        wide = dot(mixer_ref[...], high)
        values = wide[:size] + wide[size:] + dot(mixer_ref[:size], low) + bias_ref[...]
        out_ref[:, 8 * b : 8 * b + 8, :] = values.reshape(channels, 8, NZ)


def pointwise(field, summing, point_weights, point_bias):
    channels = field.shape[0]
    blocks = 2
    turned = point_weights.T
    bias = point_bias[:, None]
    size = 8 * channels
    block = pl.BlockSpec((channels, 8 * blocks, NZ), lambda s: (0, s, 0))
    return pl.pallas_call(
        functools.partial(pointwise_kernel, channels=channels, blocks=blocks),
        grid=(NY // (8 * blocks),),
        in_specs=[full(summing.shape), full(turned.shape), full(bias.shape), block],
        out_specs=block,
        out_shape=pltpu.HBM(field.shape, F32),
        scratch_shapes=[pltpu.VMEM((2 * size, size), BF16), pltpu.VMEM((size, 1), F32)],
        compiler_params=params(LIMIT),
        cost_estimate=pl.CostEstimate(flops=4 * 10**9, bytes_accessed=24 * MIB, transcendentals=0),
        name="pointwise",
    )(*in_hbm(summing, turned, bias, field))


TAIL = (
    0.28208447628636224, 0.2824095107622592, 0.24285420127949567, 0.20367621235863168, -0.028966708844937322,
    0.28146769954808826, -0.490173103351073, 0.2860108822904108, -0.0593632144096072,
)


def normal(values):
    bell = jnp.exp(-0.5 * values * values)
    t = 1.0 / (1.0 + (0.5 * INV_SQRT_TWO) * jnp.abs(values))
    tail = 0.5 * TAIL[-1]
    for factor in TAIL[-2::-1]:
        tail = tail * t + 0.5 * factor
    tail = tail * t * bell
    return jnp.where(values < 0.0, tail, 1.0 - tail), values * bell * INV_SQRT_TWO_PI


def cell_group(inv_y, inv_z, modes_ref, pre_ref, cot_ref, act_ref, first, count, channels):
    lines = []
    for g in range(0, count, GROUP):
        lines += inverse_y_group(modes_ref, inv_y, first + g, channels)
    lines = jnp.concatenate(lines, axis=0)
    high = lines.astype(BF16).astype(F32)
    low = lines - high
    at_even = (lane_index(lines.shape) // MZ) % 2 == 0
    spectral = [
        dot(jnp.concatenate([high, side], axis=1).astype(BF16), table)
        for side, table in zip((jnp.where(at_even, low, roll(high, MZ)), jnp.where(at_even, roll(high, -MZ), low)), inv_z)
    ]
    slopes = []
    for q in range(count):
        before = spectral[q % 2][q // 2 * NY : (q // 2 + 1) * NY] + pre_ref[q]
        cdf, bent = normal(before)
        act_ref[q] = (before * cdf).astype(BF16)
        slopes.append(cot_ref[q].astype(F32) * (cdf + bent))
    return slopes


def early_cell_kernel(
    inv_y, inv_z0, inv_z1, table_z, table_y, modes_ref, pre_ref, cot_ref, act_ref, slope_ref, out_ref,
    *, channels, count, rows,
):
    step = pl.program_id(0)
    slopes = cell_group(
        inv_y[...], (inv_z0[...], inv_z1[...]), modes_ref, pre_ref, cot_ref, act_ref, step * count, count, channels
    )
    for q in range(count):
        slope_ref[q] = slopes[q]
    forward_group(slopes, table_z[...], table_y[...], out_ref, step * count, rows)


def point_gradient(field_ref, slope_ref, sum_ref, channels):
    size = 8 * channels
    total = jnp.zeros((size, size), F32)
    for b in range(NY // 8):
        at = slice(8 * b, 8 * b + 8)
        f_h, f_l = split(field_ref[:, at, :].reshape(size, NZ))
        s_h, s_l = split(slope_ref[:, at, :].reshape(size, NZ))
        total += lax.dot_general(
            jnp.concatenate([f_h, f_h, f_l], axis=1),
            jnp.concatenate([s_h, s_l, s_h], axis=1),
            (((1,), (1,)), ((), ())),
            preferred_element_type=F32,
        )
    row = lax.broadcasted_iota(jnp.int32, (size, size), 0) % 8
    total = jnp.where(row == lane_index((size, size)) % 8, total, 0.0)
    return exact_dot(jnp.sum(total.reshape(channels, 8, size), axis=1), sum_ref[...])


def late_cell_kernel(
    inv_y, inv_z0, inv_z1, table_z, table_y, sum_ref, modes_ref, pre_ref, cot_ref, early_ref,
    slope_hbm, field_hbm, _, act_ref, out_ref, field_ref, slope_ref, sems, *, channels, count, rows, owners,
):
    step = pl.program_id(0)
    early = early_count(channels)
    late = channels - early
    copies = [
        pltpu.make_async_copy(field_hbm, field_ref, sems.at[0]),
        pltpu.make_async_copy(slope_hbm, slope_ref.at[pl.ds(0, early)], sems.at[1]),
    ]

    @pl.when(step == 0)
    def _():
        for copy in copies:
            copy.start()

    first = early + step * count
    slopes = cell_group(
        inv_y[...], (inv_z0[...], inv_z1[...]), modes_ref, pre_ref, cot_ref, act_ref, first, count, channels
    )
    for q in range(count):
        slope_ref[first + q] = slopes[q]
    forward_group(slopes, table_z[...], table_y[...], out_ref, step * count, rows)

    @pl.when(step == pl.num_programs(0) - 1)
    def _():
        for copy in copies:
            copy.wait()
        point = point_gradient(field_ref, slope_ref, sum_ref, channels)
        packed = jnp.concatenate([point[8 * q : 8 * q + 8] for q in range(channels // 8)], axis=1)
        zero_mode = jnp.concatenate([early_ref[0:early, 0:1], out_ref[0:late, 0:1]], axis=0)
        eye = lax.broadcasted_iota(jnp.int32, (channels, LANES), 0) == lane_index((channels, LANES))
        bias = jnp.sum(jnp.where(eye, jnp.broadcast_to(zero_mode, (channels, LANES)), 0.0), axis=0, keepdims=True)
        extra = jnp.where(lax.broadcasted_iota(jnp.int32, (8, LANES), 0) == 0, jnp.broadcast_to(bias, (8, LANES)), 0.0)
        for d in range(owners):
            out_ref[d * rows + late : d * rows + late + 8, :] = packed
            out_ref[d * rows + late + 8 : (d + 1) * rows, :] = extra


def early_count(channels):
    return channels * 3 // 4


def early_cells(inverse, forward, modes, pre, cotangent):
    channels = pre.shape[0]
    owners = MY // 2
    early = early_count(channels)
    block = pl.BlockSpec((STEP, NY, NZ), lambda s: (s, 0, 0))
    tables = (*inverse, *forward)
    act, slope, out = pl.pallas_call(
        functools.partial(early_cell_kernel, channels=channels, count=STEP, rows=early),
        grid=(early // STEP,),
        in_specs=[full(t.shape) for t in tables] + [full((owners * channels, LANES)), block, block],
        out_specs=[block, block, full((owners * early, LANES))],
        out_shape=[
            pltpu.HBM((channels, NY, NZ), BF16),
            pltpu.HBM((early, NY, NZ), F32),
            pltpu.VMEM((owners * early, LANES), F32),
        ],
        compiler_params=params(LIMIT),
        cost_estimate=pl.CostEstimate(flops=3 * 10**9, bytes_accessed=7 * MIB, transcendentals=10**6),
        name="early_cells",
    )(*in_hbm(*tables), *in_vmem(modes.reshape(owners * channels, LANES)), *in_hbm(pre, cotangent))
    return act, slope, out.reshape(owners, early, LANES)


def late_cells(inverse, forward, summing, modes, pre, cotangent, field, early, slope, act):
    channels = field.shape[0]
    owners = MY // 2
    first = early_count(channels)
    rows = channels - first + 16
    start = first // STEP
    block = pl.BlockSpec((STEP, NY, NZ), lambda s: (start + s, 0, 0))
    anywhere = pl.BlockSpec(memory_space=pl.ANY)
    tables = (*inverse, *forward, summing)
    act, out = pl.pallas_call(
        functools.partial(late_cell_kernel, channels=channels, count=STEP, rows=rows, owners=owners),
        grid=((channels - first) // STEP,),
        in_specs=[full(t.shape) for t in tables]
        + [full((owners * channels, LANES)), block, block, full((owners * first, LANES))]
        + [anywhere] * 3,
        out_specs=[block, full((owners * rows, LANES))],
        out_shape=[
            pltpu.HBM((channels, NY, NZ), BF16),
            pltpu.VMEM((owners * rows, LANES), F32),
        ],
        scratch_shapes=[
            pltpu.VMEM((channels, NY, NZ), F32),
            pltpu.VMEM((channels, NY, NZ), F32),
            pltpu.SemaphoreType.DMA((2,)),
        ],
        input_output_aliases={len(tables) + 6: 0},
        compiler_params=params(LIMIT),
        cost_estimate=pl.CostEstimate(flops=6 * 10**9, bytes_accessed=11 * MIB, transcendentals=10**6),
        name="late_cells",
    )(
        *in_hbm(*tables),
        *in_vmem(modes.reshape(owners * channels, LANES)),
        *in_hbm(pre, cotangent),
        *in_vmem(early.reshape(owners * first, LANES)),
        *in_hbm(slope, field, act),
    )
    return act, out.reshape(owners, rows, LANES)


def gradient_kernel(cos_ref, sin_ref, spec_ref, lines_ref, *refs, points, channels, unique, copies, norm, first, outputs, slots):
    last = first > 0
    if last:
        _, out_hbm, point_ref, bias_ref, sums_ref, real_ref, imag_ref, buffer, sems = refs
    else:
        out_hbm, sums_ref, real_ref, imag_ref, buffer, sems = refs
    halve_lines(lines_ref, sums_ref, points, outputs)
    half = LANES // 2
    lane = lane_index((outputs, LANES))
    scale = jnp.where(lane % MZ == 0, norm, 2.0 * norm)

    def writes(at, slot):
        return [
            pltpu.make_async_copy(
                buffer.at[slot, c],
                out_hbm.at[c, at + r * unique, :, pl.ds(first, outputs), :],
                sems.at[slot, c, r],
            )
            for r in range(copies)
            for c in range(2)
        ]

    @pl.loop(0, unique // slots)
    def _(turn):
        for slot in range(slots):
            at = slots * turn + slot

            @pl.when(turn > 0)
            def _():
                for copy in writes(at - slots, slot):
                    copy.wait()

            slope = scale * spectrum_row(cos_ref, sin_ref, sums_ref, at, slot % 2, points // 2)
            other = roll(slope, 64)
            flipped = jnp.where(lane < half, other, -other)
            real_ref[slot], imag_ref[slot] = doubled(spec_ref[at])
            for i in range(channels):
                both = real_ref[slot, pl.ds(i, 1), :] * slope + imag_ref[slot, pl.ds(i, 1), :] * flipped
                buffer[slot, 0, i] = both[:, :half]
                buffer[slot, 1, i] = both[:, half:]
            for copy in writes(at, slot):
                copy.start()

    if last:
        packed = lines_ref[0, outputs : outputs + 16, :]
        for x in range(1, points):
            packed += lines_ref[x, outputs : outputs + 16, :]
        packed = norm * packed
        for q in range(channels // 8):
            point_ref[8 * q : 8 * q + 8, :] = packed[:8, q * channels : (q + 1) * channels]
        bias_ref[...] = packed[8:9, :channels]

    for at in range(unique - slots, unique):
        for copy in writes(at, at % slots):
            copy.wait()


def gradient(cos_x, sin_x, spectrum, lines, norm, kept_x, before=()):
    points, rows, _ = lines.shape
    unique, channels, _ = spectrum.shape
    half = LANES // 2
    copies = kept_x // unique
    first = early_count(channels) if before else 0
    outputs = channels - first if before else early_count(channels)
    slots = 8 if before else 4
    anywhere = pl.BlockSpec(memory_space=pl.ANY)
    shape = jax.ShapeDtypeStruct((2, kept_x, channels, channels, half), F32)
    sums = [(channels, channels), (1, channels)] if before else []
    return pl.pallas_call(
        functools.partial(
            gradient_kernel, points=points, channels=channels, unique=unique, copies=copies, norm=norm,
            first=first, outputs=outputs, slots=slots,
        ),
        in_specs=[smem(), smem(), full(spectrum.shape), full(lines.shape)] + [anywhere] * len(before),
        out_specs=[anywhere] + [full(each) for each in sums],
        out_shape=[shape] + [jax.ShapeDtypeStruct(each, F32) for each in sums],
        scratch_shapes=[
            pltpu.VMEM((2, 2, points // 2, outputs, LANES), F32),
            pltpu.VMEM((slots, channels, LANES), F32),
            pltpu.VMEM((slots, channels, LANES), F32),
            pltpu.VMEM((slots, 2, channels, outputs, half), F32),
            pltpu.SemaphoreType.DMA((slots, 2, copies)),
        ],
        input_output_aliases={4: 0} if before else {},
        compiler_params=params(LIMIT),
        cost_estimate=pl.CostEstimate(flops=5 * 10**6, bytes_accessed=32 * MIB, transcendentals=0),
        name="weight_gradient",
    )(cos_x, sin_x, *in_vmem(spectrum, lines), *before)


def swap(lines):
    return lax.all_to_all(lines, "space", split_axis=0, concat_axis=0, tiled=True)


def suits(width_x, length_x, devices, channels, weights):
    held = weights.shape[2]
    even = np.array_equal(kept(MX, length_x) % length_x, np.arange(MX) % length_x)
    return (
        width_x == 1
        and held == 2 * MZ
        and devices * 2 == MY
        and 2 * held == LANES
        and MX % length_x == 0
        and length_x % 8 == 0
        and even
        and channels == MZ
    )


def body(lifted_field, cotangent, spectral_weights, point_weights, point_bias):
    devices = lax.axis_size("space")
    channels, width_x = lifted_field.shape[:2]
    length_x = width_x * devices
    if not suits(width_x, length_x, devices, channels, spectral_weights):
        return general_body(lifted_field, cotangent, spectral_weights, point_weights, point_bias)
    norm = float(length_x * NY * NZ) ** -0.5
    theta = angles(np.arange(length_x), np.arange(length_x), length_x)
    cos_x, sin_x = jnp.asarray(np.cos(theta), F32), jnp.asarray(np.sin(theta), F32)
    forward = forward_tables()
    inverse = inverse_tables(norm)
    summing = jnp.asarray(np.repeat(np.eye(channels), 8, axis=0), F32)

    field = lifted_field.reshape(channels, NY, NZ)
    slopes_in = cotangent.reshape(channels, NY, NZ)
    weights = jnp.transpose(spectral_weights, (0, 1, 3, 4, 2))

    lines, some = forward_modes(field, forward, weights, length_x)
    lines = swap(lines)
    folded = fold_rest(weights, some, length_x)
    spectrum, mixed = mix(cos_x, sin_x, lines, folded, norm)
    field_late, mixed = lax.optimization_barrier((field, mixed))
    modes = swap(mixed)
    pre = pointwise(field_late, summing, point_weights, point_bias)
    act, slope, early = early_cells(inverse, forward, modes, pre, slopes_in)
    early_lines = swap(early)
    activated, late = late_cells(inverse, forward, summing, modes, pre, slopes_in, field, early, slope, act)
    late_lines = swap(late)
    (grad,) = gradient(cos_x, sin_x, spectrum, early_lines, norm, MX)
    grad, grad_point, grad_bias = gradient(cos_x, sin_x, spectrum, late_lines, norm, MX, (grad,))
    return (
        activated.reshape(cotangent.shape),
        jnp.transpose(grad, (0, 1, 4, 2, 3)),
        grad_point,
        grad_bias.reshape(channels),
    )


HIGHEST = lax.Precision.HIGHEST


def trig_tables(positions, frequency, length):
    product = positions[:, None] * frequency[None, :] % length
    phase_angle = 2.0 * jnp.pi / length * product.astype(jnp.float32)
    return (jnp.cos(phase_angle), jnp.sin(phase_angle))


def kept_frequencies(kept_count, length):
    mode_index = jnp.arange(kept_count, dtype=jnp.int32)
    return jnp.where(mode_index < kept_count // 2, mode_index, length - kept_count + mode_index)


def forward_local(field_in):
    channels = field_in.shape[0]
    width_x = field_in.shape[1]
    cos_z, sin_z = trig_tables(jnp.arange(NZ, dtype=jnp.int32), jnp.arange(MZ, dtype=jnp.int32), NZ)
    table_z = jnp.concatenate([cos_z, -sin_z], axis=1)
    along_z = jnp.einsum("cxyz,zk->cxyk", field_in, table_z, precision=HIGHEST)
    z_real = along_z[..., :MZ]
    z_imag = along_z[..., MZ:]
    cos_y, sin_y = trig_tables(jnp.arange(NY, dtype=jnp.int32), kept_frequencies(MY, NY), NY)
    y_real = jnp.einsum("cxyk,yj->xcjk", z_real, cos_y, precision=HIGHEST) + jnp.einsum(
        "cxyk,yj->xcjk", z_imag, sin_y, precision=HIGHEST
    )
    y_imag = jnp.einsum("cxyk,yj->xcjk", z_imag, cos_y, precision=HIGHEST) - jnp.einsum(
        "cxyk,yj->xcjk", z_real, sin_y, precision=HIGHEST
    )
    stacked = jnp.stack([y_real, y_imag], axis=1)
    return stacked.reshape(width_x, 2, channels, MY * MZ)


def transform_x(x_lines):
    length_x = x_lines.shape[0]
    cos_x, sin_x = trig_tables(
        jnp.arange(length_x, dtype=jnp.int32), kept_frequencies(MX, length_x), length_x
    )
    norm_scale = 1.0 / float(length_x * NY * NZ) ** 0.5
    part_real = x_lines[:, 0]
    part_imag = x_lines[:, 1]
    x_real = jnp.einsum("xcm,xk->kcm", part_real, cos_x, precision=HIGHEST) + jnp.einsum(
        "xcm,xk->kcm", part_imag, sin_x, precision=HIGHEST
    )
    x_imag = jnp.einsum("xcm,xk->kcm", part_imag, cos_x, precision=HIGHEST) - jnp.einsum(
        "xcm,xk->kcm", part_real, sin_x, precision=HIGHEST
    )
    return norm_scale * jnp.stack([x_real, x_imag], axis=1)


def mix_modes(spectrum, weights):
    spec_real = spectrum[:, 0]
    spec_imag = spectrum[:, 1]
    out_real = jnp.einsum("kim,kmio->kom", spec_real, weights[0], precision=HIGHEST) - jnp.einsum(
        "kim,kmio->kom", spec_imag, weights[1], precision=HIGHEST
    )
    out_imag = jnp.einsum("kim,kmio->kom", spec_real, weights[1], precision=HIGHEST) + jnp.einsum(
        "kim,kmio->kom", spec_imag, weights[0], precision=HIGHEST
    )
    return jnp.stack([out_real, out_imag], axis=1)


def inverse_x(spectrum, positions, length_x):
    cos_x, sin_x = trig_tables(positions, kept_frequencies(MX, length_x), length_x)
    spec_real = spectrum[:, 0]
    spec_imag = spectrum[:, 1]
    a_real = jnp.einsum("kcm,xk->xcm", spec_real, cos_x, precision=HIGHEST) - jnp.einsum(
        "kcm,xk->xcm", spec_imag, sin_x, precision=HIGHEST
    )
    a_imag = jnp.einsum("kcm,xk->xcm", spec_imag, cos_x, precision=HIGHEST) + jnp.einsum(
        "kcm,xk->xcm", spec_real, sin_x, precision=HIGHEST
    )
    return jnp.stack([a_real, a_imag], axis=1)


def inverse_yz(x_lines, length_x):
    width_x = x_lines.shape[0]
    channels = x_lines.shape[2]
    mode_grid = x_lines.reshape(width_x, 2, channels, MY, MZ)
    cos_y, sin_y = trig_tables(jnp.arange(NY, dtype=jnp.int32), kept_frequencies(MY, NY), NY)
    b_real = jnp.einsum("xcjk,yj->cxyk", mode_grid[:, 0], cos_y, precision=HIGHEST) - jnp.einsum(
        "xcjk,yj->cxyk", mode_grid[:, 1], sin_y, precision=HIGHEST
    )
    b_imag = jnp.einsum("xcjk,yj->cxyk", mode_grid[:, 1], cos_y, precision=HIGHEST) + jnp.einsum(
        "xcjk,yj->cxyk", mode_grid[:, 0], sin_y, precision=HIGHEST
    )
    cos_z, sin_z = trig_tables(jnp.arange(NZ, dtype=jnp.int32), jnp.arange(MZ, dtype=jnp.int32), NZ)
    weight_z = jnp.where(jnp.arange(MZ, dtype=jnp.int32) == 0, 1.0, 2.0).astype(jnp.float32)
    table_z = jnp.concatenate([cos_z * weight_z[None, :], -sin_z * weight_z[None, :]], axis=1)
    stacked = jnp.concatenate([b_real, b_imag], axis=-1)
    result = jnp.einsum("cxyk,zk->cxyz", stacked, table_z, precision=HIGHEST)
    return result * (1.0 / float(length_x * NY * NZ) ** 0.5)


def gelu_slope(values):
    return (
        0.5 * (1.0 + lax.erf(values * INV_SQRT_TWO))
        + values * jnp.exp(-0.5 * values * values) * INV_SQRT_TWO_PI
    )


def weight_gradient(spectrum, slope_modes, first_mode):
    mode_ids = first_mode + jnp.arange(spectrum.shape[3], dtype=jnp.int32)
    weight_modes = jnp.where(mode_ids % MZ == 0, 1.0, 2.0).astype(jnp.float32)
    grad_real = jnp.einsum(
        "kim,kom->kmio", spectrum[:, 0], slope_modes[:, 0], precision=HIGHEST
    ) + jnp.einsum("kim,kom->kmio", spectrum[:, 1], slope_modes[:, 1], precision=HIGHEST)
    grad_imag = jnp.einsum(
        "kim,kom->kmio", spectrum[:, 0], slope_modes[:, 1], precision=HIGHEST
    ) - jnp.einsum("kim,kom->kmio", spectrum[:, 1], slope_modes[:, 0], precision=HIGHEST)
    stacked = jnp.stack([grad_real, grad_imag], axis=0)
    return stacked * weight_modes[None, None, :, None, None]


def to_modes(field_in):
    return transform_x(
        lax.all_to_all(forward_local(field_in), "space", split_axis=3, concat_axis=0, tiled=True)
    )


def general_body(lifted_field, cotangent, spectral_weights, point_weights, point_bias):
    devices = lax.axis_size("space")
    width_x = lifted_field.shape[1]
    length_x = width_x * devices
    spectrum = to_modes(lifted_field)
    mixed_modes = mix_modes(spectrum, spectral_weights)
    full_lines = inverse_x(mixed_modes, jnp.arange(length_x, dtype=jnp.int32), length_x)
    spectral = inverse_yz(
        lax.all_to_all(full_lines, "space", split_axis=0, concat_axis=3, tiled=True), length_x
    )
    pointwise = (
        jnp.einsum("ixyz,io->oxyz", lifted_field, point_weights, precision=HIGHEST)
        + point_bias[:, None, None, None]
    )
    before = spectral + pointwise
    activated = jax.nn.gelu(before, approximate=False).astype(jnp.bfloat16)
    slope_field = cotangent.astype(jnp.float32) * gelu_slope(before)
    local_point = jnp.einsum("ixyz,oxyz->io", lifted_field, slope_field, precision=HIGHEST)
    local_bias = jnp.sum(slope_field, axis=(1, 2, 3))
    partial = jnp.concatenate([local_point, local_bias[None, :]], axis=0)
    gathered = lax.all_gather(partial, "space", axis=0, tiled=False)
    summed = jnp.sum(gathered, axis=0)
    summed_point, summed_bias = summed[:-1], summed[-1]
    root_cells = float(length_x * NY * NZ) ** 0.5
    slope_spectrum = to_modes(slope_field)
    first_mode = lax.axis_index("space") * spectrum.shape[3]
    grad_spectral = weight_gradient(spectrum, slope_spectrum, first_mode)
    return (activated, grad_spectral, summed_point / root_cells, summed_bias / root_cells)


def solution(mesh):
    placed = (
        P("groups", "space", None, None),
        P("groups", "space", None, None),
        P(None, None, "space", None, None),
        P(),
        P(),
    )
    return jax.shard_map(
        body,
        mesh=mesh,
        in_specs=placed,
        out_specs=(
            P("groups", "space", None, None),
            P("groups", None, "space", None, None),
            P("groups", None),
            P("groups"),
        ),
        check_vma=False,
    )
```

```python
import functools

import jax
import jax.numpy as jnp
import ml_dtypes
import numpy as np
from jax import lax
from jax.experimental import pallas as pl
from jax.experimental.pallas import tpu as pltpu
from jax.sharding import PartitionSpec as P

MX = 32
MY = 32
MZ = 32
NY = 128
NZ = 256

F32 = jnp.float32
BF16 = jnp.bfloat16
INV_SQRT_TWO = 0.7071067811865476
INV_SQRT_TWO_PI = 0.3989422804014327
MIB = 1 << 20
LIMIT = 48
LANES = 128
GROUP = 4
STEP = 8


def kept(kept_count, length):
    index = np.arange(kept_count)
    return np.where(index < kept_count // 2, index, length - kept_count + index)


def angles(positions, frequency, length):
    product = positions[:, None] * frequency[None, :] % length
    return 2.0 * np.pi / length * product


def split_table(table):
    high = table.astype(ml_dtypes.bfloat16)
    return high, (table - high.astype(np.float64)).astype(ml_dtypes.bfloat16)


def lane_spread(first, second, real_table, imag_table):
    return np.concatenate(
        [real_table * first, real_table * second, imag_table * first, imag_table * second], axis=1
    )


def forward_tables():
    theta = angles(np.arange(NZ), np.arange(MZ), NZ)
    table = np.concatenate([lane_spread(f, s, np.cos(theta), -np.sin(theta)) for f, s in ((1, 0), (0, 1))], axis=0)
    high, low = split_table(table)
    table_z = np.concatenate(
        [np.concatenate([high, low], axis=1), np.concatenate([high, np.zeros_like(low)], axis=1)], axis=0
    )
    theta = angles(np.arange(NY), kept(MY, NY), NY).T
    table = np.concatenate([np.cos(theta)[0::2], np.cos(theta)[1::2], np.sin(theta)[0::2], np.sin(theta)[1::2]], axis=0)
    high, low = split_table(table)
    table_y = np.concatenate(
        [np.concatenate([high, high], axis=1), np.concatenate([low, np.zeros_like(low)], axis=1)], axis=0
    )
    return table_z, table_y


def inverse_tables(norm):
    theta = angles(np.arange(NY), kept(MY, NY), NY)
    cos_y, sin_y = np.cos(theta), np.sin(theta)
    table_y = np.concatenate([cos_y[:, 0::2], cos_y[:, 1::2], sin_y[:, 0::2], sin_y[:, 1::2]], axis=1)
    y_high, y_low = split_table(table_y)
    theta = angles(np.arange(NZ), np.arange(MZ), NZ)
    weight = np.where(np.arange(MZ) == 0, 1.0, 2.0) * norm
    parts = (np.cos(theta) * weight, -np.sin(theta) * weight)
    own, other = lane_spread(1, 0, *parts).T, lane_spread(0, 1, *parts).T
    tables_z = []
    for mine, theirs in ((own, other), (other, own)):
        high = split_table(mine)[0]
        tables_z.append(np.concatenate([high, high + split_table(theirs)[1]], axis=0))
    return np.concatenate([y_high, y_high, y_low], axis=1), *tables_z


def dot(left, right):
    return jnp.dot(left, right, preferred_element_type=F32)


def split(values):
    high = values.astype(BF16)
    return high, (values - high.astype(F32)).astype(BF16)


def lane_index(shape):
    return lax.broadcasted_iota(jnp.int32, shape, len(shape) - 1)


def roll(values, shift):
    return pltpu.roll(values, shift % LANES, len(values.shape) - 1)


def forward_group(fields, table_z, table_y, out_ref, first, rows):
    left = jnp.concatenate(
        [jnp.concatenate([fields[q], fields[q + 1]], axis=1) for q in range(0, len(fields), 2)], axis=0
    )
    lines = dot(jnp.concatenate(split(left), axis=1), table_z)
    lines = lines[:, :LANES] + lines[:, LANES:]
    half = MY // 2
    for g in range(0, len(fields) // 2, GROUP // 2):
        quad = jnp.concatenate([lines[q * NY : (q + 1) * NY] for q in range(g, g + GROUP // 2)], axis=1)
        wide = dot(table_y, jnp.concatenate(split(quad), axis=0))
        wide = wide[: 2 * MY] + wide[2 * MY :]
        for q in range(GROUP // 2):
            by_cos = wide[:MY, q * LANES : (q + 1) * LANES]
            by_sin = roll(wide[MY:, q * LANES : (q + 1) * LANES], 64)
            modes = by_cos + jnp.where(lane_index(by_sin.shape) < LANES // 2, by_sin, -by_sin)
            even, odd = modes[:half], modes[half:]
            at_even = (lane_index(even.shape) // MZ) % 2 == 0
            at = first + 2 * (g + q)
            out_ref[pl.ds(at, half, stride=rows), :] = jnp.where(at_even, even, roll(odd, MZ))
            out_ref[pl.ds(at + 1, half, stride=rows), :] = jnp.where(at_even, roll(even, -MZ), odd)


def inverse_y_group(modes_ref, y_table, first, rows):
    half = MY // 2
    pairs = []
    for q in range(GROUP // 2):
        c0 = modes_ref[pl.ds(first + 2 * q, half, stride=rows), :]
        c1 = modes_ref[pl.ds(first + 2 * q + 1, half, stride=rows), :]
        at_even = (lane_index(c0.shape) // MZ) % 2 == 0
        even = jnp.where(at_even, c0, roll(c1, MZ))
        odd = jnp.where(at_even, roll(c0, -MZ), c1)
        both = jnp.concatenate([even, odd], axis=0)
        other = roll(both, 64)
        turned = jnp.where(lane_index(both.shape) < LANES // 2, -other, other)
        pairs.append(jnp.concatenate([both, turned], axis=0))
    high, low = split(jnp.concatenate(pairs, axis=1))
    lines = dot(y_table, jnp.concatenate([high, low, high], axis=0))
    return [lines[:, q * LANES : (q + 1) * LANES] for q in range(GROUP // 2)]


def in_hbm(*arrays):
    return [pltpu.with_memory_space_constraint(each, pltpu.HBM) for each in arrays]


def in_vmem(*arrays):
    return [pltpu.with_memory_space_constraint(each, pltpu.VMEM) for each in arrays]


def full(shape):
    return pl.BlockSpec(shape, lambda *_: (0,) * len(shape))


def params(limit):
    return pltpu.CompilerParams(vmem_limit_bytes=limit * MIB)


def fold_block(pieces, out_ref, at):
    copies = pieces.shape[0]
    real, imag = pieces[0, 0], pieces[0, 1]
    for r in range(1, copies):
        real, imag = real + pieces[r, 0], imag + pieces[r, 1]
    modes = real.shape[-1]
    out_ref[at, :, :, :modes] = real
    out_ref[at, :, :, modes:] = imag


def fetches(weights_hbm, ring_ref, sems, at, slot, unique):
    copies = ring_ref.shape[1]
    return [
        pltpu.make_async_copy(weights_hbm.at[c, at + r * unique], ring_ref.at[slot, r, c], sems.at[slot, r, c])
        for r in range(copies)
        for c in range(2)
    ]


def fold_shapes(weights, unique, slots):
    copies = weights.shape[1] // unique
    shape = (unique,) + weights.shape[2:4] + (2 * weights.shape[4],)
    ring = [pltpu.VMEM((slots, copies, 2) + weights.shape[2:], F32), pltpu.SemaphoreType.DMA((slots, copies, 2))]
    return pltpu.HBM(shape, F32), ring


def forward_kernel(
    table_z, table_y, block_ref, field_hbm, weights_hbm, out_ref, folded_hbm,
    field_ref, ring_ref, folded_ref, field_sems, sems, folded_sems, *, channels, step_channels, unique, slots,
):
    steps = channels // step_channels
    per_step = slots // (steps - 1)
    fields = [
        pltpu.make_async_copy(
            field_hbm.at[pl.ds(s * step_channels, step_channels)],
            field_ref.at[pl.ds((s - 1) * step_channels, step_channels)],
            field_sems.at[s - 1],
        )
        for s in range(1, steps)
    ]
    weights = [fetches(weights_hbm, ring_ref, sems, at, at, unique) for at in range(slots)]
    stores = [pltpu.make_async_copy(folded_ref.at[at], folded_hbm.at[at], folded_sems.at[at]) for at in range(slots)]
    for copy in fields:
        copy.start()
    for each in weights:
        for copy in each:
            copy.start()
    for s in range(steps):
        if s > 0:
            fields[s - 1].wait()
            for at in range((s - 1) * per_step, s * per_step):
                for copy in weights[at]:
                    copy.wait()
                fold_block(ring_ref.at[at], folded_ref, at)
        base = (s - 1) * step_channels
        part = [block_ref[q] if s == 0 else field_ref[base + q] for q in range(step_channels)]
        forward_group(part, table_z[...], table_y[...], out_ref, s * step_channels, channels)
        if s > 0:
            for at in range((s - 1) * per_step, s * per_step):
                stores[at].start()
    for copy in stores:
        copy.wait()


FOLD_STEP = 2
FIELD_STEP = 8


def folded_early(channels):
    return (channels // FIELD_STEP - 1) * FOLD_STEP


def forward_modes(field, tables, weights, unique):
    channels = field.shape[0]
    slots = folded_early(channels)
    folded_shape, ring = fold_shapes(weights, unique, slots)
    owners = MY // 2
    anywhere = pl.BlockSpec(memory_space=pl.ANY)
    out, some = pl.pallas_call(
        functools.partial(forward_kernel, channels=channels, step_channels=FIELD_STEP, unique=unique, slots=slots),
        grid=(1,),
        in_specs=[full(t.shape) for t in tables]
        + [pl.BlockSpec((FIELD_STEP, NY, NZ), lambda s: (0, 0, 0)), anywhere, anywhere],
        out_specs=[full((owners * channels, LANES)), anywhere],
        out_shape=[pltpu.VMEM((owners * channels, LANES), F32), folded_shape],
        scratch_shapes=[
            pltpu.VMEM((channels - FIELD_STEP, NY, NZ), F32),
            ring[0],
            pltpu.VMEM((slots,) + folded_shape.shape[1:], F32),
            pltpu.SemaphoreType.DMA((channels // FIELD_STEP - 1,)),
            ring[1],
            pltpu.SemaphoreType.DMA((slots,)),
        ],
        compiler_params=params(LIMIT),
        cost_estimate=pl.CostEstimate(flops=2 * 10**9, bytes_accessed=22 * MIB, transcendentals=0),
        name="forward_yz",
    )(*in_hbm(*tables, field, field, weights))
    return out.reshape(owners, channels, LANES), some


def fold_kernel(weights_hbm, _, out_ref, ring_ref, sems, *, first, unique, slots):
    step = pl.program_id(0)
    slot = step % slots

    @pl.when(step == 0)
    def _():
        for ahead in range(slots):
            for copy in fetches(weights_hbm, ring_ref, sems, first + ahead, ahead, unique):
                copy.start()

    for copy in fetches(weights_hbm, ring_ref, sems, first + step, slot, unique):
        copy.wait()
    fold_block(ring_ref.at[slot], out_ref, 0)

    @pl.when(step + slots < pl.num_programs(0))
    def _():
        for copy in fetches(weights_hbm, ring_ref, sems, first + step + slots, slot, unique):
            copy.start()


def fold_rest(weights, some, unique):
    first = folded_early(weights.shape[2])
    slots = min(4, unique - first)
    folded_shape, ring = fold_shapes(weights, unique, slots)
    anywhere = pl.BlockSpec(memory_space=pl.ANY)
    return pl.pallas_call(
        functools.partial(fold_kernel, first=first, unique=unique, slots=slots),
        grid=(unique - first,),
        in_specs=[anywhere, anywhere],
        out_specs=pl.BlockSpec((1,) + folded_shape.shape[1:], lambda s: (first + s, 0, 0, 0)),
        out_shape=folded_shape,
        scratch_shapes=ring,
        input_output_aliases={1: 0},
        compiler_params=params(LIMIT),
        cost_estimate=pl.CostEstimate(flops=4 * 10**6, bytes_accessed=25 * MIB, transcendentals=0),
        name="fold_weights",
    )(*in_hbm(weights, some))


def halve_lines(lines_ref, sums_ref, points, channels):
    half = points // 2
    sign = jnp.where(lane_index((channels, LANES)) < LANES // 2, 1.0, -1.0)
    for x in range(half):
        near, far = lines_ref[x, :channels], lines_ref[x + half, :channels]
        for parity, value in enumerate((near + far, near - far)):
            sums_ref[parity, 0, x] = value
            sums_ref[parity, 1, x] = sign * roll(value, 64)


def spectrum_row(cos_ref, sin_ref, sums_ref, at, parity, half):
    total = cos_ref[at, 0] * sums_ref[parity, 0, 0] + sin_ref[at, 0] * sums_ref[parity, 1, 0]
    for x in range(1, half):
        total += cos_ref[at, x] * sums_ref[parity, 0, x] + sin_ref[at, x] * sums_ref[parity, 1, x]
    return total


def doubled(values):
    other = roll(values, 64)
    low = lane_index(values.shape) < LANES // 2
    return jnp.where(low, values, other), jnp.where(low, other, values)


def mix_kernel(
    cos_ref, sin_ref, lines_ref, weights_ref, spec_ref, out_ref, sums_ref, total_ref, real_ref, imag_ref,
    *, points, channels, per_step, norm,
):
    step = pl.program_id(0)
    half = points // 2

    @pl.when(step == 0)
    def _():
        halve_lines(lines_ref, sums_ref, points, channels)
        total_ref[...] = jnp.zeros_like(total_ref)

    low = lane_index((channels, LANES)) < LANES // 2
    for q in range(per_step):
        at = step * per_step + q
        parity = q % 2
        spec = norm * spectrum_row(cos_ref, sin_ref, sums_ref, at, parity, half)
        spec_ref[q] = spec
        real_ref[q], imag_ref[q] = doubled(spec)
        by_real = jnp.zeros((channels, LANES), F32)
        by_imag = jnp.zeros((channels, LANES), F32)
        for i in range(channels):
            weight = weights_ref[q, i]
            by_real += real_ref[q, pl.ds(i, 1), :] * weight
            by_imag += imag_ref[q, pl.ds(i, 1), :] * weight
        other = roll(by_imag, 64)
        mixed = by_real + jnp.where(low, -other, other)
        other = roll(mixed, 64)
        turned = jnp.where(low, -other, other)
        for x in range(half):
            total_ref[parity, x] += cos_ref[at, x] * mixed + sin_ref[at, x] * turned

    @pl.when(step == pl.num_programs(0) - 1)
    def _():
        for x in range(half):
            out_ref[x] = total_ref[0, x] + total_ref[1, x]
            out_ref[x + half] = total_ref[0, x] - total_ref[1, x]


def smem():
    return pl.BlockSpec(memory_space=pltpu.SMEM)


def mix(cos_x, sin_x, lines, weights, norm):
    points, channels, _ = lines.shape
    unique = weights.shape[0]
    per_step = min(unique, 4)
    shape = (points, channels, LANES)
    return pl.pallas_call(
        functools.partial(mix_kernel, points=points, channels=channels, per_step=per_step, norm=norm),
        grid=(unique // per_step,),
        in_specs=[
            smem(),
            smem(),
            full(shape),
            pl.BlockSpec((per_step,) + weights.shape[1:], lambda s: (s, 0, 0, 0)),
        ],
        out_specs=[
            pl.BlockSpec((per_step, channels, LANES), lambda s: (s, 0, 0)),
            full(shape),
        ],
        out_shape=[
            pltpu.VMEM((unique, channels, LANES), F32),
            pltpu.VMEM(shape, F32),
        ],
        scratch_shapes=[
            pltpu.VMEM((2, 2, points // 2, channels, LANES), F32),
            pltpu.VMEM((2, points // 2, channels, LANES), F32),
            pltpu.VMEM((per_step, channels, LANES), F32),
            pltpu.VMEM((per_step, channels, LANES), F32),
        ],
        compiler_params=params(LIMIT),
        cost_estimate=pl.CostEstimate(flops=2 * 10**7, bytes_accessed=9 * MIB, transcendentals=0),
        name="mix_modes",
    )(cos_x, sin_x, *in_vmem(lines), *in_hbm(weights))


def exact_dot(left, right):
    return jnp.dot(left, right, precision=lax.Precision.HIGHEST, preferred_element_type=F32)


def pointwise_kernel(sum_ref, turned_ref, bias_in_ref, field_ref, out_ref, mixer_ref, bias_ref, *, channels, blocks):
    size = 8 * channels

    @pl.when(pl.program_id(0) == 0)
    def _():
        wide = exact_dot(sum_ref[...], turned_ref[...])
        wide = lax.dot_general(
            wide, sum_ref[...], (((1,), (1,)), ((), ())), precision=lax.Precision.HIGHEST, preferred_element_type=F32
        )
        row = lax.broadcasted_iota(jnp.int32, (size, size), 0) % 8
        high, low = split(jnp.where(row == lane_index((size, size)) % 8, wide, 0.0))
        mixer_ref[:size] = high
        mixer_ref[size:] = low
        bias_ref[...] = exact_dot(sum_ref[...], bias_in_ref[...])

    for b in range(blocks):
        high, low = split(field_ref[:, 8 * b : 8 * b + 8, :].reshape(size, NZ))
        wide = dot(mixer_ref[...], high)
        values = wide[:size] + wide[size:] + dot(mixer_ref[:size], low) + bias_ref[...]
        out_ref[:, 8 * b : 8 * b + 8, :] = values.reshape(channels, 8, NZ)


def pointwise(field, summing, point_weights, point_bias):
    channels = field.shape[0]
    blocks = 2
    turned = point_weights.T
    bias = point_bias[:, None]
    size = 8 * channels
    block = pl.BlockSpec((channels, 8 * blocks, NZ), lambda s: (0, s, 0))
    return pl.pallas_call(
        functools.partial(pointwise_kernel, channels=channels, blocks=blocks),
        grid=(NY // (8 * blocks),),
        in_specs=[full(summing.shape), full(turned.shape), full(bias.shape), block],
        out_specs=block,
        out_shape=pltpu.HBM(field.shape, F32),
        scratch_shapes=[pltpu.VMEM((2 * size, size), BF16), pltpu.VMEM((size, 1), F32)],
        compiler_params=params(LIMIT),
        cost_estimate=pl.CostEstimate(flops=4 * 10**9, bytes_accessed=24 * MIB, transcendentals=0),
        name="pointwise",
    )(*in_hbm(summing, turned, bias, field))


def cell_group(inv_y, inv_z, modes_ref, pre_ref, cot_ref, act_ref, first, count, channels):
    lines = []
    for g in range(0, count, GROUP):
        lines += inverse_y_group(modes_ref, inv_y, first + g, channels)
    lines = jnp.concatenate(lines, axis=0)
    high = lines.astype(BF16).astype(F32)
    low = lines - high
    at_even = (lane_index(lines.shape) // MZ) % 2 == 0
    spectral = [
        dot(jnp.concatenate([high, side], axis=1).astype(BF16), table)
        for side, table in zip((jnp.where(at_even, low, roll(high, MZ)), jnp.where(at_even, roll(high, -MZ), low)), inv_z)
    ]
    slopes = []
    for q in range(count):
        before = spectral[q % 2][q // 2 * NY : (q // 2 + 1) * NY] + pre_ref[q]
        cdf = 0.5 + 0.5 * lax.erf(before * INV_SQRT_TWO)
        act_ref[q] = (before * cdf).astype(BF16)
        pdf = jnp.exp(-0.5 * before * before) * INV_SQRT_TWO_PI
        slopes.append(cot_ref[q].astype(F32) * (cdf + before * pdf))
    return slopes


def early_cell_kernel(
    inv_y, inv_z0, inv_z1, table_z, table_y, modes_ref, pre_ref, cot_ref, act_ref, slope_ref, out_ref,
    *, channels, count, rows,
):
    step = pl.program_id(0)
    slopes = cell_group(
        inv_y[...], (inv_z0[...], inv_z1[...]), modes_ref, pre_ref, cot_ref, act_ref, step * count, count, channels
    )
    for q in range(count):
        slope_ref[q] = slopes[q]
    forward_group(slopes, table_z[...], table_y[...], out_ref, step * count, rows)


def point_gradient(field_ref, slope_ref, sum_ref, channels):
    size = 8 * channels
    total = jnp.zeros((size, size), F32)
    for b in range(NY // 8):
        at = slice(8 * b, 8 * b + 8)
        f_h, f_l = split(field_ref[:, at, :].reshape(size, NZ))
        s_h, s_l = split(slope_ref[:, at, :].reshape(size, NZ))
        total += lax.dot_general(
            jnp.concatenate([f_h, f_h, f_l], axis=1),
            jnp.concatenate([s_h, s_l, s_h], axis=1),
            (((1,), (1,)), ((), ())),
            preferred_element_type=F32,
        )
    row = lax.broadcasted_iota(jnp.int32, (size, size), 0) % 8
    total = jnp.where(row == lane_index((size, size)) % 8, total, 0.0)
    return exact_dot(jnp.sum(total.reshape(channels, 8, size), axis=1), sum_ref[...])


def late_cell_kernel(
    inv_y, inv_z0, inv_z1, table_z, table_y, sum_ref, modes_ref, pre_ref, cot_ref, early_ref,
    slope_hbm, field_hbm, _, act_ref, out_ref, field_ref, slope_ref, sems, *, channels, count, rows, owners,
):
    step = pl.program_id(0)
    early = early_count(channels)
    late = channels - early
    copies = [
        pltpu.make_async_copy(field_hbm, field_ref, sems.at[0]),
        pltpu.make_async_copy(slope_hbm, slope_ref.at[pl.ds(0, early)], sems.at[1]),
    ]

    @pl.when(step == 0)
    def _():
        for copy in copies:
            copy.start()

    first = early + step * count
    slopes = cell_group(
        inv_y[...], (inv_z0[...], inv_z1[...]), modes_ref, pre_ref, cot_ref, act_ref, first, count, channels
    )
    for q in range(count):
        slope_ref[first + q] = slopes[q]
    forward_group(slopes, table_z[...], table_y[...], out_ref, step * count, rows)

    @pl.when(step == pl.num_programs(0) - 1)
    def _():
        for copy in copies:
            copy.wait()
        point = point_gradient(field_ref, slope_ref, sum_ref, channels)
        packed = jnp.concatenate([point[8 * q : 8 * q + 8] for q in range(channels // 8)], axis=1)
        zero_mode = jnp.concatenate([early_ref[0:early, 0:1], out_ref[0:late, 0:1]], axis=0)
        eye = lax.broadcasted_iota(jnp.int32, (channels, LANES), 0) == lane_index((channels, LANES))
        bias = jnp.sum(jnp.where(eye, jnp.broadcast_to(zero_mode, (channels, LANES)), 0.0), axis=0, keepdims=True)
        extra = jnp.where(lax.broadcasted_iota(jnp.int32, (8, LANES), 0) == 0, jnp.broadcast_to(bias, (8, LANES)), 0.0)
        for d in range(owners):
            out_ref[d * rows + late : d * rows + late + 8, :] = packed
            out_ref[d * rows + late + 8 : (d + 1) * rows, :] = extra


def early_count(channels):
    return channels * 3 // 4


def early_cells(inverse, forward, modes, pre, cotangent):
    channels = pre.shape[0]
    owners = MY // 2
    early = early_count(channels)
    block = pl.BlockSpec((STEP, NY, NZ), lambda s: (s, 0, 0))
    tables = (*inverse, *forward)
    act, slope, out = pl.pallas_call(
        functools.partial(early_cell_kernel, channels=channels, count=STEP, rows=early),
        grid=(early // STEP,),
        in_specs=[full(t.shape) for t in tables] + [full((owners * channels, LANES)), block, block],
        out_specs=[block, block, full((owners * early, LANES))],
        out_shape=[
            pltpu.HBM((channels, NY, NZ), BF16),
            pltpu.HBM((early, NY, NZ), F32),
            pltpu.VMEM((owners * early, LANES), F32),
        ],
        compiler_params=params(LIMIT),
        cost_estimate=pl.CostEstimate(flops=3 * 10**9, bytes_accessed=7 * MIB, transcendentals=10**6),
        name="early_cells",
    )(*in_hbm(*tables), *in_vmem(modes.reshape(owners * channels, LANES)), *in_hbm(pre, cotangent))
    return act, slope, out.reshape(owners, early, LANES)


def late_cells(inverse, forward, summing, modes, pre, cotangent, field, early, slope, act):
    channels = field.shape[0]
    owners = MY // 2
    first = early_count(channels)
    rows = channels - first + 16
    start = first // STEP
    block = pl.BlockSpec((STEP, NY, NZ), lambda s: (start + s, 0, 0))
    anywhere = pl.BlockSpec(memory_space=pl.ANY)
    tables = (*inverse, *forward, summing)
    act, out = pl.pallas_call(
        functools.partial(late_cell_kernel, channels=channels, count=STEP, rows=rows, owners=owners),
        grid=((channels - first) // STEP,),
        in_specs=[full(t.shape) for t in tables]
        + [full((owners * channels, LANES)), block, block, full((owners * first, LANES))]
        + [anywhere] * 3,
        out_specs=[block, full((owners * rows, LANES))],
        out_shape=[
            pltpu.HBM((channels, NY, NZ), BF16),
            pltpu.VMEM((owners * rows, LANES), F32),
        ],
        scratch_shapes=[
            pltpu.VMEM((channels, NY, NZ), F32),
            pltpu.VMEM((channels, NY, NZ), F32),
            pltpu.SemaphoreType.DMA((2,)),
        ],
        input_output_aliases={len(tables) + 6: 0},
        compiler_params=params(LIMIT),
        cost_estimate=pl.CostEstimate(flops=6 * 10**9, bytes_accessed=11 * MIB, transcendentals=10**6),
        name="late_cells",
    )(
        *in_hbm(*tables),
        *in_vmem(modes.reshape(owners * channels, LANES)),
        *in_hbm(pre, cotangent),
        *in_vmem(early.reshape(owners * first, LANES)),
        *in_hbm(slope, field, act),
    )
    return act, out.reshape(owners, rows, LANES)


def gradient_kernel(cos_ref, sin_ref, spec_ref, lines_ref, *refs, points, channels, unique, copies, norm, first, outputs, slots):
    last = first > 0
    if last:
        _, out_hbm, point_ref, bias_ref, sums_ref, real_ref, imag_ref, buffer, sems = refs
    else:
        out_hbm, sums_ref, real_ref, imag_ref, buffer, sems = refs
    halve_lines(lines_ref, sums_ref, points, outputs)
    half = LANES // 2
    lane = lane_index((outputs, LANES))
    scale = jnp.where(lane % MZ == 0, norm, 2.0 * norm)

    def writes(at, slot):
        return [
            pltpu.make_async_copy(
                buffer.at[slot, c],
                out_hbm.at[c, at + r * unique, :, pl.ds(first, outputs), :],
                sems.at[slot, c, r],
            )
            for r in range(copies)
            for c in range(2)
        ]

    @pl.loop(0, unique // slots)
    def _(turn):
        for slot in range(slots):
            at = slots * turn + slot

            @pl.when(turn > 0)
            def _():
                for copy in writes(at - slots, slot):
                    copy.wait()

            slope = scale * spectrum_row(cos_ref, sin_ref, sums_ref, at, slot % 2, points // 2)
            other = roll(slope, 64)
            flipped = jnp.where(lane < half, other, -other)
            real_ref[slot], imag_ref[slot] = doubled(spec_ref[at])
            for i in range(channels):
                both = real_ref[slot, pl.ds(i, 1), :] * slope + imag_ref[slot, pl.ds(i, 1), :] * flipped
                buffer[slot, 0, i] = both[:, :half]
                buffer[slot, 1, i] = both[:, half:]
            for copy in writes(at, slot):
                copy.start()

    if last:
        packed = lines_ref[0, outputs : outputs + 16, :]
        for x in range(1, points):
            packed += lines_ref[x, outputs : outputs + 16, :]
        packed = norm * packed
        for q in range(channels // 8):
            point_ref[8 * q : 8 * q + 8, :] = packed[:8, q * channels : (q + 1) * channels]
        bias_ref[...] = packed[8:9, :channels]

    for at in range(unique - slots, unique):
        for copy in writes(at, at % slots):
            copy.wait()


def gradient(cos_x, sin_x, spectrum, lines, norm, kept_x, before=()):
    points, rows, _ = lines.shape
    unique, channels, _ = spectrum.shape
    half = LANES // 2
    copies = kept_x // unique
    first = early_count(channels) if before else 0
    outputs = channels - first if before else early_count(channels)
    slots = 8 if before else 4
    anywhere = pl.BlockSpec(memory_space=pl.ANY)
    shape = jax.ShapeDtypeStruct((2, kept_x, channels, channels, half), F32)
    sums = [(channels, channels), (1, channels)] if before else []
    return pl.pallas_call(
        functools.partial(
            gradient_kernel, points=points, channels=channels, unique=unique, copies=copies, norm=norm,
            first=first, outputs=outputs, slots=slots,
        ),
        in_specs=[smem(), smem(), full(spectrum.shape), full(lines.shape)] + [anywhere] * len(before),
        out_specs=[anywhere] + [full(each) for each in sums],
        out_shape=[shape] + [jax.ShapeDtypeStruct(each, F32) for each in sums],
        scratch_shapes=[
            pltpu.VMEM((2, 2, points // 2, outputs, LANES), F32),
            pltpu.VMEM((slots, channels, LANES), F32),
            pltpu.VMEM((slots, channels, LANES), F32),
            pltpu.VMEM((slots, 2, channels, outputs, half), F32),
            pltpu.SemaphoreType.DMA((slots, 2, copies)),
        ],
        input_output_aliases={4: 0} if before else {},
        compiler_params=params(LIMIT),
        cost_estimate=pl.CostEstimate(flops=5 * 10**6, bytes_accessed=32 * MIB, transcendentals=0),
        name="weight_gradient",
    )(cos_x, sin_x, *in_vmem(spectrum, lines), *before)


def swap(lines):
    return lax.all_to_all(lines, "space", split_axis=0, concat_axis=0, tiled=True)


def suits(width_x, length_x, devices, channels, weights):
    held = weights.shape[2]
    even = np.array_equal(kept(MX, length_x) % length_x, np.arange(MX) % length_x)
    return (
        width_x == 1
        and held == 2 * MZ
        and devices * 2 == MY
        and 2 * held == LANES
        and MX % length_x == 0
        and length_x % 8 == 0
        and even
        and channels == MZ
    )


def body(lifted_field, cotangent, spectral_weights, point_weights, point_bias):
    devices = lax.axis_size("space")
    channels, width_x = lifted_field.shape[:2]
    length_x = width_x * devices
    if not suits(width_x, length_x, devices, channels, spectral_weights):
        return general_body(lifted_field, cotangent, spectral_weights, point_weights, point_bias)
    norm = float(length_x * NY * NZ) ** -0.5
    theta = angles(np.arange(length_x), np.arange(length_x), length_x)
    cos_x, sin_x = jnp.asarray(np.cos(theta), F32), jnp.asarray(np.sin(theta), F32)
    forward = forward_tables()
    inverse = inverse_tables(norm)
    summing = jnp.asarray(np.repeat(np.eye(channels), 8, axis=0), F32)

    field = lifted_field.reshape(channels, NY, NZ)
    slopes_in = cotangent.reshape(channels, NY, NZ)
    weights = jnp.transpose(spectral_weights, (0, 1, 3, 4, 2))

    lines, some = forward_modes(field, forward, weights, length_x)
    lines = swap(lines)
    folded = fold_rest(weights, some, length_x)
    spectrum, mixed = mix(cos_x, sin_x, lines, folded, norm)
    field_late, mixed = lax.optimization_barrier((field, mixed))
    modes = swap(mixed)
    pre = pointwise(field_late, summing, point_weights, point_bias)
    act, slope, early = early_cells(inverse, forward, modes, pre, slopes_in)
    early_lines = swap(early)
    activated, late = late_cells(inverse, forward, summing, modes, pre, slopes_in, field, early, slope, act)
    late_lines = swap(late)
    (grad,) = gradient(cos_x, sin_x, spectrum, early_lines, norm, MX)
    grad, grad_point, grad_bias = gradient(cos_x, sin_x, spectrum, late_lines, norm, MX, (grad,))
    return (
        activated.reshape(cotangent.shape),
        jnp.transpose(grad, (0, 1, 4, 2, 3)),
        grad_point,
        grad_bias.reshape(channels),
    )


HIGHEST = lax.Precision.HIGHEST


def trig_tables(positions, frequency, length):
    product = positions[:, None] * frequency[None, :] % length
    phase_angle = 2.0 * jnp.pi / length * product.astype(jnp.float32)
    return (jnp.cos(phase_angle), jnp.sin(phase_angle))


def kept_frequencies(kept_count, length):
    mode_index = jnp.arange(kept_count, dtype=jnp.int32)
    return jnp.where(mode_index < kept_count // 2, mode_index, length - kept_count + mode_index)


def forward_local(field_in):
    channels = field_in.shape[0]
    width_x = field_in.shape[1]
    cos_z, sin_z = trig_tables(jnp.arange(NZ, dtype=jnp.int32), jnp.arange(MZ, dtype=jnp.int32), NZ)
    table_z = jnp.concatenate([cos_z, -sin_z], axis=1)
    along_z = jnp.einsum("cxyz,zk->cxyk", field_in, table_z, precision=HIGHEST)
    z_real = along_z[..., :MZ]
    z_imag = along_z[..., MZ:]
    cos_y, sin_y = trig_tables(jnp.arange(NY, dtype=jnp.int32), kept_frequencies(MY, NY), NY)
    y_real = jnp.einsum("cxyk,yj->xcjk", z_real, cos_y, precision=HIGHEST) + jnp.einsum(
        "cxyk,yj->xcjk", z_imag, sin_y, precision=HIGHEST
    )
    y_imag = jnp.einsum("cxyk,yj->xcjk", z_imag, cos_y, precision=HIGHEST) - jnp.einsum(
        "cxyk,yj->xcjk", z_real, sin_y, precision=HIGHEST
    )
    stacked = jnp.stack([y_real, y_imag], axis=1)
    return stacked.reshape(width_x, 2, channels, MY * MZ)


def transform_x(x_lines):
    length_x = x_lines.shape[0]
    cos_x, sin_x = trig_tables(
        jnp.arange(length_x, dtype=jnp.int32), kept_frequencies(MX, length_x), length_x
    )
    norm_scale = 1.0 / float(length_x * NY * NZ) ** 0.5
    part_real = x_lines[:, 0]
    part_imag = x_lines[:, 1]
    x_real = jnp.einsum("xcm,xk->kcm", part_real, cos_x, precision=HIGHEST) + jnp.einsum(
        "xcm,xk->kcm", part_imag, sin_x, precision=HIGHEST
    )
    x_imag = jnp.einsum("xcm,xk->kcm", part_imag, cos_x, precision=HIGHEST) - jnp.einsum(
        "xcm,xk->kcm", part_real, sin_x, precision=HIGHEST
    )
    return norm_scale * jnp.stack([x_real, x_imag], axis=1)


def mix_modes(spectrum, weights):
    spec_real = spectrum[:, 0]
    spec_imag = spectrum[:, 1]
    out_real = jnp.einsum("kim,kmio->kom", spec_real, weights[0], precision=HIGHEST) - jnp.einsum(
        "kim,kmio->kom", spec_imag, weights[1], precision=HIGHEST
    )
    out_imag = jnp.einsum("kim,kmio->kom", spec_real, weights[1], precision=HIGHEST) + jnp.einsum(
        "kim,kmio->kom", spec_imag, weights[0], precision=HIGHEST
    )
    return jnp.stack([out_real, out_imag], axis=1)


def inverse_x(spectrum, positions, length_x):
    cos_x, sin_x = trig_tables(positions, kept_frequencies(MX, length_x), length_x)
    spec_real = spectrum[:, 0]
    spec_imag = spectrum[:, 1]
    a_real = jnp.einsum("kcm,xk->xcm", spec_real, cos_x, precision=HIGHEST) - jnp.einsum(
        "kcm,xk->xcm", spec_imag, sin_x, precision=HIGHEST
    )
    a_imag = jnp.einsum("kcm,xk->xcm", spec_imag, cos_x, precision=HIGHEST) + jnp.einsum(
        "kcm,xk->xcm", spec_real, sin_x, precision=HIGHEST
    )
    return jnp.stack([a_real, a_imag], axis=1)


def inverse_yz(x_lines, length_x):
    width_x = x_lines.shape[0]
    channels = x_lines.shape[2]
    mode_grid = x_lines.reshape(width_x, 2, channels, MY, MZ)
    cos_y, sin_y = trig_tables(jnp.arange(NY, dtype=jnp.int32), kept_frequencies(MY, NY), NY)
    b_real = jnp.einsum("xcjk,yj->cxyk", mode_grid[:, 0], cos_y, precision=HIGHEST) - jnp.einsum(
        "xcjk,yj->cxyk", mode_grid[:, 1], sin_y, precision=HIGHEST
    )
    b_imag = jnp.einsum("xcjk,yj->cxyk", mode_grid[:, 1], cos_y, precision=HIGHEST) + jnp.einsum(
        "xcjk,yj->cxyk", mode_grid[:, 0], sin_y, precision=HIGHEST
    )
    cos_z, sin_z = trig_tables(jnp.arange(NZ, dtype=jnp.int32), jnp.arange(MZ, dtype=jnp.int32), NZ)
    weight_z = jnp.where(jnp.arange(MZ, dtype=jnp.int32) == 0, 1.0, 2.0).astype(jnp.float32)
    table_z = jnp.concatenate([cos_z * weight_z[None, :], -sin_z * weight_z[None, :]], axis=1)
    stacked = jnp.concatenate([b_real, b_imag], axis=-1)
    result = jnp.einsum("cxyk,zk->cxyz", stacked, table_z, precision=HIGHEST)
    return result * (1.0 / float(length_x * NY * NZ) ** 0.5)


def gelu_slope(values):
    return (
        0.5 * (1.0 + lax.erf(values * INV_SQRT_TWO))
        + values * jnp.exp(-0.5 * values * values) * INV_SQRT_TWO_PI
    )


def weight_gradient(spectrum, slope_modes, first_mode):
    mode_ids = first_mode + jnp.arange(spectrum.shape[3], dtype=jnp.int32)
    weight_modes = jnp.where(mode_ids % MZ == 0, 1.0, 2.0).astype(jnp.float32)
    grad_real = jnp.einsum(
        "kim,kom->kmio", spectrum[:, 0], slope_modes[:, 0], precision=HIGHEST
    ) + jnp.einsum("kim,kom->kmio", spectrum[:, 1], slope_modes[:, 1], precision=HIGHEST)
    grad_imag = jnp.einsum(
        "kim,kom->kmio", spectrum[:, 0], slope_modes[:, 1], precision=HIGHEST
    ) - jnp.einsum("kim,kom->kmio", spectrum[:, 1], slope_modes[:, 0], precision=HIGHEST)
    stacked = jnp.stack([grad_real, grad_imag], axis=0)
    return stacked * weight_modes[None, None, :, None, None]


def to_modes(field_in):
    return transform_x(
        lax.all_to_all(forward_local(field_in), "space", split_axis=3, concat_axis=0, tiled=True)
    )


def general_body(lifted_field, cotangent, spectral_weights, point_weights, point_bias):
    devices = lax.axis_size("space")
    width_x = lifted_field.shape[1]
    length_x = width_x * devices
    spectrum = to_modes(lifted_field)
    mixed_modes = mix_modes(spectrum, spectral_weights)
    full_lines = inverse_x(mixed_modes, jnp.arange(length_x, dtype=jnp.int32), length_x)
    spectral = inverse_yz(
        lax.all_to_all(full_lines, "space", split_axis=0, concat_axis=3, tiled=True), length_x
    )
    pointwise = (
        jnp.einsum("ixyz,io->oxyz", lifted_field, point_weights, precision=HIGHEST)
        + point_bias[:, None, None, None]
    )
    before = spectral + pointwise
    activated = jax.nn.gelu(before, approximate=False).astype(jnp.bfloat16)
    slope_field = cotangent.astype(jnp.float32) * gelu_slope(before)
    local_point = jnp.einsum("ixyz,oxyz->io", lifted_field, slope_field, precision=HIGHEST)
    local_bias = jnp.sum(slope_field, axis=(1, 2, 3))
    partial = jnp.concatenate([local_point, local_bias[None, :]], axis=0)
    gathered = lax.all_gather(partial, "space", axis=0, tiled=False)
    summed = jnp.sum(gathered, axis=0)
    summed_point, summed_bias = summed[:-1], summed[-1]
    root_cells = float(length_x * NY * NZ) ** 0.5
    slope_spectrum = to_modes(slope_field)
    first_mode = lax.axis_index("space") * spectrum.shape[3]
    grad_spectral = weight_gradient(spectrum, slope_spectrum, first_mode)
    return (activated, grad_spectral, summed_point / root_cells, summed_bias / root_cells)


def solution(mesh):
    placed = (
        P("groups", "space", None, None),
        P("groups", "space", None, None),
        P(None, None, "space", None, None),
        P(),
        P(),
    )
    return jax.shard_map(
        body,
        mesh=mesh,
        in_specs=placed,
        out_specs=(
            P("groups", "space", None, None),
            P("groups", None, "space", None, None),
            P("groups", None),
            P("groups"),
        ),
        check_vma=False,
    )
```

```python
import functools

import jax
import jax.numpy as jnp
import ml_dtypes
import numpy as np
from jax import lax
from jax.experimental import pallas as pl
from jax.experimental.pallas import tpu as pltpu
from jax.sharding import PartitionSpec as P

MX = 32
MY = 32
MZ = 32
NY = 128
NZ = 256

F32 = jnp.float32
BF16 = jnp.bfloat16
INV_SQRT_TWO = 0.7071067811865476
INV_SQRT_TWO_PI = 0.3989422804014327
MIB = 1 << 20
LIMIT = 48
LANES = 128
GROUP = 4
STEP = 8


def kept(kept_count, length):
    index = np.arange(kept_count)
    return np.where(index < kept_count // 2, index, length - kept_count + index)


def angles(positions, frequency, length):
    product = positions[:, None] * frequency[None, :] % length
    return 2.0 * np.pi / length * product


def split_table(table):
    high = table.astype(ml_dtypes.bfloat16)
    return high, (table - high.astype(np.float64)).astype(ml_dtypes.bfloat16)


def lane_spread(first, second, real_table, imag_table):
    return np.concatenate(
        [real_table * first, real_table * second, imag_table * first, imag_table * second], axis=1
    )


def forward_tables():
    theta = angles(np.arange(NZ), np.arange(MZ), NZ)
    table = np.concatenate([lane_spread(f, s, np.cos(theta), -np.sin(theta)) for f, s in ((1, 0), (0, 1))], axis=0)
    high, low = split_table(table)
    table_z = np.concatenate(
        [np.concatenate([high, low], axis=1), np.concatenate([high, np.zeros_like(low)], axis=1)], axis=0
    )
    theta = angles(np.arange(NY), kept(MY, NY), NY).T
    table = np.concatenate([np.cos(theta)[0::2], np.cos(theta)[1::2], np.sin(theta)[0::2], np.sin(theta)[1::2]], axis=0)
    high, low = split_table(table)
    table_y = np.concatenate(
        [np.concatenate([high, high], axis=1), np.concatenate([low, np.zeros_like(low)], axis=1)], axis=0
    )
    return table_z, table_y


def inverse_tables(norm):
    theta = angles(np.arange(NY), kept(MY, NY), NY)
    cos_y, sin_y = np.cos(theta), np.sin(theta)
    table_y = np.concatenate([cos_y[:, 0::2], cos_y[:, 1::2], sin_y[:, 0::2], sin_y[:, 1::2]], axis=1)
    y_high, y_low = split_table(table_y)
    theta = angles(np.arange(NZ), np.arange(MZ), NZ)
    weight = np.where(np.arange(MZ) == 0, 1.0, 2.0) * norm
    parts = (np.cos(theta) * weight, -np.sin(theta) * weight)
    own, other = lane_spread(1, 0, *parts).T, lane_spread(0, 1, *parts).T
    tables_z = []
    for mine, theirs in ((own, other), (other, own)):
        high = split_table(mine)[0]
        tables_z.append(np.concatenate([high, high + split_table(theirs)[1]], axis=0))
    return np.concatenate([y_high, y_high, y_low], axis=1), *tables_z


def dot(left, right):
    return jnp.dot(left, right, preferred_element_type=F32)


def split(values):
    high = values.astype(BF16)
    return high, (values - high.astype(F32)).astype(BF16)


def lane_index(shape):
    return lax.broadcasted_iota(jnp.int32, shape, len(shape) - 1)


def roll(values, shift):
    return pltpu.roll(values, shift % LANES, len(values.shape) - 1)


def forward_group(fields, table_z, table_y, out_ref, first, rows):
    left = jnp.concatenate(
        [jnp.concatenate([fields[q], fields[q + 1]], axis=1) for q in range(0, len(fields), 2)], axis=0
    )
    lines = dot(jnp.concatenate(split(left), axis=1), table_z)
    lines = lines[:, :LANES] + lines[:, LANES:]
    half = MY // 2
    for g in range(0, len(fields) // 2, GROUP // 2):
        quad = jnp.concatenate([lines[q * NY : (q + 1) * NY] for q in range(g, g + GROUP // 2)], axis=1)
        wide = dot(table_y, jnp.concatenate(split(quad), axis=0))
        wide = wide[: 2 * MY] + wide[2 * MY :]
        for q in range(GROUP // 2):
            by_cos = wide[:MY, q * LANES : (q + 1) * LANES]
            by_sin = roll(wide[MY:, q * LANES : (q + 1) * LANES], 64)
            modes = by_cos + jnp.where(lane_index(by_sin.shape) < LANES // 2, by_sin, -by_sin)
            even, odd = modes[:half], modes[half:]
            at_even = (lane_index(even.shape) // MZ) % 2 == 0
            at = first + 2 * (g + q)
            out_ref[pl.ds(at, half, stride=rows), :] = jnp.where(at_even, even, roll(odd, MZ))
            out_ref[pl.ds(at + 1, half, stride=rows), :] = jnp.where(at_even, roll(even, -MZ), odd)


def inverse_y_group(modes_ref, y_table, first, rows):
    half = MY // 2
    pairs = []
    for q in range(GROUP // 2):
        c0 = modes_ref[pl.ds(first + 2 * q, half, stride=rows), :]
        c1 = modes_ref[pl.ds(first + 2 * q + 1, half, stride=rows), :]
        at_even = (lane_index(c0.shape) // MZ) % 2 == 0
        even = jnp.where(at_even, c0, roll(c1, MZ))
        odd = jnp.where(at_even, roll(c0, -MZ), c1)
        both = jnp.concatenate([even, odd], axis=0)
        other = roll(both, 64)
        turned = jnp.where(lane_index(both.shape) < LANES // 2, -other, other)
        pairs.append(jnp.concatenate([both, turned], axis=0))
    high, low = split(jnp.concatenate(pairs, axis=1))
    lines = dot(y_table, jnp.concatenate([high, low, high], axis=0))
    return [lines[:, q * LANES : (q + 1) * LANES] for q in range(GROUP // 2)]


def in_hbm(*arrays):
    return [pltpu.with_memory_space_constraint(each, pltpu.HBM) for each in arrays]


def in_vmem(*arrays):
    return [pltpu.with_memory_space_constraint(each, pltpu.VMEM) for each in arrays]


def full(shape):
    return pl.BlockSpec(shape, lambda *_: (0,) * len(shape))


def params(limit):
    return pltpu.CompilerParams(vmem_limit_bytes=limit * MIB)


def fold_block(pieces, out_ref, at):
    copies = pieces.shape[0]
    real, imag = pieces[0, 0], pieces[0, 1]
    for r in range(1, copies):
        real, imag = real + pieces[r, 0], imag + pieces[r, 1]
    modes = real.shape[-1]
    out_ref[at, :, :, :modes] = real
    out_ref[at, :, :, modes:] = imag


def fetches(weights_hbm, ring_ref, sems, at, slot, unique):
    copies = ring_ref.shape[1]
    return [
        pltpu.make_async_copy(weights_hbm.at[c, at + r * unique], ring_ref.at[slot, r, c], sems.at[slot, r, c])
        for r in range(copies)
        for c in range(2)
    ]


def fold_shapes(weights, unique, slots):
    copies = weights.shape[1] // unique
    shape = (unique,) + weights.shape[2:4] + (2 * weights.shape[4],)
    ring = [pltpu.VMEM((slots, copies, 2) + weights.shape[2:], F32), pltpu.SemaphoreType.DMA((slots, copies, 2))]
    return pltpu.HBM(shape, F32), ring


def forward_kernel(
    table_z, table_y, field_ref, weights_hbm, out_ref, folded_ref, ring_ref, sems,
    *, channels, step_channels, per_step, unique, slots,
):
    step = pl.program_id(0)

    def transform():
        fields = [field_ref[q] for q in range(step_channels)]
        forward_group(fields, table_z[...], table_y[...], out_ref, step * step_channels, channels)

    @pl.when(step == 0)
    def _():
        for at in range(slots):
            for copy in fetches(weights_hbm, ring_ref, sems, at, at, unique):
                copy.start()
        transform()

    @pl.when(step > 0)
    def _():
        for q in range(per_step):
            at = (step - 1) * per_step + q
            for copy in fetches(weights_hbm, ring_ref, sems, at, at, unique):
                copy.wait()
            fold_block(ring_ref.at[at], folded_ref, q)
        transform()


FOLD_STEP = 2
FIELD_STEP = 8


def folded_early(channels):
    return (channels // FIELD_STEP - 1) * FOLD_STEP


def forward_modes(field, tables, weights, unique):
    channels = field.shape[0]
    slots = folded_early(channels)
    folded_shape, ring = fold_shapes(weights, unique, slots)
    owners = MY // 2
    out, some = pl.pallas_call(
        functools.partial(
            forward_kernel, channels=channels, step_channels=FIELD_STEP, per_step=FOLD_STEP, unique=unique, slots=slots
        ),
        grid=(channels // FIELD_STEP,),
        in_specs=[full(t.shape) for t in tables]
        + [pl.BlockSpec((FIELD_STEP, NY, NZ), lambda s: (s, 0, 0)), pl.BlockSpec(memory_space=pl.ANY)],
        out_specs=[
            full((owners * channels, LANES)),
            pl.BlockSpec((FOLD_STEP,) + folded_shape.shape[1:], lambda s: (jnp.maximum(s - 1, 0), 0, 0, 0)),
        ],
        out_shape=[pltpu.VMEM((owners * channels, LANES), F32), folded_shape],
        scratch_shapes=ring,
        compiler_params=params(LIMIT),
        cost_estimate=pl.CostEstimate(flops=2 * 10**9, bytes_accessed=22 * MIB, transcendentals=0),
        name="forward_yz",
    )(*in_hbm(*tables, field, weights))
    return out.reshape(owners, channels, LANES), some


def fold_kernel(weights_hbm, _, out_ref, ring_ref, sems, *, first, unique, slots):
    step = pl.program_id(0)
    slot = step % slots

    @pl.when(step == 0)
    def _():
        for ahead in range(slots):
            for copy in fetches(weights_hbm, ring_ref, sems, first + ahead, ahead, unique):
                copy.start()

    for copy in fetches(weights_hbm, ring_ref, sems, first + step, slot, unique):
        copy.wait()
    fold_block(ring_ref.at[slot], out_ref, 0)

    @pl.when(step + slots < pl.num_programs(0))
    def _():
        for copy in fetches(weights_hbm, ring_ref, sems, first + step + slots, slot, unique):
            copy.start()


def fold_rest(weights, some, unique):
    first = folded_early(weights.shape[2])
    slots = min(4, unique - first)
    folded_shape, ring = fold_shapes(weights, unique, slots)
    anywhere = pl.BlockSpec(memory_space=pl.ANY)
    return pl.pallas_call(
        functools.partial(fold_kernel, first=first, unique=unique, slots=slots),
        grid=(unique - first,),
        in_specs=[anywhere, anywhere],
        out_specs=pl.BlockSpec((1,) + folded_shape.shape[1:], lambda s: (first + s, 0, 0, 0)),
        out_shape=folded_shape,
        scratch_shapes=ring,
        input_output_aliases={1: 0},
        compiler_params=params(LIMIT),
        cost_estimate=pl.CostEstimate(flops=4 * 10**6, bytes_accessed=25 * MIB, transcendentals=0),
        name="fold_weights",
    )(*in_hbm(weights, some))


def halve_lines(lines_ref, sums_ref, points, channels):
    half = points // 2
    sign = jnp.where(lane_index((channels, LANES)) < LANES // 2, 1.0, -1.0)
    for x in range(half):
        near, far = lines_ref[x, :channels], lines_ref[x + half, :channels]
        for parity, value in enumerate((near + far, near - far)):
            sums_ref[parity, 0, x] = value
            sums_ref[parity, 1, x] = sign * roll(value, 64)


def spectrum_row(cos_ref, sin_ref, sums_ref, at, parity, half):
    total = cos_ref[at, 0] * sums_ref[parity, 0, 0] + sin_ref[at, 0] * sums_ref[parity, 1, 0]
    for x in range(1, half):
        total += cos_ref[at, x] * sums_ref[parity, 0, x] + sin_ref[at, x] * sums_ref[parity, 1, x]
    return total


def doubled(values):
    other = roll(values, 64)
    low = lane_index(values.shape) < LANES // 2
    return jnp.where(low, values, other), jnp.where(low, other, values)


def mix_kernel(
    cos_ref, sin_ref, lines_ref, weights_ref, spec_ref, out_ref, sums_ref, total_ref, real_ref, imag_ref,
    *, points, channels, per_step, norm,
):
    step = pl.program_id(0)
    half = points // 2

    @pl.when(step == 0)
    def _():
        halve_lines(lines_ref, sums_ref, points, channels)
        total_ref[...] = jnp.zeros_like(total_ref)

    low = lane_index((channels, LANES)) < LANES // 2
    for q in range(per_step):
        at = step * per_step + q
        parity = q % 2
        spec = norm * spectrum_row(cos_ref, sin_ref, sums_ref, at, parity, half)
        spec_ref[q] = spec
        real_ref[q], imag_ref[q] = doubled(spec)
        by_real = jnp.zeros((channels, LANES), F32)
        by_imag = jnp.zeros((channels, LANES), F32)
        for i in range(channels):
            weight = weights_ref[q, i]
            by_real += real_ref[q, pl.ds(i, 1), :] * weight
            by_imag += imag_ref[q, pl.ds(i, 1), :] * weight
        other = roll(by_imag, 64)
        mixed = by_real + jnp.where(low, -other, other)
        other = roll(mixed, 64)
        turned = jnp.where(low, -other, other)
        for x in range(half):
            total_ref[parity, x] += cos_ref[at, x] * mixed + sin_ref[at, x] * turned

    @pl.when(step == pl.num_programs(0) - 1)
    def _():
        for x in range(half):
            out_ref[x] = total_ref[0, x] + total_ref[1, x]
            out_ref[x + half] = total_ref[0, x] - total_ref[1, x]


def smem():
    return pl.BlockSpec(memory_space=pltpu.SMEM)


def mix(cos_x, sin_x, lines, weights, norm):
    points, channels, _ = lines.shape
    unique = weights.shape[0]
    per_step = 2
    shape = (points, channels, LANES)
    return pl.pallas_call(
        functools.partial(mix_kernel, points=points, channels=channels, per_step=per_step, norm=norm),
        grid=(unique // per_step,),
        in_specs=[
            smem(),
            smem(),
            full(shape),
            pl.BlockSpec((per_step,) + weights.shape[1:], lambda s: (s, 0, 0, 0)),
        ],
        out_specs=[
            pl.BlockSpec((per_step, channels, LANES), lambda s: (s, 0, 0)),
            full(shape),
        ],
        out_shape=[
            pltpu.VMEM((unique, channels, LANES), F32),
            pltpu.VMEM(shape, F32),
        ],
        scratch_shapes=[
            pltpu.VMEM((2, 2, points // 2, channels, LANES), F32),
            pltpu.VMEM((2, points // 2, channels, LANES), F32),
            pltpu.VMEM((per_step, channels, LANES), F32),
            pltpu.VMEM((per_step, channels, LANES), F32),
        ],
        compiler_params=params(LIMIT),
        cost_estimate=pl.CostEstimate(flops=2 * 10**7, bytes_accessed=9 * MIB, transcendentals=0),
        name="mix_modes",
    )(cos_x, sin_x, *in_vmem(lines), *in_hbm(weights))


def exact_dot(left, right):
    return jnp.dot(left, right, precision=lax.Precision.HIGHEST, preferred_element_type=F32)


def pointwise_kernel(sum_ref, turned_ref, bias_in_ref, field_ref, out_ref, mixer_ref, bias_ref, *, channels, blocks):
    size = 8 * channels

    @pl.when(pl.program_id(0) == 0)
    def _():
        wide = exact_dot(sum_ref[...], turned_ref[...])
        wide = lax.dot_general(
            wide, sum_ref[...], (((1,), (1,)), ((), ())), precision=lax.Precision.HIGHEST, preferred_element_type=F32
        )
        row = lax.broadcasted_iota(jnp.int32, (size, size), 0) % 8
        high, low = split(jnp.where(row == lane_index((size, size)) % 8, wide, 0.0))
        mixer_ref[:size] = high
        mixer_ref[size:] = low
        bias_ref[...] = exact_dot(sum_ref[...], bias_in_ref[...])

    for b in range(blocks):
        high, low = split(field_ref[:, 8 * b : 8 * b + 8, :].reshape(size, NZ))
        wide = dot(mixer_ref[...], high)
        values = wide[:size] + wide[size:] + dot(mixer_ref[:size], low) + bias_ref[...]
        out_ref[:, 8 * b : 8 * b + 8, :] = values.reshape(channels, 8, NZ)


def pointwise(field, summing, point_weights, point_bias):
    channels = field.shape[0]
    blocks = 2
    turned = point_weights.T
    bias = point_bias[:, None]
    size = 8 * channels
    block = pl.BlockSpec((channels, 8 * blocks, NZ), lambda s: (0, s, 0))
    return pl.pallas_call(
        functools.partial(pointwise_kernel, channels=channels, blocks=blocks),
        grid=(NY // (8 * blocks),),
        in_specs=[full(summing.shape), full(turned.shape), full(bias.shape), block],
        out_specs=block,
        out_shape=pltpu.HBM(field.shape, F32),
        scratch_shapes=[pltpu.VMEM((2 * size, size), BF16), pltpu.VMEM((size, 1), F32)],
        compiler_params=params(LIMIT),
        cost_estimate=pl.CostEstimate(flops=4 * 10**9, bytes_accessed=24 * MIB, transcendentals=0),
        name="pointwise",
    )(*in_hbm(summing, turned, bias, field))


def cell_group(inv_y, inv_z, modes_ref, pre_ref, cot_ref, act_ref, first, count, channels):
    lines = []
    for g in range(0, count, GROUP):
        lines += inverse_y_group(modes_ref, inv_y, first + g, channels)
    lines = jnp.concatenate(lines, axis=0)
    high = lines.astype(BF16).astype(F32)
    low = lines - high
    at_even = (lane_index(lines.shape) // MZ) % 2 == 0
    spectral = [
        dot(jnp.concatenate([high, side], axis=1).astype(BF16), table)
        for side, table in zip((jnp.where(at_even, low, roll(high, MZ)), jnp.where(at_even, roll(high, -MZ), low)), inv_z)
    ]
    slopes = []
    for q in range(count):
        before = spectral[q % 2][q // 2 * NY : (q // 2 + 1) * NY] + pre_ref[q]
        cdf = 0.5 + 0.5 * lax.erf(before * INV_SQRT_TWO)
        act_ref[q] = (before * cdf).astype(BF16)
        pdf = jnp.exp(-0.5 * before * before) * INV_SQRT_TWO_PI
        slopes.append(cot_ref[q].astype(F32) * (cdf + before * pdf))
    return slopes


def early_cell_kernel(
    inv_y, inv_z0, inv_z1, table_z, table_y, modes_ref, pre_ref, cot_ref, act_ref, slope_ref, out_ref,
    *, channels, count, rows,
):
    step = pl.program_id(0)
    slopes = cell_group(
        inv_y[...], (inv_z0[...], inv_z1[...]), modes_ref, pre_ref, cot_ref, act_ref, step * count, count, channels
    )
    for q in range(count):
        slope_ref[q] = slopes[q]
    forward_group(slopes, table_z[...], table_y[...], out_ref, step * count, rows)


def point_gradient(field_ref, slope_ref, sum_ref, channels):
    size = 8 * channels
    total = jnp.zeros((size, size), F32)
    for b in range(NY // 8):
        at = slice(8 * b, 8 * b + 8)
        f_h, f_l = split(field_ref[:, at, :].reshape(size, NZ))
        s_h, s_l = split(slope_ref[:, at, :].reshape(size, NZ))
        total += lax.dot_general(
            jnp.concatenate([f_h, f_h, f_l], axis=1),
            jnp.concatenate([s_h, s_l, s_h], axis=1),
            (((1,), (1,)), ((), ())),
            preferred_element_type=F32,
        )
    row = lax.broadcasted_iota(jnp.int32, (size, size), 0) % 8
    total = jnp.where(row == lane_index((size, size)) % 8, total, 0.0)
    return exact_dot(jnp.sum(total.reshape(channels, 8, size), axis=1), sum_ref[...])


def late_cell_kernel(
    inv_y, inv_z0, inv_z1, table_z, table_y, sum_ref, modes_ref, pre_ref, cot_ref, early_ref,
    slope_hbm, field_hbm, _, act_ref, out_ref, field_ref, slope_ref, sems, *, channels, count, rows, owners,
):
    step = pl.program_id(0)
    early = early_count(channels)
    late = channels - early
    copies = [
        pltpu.make_async_copy(field_hbm, field_ref, sems.at[0]),
        pltpu.make_async_copy(slope_hbm, slope_ref.at[pl.ds(0, early)], sems.at[1]),
    ]

    @pl.when(step == 0)
    def _():
        for copy in copies:
            copy.start()

    first = early + step * count
    slopes = cell_group(
        inv_y[...], (inv_z0[...], inv_z1[...]), modes_ref, pre_ref, cot_ref, act_ref, first, count, channels
    )
    for q in range(count):
        slope_ref[first + q] = slopes[q]
    forward_group(slopes, table_z[...], table_y[...], out_ref, step * count, rows)

    @pl.when(step == pl.num_programs(0) - 1)
    def _():
        for copy in copies:
            copy.wait()
        point = point_gradient(field_ref, slope_ref, sum_ref, channels)
        packed = jnp.concatenate([point[8 * q : 8 * q + 8] for q in range(channels // 8)], axis=1)
        zero_mode = jnp.concatenate([early_ref[0:early, 0:1], out_ref[0:late, 0:1]], axis=0)
        eye = lax.broadcasted_iota(jnp.int32, (channels, LANES), 0) == lane_index((channels, LANES))
        bias = jnp.sum(jnp.where(eye, jnp.broadcast_to(zero_mode, (channels, LANES)), 0.0), axis=0, keepdims=True)
        extra = jnp.where(lax.broadcasted_iota(jnp.int32, (8, LANES), 0) == 0, jnp.broadcast_to(bias, (8, LANES)), 0.0)
        for d in range(owners):
            out_ref[d * rows + late : d * rows + late + 8, :] = packed
            out_ref[d * rows + late + 8 : (d + 1) * rows, :] = extra


def early_count(channels):
    return channels * 3 // 4


def early_cells(inverse, forward, modes, pre, cotangent):
    channels = pre.shape[0]
    owners = MY // 2
    early = early_count(channels)
    block = pl.BlockSpec((STEP, NY, NZ), lambda s: (s, 0, 0))
    tables = (*inverse, *forward)
    act, slope, out = pl.pallas_call(
        functools.partial(early_cell_kernel, channels=channels, count=STEP, rows=early),
        grid=(early // STEP,),
        in_specs=[full(t.shape) for t in tables] + [full((owners * channels, LANES)), block, block],
        out_specs=[block, block, full((owners * early, LANES))],
        out_shape=[
            pltpu.HBM((channels, NY, NZ), BF16),
            pltpu.HBM((early, NY, NZ), F32),
            pltpu.VMEM((owners * early, LANES), F32),
        ],
        compiler_params=params(LIMIT),
        cost_estimate=pl.CostEstimate(flops=3 * 10**9, bytes_accessed=7 * MIB, transcendentals=10**6),
        name="early_cells",
    )(*in_hbm(*tables), *in_vmem(modes.reshape(owners * channels, LANES)), *in_hbm(pre, cotangent))
    return act, slope, out.reshape(owners, early, LANES)


def late_cells(inverse, forward, summing, modes, pre, cotangent, field, early, slope, act):
    channels = field.shape[0]
    owners = MY // 2
    first = early_count(channels)
    rows = channels - first + 16
    start = first // STEP
    block = pl.BlockSpec((STEP, NY, NZ), lambda s: (start + s, 0, 0))
    anywhere = pl.BlockSpec(memory_space=pl.ANY)
    tables = (*inverse, *forward, summing)
    act, out = pl.pallas_call(
        functools.partial(late_cell_kernel, channels=channels, count=STEP, rows=rows, owners=owners),
        grid=((channels - first) // STEP,),
        in_specs=[full(t.shape) for t in tables]
        + [full((owners * channels, LANES)), block, block, full((owners * first, LANES))]
        + [anywhere] * 3,
        out_specs=[block, full((owners * rows, LANES))],
        out_shape=[
            pltpu.HBM((channels, NY, NZ), BF16),
            pltpu.VMEM((owners * rows, LANES), F32),
        ],
        scratch_shapes=[
            pltpu.VMEM((channels, NY, NZ), F32),
            pltpu.VMEM((channels, NY, NZ), F32),
            pltpu.SemaphoreType.DMA((2,)),
        ],
        input_output_aliases={len(tables) + 6: 0},
        compiler_params=params(LIMIT),
        cost_estimate=pl.CostEstimate(flops=6 * 10**9, bytes_accessed=11 * MIB, transcendentals=10**6),
        name="late_cells",
    )(
        *in_hbm(*tables),
        *in_vmem(modes.reshape(owners * channels, LANES)),
        *in_hbm(pre, cotangent),
        *in_vmem(early.reshape(owners * first, LANES)),
        *in_hbm(slope, field, act),
    )
    return act, out.reshape(owners, rows, LANES)


def join(core, near_ref, far_ref, lines_ref):
    chips, cores = near_ref.shape[:2]
    for p in range(chips):
        lines_ref[cores * p + core] = near_ref[p, core]
        lines_ref[cores * p + 1 - core] = far_ref[p, core]


def gradient_kernel(core_ref, cos_ref, sin_ref, spec_ref, near_ref, far_ref, *refs, points, channels, unique, copies, norm, first, outputs, slots):
    last = first > 0
    if last:
        _, out_hbm, point_ref, bias_ref, lines_ref, sums_ref, real_ref, imag_ref, buffer, sems = refs
    else:
        out_hbm, lines_ref, sums_ref, real_ref, imag_ref, buffer, sems = refs
    join(core_ref[0], near_ref, far_ref, lines_ref)
    halve_lines(lines_ref, sums_ref, points, outputs)
    half = LANES // 2
    lane = lane_index((outputs, LANES))
    scale = jnp.where(lane % MZ == 0, norm, 2.0 * norm)

    def writes(at, slot):
        return [
            pltpu.make_async_copy(
                buffer.at[slot, c],
                out_hbm.at[c, at + r * unique, :, pl.ds(first, outputs), :],
                sems.at[slot, c, r],
            )
            for r in range(copies)
            for c in range(2)
        ]

    @pl.loop(0, unique // slots)
    def _(turn):
        for slot in range(slots):
            at = slots * turn + slot

            @pl.when(turn > 0)
            def _():
                for copy in writes(at - slots, slot):
                    copy.wait()

            slope = scale * spectrum_row(cos_ref, sin_ref, sums_ref, at, slot % 2, points // 2)
            other = roll(slope, 64)
            flipped = jnp.where(lane < half, other, -other)
            real_ref[slot], imag_ref[slot] = doubled(spec_ref[at])
            for i in range(channels):
                both = real_ref[slot, pl.ds(i, 1), :] * slope + imag_ref[slot, pl.ds(i, 1), :] * flipped
                buffer[slot, 0, i] = both[:, :half]
                buffer[slot, 1, i] = both[:, half:]
            for copy in writes(at, slot):
                copy.start()

    if last:
        packed = lines_ref[0, outputs : outputs + 16, :]
        for x in range(1, points):
            packed += lines_ref[x, outputs : outputs + 16, :]
        packed = norm * packed
        for q in range(channels // 8):
            point_ref[8 * q : 8 * q + 8, :] = packed[:8, q * channels : (q + 1) * channels]
        bias_ref[...] = packed[8:9, :channels]

    for at in range(unique - slots, unique):
        for copy in writes(at, at % slots):
            copy.wait()


def gradient(core, cos_x, sin_x, spectrum, near, far, norm, kept_x, before=()):
    chips, cores, rows, _ = near.shape
    points = chips * cores
    unique, channels, _ = spectrum.shape
    half = LANES // 2
    copies = kept_x // unique
    first = early_count(channels) if before else 0
    outputs = channels - first if before else early_count(channels)
    slots = 8 if before else 4
    anywhere = pl.BlockSpec(memory_space=pl.ANY)
    shape = jax.ShapeDtypeStruct((2, kept_x, channels, channels, half), F32)
    sums = [(channels, channels), (1, channels)] if before else []
    return pl.pallas_call(
        functools.partial(
            gradient_kernel, points=points, channels=channels, unique=unique, copies=copies, norm=norm,
            first=first, outputs=outputs, slots=slots,
        ),
        in_specs=[smem(), smem(), smem(), full(spectrum.shape), full(near.shape), full(far.shape)]
        + [anywhere] * len(before),
        out_specs=[anywhere] + [full(each) for each in sums],
        out_shape=[shape] + [jax.ShapeDtypeStruct(each, F32) for each in sums],
        scratch_shapes=[
            pltpu.VMEM((points, rows, LANES), F32),
            pltpu.VMEM((2, 2, points // 2, outputs, LANES), F32),
            pltpu.VMEM((slots, channels, LANES), F32),
            pltpu.VMEM((slots, channels, LANES), F32),
            pltpu.VMEM((slots, 2, channels, outputs, half), F32),
            pltpu.SemaphoreType.DMA((slots, 2, copies)),
        ],
        input_output_aliases={6: 0} if before else {},
        compiler_params=params(LIMIT),
        cost_estimate=pl.CostEstimate(flops=5 * 10**6, bytes_accessed=32 * MIB, transcendentals=0),
        name="weight_gradient",
    )(core, cos_x, sin_x, *in_vmem(spectrum, near, far), *before)


def swap(lines):
    return lax.all_to_all(lines, "space", split_axis=0, concat_axis=0, tiled=True)


CORES = 2


def swap_chips(lines):
    devices, rows, lanes = lines.shape
    chips = devices // CORES
    groups = [[p * CORES + q for p in range(chips)] for q in range(CORES)]
    near = lax.all_to_all(
        lines.reshape(chips, CORES * rows, lanes), "space", split_axis=0, concat_axis=0, tiled=True, axis_index_groups=groups
    )
    return near.reshape(chips, CORES, rows, lanes)


def swap_cores(near, devices):
    return lax.ppermute(near, "space", [(d, d ^ 1) for d in range(devices)])


def suits(width_x, length_x, devices, channels, weights):
    held = weights.shape[2]
    even = np.array_equal(kept(MX, length_x) % length_x, np.arange(MX) % length_x)
    return (
        width_x == 1
        and held == 2 * MZ
        and devices * 2 == MY
        and 2 * held == LANES
        and MX % length_x == 0
        and length_x % 8 == 0
        and even
        and channels == MZ
    )


def body(lifted_field, cotangent, spectral_weights, point_weights, point_bias):
    devices = lax.axis_size("space")
    channels, width_x = lifted_field.shape[:2]
    length_x = width_x * devices
    if not suits(width_x, length_x, devices, channels, spectral_weights):
        return general_body(lifted_field, cotangent, spectral_weights, point_weights, point_bias)
    norm = float(length_x * NY * NZ) ** -0.5
    theta = angles(np.arange(length_x), np.arange(length_x), length_x)
    cos_x, sin_x = jnp.asarray(np.cos(theta), F32), jnp.asarray(np.sin(theta), F32)
    forward = forward_tables()
    inverse = inverse_tables(norm)
    summing = jnp.asarray(np.repeat(np.eye(channels), 8, axis=0), F32)

    field = lifted_field.reshape(channels, NY, NZ)
    slopes_in = cotangent.reshape(channels, NY, NZ)
    weights = jnp.transpose(spectral_weights, (0, 1, 3, 4, 2))

    lines, some = forward_modes(field, forward, weights, length_x)
    lines = swap(lines)
    folded = fold_rest(weights, some, length_x)
    spectrum, mixed = mix(cos_x, sin_x, lines, folded, norm)
    field_late, mixed = lax.optimization_barrier((field, mixed))
    modes = swap(mixed)
    pre = pointwise(field_late, summing, point_weights, point_bias)
    act, slope, early = early_cells(inverse, forward, modes, pre, slopes_in)
    early_near = swap_chips(early)
    activated, late = late_cells(inverse, forward, summing, modes, pre, slopes_in, field, early, slope, act)
    early_near, late = lax.optimization_barrier((early_near, late))
    early_far = swap_cores(early_near, devices)
    late_near = swap_chips(late)
    core = lax.axis_index("space")[None] & (CORES - 1)
    (grad,) = gradient(core, cos_x, sin_x, spectrum, early_near, early_far, norm, MX)
    late_near, grad = lax.optimization_barrier((late_near, grad))
    late_far = swap_cores(late_near, devices)
    grad, grad_point, grad_bias = gradient(core, cos_x, sin_x, spectrum, late_near, late_far, norm, MX, (grad,))
    return (
        activated.reshape(cotangent.shape),
        jnp.transpose(grad, (0, 1, 4, 2, 3)),
        grad_point,
        grad_bias.reshape(channels),
    )


HIGHEST = lax.Precision.HIGHEST


def trig_tables(positions, frequency, length):
    product = positions[:, None] * frequency[None, :] % length
    phase_angle = 2.0 * jnp.pi / length * product.astype(jnp.float32)
    return (jnp.cos(phase_angle), jnp.sin(phase_angle))


def kept_frequencies(kept_count, length):
    mode_index = jnp.arange(kept_count, dtype=jnp.int32)
    return jnp.where(mode_index < kept_count // 2, mode_index, length - kept_count + mode_index)


def forward_local(field_in):
    channels = field_in.shape[0]
    width_x = field_in.shape[1]
    cos_z, sin_z = trig_tables(jnp.arange(NZ, dtype=jnp.int32), jnp.arange(MZ, dtype=jnp.int32), NZ)
    table_z = jnp.concatenate([cos_z, -sin_z], axis=1)
    along_z = jnp.einsum("cxyz,zk->cxyk", field_in, table_z, precision=HIGHEST)
    z_real = along_z[..., :MZ]
    z_imag = along_z[..., MZ:]
    cos_y, sin_y = trig_tables(jnp.arange(NY, dtype=jnp.int32), kept_frequencies(MY, NY), NY)
    y_real = jnp.einsum("cxyk,yj->xcjk", z_real, cos_y, precision=HIGHEST) + jnp.einsum(
        "cxyk,yj->xcjk", z_imag, sin_y, precision=HIGHEST
    )
    y_imag = jnp.einsum("cxyk,yj->xcjk", z_imag, cos_y, precision=HIGHEST) - jnp.einsum(
        "cxyk,yj->xcjk", z_real, sin_y, precision=HIGHEST
    )
    stacked = jnp.stack([y_real, y_imag], axis=1)
    return stacked.reshape(width_x, 2, channels, MY * MZ)


def transform_x(x_lines):
    length_x = x_lines.shape[0]
    cos_x, sin_x = trig_tables(
        jnp.arange(length_x, dtype=jnp.int32), kept_frequencies(MX, length_x), length_x
    )
    norm_scale = 1.0 / float(length_x * NY * NZ) ** 0.5
    part_real = x_lines[:, 0]
    part_imag = x_lines[:, 1]
    x_real = jnp.einsum("xcm,xk->kcm", part_real, cos_x, precision=HIGHEST) + jnp.einsum(
        "xcm,xk->kcm", part_imag, sin_x, precision=HIGHEST
    )
    x_imag = jnp.einsum("xcm,xk->kcm", part_imag, cos_x, precision=HIGHEST) - jnp.einsum(
        "xcm,xk->kcm", part_real, sin_x, precision=HIGHEST
    )
    return norm_scale * jnp.stack([x_real, x_imag], axis=1)


def mix_modes(spectrum, weights):
    spec_real = spectrum[:, 0]
    spec_imag = spectrum[:, 1]
    out_real = jnp.einsum("kim,kmio->kom", spec_real, weights[0], precision=HIGHEST) - jnp.einsum(
        "kim,kmio->kom", spec_imag, weights[1], precision=HIGHEST
    )
    out_imag = jnp.einsum("kim,kmio->kom", spec_real, weights[1], precision=HIGHEST) + jnp.einsum(
        "kim,kmio->kom", spec_imag, weights[0], precision=HIGHEST
    )
    return jnp.stack([out_real, out_imag], axis=1)


def inverse_x(spectrum, positions, length_x):
    cos_x, sin_x = trig_tables(positions, kept_frequencies(MX, length_x), length_x)
    spec_real = spectrum[:, 0]
    spec_imag = spectrum[:, 1]
    a_real = jnp.einsum("kcm,xk->xcm", spec_real, cos_x, precision=HIGHEST) - jnp.einsum(
        "kcm,xk->xcm", spec_imag, sin_x, precision=HIGHEST
    )
    a_imag = jnp.einsum("kcm,xk->xcm", spec_imag, cos_x, precision=HIGHEST) + jnp.einsum(
        "kcm,xk->xcm", spec_real, sin_x, precision=HIGHEST
    )
    return jnp.stack([a_real, a_imag], axis=1)


def inverse_yz(x_lines, length_x):
    width_x = x_lines.shape[0]
    channels = x_lines.shape[2]
    mode_grid = x_lines.reshape(width_x, 2, channels, MY, MZ)
    cos_y, sin_y = trig_tables(jnp.arange(NY, dtype=jnp.int32), kept_frequencies(MY, NY), NY)
    b_real = jnp.einsum("xcjk,yj->cxyk", mode_grid[:, 0], cos_y, precision=HIGHEST) - jnp.einsum(
        "xcjk,yj->cxyk", mode_grid[:, 1], sin_y, precision=HIGHEST
    )
    b_imag = jnp.einsum("xcjk,yj->cxyk", mode_grid[:, 1], cos_y, precision=HIGHEST) + jnp.einsum(
        "xcjk,yj->cxyk", mode_grid[:, 0], sin_y, precision=HIGHEST
    )
    cos_z, sin_z = trig_tables(jnp.arange(NZ, dtype=jnp.int32), jnp.arange(MZ, dtype=jnp.int32), NZ)
    weight_z = jnp.where(jnp.arange(MZ, dtype=jnp.int32) == 0, 1.0, 2.0).astype(jnp.float32)
    table_z = jnp.concatenate([cos_z * weight_z[None, :], -sin_z * weight_z[None, :]], axis=1)
    stacked = jnp.concatenate([b_real, b_imag], axis=-1)
    result = jnp.einsum("cxyk,zk->cxyz", stacked, table_z, precision=HIGHEST)
    return result * (1.0 / float(length_x * NY * NZ) ** 0.5)


def gelu_slope(values):
    return (
        0.5 * (1.0 + lax.erf(values * INV_SQRT_TWO))
        + values * jnp.exp(-0.5 * values * values) * INV_SQRT_TWO_PI
    )


def weight_gradient(spectrum, slope_modes, first_mode):
    mode_ids = first_mode + jnp.arange(spectrum.shape[3], dtype=jnp.int32)
    weight_modes = jnp.where(mode_ids % MZ == 0, 1.0, 2.0).astype(jnp.float32)
    grad_real = jnp.einsum(
        "kim,kom->kmio", spectrum[:, 0], slope_modes[:, 0], precision=HIGHEST
    ) + jnp.einsum("kim,kom->kmio", spectrum[:, 1], slope_modes[:, 1], precision=HIGHEST)
    grad_imag = jnp.einsum(
        "kim,kom->kmio", spectrum[:, 0], slope_modes[:, 1], precision=HIGHEST
    ) - jnp.einsum("kim,kom->kmio", spectrum[:, 1], slope_modes[:, 0], precision=HIGHEST)
    stacked = jnp.stack([grad_real, grad_imag], axis=0)
    return stacked * weight_modes[None, None, :, None, None]


def to_modes(field_in):
    return transform_x(
        lax.all_to_all(forward_local(field_in), "space", split_axis=3, concat_axis=0, tiled=True)
    )


def general_body(lifted_field, cotangent, spectral_weights, point_weights, point_bias):
    devices = lax.axis_size("space")
    width_x = lifted_field.shape[1]
    length_x = width_x * devices
    spectrum = to_modes(lifted_field)
    mixed_modes = mix_modes(spectrum, spectral_weights)
    full_lines = inverse_x(mixed_modes, jnp.arange(length_x, dtype=jnp.int32), length_x)
    spectral = inverse_yz(
        lax.all_to_all(full_lines, "space", split_axis=0, concat_axis=3, tiled=True), length_x
    )
    pointwise = (
        jnp.einsum("ixyz,io->oxyz", lifted_field, point_weights, precision=HIGHEST)
        + point_bias[:, None, None, None]
    )
    before = spectral + pointwise
    activated = jax.nn.gelu(before, approximate=False).astype(jnp.bfloat16)
    slope_field = cotangent.astype(jnp.float32) * gelu_slope(before)
    local_point = jnp.einsum("ixyz,oxyz->io", lifted_field, slope_field, precision=HIGHEST)
    local_bias = jnp.sum(slope_field, axis=(1, 2, 3))
    partial = jnp.concatenate([local_point, local_bias[None, :]], axis=0)
    gathered = lax.all_gather(partial, "space", axis=0, tiled=False)
    summed = jnp.sum(gathered, axis=0)
    summed_point, summed_bias = summed[:-1], summed[-1]
    root_cells = float(length_x * NY * NZ) ** 0.5
    slope_spectrum = to_modes(slope_field)
    first_mode = lax.axis_index("space") * spectrum.shape[3]
    grad_spectral = weight_gradient(spectrum, slope_spectrum, first_mode)
    return (activated, grad_spectral, summed_point / root_cells, summed_bias / root_cells)


def solution(mesh):
    placed = (
        P("groups", "space", None, None),
        P("groups", "space", None, None),
        P(None, None, "space", None, None),
        P(),
        P(),
    )
    return jax.shard_map(
        body,
        mesh=mesh,
        in_specs=placed,
        out_specs=(
            P("groups", "space", None, None),
            P("groups", None, "space", None, None),
            P("groups", None),
            P("groups"),
        ),
        check_vma=False,
    )
```

```python
import functools

import jax
import jax.numpy as jnp
import ml_dtypes
import numpy as np
from jax import lax
from jax.experimental import pallas as pl
from jax.experimental.pallas import tpu as pltpu
from jax.sharding import PartitionSpec as P

MX = 32
MY = 32
MZ = 32
NY = 128
NZ = 256

F32 = jnp.float32
BF16 = jnp.bfloat16
INV_SQRT_TWO = 0.7071067811865476
INV_SQRT_TWO_PI = 0.3989422804014327
MIB = 1 << 20
LIMIT = 48
LANES = 128
GROUP = 4
EARLY_STEP = 12
STEP = 8


def kept(kept_count, length):
    index = np.arange(kept_count)
    return np.where(index < kept_count // 2, index, length - kept_count + index)


def angles(positions, frequency, length):
    product = positions[:, None] * frequency[None, :] % length
    return 2.0 * np.pi / length * product


def split_table(table):
    high = table.astype(ml_dtypes.bfloat16)
    return high, (table - high.astype(np.float64)).astype(ml_dtypes.bfloat16)


def lane_spread(first, second, real_table, imag_table):
    return np.concatenate(
        [real_table * first, real_table * second, imag_table * first, imag_table * second], axis=1
    )


def forward_tables():
    theta = angles(np.arange(NZ), np.arange(MZ), NZ)
    table = np.concatenate([lane_spread(f, s, np.cos(theta), -np.sin(theta)) for f, s in ((1, 0), (0, 1))], axis=0)
    high, low = split_table(table)
    table_z = np.concatenate(
        [np.concatenate([high, low], axis=1), np.concatenate([high, np.zeros_like(low)], axis=1)], axis=0
    )
    theta = angles(np.arange(NY), kept(MY, NY), NY).T
    table = np.concatenate([np.cos(theta)[0::2], np.cos(theta)[1::2], np.sin(theta)[0::2], np.sin(theta)[1::2]], axis=0)
    high, low = split_table(table)
    table_y = np.concatenate(
        [np.concatenate([high, high], axis=1), np.concatenate([low, np.zeros_like(low)], axis=1)], axis=0
    )
    return table_z, table_y


def inverse_tables(norm):
    theta = angles(np.arange(NY), kept(MY, NY), NY)
    cos_y, sin_y = np.cos(theta), np.sin(theta)
    table_y = np.concatenate([cos_y[:, 0::2], cos_y[:, 1::2], sin_y[:, 0::2], sin_y[:, 1::2]], axis=1)
    y_high, y_low = split_table(table_y)
    theta = angles(np.arange(NZ), np.arange(MZ), NZ)
    weight = np.where(np.arange(MZ) == 0, 1.0, 2.0) * norm
    parts = (np.cos(theta) * weight, -np.sin(theta) * weight)
    own, other = lane_spread(1, 0, *parts).T, lane_spread(0, 1, *parts).T
    tables_z = []
    for mine, theirs in ((own, other), (other, own)):
        high = split_table(mine)[0]
        tables_z.append(np.concatenate([high, high + split_table(theirs)[1]], axis=0))
    return np.concatenate([y_high, y_high, y_low], axis=1), *tables_z


def dot(left, right):
    return jnp.dot(left, right, preferred_element_type=F32)


def split(values):
    high = values.astype(BF16)
    return high, (values - high.astype(F32)).astype(BF16)


def lane_index(shape):
    return lax.broadcasted_iota(jnp.int32, shape, len(shape) - 1)


def roll(values, shift):
    return pltpu.roll(values, shift % LANES, len(values.shape) - 1)


def forward_group(fields, table_z, table_y, out_ref, first, rows):
    left = jnp.concatenate(
        [jnp.concatenate([fields[q], fields[q + 1]], axis=1) for q in range(0, len(fields), 2)], axis=0
    )
    lines = dot(jnp.concatenate(split(left), axis=1), table_z)
    lines = lines[:, :LANES] + lines[:, LANES:]
    half = MY // 2
    for g in range(0, len(fields) // 2, GROUP // 2):
        quad = jnp.concatenate([lines[q * NY : (q + 1) * NY] for q in range(g, g + GROUP // 2)], axis=1)
        wide = dot(table_y, jnp.concatenate(split(quad), axis=0))
        wide = wide[: 2 * MY] + wide[2 * MY :]
        for q in range(GROUP // 2):
            by_cos = wide[:MY, q * LANES : (q + 1) * LANES]
            by_sin = roll(wide[MY:, q * LANES : (q + 1) * LANES], 64)
            modes = by_cos + jnp.where(lane_index(by_sin.shape) < LANES // 2, by_sin, -by_sin)
            even, odd = modes[:half], modes[half:]
            at_even = (lane_index(even.shape) // MZ) % 2 == 0
            at = first + 2 * (g + q)
            out_ref[pl.ds(at, half, stride=rows), :] = jnp.where(at_even, even, roll(odd, MZ))
            out_ref[pl.ds(at + 1, half, stride=rows), :] = jnp.where(at_even, roll(even, -MZ), odd)


def inverse_y_group(modes_ref, y_table, first, rows):
    half = MY // 2
    pairs = []
    for q in range(GROUP // 2):
        c0 = modes_ref[pl.ds(first + 2 * q, half, stride=rows), :]
        c1 = modes_ref[pl.ds(first + 2 * q + 1, half, stride=rows), :]
        at_even = (lane_index(c0.shape) // MZ) % 2 == 0
        even = jnp.where(at_even, c0, roll(c1, MZ))
        odd = jnp.where(at_even, roll(c0, -MZ), c1)
        both = jnp.concatenate([even, odd], axis=0)
        other = roll(both, 64)
        turned = jnp.where(lane_index(both.shape) < LANES // 2, -other, other)
        pairs.append(jnp.concatenate([both, turned], axis=0))
    high, low = split(jnp.concatenate(pairs, axis=1))
    lines = dot(y_table, jnp.concatenate([high, low, high], axis=0))
    return [lines[:, q * LANES : (q + 1) * LANES] for q in range(GROUP // 2)]


def in_hbm(*arrays):
    return [pltpu.with_memory_space_constraint(each, pltpu.HBM) for each in arrays]


def in_vmem(*arrays):
    return [pltpu.with_memory_space_constraint(each, pltpu.VMEM) for each in arrays]


def full(shape):
    return pl.BlockSpec(shape, lambda *_: (0,) * len(shape))


def params(limit):
    return pltpu.CompilerParams(vmem_limit_bytes=limit * MIB)


def fold_block(pieces, out_ref, at):
    copies = pieces.shape[0]
    real, imag = pieces[0, 0], pieces[0, 1]
    for r in range(1, copies):
        real, imag = real + pieces[r, 0], imag + pieces[r, 1]
    modes = real.shape[-1]
    out_ref[at, :, :, :modes] = real
    out_ref[at, :, :, modes:] = imag


def fetches(weights_hbm, ring_ref, sems, at, slot, unique):
    copies = ring_ref.shape[1]
    return [
        pltpu.make_async_copy(weights_hbm.at[c, at + r * unique], ring_ref.at[slot, r, c], sems.at[slot, r, c])
        for r in range(copies)
        for c in range(2)
    ]


def fold_shapes(weights, unique, slots):
    copies = weights.shape[1] // unique
    shape = (unique,) + weights.shape[2:4] + (2 * weights.shape[4],)
    ring = [pltpu.VMEM((slots, copies, 2) + weights.shape[2:], F32), pltpu.SemaphoreType.DMA((slots, copies, 2))]
    return pltpu.HBM(shape, F32), ring


def forward_kernel(
    table_z, table_y, field_ref, weights_hbm, out_ref, folded_ref, ring_ref, sems,
    *, channels, step_channels, per_step, unique, slots,
):
    step = pl.program_id(0)

    def transform():
        fields = [field_ref[q] for q in range(step_channels)]
        forward_group(fields, table_z[...], table_y[...], out_ref, step * step_channels, channels)

    @pl.when(step == 0)
    def _():
        for at in range(slots):
            for copy in fetches(weights_hbm, ring_ref, sems, at, at, unique):
                copy.start()
        transform()

    @pl.when(step > 0)
    def _():
        for q in range(per_step):
            at = (step - 1) * per_step + q
            for copy in fetches(weights_hbm, ring_ref, sems, at, at, unique):
                copy.wait()
            fold_block(ring_ref.at[at], folded_ref, q)
        transform()


FOLD_STEP = 2
FIELD_STEP = 8


def folded_early(channels):
    return (channels // FIELD_STEP - 1) * FOLD_STEP


def forward_modes(field, tables, weights, unique):
    channels = field.shape[0]
    slots = folded_early(channels)
    folded_shape, ring = fold_shapes(weights, unique, slots)
    owners = MY // 2
    out, some = pl.pallas_call(
        functools.partial(
            forward_kernel, channels=channels, step_channels=FIELD_STEP, per_step=FOLD_STEP, unique=unique, slots=slots
        ),
        grid=(channels // FIELD_STEP,),
        in_specs=[full(t.shape) for t in tables]
        + [pl.BlockSpec((FIELD_STEP, NY, NZ), lambda s: (s, 0, 0)), pl.BlockSpec(memory_space=pl.ANY)],
        out_specs=[
            full((owners * channels, LANES)),
            pl.BlockSpec((FOLD_STEP,) + folded_shape.shape[1:], lambda s: (jnp.maximum(s - 1, 0), 0, 0, 0)),
        ],
        out_shape=[pltpu.VMEM((owners * channels, LANES), F32), folded_shape],
        scratch_shapes=ring,
        compiler_params=params(LIMIT),
        cost_estimate=pl.CostEstimate(flops=2 * 10**9, bytes_accessed=22 * MIB, transcendentals=0),
        name="forward_yz",
    )(*in_hbm(*tables, field, weights))
    return out.reshape(owners, channels, LANES), some


def fold_kernel(weights_hbm, _, out_ref, ring_ref, sems, *, first, unique, slots):
    step = pl.program_id(0)
    slot = step % slots

    @pl.when(step == 0)
    def _():
        for ahead in range(slots):
            for copy in fetches(weights_hbm, ring_ref, sems, first + ahead, ahead, unique):
                copy.start()

    for copy in fetches(weights_hbm, ring_ref, sems, first + step, slot, unique):
        copy.wait()
    fold_block(ring_ref.at[slot], out_ref, 0)

    @pl.when(step + slots < pl.num_programs(0))
    def _():
        for copy in fetches(weights_hbm, ring_ref, sems, first + step + slots, slot, unique):
            copy.start()


def fold_rest(weights, some, unique):
    first = folded_early(weights.shape[2])
    slots = min(4, unique - first)
    folded_shape, ring = fold_shapes(weights, unique, slots)
    anywhere = pl.BlockSpec(memory_space=pl.ANY)
    return pl.pallas_call(
        functools.partial(fold_kernel, first=first, unique=unique, slots=slots),
        grid=(unique - first,),
        in_specs=[anywhere, anywhere],
        out_specs=pl.BlockSpec((1,) + folded_shape.shape[1:], lambda s: (first + s, 0, 0, 0)),
        out_shape=folded_shape,
        scratch_shapes=ring,
        input_output_aliases={1: 0},
        compiler_params=params(LIMIT),
        cost_estimate=pl.CostEstimate(flops=4 * 10**6, bytes_accessed=25 * MIB, transcendentals=0),
        name="fold_weights",
    )(*in_hbm(weights, some))


def halve_lines(lines_ref, sums_ref, points, channels):
    half = points // 2
    sign = jnp.where(lane_index((channels, LANES)) < LANES // 2, 1.0, -1.0)
    for x in range(half):
        near, far = lines_ref[x, :channels], lines_ref[x + half, :channels]
        for parity, value in enumerate((near + far, near - far)):
            sums_ref[parity, 0, x] = value
            sums_ref[parity, 1, x] = sign * roll(value, 64)


def spectrum_row(cos_ref, sin_ref, sums_ref, at, parity, half):
    total = cos_ref[at, 0] * sums_ref[parity, 0, 0] + sin_ref[at, 0] * sums_ref[parity, 1, 0]
    for x in range(1, half):
        total += cos_ref[at, x] * sums_ref[parity, 0, x] + sin_ref[at, x] * sums_ref[parity, 1, x]
    return total


def doubled(values):
    other = roll(values, 64)
    low = lane_index(values.shape) < LANES // 2
    return jnp.where(low, values, other), jnp.where(low, other, values)


def mix_kernel(
    cos_ref, sin_ref, lines_ref, weights_ref, spec_ref, out_ref, sums_ref, total_ref, real_ref, imag_ref,
    *, points, channels, per_step, norm,
):
    step = pl.program_id(0)
    half = points // 2

    @pl.when(step == 0)
    def _():
        halve_lines(lines_ref, sums_ref, points, channels)
        total_ref[...] = jnp.zeros_like(total_ref)

    low = lane_index((channels, LANES)) < LANES // 2
    for q in range(per_step):
        at = step * per_step + q
        parity = q % 2
        spec = norm * spectrum_row(cos_ref, sin_ref, sums_ref, at, parity, half)
        spec_ref[q] = spec
        real_ref[q], imag_ref[q] = doubled(spec)
        by_real = jnp.zeros((channels, LANES), F32)
        by_imag = jnp.zeros((channels, LANES), F32)
        for i in range(channels):
            weight = weights_ref[q, i]
            by_real += real_ref[q, pl.ds(i, 1), :] * weight
            by_imag += imag_ref[q, pl.ds(i, 1), :] * weight
        other = roll(by_imag, 64)
        mixed = by_real + jnp.where(low, -other, other)
        other = roll(mixed, 64)
        turned = jnp.where(low, -other, other)
        for x in range(half):
            total_ref[parity, x] += cos_ref[at, x] * mixed + sin_ref[at, x] * turned

    @pl.when(step == pl.num_programs(0) - 1)
    def _():
        for x in range(half):
            out_ref[x] = total_ref[0, x] + total_ref[1, x]
            out_ref[x + half] = total_ref[0, x] - total_ref[1, x]


def smem():
    return pl.BlockSpec(memory_space=pltpu.SMEM)


def mix(cos_x, sin_x, lines, weights, norm):
    points, channels, _ = lines.shape
    unique = weights.shape[0]
    per_step = min(unique, 8)
    shape = (points, channels, LANES)
    return pl.pallas_call(
        functools.partial(mix_kernel, points=points, channels=channels, per_step=per_step, norm=norm),
        grid=(unique // per_step,),
        in_specs=[
            smem(),
            smem(),
            full(shape),
            pl.BlockSpec((per_step,) + weights.shape[1:], lambda s: (s, 0, 0, 0)),
        ],
        out_specs=[
            pl.BlockSpec((per_step, channels, LANES), lambda s: (s, 0, 0)),
            full(shape),
        ],
        out_shape=[
            pltpu.VMEM((unique, channels, LANES), F32),
            pltpu.VMEM(shape, F32),
        ],
        scratch_shapes=[
            pltpu.VMEM((2, 2, points // 2, channels, LANES), F32),
            pltpu.VMEM((2, points // 2, channels, LANES), F32),
            pltpu.VMEM((per_step, channels, LANES), F32),
            pltpu.VMEM((per_step, channels, LANES), F32),
        ],
        compiler_params=params(LIMIT),
        cost_estimate=pl.CostEstimate(flops=2 * 10**7, bytes_accessed=9 * MIB, transcendentals=0),
        name="mix_modes",
    )(cos_x, sin_x, *in_vmem(lines), *in_hbm(weights))


def exact_dot(left, right):
    return jnp.dot(left, right, precision=lax.Precision.HIGHEST, preferred_element_type=F32)


def pointwise_kernel(sum_ref, turned_ref, bias_in_ref, field_ref, out_ref, mixer_ref, bias_ref, *, channels, blocks):
    size = 8 * channels

    @pl.when(pl.program_id(0) == 0)
    def _():
        wide = exact_dot(sum_ref[...], turned_ref[...])
        wide = lax.dot_general(
            wide, sum_ref[...], (((1,), (1,)), ((), ())), precision=lax.Precision.HIGHEST, preferred_element_type=F32
        )
        row = lax.broadcasted_iota(jnp.int32, (size, size), 0) % 8
        high, low = split(jnp.where(row == lane_index((size, size)) % 8, wide, 0.0))
        mixer_ref[:size] = high
        mixer_ref[size:] = low
        bias_ref[...] = exact_dot(sum_ref[...], bias_in_ref[...])

    for b in range(blocks):
        high, low = split(field_ref[:, 8 * b : 8 * b + 8, :].reshape(size, NZ))
        wide = dot(mixer_ref[...], high)
        values = wide[:size] + wide[size:] + dot(mixer_ref[:size], low) + bias_ref[...]
        out_ref[:, 8 * b : 8 * b + 8, :] = values.reshape(channels, 8, NZ)


def pointwise(field, summing, point_weights, point_bias):
    channels = field.shape[0]
    blocks = 2
    turned = point_weights.T
    bias = point_bias[:, None]
    size = 8 * channels
    block = pl.BlockSpec((channels, 8 * blocks, NZ), lambda s: (0, s, 0))
    return pl.pallas_call(
        functools.partial(pointwise_kernel, channels=channels, blocks=blocks),
        grid=(NY // (8 * blocks),),
        in_specs=[full(summing.shape), full(turned.shape), full(bias.shape), block],
        out_specs=block,
        out_shape=pltpu.HBM(field.shape, F32),
        scratch_shapes=[pltpu.VMEM((2 * size, size), BF16), pltpu.VMEM((size, 1), F32)],
        compiler_params=params(LIMIT),
        cost_estimate=pl.CostEstimate(flops=4 * 10**9, bytes_accessed=24 * MIB, transcendentals=0),
        name="pointwise",
    )(*in_hbm(summing, turned, bias, field))


def cell_group(inv_y, inv_z, modes_ref, pre_ref, cot_ref, act_ref, first, count, channels):
    lines = []
    for g in range(0, count, GROUP):
        lines += inverse_y_group(modes_ref, inv_y, first + g, channels)
    lines = jnp.concatenate(lines, axis=0)
    high = lines.astype(BF16).astype(F32)
    low = lines - high
    at_even = (lane_index(lines.shape) // MZ) % 2 == 0
    spectral = [
        dot(jnp.concatenate([high, side], axis=1).astype(BF16), table)
        for side, table in zip((jnp.where(at_even, low, roll(high, MZ)), jnp.where(at_even, roll(high, -MZ), low)), inv_z)
    ]
    slopes = []
    for q in range(count):
        before = spectral[q % 2][q // 2 * NY : (q // 2 + 1) * NY] + pre_ref[q]
        cdf = 0.5 + 0.5 * lax.erf(before * INV_SQRT_TWO)
        act_ref[q] = (before * cdf).astype(BF16)
        pdf = jnp.exp(-0.5 * before * before) * INV_SQRT_TWO_PI
        slopes.append(cot_ref[q].astype(F32) * (cdf + before * pdf))
    return slopes


def early_cell_kernel(
    inv_y, inv_z0, inv_z1, table_z, table_y, modes_ref, pre_ref, cot_ref, act_ref, slope_ref, out_ref,
    *, channels, count, rows,
):
    step = pl.program_id(0)
    slopes = cell_group(
        inv_y[...], (inv_z0[...], inv_z1[...]), modes_ref, pre_ref, cot_ref, act_ref, step * count, count, channels
    )
    for q in range(count):
        slope_ref[q] = slopes[q]
    forward_group(slopes, table_z[...], table_y[...], out_ref, step * count, rows)


def point_gradient(field_ref, slope_ref, sum_ref, channels):
    size = 8 * channels
    total = jnp.zeros((size, size), F32)
    for b in range(NY // 8):
        at = slice(8 * b, 8 * b + 8)
        f_h, f_l = split(field_ref[:, at, :].reshape(size, NZ))
        s_h, s_l = split(slope_ref[:, at, :].reshape(size, NZ))
        total += lax.dot_general(
            jnp.concatenate([f_h, f_h, f_l], axis=1),
            jnp.concatenate([s_h, s_l, s_h], axis=1),
            (((1,), (1,)), ((), ())),
            preferred_element_type=F32,
        )
    row = lax.broadcasted_iota(jnp.int32, (size, size), 0) % 8
    total = jnp.where(row == lane_index((size, size)) % 8, total, 0.0)
    return exact_dot(jnp.sum(total.reshape(channels, 8, size), axis=1), sum_ref[...])


def late_cell_kernel(
    inv_y, inv_z0, inv_z1, table_z, table_y, sum_ref, modes_ref, pre_ref, cot_ref, early_ref,
    slope_hbm, field_hbm, _, act_ref, out_ref, field_ref, slope_ref, sems, *, channels, count, rows, owners,
):
    step = pl.program_id(0)
    early = early_count(channels)
    late = channels - early
    copies = [
        pltpu.make_async_copy(field_hbm, field_ref, sems.at[0]),
        pltpu.make_async_copy(slope_hbm, slope_ref.at[pl.ds(0, early)], sems.at[1]),
    ]

    @pl.when(step == 0)
    def _():
        for copy in copies:
            copy.start()

    first = early + step * count
    slopes = cell_group(
        inv_y[...], (inv_z0[...], inv_z1[...]), modes_ref, pre_ref, cot_ref, act_ref, first, count, channels
    )
    for q in range(count):
        slope_ref[first + q] = slopes[q]
    forward_group(slopes, table_z[...], table_y[...], out_ref, step * count, rows)

    @pl.when(step == pl.num_programs(0) - 1)
    def _():
        for copy in copies:
            copy.wait()
        point = point_gradient(field_ref, slope_ref, sum_ref, channels)
        packed = jnp.concatenate([point[8 * q : 8 * q + 8] for q in range(channels // 8)], axis=1)
        zero_mode = jnp.concatenate([early_ref[0:early, 0:1], out_ref[0:late, 0:1]], axis=0)
        eye = lax.broadcasted_iota(jnp.int32, (channels, LANES), 0) == lane_index((channels, LANES))
        bias = jnp.sum(jnp.where(eye, jnp.broadcast_to(zero_mode, (channels, LANES)), 0.0), axis=0, keepdims=True)
        extra = jnp.where(lax.broadcasted_iota(jnp.int32, (8, LANES), 0) == 0, jnp.broadcast_to(bias, (8, LANES)), 0.0)
        for d in range(owners):
            out_ref[d * rows + late : d * rows + late + 8, :] = packed
            out_ref[d * rows + late + 8 : (d + 1) * rows, :] = extra


def early_count(channels):
    return channels * 3 // 4


def early_cells(inverse, forward, modes, pre, cotangent):
    channels = pre.shape[0]
    owners = MY // 2
    early = early_count(channels)
    block = pl.BlockSpec((EARLY_STEP, NY, NZ), lambda s: (s, 0, 0))
    tables = (*inverse, *forward)
    act, slope, out = pl.pallas_call(
        functools.partial(early_cell_kernel, channels=channels, count=EARLY_STEP, rows=early),
        grid=(early // EARLY_STEP,),
        in_specs=[full(t.shape) for t in tables] + [full((owners * channels, LANES)), block, block],
        out_specs=[block, block, full((owners * early, LANES))],
        out_shape=[
            pltpu.HBM((channels, NY, NZ), BF16),
            pltpu.HBM((early, NY, NZ), F32),
            pltpu.VMEM((owners * early, LANES), F32),
        ],
        compiler_params=params(LIMIT),
        cost_estimate=pl.CostEstimate(flops=3 * 10**9, bytes_accessed=7 * MIB, transcendentals=10**6),
        name="early_cells",
    )(*in_hbm(*tables), *in_vmem(modes.reshape(owners * channels, LANES)), *in_hbm(pre, cotangent))
    return act, slope, out.reshape(owners, early, LANES)


def late_cells(inverse, forward, summing, modes, pre, cotangent, field, early, slope, act):
    channels = field.shape[0]
    owners = MY // 2
    first = early_count(channels)
    rows = channels - first + 16
    start = first // STEP
    block = pl.BlockSpec((STEP, NY, NZ), lambda s: (start + s, 0, 0))
    anywhere = pl.BlockSpec(memory_space=pl.ANY)
    tables = (*inverse, *forward, summing)
    act, out = pl.pallas_call(
        functools.partial(late_cell_kernel, channels=channels, count=STEP, rows=rows, owners=owners),
        grid=((channels - first) // STEP,),
        in_specs=[full(t.shape) for t in tables]
        + [full((owners * channels, LANES)), block, block, full((owners * first, LANES))]
        + [anywhere] * 3,
        out_specs=[block, full((owners * rows, LANES))],
        out_shape=[
            pltpu.HBM((channels, NY, NZ), BF16),
            pltpu.VMEM((owners * rows, LANES), F32),
        ],
        scratch_shapes=[
            pltpu.VMEM((channels, NY, NZ), F32),
            pltpu.VMEM((channels, NY, NZ), F32),
            pltpu.SemaphoreType.DMA((2,)),
        ],
        input_output_aliases={len(tables) + 6: 0},
        compiler_params=params(LIMIT),
        cost_estimate=pl.CostEstimate(flops=6 * 10**9, bytes_accessed=11 * MIB, transcendentals=10**6),
        name="late_cells",
    )(
        *in_hbm(*tables),
        *in_vmem(modes.reshape(owners * channels, LANES)),
        *in_hbm(pre, cotangent),
        *in_vmem(early.reshape(owners * first, LANES)),
        *in_hbm(slope, field, act),
    )
    return act, out.reshape(owners, rows, LANES)


def gradient_kernel(cos_ref, sin_ref, spec_ref, lines_ref, *refs, points, channels, unique, copies, norm, first, outputs, slots):
    last = first > 0
    if last:
        _, out_hbm, point_ref, bias_ref, sums_ref, real_ref, imag_ref, buffer, sems = refs
    else:
        out_hbm, sums_ref, real_ref, imag_ref, buffer, sems = refs
    halve_lines(lines_ref, sums_ref, points, outputs)
    half = LANES // 2
    lane = lane_index((outputs, LANES))
    scale = jnp.where(lane % MZ == 0, norm, 2.0 * norm)

    def writes(at, slot):
        return [
            pltpu.make_async_copy(
                buffer.at[slot, c],
                out_hbm.at[c, at + r * unique, :, pl.ds(first, outputs), :],
                sems.at[slot, c, r],
            )
            for r in range(copies)
            for c in range(2)
        ]

    @pl.loop(0, unique // slots)
    def _(turn):
        for slot in range(slots):
            at = slots * turn + slot

            @pl.when(turn > 0)
            def _():
                for copy in writes(at - slots, slot):
                    copy.wait()

            slope = scale * spectrum_row(cos_ref, sin_ref, sums_ref, at, slot % 2, points // 2)
            other = roll(slope, 64)
            flipped = jnp.where(lane < half, other, -other)
            real_ref[slot], imag_ref[slot] = doubled(spec_ref[at])
            for i in range(channels):
                both = real_ref[slot, pl.ds(i, 1), :] * slope + imag_ref[slot, pl.ds(i, 1), :] * flipped
                buffer[slot, 0, i] = both[:, :half]
                buffer[slot, 1, i] = both[:, half:]
            for copy in writes(at, slot):
                copy.start()

    if last:
        packed = lines_ref[0, outputs : outputs + 16, :]
        for x in range(1, points):
            packed += lines_ref[x, outputs : outputs + 16, :]
        packed = norm * packed
        for q in range(channels // 8):
            point_ref[8 * q : 8 * q + 8, :] = packed[:8, q * channels : (q + 1) * channels]
        bias_ref[...] = packed[8:9, :channels]

    for at in range(unique - slots, unique):
        for copy in writes(at, at % slots):
            copy.wait()


def gradient(cos_x, sin_x, spectrum, lines, norm, kept_x, before=()):
    points, rows, _ = lines.shape
    unique, channels, _ = spectrum.shape
    half = LANES // 2
    copies = kept_x // unique
    first = early_count(channels) if before else 0
    outputs = channels - first if before else early_count(channels)
    slots = 8
    anywhere = pl.BlockSpec(memory_space=pl.ANY)
    shape = jax.ShapeDtypeStruct((2, kept_x, channels, channels, half), F32)
    sums = [(channels, channels), (1, channels)] if before else []
    return pl.pallas_call(
        functools.partial(
            gradient_kernel, points=points, channels=channels, unique=unique, copies=copies, norm=norm,
            first=first, outputs=outputs, slots=slots,
        ),
        in_specs=[smem(), smem(), full(spectrum.shape), full(lines.shape)] + [anywhere] * len(before),
        out_specs=[anywhere] + [full(each) for each in sums],
        out_shape=[shape] + [jax.ShapeDtypeStruct(each, F32) for each in sums],
        scratch_shapes=[
            pltpu.VMEM((2, 2, points // 2, outputs, LANES), F32),
            pltpu.VMEM((slots, channels, LANES), F32),
            pltpu.VMEM((slots, channels, LANES), F32),
            pltpu.VMEM((slots, 2, channels, outputs, half), F32),
            pltpu.SemaphoreType.DMA((slots, 2, copies)),
        ],
        input_output_aliases={4: 0} if before else {},
        compiler_params=params(LIMIT),
        cost_estimate=pl.CostEstimate(flops=5 * 10**6, bytes_accessed=32 * MIB, transcendentals=0),
        name="weight_gradient",
    )(cos_x, sin_x, *in_vmem(spectrum, lines), *before)


def swap(lines):
    return lax.all_to_all(lines, "space", split_axis=0, concat_axis=0, tiled=True)


def suits(width_x, length_x, devices, channels, weights):
    held = weights.shape[2]
    even = np.array_equal(kept(MX, length_x) % length_x, np.arange(MX) % length_x)
    return (
        width_x == 1
        and held == 2 * MZ
        and devices * 2 == MY
        and 2 * held == LANES
        and MX % length_x == 0
        and length_x % 8 == 0
        and even
        and channels == MZ
    )


def body(lifted_field, cotangent, spectral_weights, point_weights, point_bias):
    devices = lax.axis_size("space")
    channels, width_x = lifted_field.shape[:2]
    length_x = width_x * devices
    if not suits(width_x, length_x, devices, channels, spectral_weights):
        return general_body(lifted_field, cotangent, spectral_weights, point_weights, point_bias)
    norm = float(length_x * NY * NZ) ** -0.5
    theta = angles(np.arange(length_x), np.arange(length_x), length_x)
    cos_x, sin_x = jnp.asarray(np.cos(theta), F32), jnp.asarray(np.sin(theta), F32)
    forward = forward_tables()
    inverse = inverse_tables(norm)
    summing = jnp.asarray(np.repeat(np.eye(channels), 8, axis=0), F32)

    field = lifted_field.reshape(channels, NY, NZ)
    slopes_in = cotangent.reshape(channels, NY, NZ)
    weights = jnp.transpose(spectral_weights, (0, 1, 3, 4, 2))

    lines, some = forward_modes(field, forward, weights, length_x)
    lines = swap(lines)
    folded = fold_rest(weights, some, length_x)
    spectrum, mixed = mix(cos_x, sin_x, lines, folded, norm)
    field_late, mixed = lax.optimization_barrier((field, mixed))
    modes = swap(mixed)
    pre = pointwise(field_late, summing, point_weights, point_bias)
    act, slope, early = early_cells(inverse, forward, modes, pre, slopes_in)
    early_lines = swap(early)
    activated, late = late_cells(inverse, forward, summing, modes, pre, slopes_in, field, early, slope, act)
    late_lines = swap(late)
    (grad,) = gradient(cos_x, sin_x, spectrum, early_lines, norm, MX)
    grad, grad_point, grad_bias = gradient(cos_x, sin_x, spectrum, late_lines, norm, MX, (grad,))
    return (
        activated.reshape(cotangent.shape),
        jnp.transpose(grad, (0, 1, 4, 2, 3)),
        grad_point,
        grad_bias.reshape(channels),
    )


HIGHEST = lax.Precision.HIGHEST


def trig_tables(positions, frequency, length):
    product = positions[:, None] * frequency[None, :] % length
    phase_angle = 2.0 * jnp.pi / length * product.astype(jnp.float32)
    return (jnp.cos(phase_angle), jnp.sin(phase_angle))


def kept_frequencies(kept_count, length):
    mode_index = jnp.arange(kept_count, dtype=jnp.int32)
    return jnp.where(mode_index < kept_count // 2, mode_index, length - kept_count + mode_index)


def forward_local(field_in):
    channels = field_in.shape[0]
    width_x = field_in.shape[1]
    cos_z, sin_z = trig_tables(jnp.arange(NZ, dtype=jnp.int32), jnp.arange(MZ, dtype=jnp.int32), NZ)
    table_z = jnp.concatenate([cos_z, -sin_z], axis=1)
    along_z = jnp.einsum("cxyz,zk->cxyk", field_in, table_z, precision=HIGHEST)
    z_real = along_z[..., :MZ]
    z_imag = along_z[..., MZ:]
    cos_y, sin_y = trig_tables(jnp.arange(NY, dtype=jnp.int32), kept_frequencies(MY, NY), NY)
    y_real = jnp.einsum("cxyk,yj->xcjk", z_real, cos_y, precision=HIGHEST) + jnp.einsum(
        "cxyk,yj->xcjk", z_imag, sin_y, precision=HIGHEST
    )
    y_imag = jnp.einsum("cxyk,yj->xcjk", z_imag, cos_y, precision=HIGHEST) - jnp.einsum(
        "cxyk,yj->xcjk", z_real, sin_y, precision=HIGHEST
    )
    stacked = jnp.stack([y_real, y_imag], axis=1)
    return stacked.reshape(width_x, 2, channels, MY * MZ)


def transform_x(x_lines):
    length_x = x_lines.shape[0]
    cos_x, sin_x = trig_tables(
        jnp.arange(length_x, dtype=jnp.int32), kept_frequencies(MX, length_x), length_x
    )
    norm_scale = 1.0 / float(length_x * NY * NZ) ** 0.5
    part_real = x_lines[:, 0]
    part_imag = x_lines[:, 1]
    x_real = jnp.einsum("xcm,xk->kcm", part_real, cos_x, precision=HIGHEST) + jnp.einsum(
        "xcm,xk->kcm", part_imag, sin_x, precision=HIGHEST
    )
    x_imag = jnp.einsum("xcm,xk->kcm", part_imag, cos_x, precision=HIGHEST) - jnp.einsum(
        "xcm,xk->kcm", part_real, sin_x, precision=HIGHEST
    )
    return norm_scale * jnp.stack([x_real, x_imag], axis=1)


def mix_modes(spectrum, weights):
    spec_real = spectrum[:, 0]
    spec_imag = spectrum[:, 1]
    out_real = jnp.einsum("kim,kmio->kom", spec_real, weights[0], precision=HIGHEST) - jnp.einsum(
        "kim,kmio->kom", spec_imag, weights[1], precision=HIGHEST
    )
    out_imag = jnp.einsum("kim,kmio->kom", spec_real, weights[1], precision=HIGHEST) + jnp.einsum(
        "kim,kmio->kom", spec_imag, weights[0], precision=HIGHEST
    )
    return jnp.stack([out_real, out_imag], axis=1)


def inverse_x(spectrum, positions, length_x):
    cos_x, sin_x = trig_tables(positions, kept_frequencies(MX, length_x), length_x)
    spec_real = spectrum[:, 0]
    spec_imag = spectrum[:, 1]
    a_real = jnp.einsum("kcm,xk->xcm", spec_real, cos_x, precision=HIGHEST) - jnp.einsum(
        "kcm,xk->xcm", spec_imag, sin_x, precision=HIGHEST
    )
    a_imag = jnp.einsum("kcm,xk->xcm", spec_imag, cos_x, precision=HIGHEST) + jnp.einsum(
        "kcm,xk->xcm", spec_real, sin_x, precision=HIGHEST
    )
    return jnp.stack([a_real, a_imag], axis=1)


def inverse_yz(x_lines, length_x):
    width_x = x_lines.shape[0]
    channels = x_lines.shape[2]
    mode_grid = x_lines.reshape(width_x, 2, channels, MY, MZ)
    cos_y, sin_y = trig_tables(jnp.arange(NY, dtype=jnp.int32), kept_frequencies(MY, NY), NY)
    b_real = jnp.einsum("xcjk,yj->cxyk", mode_grid[:, 0], cos_y, precision=HIGHEST) - jnp.einsum(
        "xcjk,yj->cxyk", mode_grid[:, 1], sin_y, precision=HIGHEST
    )
    b_imag = jnp.einsum("xcjk,yj->cxyk", mode_grid[:, 1], cos_y, precision=HIGHEST) + jnp.einsum(
        "xcjk,yj->cxyk", mode_grid[:, 0], sin_y, precision=HIGHEST
    )
    cos_z, sin_z = trig_tables(jnp.arange(NZ, dtype=jnp.int32), jnp.arange(MZ, dtype=jnp.int32), NZ)
    weight_z = jnp.where(jnp.arange(MZ, dtype=jnp.int32) == 0, 1.0, 2.0).astype(jnp.float32)
    table_z = jnp.concatenate([cos_z * weight_z[None, :], -sin_z * weight_z[None, :]], axis=1)
    stacked = jnp.concatenate([b_real, b_imag], axis=-1)
    result = jnp.einsum("cxyk,zk->cxyz", stacked, table_z, precision=HIGHEST)
    return result * (1.0 / float(length_x * NY * NZ) ** 0.5)


def gelu_slope(values):
    return (
        0.5 * (1.0 + lax.erf(values * INV_SQRT_TWO))
        + values * jnp.exp(-0.5 * values * values) * INV_SQRT_TWO_PI
    )


def weight_gradient(spectrum, slope_modes, first_mode):
    mode_ids = first_mode + jnp.arange(spectrum.shape[3], dtype=jnp.int32)
    weight_modes = jnp.where(mode_ids % MZ == 0, 1.0, 2.0).astype(jnp.float32)
    grad_real = jnp.einsum(
        "kim,kom->kmio", spectrum[:, 0], slope_modes[:, 0], precision=HIGHEST
    ) + jnp.einsum("kim,kom->kmio", spectrum[:, 1], slope_modes[:, 1], precision=HIGHEST)
    grad_imag = jnp.einsum(
        "kim,kom->kmio", spectrum[:, 0], slope_modes[:, 1], precision=HIGHEST
    ) - jnp.einsum("kim,kom->kmio", spectrum[:, 1], slope_modes[:, 0], precision=HIGHEST)
    stacked = jnp.stack([grad_real, grad_imag], axis=0)
    return stacked * weight_modes[None, None, :, None, None]


def to_modes(field_in):
    return transform_x(
        lax.all_to_all(forward_local(field_in), "space", split_axis=3, concat_axis=0, tiled=True)
    )


def general_body(lifted_field, cotangent, spectral_weights, point_weights, point_bias):
    devices = lax.axis_size("space")
    width_x = lifted_field.shape[1]
    length_x = width_x * devices
    spectrum = to_modes(lifted_field)
    mixed_modes = mix_modes(spectrum, spectral_weights)
    full_lines = inverse_x(mixed_modes, jnp.arange(length_x, dtype=jnp.int32), length_x)
    spectral = inverse_yz(
        lax.all_to_all(full_lines, "space", split_axis=0, concat_axis=3, tiled=True), length_x
    )
    pointwise = (
        jnp.einsum("ixyz,io->oxyz", lifted_field, point_weights, precision=HIGHEST)
        + point_bias[:, None, None, None]
    )
    before = spectral + pointwise
    activated = jax.nn.gelu(before, approximate=False).astype(jnp.bfloat16)
    slope_field = cotangent.astype(jnp.float32) * gelu_slope(before)
    local_point = jnp.einsum("ixyz,oxyz->io", lifted_field, slope_field, precision=HIGHEST)
    local_bias = jnp.sum(slope_field, axis=(1, 2, 3))
    partial = jnp.concatenate([local_point, local_bias[None, :]], axis=0)
    gathered = lax.all_gather(partial, "space", axis=0, tiled=False)
    summed = jnp.sum(gathered, axis=0)
    summed_point, summed_bias = summed[:-1], summed[-1]
    root_cells = float(length_x * NY * NZ) ** 0.5
    slope_spectrum = to_modes(slope_field)
    first_mode = lax.axis_index("space") * spectrum.shape[3]
    grad_spectral = weight_gradient(spectrum, slope_spectrum, first_mode)
    return (activated, grad_spectral, summed_point / root_cells, summed_bias / root_cells)


def solution(mesh):
    placed = (
        P("groups", "space", None, None),
        P("groups", "space", None, None),
        P(None, None, "space", None, None),
        P(),
        P(),
    )
    return jax.shard_map(
        body,
        mesh=mesh,
        in_specs=placed,
        out_specs=(
            P("groups", "space", None, None),
            P("groups", None, "space", None, None),
            P("groups", None),
            P("groups"),
        ),
        check_vma=False,
    )
```

```python
import functools

import jax
import jax.numpy as jnp
import ml_dtypes
import numpy as np
from jax import lax
from jax.experimental import pallas as pl
from jax.experimental.pallas import tpu as pltpu
from jax.sharding import PartitionSpec as P

MX = 32
MY = 32
MZ = 32
NY = 128
NZ = 256

F32 = jnp.float32
BF16 = jnp.bfloat16
INV_SQRT_TWO = 0.7071067811865476
INV_SQRT_TWO_PI = 0.3989422804014327
MIB = 1 << 20
LIMIT = 48
LANES = 128
GROUP = 4
EARLY_STEP = 12
STEP = 8


def kept(kept_count, length):
    index = np.arange(kept_count)
    return np.where(index < kept_count // 2, index, length - kept_count + index)


def angles(positions, frequency, length):
    product = positions[:, None] * frequency[None, :] % length
    return 2.0 * np.pi / length * product


def split_table(table):
    high = table.astype(ml_dtypes.bfloat16)
    return high, (table - high.astype(np.float64)).astype(ml_dtypes.bfloat16)


def lane_spread(first, second, real_table, imag_table):
    return np.concatenate(
        [real_table * first, real_table * second, imag_table * first, imag_table * second], axis=1
    )


def forward_tables():
    theta = angles(np.arange(NZ), np.arange(MZ), NZ)
    table = np.concatenate([lane_spread(f, s, np.cos(theta), -np.sin(theta)) for f, s in ((1, 0), (0, 1))], axis=0)
    high, low = split_table(table)
    table_z = np.concatenate(
        [np.concatenate([high, low], axis=1), np.concatenate([high, np.zeros_like(low)], axis=1)], axis=0
    )
    theta = angles(np.arange(NY), kept(MY, NY), NY).T
    table = np.concatenate([np.cos(theta)[0::2], np.cos(theta)[1::2], np.sin(theta)[0::2], np.sin(theta)[1::2]], axis=0)
    high, low = split_table(table)
    table_y = np.concatenate(
        [np.concatenate([high, high], axis=1), np.concatenate([low, np.zeros_like(low)], axis=1)], axis=0
    )
    return table_z, table_y


def inverse_tables(norm):
    theta = angles(np.arange(NY), kept(MY, NY), NY)
    cos_y, sin_y = np.cos(theta), np.sin(theta)
    table_y = np.concatenate([cos_y[:, 0::2], cos_y[:, 1::2], sin_y[:, 0::2], sin_y[:, 1::2]], axis=1)
    y_high, y_low = split_table(table_y)
    theta = angles(np.arange(NZ), np.arange(MZ), NZ)
    weight = np.where(np.arange(MZ) == 0, 1.0, 2.0) * norm
    parts = (np.cos(theta) * weight, -np.sin(theta) * weight)
    own, other = lane_spread(1, 0, *parts).T, lane_spread(0, 1, *parts).T
    tables_z = []
    for mine, theirs in ((own, other), (other, own)):
        high = split_table(mine)[0]
        tables_z.append(np.concatenate([high, high + split_table(theirs)[1]], axis=0))
    return np.concatenate([y_high, y_high, y_low], axis=1), *tables_z


def dot(left, right):
    return jnp.dot(left, right, preferred_element_type=F32)


def split(values):
    high = values.astype(BF16)
    return high, (values - high.astype(F32)).astype(BF16)


def lane_index(shape):
    return lax.broadcasted_iota(jnp.int32, shape, len(shape) - 1)


def roll(values, shift):
    return pltpu.roll(values, shift % LANES, len(values.shape) - 1)


def forward_group(fields, table_z, table_y, out_ref, first, rows):
    left = jnp.concatenate(
        [jnp.concatenate([fields[q], fields[q + 1]], axis=1) for q in range(0, len(fields), 2)], axis=0
    )
    lines = dot(jnp.concatenate(split(left), axis=1), table_z)
    lines = lines[:, :LANES] + lines[:, LANES:]
    half = MY // 2
    for g in range(0, len(fields) // 2, GROUP // 2):
        quad = jnp.concatenate([lines[q * NY : (q + 1) * NY] for q in range(g, g + GROUP // 2)], axis=1)
        wide = dot(table_y, jnp.concatenate(split(quad), axis=0))
        wide = wide[: 2 * MY] + wide[2 * MY :]
        for q in range(GROUP // 2):
            by_cos = wide[:MY, q * LANES : (q + 1) * LANES]
            by_sin = roll(wide[MY:, q * LANES : (q + 1) * LANES], 64)
            modes = by_cos + jnp.where(lane_index(by_sin.shape) < LANES // 2, by_sin, -by_sin)
            even, odd = modes[:half], modes[half:]
            at_even = (lane_index(even.shape) // MZ) % 2 == 0
            at = first + 2 * (g + q)
            out_ref[pl.ds(at, half, stride=rows), :] = jnp.where(at_even, even, roll(odd, MZ))
            out_ref[pl.ds(at + 1, half, stride=rows), :] = jnp.where(at_even, roll(even, -MZ), odd)


def inverse_y_group(modes_ref, y_table, first, rows):
    half = MY // 2
    pairs = []
    for q in range(GROUP // 2):
        c0 = modes_ref[pl.ds(first + 2 * q, half, stride=rows), :]
        c1 = modes_ref[pl.ds(first + 2 * q + 1, half, stride=rows), :]
        at_even = (lane_index(c0.shape) // MZ) % 2 == 0
        even = jnp.where(at_even, c0, roll(c1, MZ))
        odd = jnp.where(at_even, roll(c0, -MZ), c1)
        both = jnp.concatenate([even, odd], axis=0)
        other = roll(both, 64)
        turned = jnp.where(lane_index(both.shape) < LANES // 2, -other, other)
        pairs.append(jnp.concatenate([both, turned], axis=0))
    high, low = split(jnp.concatenate(pairs, axis=1))
    lines = dot(y_table, jnp.concatenate([high, low, high], axis=0))
    return [lines[:, q * LANES : (q + 1) * LANES] for q in range(GROUP // 2)]


def in_hbm(*arrays):
    return [pltpu.with_memory_space_constraint(each, pltpu.HBM) for each in arrays]


def in_vmem(*arrays):
    return [pltpu.with_memory_space_constraint(each, pltpu.VMEM) for each in arrays]


def full(shape):
    return pl.BlockSpec(shape, lambda *_: (0,) * len(shape))


def params(limit):
    return pltpu.CompilerParams(vmem_limit_bytes=limit * MIB)


def fold_block(pieces, out_ref, at):
    copies = pieces.shape[0]
    real, imag = pieces[0, 0], pieces[0, 1]
    for r in range(1, copies):
        real, imag = real + pieces[r, 0], imag + pieces[r, 1]
    modes = real.shape[-1]
    out_ref[at, :, :, :modes] = real
    out_ref[at, :, :, modes:] = imag


def fetches(weights_hbm, ring_ref, sems, at, slot, unique):
    copies = ring_ref.shape[1]
    return [
        pltpu.make_async_copy(weights_hbm.at[c, at + r * unique], ring_ref.at[slot, r, c], sems.at[slot, r, c])
        for r in range(copies)
        for c in range(2)
    ]


def fold_shapes(weights, unique, slots):
    copies = weights.shape[1] // unique
    shape = (unique,) + weights.shape[2:4] + (2 * weights.shape[4],)
    ring = [pltpu.VMEM((slots, copies, 2) + weights.shape[2:], F32), pltpu.SemaphoreType.DMA((slots, copies, 2))]
    return pltpu.HBM(shape, F32), ring


def forward_kernel(
    table_z, table_y, field_ref, weights_hbm, out_ref, folded_ref, ring_ref, sems,
    *, channels, step_channels, per_step, unique, slots,
):
    step = pl.program_id(0)

    def transform():
        fields = [field_ref[q] for q in range(step_channels)]
        forward_group(fields, table_z[...], table_y[...], out_ref, step * step_channels, channels)

    folding = (step > 0) & (step <= slots // per_step)

    @pl.when(step == 0)
    def _():
        for at in range(slots):
            for copy in fetches(weights_hbm, ring_ref, sems, at, at, unique):
                copy.start()

    @pl.when(jnp.logical_not(folding))
    def _():
        transform()

    @pl.when(folding)
    def _():
        for q in range(per_step):
            at = (step - 1) * per_step + q
            for copy in fetches(weights_hbm, ring_ref, sems, at, at, unique):
                copy.wait()
            fold_block(ring_ref.at[at], folded_ref, q)
        transform()


FOLD_STEP = 2
FIELD_STEP = 8


def folded_early(channels):
    return (channels // FIELD_STEP - 2) * FOLD_STEP


def forward_modes(field, tables, weights, unique):
    channels = field.shape[0]
    slots = folded_early(channels)
    folded_shape, ring = fold_shapes(weights, unique, slots)
    owners = MY // 2
    out, some = pl.pallas_call(
        functools.partial(
            forward_kernel, channels=channels, step_channels=FIELD_STEP, per_step=FOLD_STEP, unique=unique, slots=slots
        ),
        grid=(channels // FIELD_STEP,),
        in_specs=[full(t.shape) for t in tables]
        + [pl.BlockSpec((FIELD_STEP, NY, NZ), lambda s: (s, 0, 0)), pl.BlockSpec(memory_space=pl.ANY)],
        out_specs=[
            full((owners * channels, LANES)),
            pl.BlockSpec((FOLD_STEP,) + folded_shape.shape[1:], lambda s: (jnp.clip(s - 1, 0, slots // FOLD_STEP - 1), 0, 0, 0)),
        ],
        out_shape=[pltpu.VMEM((owners * channels, LANES), F32), folded_shape],
        scratch_shapes=ring,
        compiler_params=params(LIMIT),
        cost_estimate=pl.CostEstimate(flops=2 * 10**9, bytes_accessed=22 * MIB, transcendentals=0),
        name="forward_yz",
    )(*in_hbm(*tables, field, weights))
    return out.reshape(owners, channels, LANES), some


def fold_kernel(weights_hbm, _, out_ref, ring_ref, sems, *, first, unique, slots):
    step = pl.program_id(0)

    def fetch(turn):
        slot = turn % slots
        return [
            copy
            for q in range(FOLD_STEP)
            for copy in fetches(weights_hbm, ring_ref, sems, first + turn * FOLD_STEP + q, slot * FOLD_STEP + q, unique)
        ]

    @pl.when(step == 0)
    def _():
        for ahead in range(slots):
            for copy in fetch(ahead):
                copy.start()

    for copy in fetch(step):
        copy.wait()
    for q in range(FOLD_STEP):
        fold_block(ring_ref.at[step % slots * FOLD_STEP + q], out_ref, q)

    @pl.when(step + slots < pl.num_programs(0))
    def _():
        for copy in fetch(step + slots):
            copy.start()


def fold_rest(weights, some, unique):
    first = folded_early(weights.shape[2])
    steps = (unique - first) // FOLD_STEP
    slots = min(3, steps)
    folded_shape, ring = fold_shapes(weights, unique, slots * FOLD_STEP)
    anywhere = pl.BlockSpec(memory_space=pl.ANY)
    return pl.pallas_call(
        functools.partial(fold_kernel, first=first, unique=unique, slots=slots),
        grid=(steps,),
        in_specs=[anywhere, anywhere],
        out_specs=pl.BlockSpec((FOLD_STEP,) + folded_shape.shape[1:], lambda s: (first // FOLD_STEP + s, 0, 0, 0)),
        out_shape=folded_shape,
        scratch_shapes=ring,
        input_output_aliases={1: 0},
        compiler_params=params(LIMIT),
        cost_estimate=pl.CostEstimate(flops=4 * 10**6, bytes_accessed=30 * MIB, transcendentals=0),
        name="fold_weights",
    )(*in_hbm(weights, some))


def halve_lines(lines_ref, sums_ref, points, channels):
    half = points // 2
    sign = jnp.where(lane_index((channels, LANES)) < LANES // 2, 1.0, -1.0)
    for x in range(half):
        near, far = lines_ref[x, :channels], lines_ref[x + half, :channels]
        for parity, value in enumerate((near + far, near - far)):
            sums_ref[parity, 0, x] = value
            sums_ref[parity, 1, x] = sign * roll(value, 64)


def spectrum_row(cos_ref, sin_ref, sums_ref, at, parity, half):
    total = cos_ref[at, 0] * sums_ref[parity, 0, 0] + sin_ref[at, 0] * sums_ref[parity, 1, 0]
    for x in range(1, half):
        total += cos_ref[at, x] * sums_ref[parity, 0, x] + sin_ref[at, x] * sums_ref[parity, 1, x]
    return total


def doubled(values):
    other = roll(values, 64)
    low = lane_index(values.shape) < LANES // 2
    return jnp.where(low, values, other), jnp.where(low, other, values)


def mix_kernel(
    cos_ref, sin_ref, lines_ref, weights_ref, spec_ref, out_ref, sums_ref, total_ref, real_ref, imag_ref,
    *, points, channels, per_step, norm,
):
    step = pl.program_id(0)
    half = points // 2

    @pl.when(step == 0)
    def _():
        halve_lines(lines_ref, sums_ref, points, channels)
        total_ref[...] = jnp.zeros_like(total_ref)

    low = lane_index((channels, LANES)) < LANES // 2
    for q in range(per_step):
        at = step * per_step + q
        parity = q % 2
        spec = norm * spectrum_row(cos_ref, sin_ref, sums_ref, at, parity, half)
        spec_ref[q] = spec
        real_ref[q], imag_ref[q] = doubled(spec)
        by_real = jnp.zeros((channels, LANES), F32)
        by_imag = jnp.zeros((channels, LANES), F32)
        for i in range(channels):
            weight = weights_ref[q, i]
            by_real += real_ref[q, pl.ds(i, 1), :] * weight
            by_imag += imag_ref[q, pl.ds(i, 1), :] * weight
        other = roll(by_imag, 64)
        mixed = by_real + jnp.where(low, -other, other)
        other = roll(mixed, 64)
        turned = jnp.where(low, -other, other)
        for x in range(half):
            total_ref[parity, x] += cos_ref[at, x] * mixed + sin_ref[at, x] * turned

    @pl.when(step == pl.num_programs(0) - 1)
    def _():
        for x in range(half):
            out_ref[x] = total_ref[0, x] + total_ref[1, x]
            out_ref[x + half] = total_ref[0, x] - total_ref[1, x]


def smem():
    return pl.BlockSpec(memory_space=pltpu.SMEM)


def mix(cos_x, sin_x, lines, weights, norm):
    points, channels, _ = lines.shape
    unique = weights.shape[0]
    per_step = min(unique, 8)
    shape = (points, channels, LANES)
    return pl.pallas_call(
        functools.partial(mix_kernel, points=points, channels=channels, per_step=per_step, norm=norm),
        grid=(unique // per_step,),
        in_specs=[
            smem(),
            smem(),
            full(shape),
            pl.BlockSpec((per_step,) + weights.shape[1:], lambda s: (s, 0, 0, 0)),
        ],
        out_specs=[
            pl.BlockSpec((per_step, channels, LANES), lambda s: (s, 0, 0)),
            full(shape),
        ],
        out_shape=[
            pltpu.VMEM((unique, channels, LANES), F32),
            pltpu.VMEM(shape, F32),
        ],
        scratch_shapes=[
            pltpu.VMEM((2, 2, points // 2, channels, LANES), F32),
            pltpu.VMEM((2, points // 2, channels, LANES), F32),
            pltpu.VMEM((per_step, channels, LANES), F32),
            pltpu.VMEM((per_step, channels, LANES), F32),
        ],
        compiler_params=params(LIMIT),
        cost_estimate=pl.CostEstimate(flops=2 * 10**7, bytes_accessed=9 * MIB, transcendentals=0),
        name="mix_modes",
    )(cos_x, sin_x, *in_vmem(lines), *in_hbm(weights))


def exact_dot(left, right):
    return jnp.dot(left, right, precision=lax.Precision.HIGHEST, preferred_element_type=F32)


def pointwise_kernel(sum_ref, turned_ref, bias_in_ref, field_ref, out_ref, mixer_ref, bias_ref, *, channels, blocks):
    size = 8 * channels

    @pl.when(pl.program_id(0) == 0)
    def _():
        wide = exact_dot(sum_ref[...], turned_ref[...])
        wide = lax.dot_general(
            wide, sum_ref[...], (((1,), (1,)), ((), ())), precision=lax.Precision.HIGHEST, preferred_element_type=F32
        )
        row = lax.broadcasted_iota(jnp.int32, (size, size), 0) % 8
        high, low = split(jnp.where(row == lane_index((size, size)) % 8, wide, 0.0))
        mixer_ref[:size] = high
        mixer_ref[size:] = low
        bias_ref[...] = exact_dot(sum_ref[...], bias_in_ref[...])

    for b in range(blocks):
        high, low = split(field_ref[:, 8 * b : 8 * b + 8, :].reshape(size, NZ))
        wide = dot(mixer_ref[...], high)
        values = wide[:size] + wide[size:] + dot(mixer_ref[:size], low) + bias_ref[...]
        out_ref[:, 8 * b : 8 * b + 8, :] = values.reshape(channels, 8, NZ)


def pointwise(field, summing, point_weights, point_bias):
    channels = field.shape[0]
    blocks = 2
    turned = point_weights.T
    bias = point_bias[:, None]
    size = 8 * channels
    block = pl.BlockSpec((channels, 8 * blocks, NZ), lambda s: (0, s, 0))
    return pl.pallas_call(
        functools.partial(pointwise_kernel, channels=channels, blocks=blocks),
        grid=(NY // (8 * blocks),),
        in_specs=[full(summing.shape), full(turned.shape), full(bias.shape), block],
        out_specs=block,
        out_shape=pltpu.HBM(field.shape, F32),
        scratch_shapes=[pltpu.VMEM((2 * size, size), BF16), pltpu.VMEM((size, 1), F32)],
        compiler_params=params(LIMIT),
        cost_estimate=pl.CostEstimate(flops=4 * 10**9, bytes_accessed=24 * MIB, transcendentals=0),
        name="pointwise",
    )(*in_hbm(summing, turned, bias, field))


def cell_group(inv_y, inv_z, modes_ref, pre_ref, cot_ref, act_ref, first, count, channels):
    lines = []
    for g in range(0, count, GROUP):
        lines += inverse_y_group(modes_ref, inv_y, first + g, channels)
    lines = jnp.concatenate(lines, axis=0)
    high = lines.astype(BF16).astype(F32)
    low = lines - high
    at_even = (lane_index(lines.shape) // MZ) % 2 == 0
    spectral = [
        dot(jnp.concatenate([high, side], axis=1).astype(BF16), table)
        for side, table in zip((jnp.where(at_even, low, roll(high, MZ)), jnp.where(at_even, roll(high, -MZ), low)), inv_z)
    ]
    slopes = []
    for q in range(count):
        before = spectral[q % 2][q // 2 * NY : (q // 2 + 1) * NY] + pre_ref[q]
        cdf = 0.5 + 0.5 * lax.erf(before * INV_SQRT_TWO)
        act_ref[q] = (before * cdf).astype(BF16)
        pdf = jnp.exp(-0.5 * before * before) * INV_SQRT_TWO_PI
        slopes.append(cot_ref[q].astype(F32) * (cdf + before * pdf))
    return slopes


def early_cell_kernel(
    inv_y, inv_z0, inv_z1, table_z, table_y, modes_ref, pre_ref, cot_ref, act_ref, slope_ref, out_ref,
    *, channels, count, rows,
):
    step = pl.program_id(0)
    slopes = cell_group(
        inv_y[...], (inv_z0[...], inv_z1[...]), modes_ref, pre_ref, cot_ref, act_ref, step * count, count, channels
    )
    for q in range(count):
        slope_ref[q] = slopes[q]
    forward_group(slopes, table_z[...], table_y[...], out_ref, step * count, rows)


def point_gradient(field_ref, slope_ref, sum_ref, channels):
    size = 8 * channels
    total = jnp.zeros((size, size), F32)
    for b in range(NY // 8):
        at = slice(8 * b, 8 * b + 8)
        f_h, f_l = split(field_ref[:, at, :].reshape(size, NZ))
        s_h, s_l = split(slope_ref[:, at, :].reshape(size, NZ))
        total += lax.dot_general(
            jnp.concatenate([f_h, f_h, f_l], axis=1),
            jnp.concatenate([s_h, s_l, s_h], axis=1),
            (((1,), (1,)), ((), ())),
            preferred_element_type=F32,
        )
    row = lax.broadcasted_iota(jnp.int32, (size, size), 0) % 8
    total = jnp.where(row == lane_index((size, size)) % 8, total, 0.0)
    return exact_dot(jnp.sum(total.reshape(channels, 8, size), axis=1), sum_ref[...])


def late_cell_kernel(
    inv_y, inv_z0, inv_z1, table_z, table_y, sum_ref, modes_ref, pre_ref, cot_ref, early_ref,
    slope_hbm, field_hbm, _, act_ref, out_ref, field_ref, slope_ref, sems, *, channels, count, rows, owners,
):
    step = pl.program_id(0)
    early = early_count(channels)
    late = channels - early
    copies = [
        pltpu.make_async_copy(field_hbm, field_ref, sems.at[0]),
        pltpu.make_async_copy(slope_hbm, slope_ref.at[pl.ds(0, early)], sems.at[1]),
    ]

    @pl.when(step == 0)
    def _():
        for copy in copies:
            copy.start()

    first = early + step * count
    slopes = cell_group(
        inv_y[...], (inv_z0[...], inv_z1[...]), modes_ref, pre_ref, cot_ref, act_ref, first, count, channels
    )
    for q in range(count):
        slope_ref[first + q] = slopes[q]
    forward_group(slopes, table_z[...], table_y[...], out_ref, step * count, rows)

    @pl.when(step == pl.num_programs(0) - 1)
    def _():
        for copy in copies:
            copy.wait()
        point = point_gradient(field_ref, slope_ref, sum_ref, channels)
        packed = jnp.concatenate([point[8 * q : 8 * q + 8] for q in range(channels // 8)], axis=1)
        zero_mode = jnp.concatenate([early_ref[0:early, 0:1], out_ref[0:late, 0:1]], axis=0)
        eye = lax.broadcasted_iota(jnp.int32, (channels, LANES), 0) == lane_index((channels, LANES))
        bias = jnp.sum(jnp.where(eye, jnp.broadcast_to(zero_mode, (channels, LANES)), 0.0), axis=0, keepdims=True)
        extra = jnp.where(lax.broadcasted_iota(jnp.int32, (8, LANES), 0) == 0, jnp.broadcast_to(bias, (8, LANES)), 0.0)
        for d in range(owners):
            out_ref[d * rows + late : d * rows + late + 8, :] = packed
            out_ref[d * rows + late + 8 : (d + 1) * rows, :] = extra


def early_count(channels):
    return channels * 3 // 4


def early_cells(inverse, forward, modes, pre, cotangent):
    channels = pre.shape[0]
    owners = MY // 2
    early = early_count(channels)
    block = pl.BlockSpec((EARLY_STEP, NY, NZ), lambda s: (s, 0, 0))
    tables = (*inverse, *forward)
    act, slope, out = pl.pallas_call(
        functools.partial(early_cell_kernel, channels=channels, count=EARLY_STEP, rows=early),
        grid=(early // EARLY_STEP,),
        in_specs=[full(t.shape) for t in tables] + [full((owners * channels, LANES)), block, block],
        out_specs=[block, block, full((owners * early, LANES))],
        out_shape=[
            pltpu.HBM((channels, NY, NZ), BF16),
            pltpu.HBM((early, NY, NZ), F32),
            pltpu.VMEM((owners * early, LANES), F32),
        ],
        compiler_params=params(LIMIT),
        cost_estimate=pl.CostEstimate(flops=3 * 10**9, bytes_accessed=7 * MIB, transcendentals=10**6),
        name="early_cells",
    )(*in_hbm(*tables), *in_vmem(modes.reshape(owners * channels, LANES)), *in_hbm(pre, cotangent))
    return act, slope, out.reshape(owners, early, LANES)


def late_cells(inverse, forward, summing, modes, pre, cotangent, field, early, slope, act):
    channels = field.shape[0]
    owners = MY // 2
    first = early_count(channels)
    rows = channels - first + 16
    start = first // STEP
    block = pl.BlockSpec((STEP, NY, NZ), lambda s: (start + s, 0, 0))
    anywhere = pl.BlockSpec(memory_space=pl.ANY)
    tables = (*inverse, *forward, summing)
    act, out = pl.pallas_call(
        functools.partial(late_cell_kernel, channels=channels, count=STEP, rows=rows, owners=owners),
        grid=((channels - first) // STEP,),
        in_specs=[full(t.shape) for t in tables]
        + [full((owners * channels, LANES)), block, block, full((owners * first, LANES))]
        + [anywhere] * 3,
        out_specs=[block, full((owners * rows, LANES))],
        out_shape=[
            pltpu.HBM((channels, NY, NZ), BF16),
            pltpu.VMEM((owners * rows, LANES), F32),
        ],
        scratch_shapes=[
            pltpu.VMEM((channels, NY, NZ), F32),
            pltpu.VMEM((channels, NY, NZ), F32),
            pltpu.SemaphoreType.DMA((2,)),
        ],
        input_output_aliases={len(tables) + 6: 0},
        compiler_params=params(LIMIT),
        cost_estimate=pl.CostEstimate(flops=6 * 10**9, bytes_accessed=11 * MIB, transcendentals=10**6),
        name="late_cells",
    )(
        *in_hbm(*tables),
        *in_vmem(modes.reshape(owners * channels, LANES)),
        *in_hbm(pre, cotangent),
        *in_vmem(early.reshape(owners * first, LANES)),
        *in_hbm(slope, field, act),
    )
    return act, out.reshape(owners, rows, LANES)


def gradient_kernel(cos_ref, sin_ref, spec_ref, lines_ref, *refs, points, channels, unique, copies, norm, first, outputs, slots):
    last = first > 0
    if last:
        _, out_hbm, point_ref, bias_ref, sums_ref, real_ref, imag_ref, buffer, sems = refs
    else:
        out_hbm, sums_ref, real_ref, imag_ref, buffer, sems = refs
    halve_lines(lines_ref, sums_ref, points, outputs)
    half = LANES // 2
    lane = lane_index((outputs, LANES))
    scale = jnp.where(lane % MZ == 0, norm, 2.0 * norm)

    def writes(at, slot):
        return [
            pltpu.make_async_copy(
                buffer.at[slot, c],
                out_hbm.at[c, at + r * unique, :, pl.ds(first, outputs), :],
                sems.at[slot, c, r],
            )
            for r in range(copies)
            for c in range(2)
        ]

    @pl.loop(0, unique // slots)
    def _(turn):
        for slot in range(slots):
            at = slots * turn + slot

            @pl.when(turn > 0)
            def _():
                for copy in writes(at - slots, slot):
                    copy.wait()

            slope = scale * spectrum_row(cos_ref, sin_ref, sums_ref, at, slot % 2, points // 2)
            other = roll(slope, 64)
            flipped = jnp.where(lane < half, other, -other)
            real_ref[slot], imag_ref[slot] = doubled(spec_ref[at])
            for i in range(channels):
                both = real_ref[slot, pl.ds(i, 1), :] * slope + imag_ref[slot, pl.ds(i, 1), :] * flipped
                buffer[slot, 0, i] = both[:, :half]
                buffer[slot, 1, i] = both[:, half:]
            for copy in writes(at, slot):
                copy.start()

    if last:
        packed = lines_ref[0, outputs : outputs + 16, :]
        for x in range(1, points):
            packed += lines_ref[x, outputs : outputs + 16, :]
        packed = norm * packed
        for q in range(channels // 8):
            point_ref[8 * q : 8 * q + 8, :] = packed[:8, q * channels : (q + 1) * channels]
        bias_ref[...] = packed[8:9, :channels]

    for at in range(unique - slots, unique):
        for copy in writes(at, at % slots):
            copy.wait()


def gradient(cos_x, sin_x, spectrum, lines, norm, kept_x, before=()):
    points, rows, _ = lines.shape
    unique, channels, _ = spectrum.shape
    half = LANES // 2
    copies = kept_x // unique
    first = early_count(channels) if before else 0
    outputs = channels - first if before else early_count(channels)
    slots = 8
    anywhere = pl.BlockSpec(memory_space=pl.ANY)
    shape = jax.ShapeDtypeStruct((2, kept_x, channels, channels, half), F32)
    sums = [(channels, channels), (1, channels)] if before else []
    return pl.pallas_call(
        functools.partial(
            gradient_kernel, points=points, channels=channels, unique=unique, copies=copies, norm=norm,
            first=first, outputs=outputs, slots=slots,
        ),
        in_specs=[smem(), smem(), full(spectrum.shape), full(lines.shape)] + [anywhere] * len(before),
        out_specs=[anywhere] + [full(each) for each in sums],
        out_shape=[shape] + [jax.ShapeDtypeStruct(each, F32) for each in sums],
        scratch_shapes=[
            pltpu.VMEM((2, 2, points // 2, outputs, LANES), F32),
            pltpu.VMEM((slots, channels, LANES), F32),
            pltpu.VMEM((slots, channels, LANES), F32),
            pltpu.VMEM((slots, 2, channels, outputs, half), F32),
            pltpu.SemaphoreType.DMA((slots, 2, copies)),
        ],
        input_output_aliases={4: 0} if before else {},
        compiler_params=params(LIMIT),
        cost_estimate=pl.CostEstimate(flops=5 * 10**6, bytes_accessed=32 * MIB, transcendentals=0),
        name="weight_gradient",
    )(cos_x, sin_x, *in_vmem(spectrum, lines), *before)


def swap(lines):
    return lax.all_to_all(lines, "space", split_axis=0, concat_axis=0, tiled=True)


def suits(width_x, length_x, devices, channels, weights):
    held = weights.shape[2]
    even = np.array_equal(kept(MX, length_x) % length_x, np.arange(MX) % length_x)
    return (
        width_x == 1
        and held == 2 * MZ
        and devices * 2 == MY
        and 2 * held == LANES
        and MX % length_x == 0
        and length_x % 8 == 0
        and even
        and channels == MZ
    )


def body(lifted_field, cotangent, spectral_weights, point_weights, point_bias):
    devices = lax.axis_size("space")
    channels, width_x = lifted_field.shape[:2]
    length_x = width_x * devices
    if not suits(width_x, length_x, devices, channels, spectral_weights):
        return general_body(lifted_field, cotangent, spectral_weights, point_weights, point_bias)
    norm = float(length_x * NY * NZ) ** -0.5
    theta = angles(np.arange(length_x), np.arange(length_x), length_x)
    cos_x, sin_x = jnp.asarray(np.cos(theta), F32), jnp.asarray(np.sin(theta), F32)
    forward = forward_tables()
    inverse = inverse_tables(norm)
    summing = jnp.asarray(np.repeat(np.eye(channels), 8, axis=0), F32)

    field = lifted_field.reshape(channels, NY, NZ)
    slopes_in = cotangent.reshape(channels, NY, NZ)
    weights = jnp.transpose(spectral_weights, (0, 1, 3, 4, 2))

    lines, some = forward_modes(field, forward, weights, length_x)
    lines = swap(lines)
    folded = fold_rest(weights, some, length_x)
    spectrum, mixed = mix(cos_x, sin_x, lines, folded, norm)
    field_late, mixed = lax.optimization_barrier((field, mixed))
    modes = swap(mixed)
    pre = pointwise(field_late, summing, point_weights, point_bias)
    act, slope, early = early_cells(inverse, forward, modes, pre, slopes_in)
    early_lines = swap(early)
    activated, late = late_cells(inverse, forward, summing, modes, pre, slopes_in, field, early, slope, act)
    late_lines = swap(late)
    (grad,) = gradient(cos_x, sin_x, spectrum, early_lines, norm, MX)
    grad, grad_point, grad_bias = gradient(cos_x, sin_x, spectrum, late_lines, norm, MX, (grad,))
    return (
        activated.reshape(cotangent.shape),
        jnp.transpose(grad, (0, 1, 4, 2, 3)),
        grad_point,
        grad_bias.reshape(channels),
    )


HIGHEST = lax.Precision.HIGHEST


def trig_tables(positions, frequency, length):
    product = positions[:, None] * frequency[None, :] % length
    phase_angle = 2.0 * jnp.pi / length * product.astype(jnp.float32)
    return (jnp.cos(phase_angle), jnp.sin(phase_angle))


def kept_frequencies(kept_count, length):
    mode_index = jnp.arange(kept_count, dtype=jnp.int32)
    return jnp.where(mode_index < kept_count // 2, mode_index, length - kept_count + mode_index)


def forward_local(field_in):
    channels = field_in.shape[0]
    width_x = field_in.shape[1]
    cos_z, sin_z = trig_tables(jnp.arange(NZ, dtype=jnp.int32), jnp.arange(MZ, dtype=jnp.int32), NZ)
    table_z = jnp.concatenate([cos_z, -sin_z], axis=1)
    along_z = jnp.einsum("cxyz,zk->cxyk", field_in, table_z, precision=HIGHEST)
    z_real = along_z[..., :MZ]
    z_imag = along_z[..., MZ:]
    cos_y, sin_y = trig_tables(jnp.arange(NY, dtype=jnp.int32), kept_frequencies(MY, NY), NY)
    y_real = jnp.einsum("cxyk,yj->xcjk", z_real, cos_y, precision=HIGHEST) + jnp.einsum(
        "cxyk,yj->xcjk", z_imag, sin_y, precision=HIGHEST
    )
    y_imag = jnp.einsum("cxyk,yj->xcjk", z_imag, cos_y, precision=HIGHEST) - jnp.einsum(
        "cxyk,yj->xcjk", z_real, sin_y, precision=HIGHEST
    )
    stacked = jnp.stack([y_real, y_imag], axis=1)
    return stacked.reshape(width_x, 2, channels, MY * MZ)


def transform_x(x_lines):
    length_x = x_lines.shape[0]
    cos_x, sin_x = trig_tables(
        jnp.arange(length_x, dtype=jnp.int32), kept_frequencies(MX, length_x), length_x
    )
    norm_scale = 1.0 / float(length_x * NY * NZ) ** 0.5
    part_real = x_lines[:, 0]
    part_imag = x_lines[:, 1]
    x_real = jnp.einsum("xcm,xk->kcm", part_real, cos_x, precision=HIGHEST) + jnp.einsum(
        "xcm,xk->kcm", part_imag, sin_x, precision=HIGHEST
    )
    x_imag = jnp.einsum("xcm,xk->kcm", part_imag, cos_x, precision=HIGHEST) - jnp.einsum(
        "xcm,xk->kcm", part_real, sin_x, precision=HIGHEST
    )
    return norm_scale * jnp.stack([x_real, x_imag], axis=1)


def mix_modes(spectrum, weights):
    spec_real = spectrum[:, 0]
    spec_imag = spectrum[:, 1]
    out_real = jnp.einsum("kim,kmio->kom", spec_real, weights[0], precision=HIGHEST) - jnp.einsum(
        "kim,kmio->kom", spec_imag, weights[1], precision=HIGHEST
    )
    out_imag = jnp.einsum("kim,kmio->kom", spec_real, weights[1], precision=HIGHEST) + jnp.einsum(
        "kim,kmio->kom", spec_imag, weights[0], precision=HIGHEST
    )
    return jnp.stack([out_real, out_imag], axis=1)


def inverse_x(spectrum, positions, length_x):
    cos_x, sin_x = trig_tables(positions, kept_frequencies(MX, length_x), length_x)
    spec_real = spectrum[:, 0]
    spec_imag = spectrum[:, 1]
    a_real = jnp.einsum("kcm,xk->xcm", spec_real, cos_x, precision=HIGHEST) - jnp.einsum(
        "kcm,xk->xcm", spec_imag, sin_x, precision=HIGHEST
    )
    a_imag = jnp.einsum("kcm,xk->xcm", spec_imag, cos_x, precision=HIGHEST) + jnp.einsum(
        "kcm,xk->xcm", spec_real, sin_x, precision=HIGHEST
    )
    return jnp.stack([a_real, a_imag], axis=1)


def inverse_yz(x_lines, length_x):
    width_x = x_lines.shape[0]
    channels = x_lines.shape[2]
    mode_grid = x_lines.reshape(width_x, 2, channels, MY, MZ)
    cos_y, sin_y = trig_tables(jnp.arange(NY, dtype=jnp.int32), kept_frequencies(MY, NY), NY)
    b_real = jnp.einsum("xcjk,yj->cxyk", mode_grid[:, 0], cos_y, precision=HIGHEST) - jnp.einsum(
        "xcjk,yj->cxyk", mode_grid[:, 1], sin_y, precision=HIGHEST
    )
    b_imag = jnp.einsum("xcjk,yj->cxyk", mode_grid[:, 1], cos_y, precision=HIGHEST) + jnp.einsum(
        "xcjk,yj->cxyk", mode_grid[:, 0], sin_y, precision=HIGHEST
    )
    cos_z, sin_z = trig_tables(jnp.arange(NZ, dtype=jnp.int32), jnp.arange(MZ, dtype=jnp.int32), NZ)
    weight_z = jnp.where(jnp.arange(MZ, dtype=jnp.int32) == 0, 1.0, 2.0).astype(jnp.float32)
    table_z = jnp.concatenate([cos_z * weight_z[None, :], -sin_z * weight_z[None, :]], axis=1)
    stacked = jnp.concatenate([b_real, b_imag], axis=-1)
    result = jnp.einsum("cxyk,zk->cxyz", stacked, table_z, precision=HIGHEST)
    return result * (1.0 / float(length_x * NY * NZ) ** 0.5)


def gelu_slope(values):
    return (
        0.5 * (1.0 + lax.erf(values * INV_SQRT_TWO))
        + values * jnp.exp(-0.5 * values * values) * INV_SQRT_TWO_PI
    )


def weight_gradient(spectrum, slope_modes, first_mode):
    mode_ids = first_mode + jnp.arange(spectrum.shape[3], dtype=jnp.int32)
    weight_modes = jnp.where(mode_ids % MZ == 0, 1.0, 2.0).astype(jnp.float32)
    grad_real = jnp.einsum(
        "kim,kom->kmio", spectrum[:, 0], slope_modes[:, 0], precision=HIGHEST
    ) + jnp.einsum("kim,kom->kmio", spectrum[:, 1], slope_modes[:, 1], precision=HIGHEST)
    grad_imag = jnp.einsum(
        "kim,kom->kmio", spectrum[:, 0], slope_modes[:, 1], precision=HIGHEST
    ) - jnp.einsum("kim,kom->kmio", spectrum[:, 1], slope_modes[:, 0], precision=HIGHEST)
    stacked = jnp.stack([grad_real, grad_imag], axis=0)
    return stacked * weight_modes[None, None, :, None, None]


def to_modes(field_in):
    return transform_x(
        lax.all_to_all(forward_local(field_in), "space", split_axis=3, concat_axis=0, tiled=True)
    )


def general_body(lifted_field, cotangent, spectral_weights, point_weights, point_bias):
    devices = lax.axis_size("space")
    width_x = lifted_field.shape[1]
    length_x = width_x * devices
    spectrum = to_modes(lifted_field)
    mixed_modes = mix_modes(spectrum, spectral_weights)
    full_lines = inverse_x(mixed_modes, jnp.arange(length_x, dtype=jnp.int32), length_x)
    spectral = inverse_yz(
        lax.all_to_all(full_lines, "space", split_axis=0, concat_axis=3, tiled=True), length_x
    )
    pointwise = (
        jnp.einsum("ixyz,io->oxyz", lifted_field, point_weights, precision=HIGHEST)
        + point_bias[:, None, None, None]
    )
    before = spectral + pointwise
    activated = jax.nn.gelu(before, approximate=False).astype(jnp.bfloat16)
    slope_field = cotangent.astype(jnp.float32) * gelu_slope(before)
    local_point = jnp.einsum("ixyz,oxyz->io", lifted_field, slope_field, precision=HIGHEST)
    local_bias = jnp.sum(slope_field, axis=(1, 2, 3))
    partial = jnp.concatenate([local_point, local_bias[None, :]], axis=0)
    gathered = lax.all_gather(partial, "space", axis=0, tiled=False)
    summed = jnp.sum(gathered, axis=0)
    summed_point, summed_bias = summed[:-1], summed[-1]
    root_cells = float(length_x * NY * NZ) ** 0.5
    slope_spectrum = to_modes(slope_field)
    first_mode = lax.axis_index("space") * spectrum.shape[3]
    grad_spectral = weight_gradient(spectrum, slope_spectrum, first_mode)
    return (activated, grad_spectral, summed_point / root_cells, summed_bias / root_cells)


def solution(mesh):
    placed = (
        P("groups", "space", None, None),
        P("groups", "space", None, None),
        P(None, None, "space", None, None),
        P(),
        P(),
    )
    return jax.shard_map(
        body,
        mesh=mesh,
        in_specs=placed,
        out_specs=(
            P("groups", "space", None, None),
            P("groups", None, "space", None, None),
            P("groups", None),
            P("groups"),
        ),
        check_vma=False,
    )
```

```python
import functools

import jax
import jax.numpy as jnp
import ml_dtypes
import numpy as np
from jax import lax
from jax.experimental import pallas as pl
from jax.experimental.pallas import tpu as pltpu
from jax.sharding import PartitionSpec as P

MX = 32
MY = 32
MZ = 32
NY = 128
NZ = 256

F32 = jnp.float32
BF16 = jnp.bfloat16
INV_SQRT_TWO = 0.7071067811865476
INV_SQRT_TWO_PI = 0.3989422804014327
MIB = 1 << 20
LIMIT = 48
LANES = 128
GROUP = 4
EARLY_STEP = 12
STEP = 8


def kept(kept_count, length):
    index = np.arange(kept_count)
    return np.where(index < kept_count // 2, index, length - kept_count + index)


def angles(positions, frequency, length):
    product = positions[:, None] * frequency[None, :] % length
    return 2.0 * np.pi / length * product


def split_table(table):
    high = table.astype(ml_dtypes.bfloat16)
    return high, (table - high.astype(np.float64)).astype(ml_dtypes.bfloat16)


def lane_spread(first, second, real_table, imag_table):
    return np.concatenate(
        [real_table * first, real_table * second, imag_table * first, imag_table * second], axis=1
    )


def forward_tables():
    theta = angles(np.arange(NZ), np.arange(MZ), NZ)
    table = np.concatenate([lane_spread(f, s, np.cos(theta), -np.sin(theta)) for f, s in ((1, 0), (0, 1))], axis=0)
    high, low = split_table(table)
    table_z = np.concatenate(
        [np.concatenate([high, low], axis=1), np.concatenate([high, np.zeros_like(low)], axis=1)], axis=0
    )
    theta = angles(np.arange(NY), kept(MY, NY), NY).T
    table = np.concatenate([np.cos(theta)[0::2], np.cos(theta)[1::2], np.sin(theta)[0::2], np.sin(theta)[1::2]], axis=0)
    high, low = split_table(table)
    table_y = np.concatenate(
        [np.concatenate([high, high], axis=1), np.concatenate([low, np.zeros_like(low)], axis=1)], axis=0
    )
    return table_z, table_y


def inverse_tables(norm):
    theta = angles(np.arange(NY), kept(MY, NY), NY)
    cos_y, sin_y = np.cos(theta), np.sin(theta)
    table_y = np.concatenate([cos_y[:, 0::2], cos_y[:, 1::2], sin_y[:, 0::2], sin_y[:, 1::2]], axis=1)
    y_high, y_low = split_table(table_y)
    theta = angles(np.arange(NZ), np.arange(MZ), NZ)
    weight = np.where(np.arange(MZ) == 0, 1.0, 2.0) * norm
    parts = (np.cos(theta) * weight, -np.sin(theta) * weight)
    own, other = lane_spread(1, 0, *parts).T, lane_spread(0, 1, *parts).T
    tables_z = []
    for mine, theirs in ((own, other), (other, own)):
        high = split_table(mine)[0]
        tables_z.append(np.concatenate([high, high + split_table(theirs)[1]], axis=0))
    return np.concatenate([y_high, y_high, y_low], axis=1), *tables_z


def dot(left, right):
    return jnp.dot(left, right, preferred_element_type=F32)


def split(values):
    high = values.astype(BF16)
    return high, (values - high.astype(F32)).astype(BF16)


def lane_index(shape):
    return lax.broadcasted_iota(jnp.int32, shape, len(shape) - 1)


def roll(values, shift):
    return pltpu.roll(values, shift % LANES, len(values.shape) - 1)


def forward_group(fields, table_z, table_y, out_ref, first, rows):
    left = jnp.concatenate(
        [jnp.concatenate([fields[q], fields[q + 1]], axis=1) for q in range(0, len(fields), 2)], axis=0
    )
    lines = dot(jnp.concatenate(split(left), axis=1), table_z)
    lines = lines[:, :LANES] + lines[:, LANES:]
    half = MY // 2
    for g in range(0, len(fields) // 2, GROUP // 2):
        quad = jnp.concatenate([lines[q * NY : (q + 1) * NY] for q in range(g, g + GROUP // 2)], axis=1)
        wide = dot(table_y, jnp.concatenate(split(quad), axis=0))
        wide = wide[: 2 * MY] + wide[2 * MY :]
        for q in range(GROUP // 2):
            by_cos = wide[:MY, q * LANES : (q + 1) * LANES]
            by_sin = roll(wide[MY:, q * LANES : (q + 1) * LANES], 64)
            modes = by_cos + jnp.where(lane_index(by_sin.shape) < LANES // 2, by_sin, -by_sin)
            even, odd = modes[:half], modes[half:]
            at_even = (lane_index(even.shape) // MZ) % 2 == 0
            at = first + 2 * (g + q)
            out_ref[pl.ds(at, half, stride=rows), :] = jnp.where(at_even, even, roll(odd, MZ))
            out_ref[pl.ds(at + 1, half, stride=rows), :] = jnp.where(at_even, roll(even, -MZ), odd)


def inverse_y_group(modes_ref, y_table, first, rows):
    half = MY // 2
    pairs = []
    for q in range(GROUP // 2):
        c0 = modes_ref[pl.ds(first + 2 * q, half, stride=rows), :]
        c1 = modes_ref[pl.ds(first + 2 * q + 1, half, stride=rows), :]
        at_even = (lane_index(c0.shape) // MZ) % 2 == 0
        even = jnp.where(at_even, c0, roll(c1, MZ))
        odd = jnp.where(at_even, roll(c0, -MZ), c1)
        both = jnp.concatenate([even, odd], axis=0)
        other = roll(both, 64)
        turned = jnp.where(lane_index(both.shape) < LANES // 2, -other, other)
        pairs.append(jnp.concatenate([both, turned], axis=0))
    high, low = split(jnp.concatenate(pairs, axis=1))
    lines = dot(y_table, jnp.concatenate([high, low, high], axis=0))
    return [lines[:, q * LANES : (q + 1) * LANES] for q in range(GROUP // 2)]


def in_hbm(*arrays):
    return [pltpu.with_memory_space_constraint(each, pltpu.HBM) for each in arrays]


def in_vmem(*arrays):
    return [pltpu.with_memory_space_constraint(each, pltpu.VMEM) for each in arrays]


def full(shape):
    return pl.BlockSpec(shape, lambda *_: (0,) * len(shape))


def params(limit):
    return pltpu.CompilerParams(vmem_limit_bytes=limit * MIB)


def fold_block(pieces, out_ref, at):
    copies = pieces.shape[0]
    real, imag = pieces[0, 0], pieces[0, 1]
    for r in range(1, copies):
        real, imag = real + pieces[r, 0], imag + pieces[r, 1]
    modes = real.shape[-1]
    out_ref[at, :, :, :modes] = real
    out_ref[at, :, :, modes:] = imag


def fetches(weights_hbm, ring_ref, sems, at, slot, unique):
    copies = ring_ref.shape[1]
    return [
        pltpu.make_async_copy(weights_hbm.at[c, at + r * unique], ring_ref.at[slot, r, c], sems.at[slot, r, c])
        for r in range(copies)
        for c in range(2)
    ]


def fold_shapes(weights, unique, slots):
    copies = weights.shape[1] // unique
    shape = (unique,) + weights.shape[2:4] + (2 * weights.shape[4],)
    ring = [pltpu.VMEM((slots, copies, 2) + weights.shape[2:], F32), pltpu.SemaphoreType.DMA((slots, copies, 2))]
    return pltpu.HBM(shape, F32), ring


def forward_kernel(
    table_z, table_y, field_ref, weights_hbm, out_ref, folded_ref, ring_ref, sems,
    *, channels, step_channels, per_step, unique, slots,
):
    step = pl.program_id(0)

    def transform():
        fields = [field_ref[q] for q in range(step_channels)]
        forward_group(fields, table_z[...], table_y[...], out_ref, step * step_channels, channels)

    folding = (step > 0) & (step <= slots // per_step)

    @pl.when(step == 0)
    def _():
        for at in range(slots):
            for copy in fetches(weights_hbm, ring_ref, sems, at, at, unique):
                copy.start()

    @pl.when(jnp.logical_not(folding))
    def _():
        transform()

    @pl.when(folding)
    def _():
        for q in range(per_step):
            at = (step - 1) * per_step + q
            for copy in fetches(weights_hbm, ring_ref, sems, at, at, unique):
                copy.wait()
            fold_block(ring_ref.at[at], folded_ref, q)
        transform()


FOLD_STEP = 2
FIELD_STEP = 8


def folded_early(channels):
    return (channels // FIELD_STEP - 2) * FOLD_STEP


def forward_modes(field, tables, weights, unique):
    channels = field.shape[0]
    slots = folded_early(channels)
    folded_shape, ring = fold_shapes(weights, unique, slots)
    owners = MY // 2
    out, some = pl.pallas_call(
        functools.partial(
            forward_kernel, channels=channels, step_channels=FIELD_STEP, per_step=FOLD_STEP, unique=unique, slots=slots
        ),
        grid=(channels // FIELD_STEP,),
        in_specs=[full(t.shape) for t in tables]
        + [pl.BlockSpec((FIELD_STEP, NY, NZ), lambda s: (s, 0, 0)), pl.BlockSpec(memory_space=pl.ANY)],
        out_specs=[
            full((owners * channels, LANES)),
            pl.BlockSpec((FOLD_STEP,) + folded_shape.shape[1:], lambda s: (jnp.clip(s - 1, 0, slots // FOLD_STEP - 1), 0, 0, 0)),
        ],
        out_shape=[pltpu.VMEM((owners * channels, LANES), F32), folded_shape],
        scratch_shapes=ring,
        compiler_params=params(LIMIT),
        cost_estimate=pl.CostEstimate(flops=2 * 10**9, bytes_accessed=22 * MIB, transcendentals=0),
        name="forward_yz",
    )(*in_hbm(*tables, field, weights))
    return out.reshape(owners, channels, LANES), some


def fold_kernel(weights_hbm, _, out_ref, ring_ref, sems, *, first, unique, slots):
    step = pl.program_id(0)

    def fetch(turn):
        slot = turn % slots
        return [
            copy
            for q in range(FOLD_STEP)
            for copy in fetches(weights_hbm, ring_ref, sems, first + turn * FOLD_STEP + q, slot * FOLD_STEP + q, unique)
        ]

    @pl.when(step == 0)
    def _():
        for ahead in range(slots):
            for copy in fetch(ahead):
                copy.start()

    for copy in fetch(step):
        copy.wait()
    for q in range(FOLD_STEP):
        fold_block(ring_ref.at[step % slots * FOLD_STEP + q], out_ref, q)

    @pl.when(step + slots < pl.num_programs(0))
    def _():
        for copy in fetch(step + slots):
            copy.start()


def fold_rest(weights, some, unique):
    first = folded_early(weights.shape[2])
    steps = (unique - first) // FOLD_STEP
    slots = min(3, steps)
    folded_shape, ring = fold_shapes(weights, unique, slots * FOLD_STEP)
    anywhere = pl.BlockSpec(memory_space=pl.ANY)
    return pl.pallas_call(
        functools.partial(fold_kernel, first=first, unique=unique, slots=slots),
        grid=(steps,),
        in_specs=[anywhere, anywhere],
        out_specs=pl.BlockSpec((FOLD_STEP,) + folded_shape.shape[1:], lambda s: (first // FOLD_STEP + s, 0, 0, 0)),
        out_shape=folded_shape,
        scratch_shapes=ring,
        input_output_aliases={1: 0},
        compiler_params=params(LIMIT),
        cost_estimate=pl.CostEstimate(flops=4 * 10**6, bytes_accessed=30 * MIB, transcendentals=0),
        name="fold_weights",
    )(*in_hbm(weights, some))


def halve_lines(lines_ref, sums_ref, points, channels):
    half = points // 2
    sign = jnp.where(lane_index((channels, LANES)) < LANES // 2, 1.0, -1.0)
    for x in range(half):
        near, far = lines_ref[x, :channels], lines_ref[x + half, :channels]
        for parity, value in enumerate((near + far, near - far)):
            sums_ref[parity, 0, x] = value
            sums_ref[parity, 1, x] = sign * roll(value, 64)


def spectrum_row(cos_ref, sin_ref, sums_ref, at, parity, half):
    total = cos_ref[at, 0] * sums_ref[parity, 0, 0] + sin_ref[at, 0] * sums_ref[parity, 1, 0]
    for x in range(1, half):
        total += cos_ref[at, x] * sums_ref[parity, 0, x] + sin_ref[at, x] * sums_ref[parity, 1, x]
    return total


def doubled(values):
    other = roll(values, 64)
    low = lane_index(values.shape) < LANES // 2
    return jnp.where(low, values, other), jnp.where(low, other, values)


def mix_kernel(
    cos_ref, sin_ref, lines_ref, weights_hbm, spec_ref, out_ref,
    sums_ref, total_ref, real_ref, imag_ref, weights_ref, sems, *, points, channels, per_step, norm,
):
    half = points // 2
    steps = points // per_step

    def fetch(step):
        count = channels // 2
        return [
            pltpu.make_async_copy(
                weights_hbm.at[pl.ds(step * per_step, per_step), pl.ds(h * count, count)],
                weights_ref.at[step % 2, :, pl.ds(h * count, count)],
                sems.at[step % 2, h],
            )
            for h in range(2)
        ]

    for copy in fetch(0):
        copy.start()
    halve_lines(lines_ref, sums_ref, points, channels)
    total_ref[...] = jnp.zeros_like(total_ref)
    low = lane_index((channels, LANES)) < LANES // 2
    for step in range(steps):
        for copy in fetch(step):
            copy.wait()
        if step + 1 < steps:
            for copy in fetch(step + 1):
                copy.start()
        for q in range(per_step):
            at = step * per_step + q
            parity = q % 2
            spec = norm * spectrum_row(cos_ref, sin_ref, sums_ref, at, parity, half)
            spec_ref[at] = spec
            real_ref[q], imag_ref[q] = doubled(spec)
            by_real = jnp.zeros((channels, LANES), F32)
            by_imag = jnp.zeros((channels, LANES), F32)
            for i in range(channels):
                weight = weights_ref[step % 2, q, i]
                by_real += real_ref[q, pl.ds(i, 1), :] * weight
                by_imag += imag_ref[q, pl.ds(i, 1), :] * weight
            other = roll(by_imag, 64)
            mixed = by_real + jnp.where(low, -other, other)
            other = roll(mixed, 64)
            turned = jnp.where(low, -other, other)
            for x in range(half):
                total_ref[parity, x] += cos_ref[at, x] * mixed + sin_ref[at, x] * turned
    for x in range(half):
        out_ref[x] = total_ref[0, x] + total_ref[1, x]
        out_ref[x + half] = total_ref[0, x] - total_ref[1, x]


def smem():
    return pl.BlockSpec(memory_space=pltpu.SMEM)


def mix(cos_x, sin_x, lines, weights, norm):
    points, channels, _ = lines.shape
    unique = weights.shape[0]
    per_step = 4
    shape = (points, channels, LANES)
    return pl.pallas_call(
        functools.partial(mix_kernel, points=points, channels=channels, per_step=per_step, norm=norm),
        grid=(1,),
        in_specs=[
            smem(),
            smem(),
            full(shape),
            pl.BlockSpec(memory_space=pl.ANY),
        ],
        out_specs=[
            full((unique, channels, LANES)),
            full(shape),
        ],
        out_shape=[
            pltpu.VMEM((unique, channels, LANES), F32),
            pltpu.VMEM(shape, F32),
        ],
        scratch_shapes=[
            pltpu.VMEM((2, 2, points // 2, channels, LANES), F32),
            pltpu.VMEM((2, points // 2, channels, LANES), F32),
            pltpu.VMEM((per_step, channels, LANES), F32),
            pltpu.VMEM((per_step, channels, LANES), F32),
            pltpu.VMEM((2, per_step) + weights.shape[1:], F32),
            pltpu.SemaphoreType.DMA((2, 2)),
        ],
        compiler_params=params(LIMIT),
        cost_estimate=pl.CostEstimate(flops=2 * 10**7, bytes_accessed=9 * MIB, transcendentals=0),
        name="mix_modes",
    )(cos_x, sin_x, *in_vmem(lines), *in_hbm(weights))


def exact_dot(left, right):
    return jnp.dot(left, right, precision=lax.Precision.HIGHEST, preferred_element_type=F32)


def pointwise_kernel(sum_ref, turned_ref, bias_in_ref, field_ref, out_ref, mixer_ref, bias_ref, *, channels, blocks):
    size = 8 * channels

    @pl.when(pl.program_id(0) == 0)
    def _():
        wide = exact_dot(sum_ref[...], turned_ref[...])
        wide = lax.dot_general(
            wide, sum_ref[...], (((1,), (1,)), ((), ())), precision=lax.Precision.HIGHEST, preferred_element_type=F32
        )
        row = lax.broadcasted_iota(jnp.int32, (size, size), 0) % 8
        high, low = split(jnp.where(row == lane_index((size, size)) % 8, wide, 0.0))
        mixer_ref[:size] = high
        mixer_ref[size:] = low
        bias_ref[...] = exact_dot(sum_ref[...], bias_in_ref[...])

    for b in range(blocks):
        high, low = split(field_ref[:, 8 * b : 8 * b + 8, :].reshape(size, NZ))
        wide = dot(mixer_ref[...], high)
        values = wide[:size] + wide[size:] + dot(mixer_ref[:size], low) + bias_ref[...]
        out_ref[:, 8 * b : 8 * b + 8, :] = values.reshape(channels, 8, NZ)


def pointwise(field, summing, point_weights, point_bias):
    channels = field.shape[0]
    blocks = 2
    turned = point_weights.T
    bias = point_bias[:, None]
    size = 8 * channels
    block = pl.BlockSpec((channels, 8 * blocks, NZ), lambda s: (0, s, 0))
    return pl.pallas_call(
        functools.partial(pointwise_kernel, channels=channels, blocks=blocks),
        grid=(NY // (8 * blocks),),
        in_specs=[full(summing.shape), full(turned.shape), full(bias.shape), block],
        out_specs=block,
        out_shape=pltpu.HBM(field.shape, F32),
        scratch_shapes=[pltpu.VMEM((2 * size, size), BF16), pltpu.VMEM((size, 1), F32)],
        compiler_params=params(LIMIT),
        cost_estimate=pl.CostEstimate(flops=4 * 10**9, bytes_accessed=24 * MIB, transcendentals=0),
        name="pointwise",
    )(*in_hbm(summing, turned, bias, field))


def cell_group(inv_y, inv_z, modes_ref, pre_ref, cot_ref, act_ref, first, count, channels):
    lines = []
    for g in range(0, count, GROUP):
        lines += inverse_y_group(modes_ref, inv_y, first + g, channels)
    lines = jnp.concatenate(lines, axis=0)
    high = lines.astype(BF16).astype(F32)
    low = lines - high
    at_even = (lane_index(lines.shape) // MZ) % 2 == 0
    spectral = [
        dot(jnp.concatenate([high, side], axis=1).astype(BF16), table)
        for side, table in zip((jnp.where(at_even, low, roll(high, MZ)), jnp.where(at_even, roll(high, -MZ), low)), inv_z)
    ]
    slopes = []
    for q in range(count):
        before = spectral[q % 2][q // 2 * NY : (q // 2 + 1) * NY] + pre_ref[q]
        cdf = 0.5 + 0.5 * lax.erf(before * INV_SQRT_TWO)
        act_ref[q] = (before * cdf).astype(BF16)
        pdf = jnp.exp(-0.5 * before * before) * INV_SQRT_TWO_PI
        slopes.append(cot_ref[q].astype(F32) * (cdf + before * pdf))
    return slopes


def early_cell_kernel(
    inv_y, inv_z0, inv_z1, table_z, table_y, modes_ref, pre_ref, cot_ref, act_ref, slope_ref, out_ref,
    *, channels, count, rows,
):
    step = pl.program_id(0)
    slopes = cell_group(
        inv_y[...], (inv_z0[...], inv_z1[...]), modes_ref, pre_ref, cot_ref, act_ref, step * count, count, channels
    )
    for q in range(count):
        slope_ref[q] = slopes[q]
    forward_group(slopes, table_z[...], table_y[...], out_ref, step * count, rows)


def point_gradient(field_ref, slope_ref, sum_ref, channels):
    size = 8 * channels
    total = jnp.zeros((size, size), F32)
    for b in range(NY // 8):
        at = slice(8 * b, 8 * b + 8)
        f_h, f_l = split(field_ref[:, at, :].reshape(size, NZ))
        s_h, s_l = split(slope_ref[:, at, :].reshape(size, NZ))
        total += lax.dot_general(
            jnp.concatenate([f_h, f_h, f_l], axis=1),
            jnp.concatenate([s_h, s_l, s_h], axis=1),
            (((1,), (1,)), ((), ())),
            preferred_element_type=F32,
        )
    row = lax.broadcasted_iota(jnp.int32, (size, size), 0) % 8
    total = jnp.where(row == lane_index((size, size)) % 8, total, 0.0)
    return exact_dot(jnp.sum(total.reshape(channels, 8, size), axis=1), sum_ref[...])


def late_cell_kernel(
    inv_y, inv_z0, inv_z1, table_z, table_y, sum_ref, modes_ref, pre_ref, cot_ref, early_ref,
    slope_hbm, field_hbm, _, act_ref, out_ref, field_ref, slope_ref, sems, *, channels, count, rows, owners,
):
    step = pl.program_id(0)
    early = early_count(channels)
    late = channels - early
    copies = [
        pltpu.make_async_copy(field_hbm, field_ref, sems.at[0]),
        pltpu.make_async_copy(slope_hbm, slope_ref.at[pl.ds(0, early)], sems.at[1]),
    ]

    @pl.when(step == 0)
    def _():
        for copy in copies:
            copy.start()

    first = early + step * count
    slopes = cell_group(
        inv_y[...], (inv_z0[...], inv_z1[...]), modes_ref, pre_ref, cot_ref, act_ref, first, count, channels
    )
    for q in range(count):
        slope_ref[first + q] = slopes[q]
    forward_group(slopes, table_z[...], table_y[...], out_ref, step * count, rows)

    @pl.when(step == pl.num_programs(0) - 1)
    def _():
        for copy in copies:
            copy.wait()
        point = point_gradient(field_ref, slope_ref, sum_ref, channels)
        packed = jnp.concatenate([point[8 * q : 8 * q + 8] for q in range(channels // 8)], axis=1)
        zero_mode = jnp.concatenate([early_ref[0:early, 0:1], out_ref[0:late, 0:1]], axis=0)
        eye = lax.broadcasted_iota(jnp.int32, (channels, LANES), 0) == lane_index((channels, LANES))
        bias = jnp.sum(jnp.where(eye, jnp.broadcast_to(zero_mode, (channels, LANES)), 0.0), axis=0, keepdims=True)
        extra = jnp.where(lax.broadcasted_iota(jnp.int32, (8, LANES), 0) == 0, jnp.broadcast_to(bias, (8, LANES)), 0.0)
        for d in range(owners):
            out_ref[d * rows + late : d * rows + late + 8, :] = packed
            out_ref[d * rows + late + 8 : (d + 1) * rows, :] = extra


def early_count(channels):
    return channels * 3 // 4


def early_cells(inverse, forward, modes, pre, cotangent):
    channels = pre.shape[0]
    owners = MY // 2
    early = early_count(channels)
    block = pl.BlockSpec((EARLY_STEP, NY, NZ), lambda s: (s, 0, 0))
    tables = (*inverse, *forward)
    act, slope, out = pl.pallas_call(
        functools.partial(early_cell_kernel, channels=channels, count=EARLY_STEP, rows=early),
        grid=(early // EARLY_STEP,),
        in_specs=[full(t.shape) for t in tables] + [full((owners * channels, LANES)), block, block],
        out_specs=[block, block, full((owners * early, LANES))],
        out_shape=[
            pltpu.HBM((channels, NY, NZ), BF16),
            pltpu.HBM((early, NY, NZ), F32),
            pltpu.VMEM((owners * early, LANES), F32),
        ],
        compiler_params=params(LIMIT),
        cost_estimate=pl.CostEstimate(flops=3 * 10**9, bytes_accessed=7 * MIB, transcendentals=10**6),
        name="early_cells",
    )(*in_hbm(*tables), *in_vmem(modes.reshape(owners * channels, LANES)), *in_hbm(pre, cotangent))
    return act, slope, out.reshape(owners, early, LANES)


def late_cells(inverse, forward, summing, modes, pre, cotangent, field, early, slope, act):
    channels = field.shape[0]
    owners = MY // 2
    first = early_count(channels)
    rows = channels - first + 16
    start = first // STEP
    block = pl.BlockSpec((STEP, NY, NZ), lambda s: (start + s, 0, 0))
    anywhere = pl.BlockSpec(memory_space=pl.ANY)
    tables = (*inverse, *forward, summing)
    act, out = pl.pallas_call(
        functools.partial(late_cell_kernel, channels=channels, count=STEP, rows=rows, owners=owners),
        grid=((channels - first) // STEP,),
        in_specs=[full(t.shape) for t in tables]
        + [full((owners * channels, LANES)), block, block, full((owners * first, LANES))]
        + [anywhere] * 3,
        out_specs=[block, full((owners * rows, LANES))],
        out_shape=[
            pltpu.HBM((channels, NY, NZ), BF16),
            pltpu.VMEM((owners * rows, LANES), F32),
        ],
        scratch_shapes=[
            pltpu.VMEM((channels, NY, NZ), F32),
            pltpu.VMEM((channels, NY, NZ), F32),
            pltpu.SemaphoreType.DMA((2,)),
        ],
        input_output_aliases={len(tables) + 6: 0},
        compiler_params=params(LIMIT),
        cost_estimate=pl.CostEstimate(flops=6 * 10**9, bytes_accessed=11 * MIB, transcendentals=10**6),
        name="late_cells",
    )(
        *in_hbm(*tables),
        *in_vmem(modes.reshape(owners * channels, LANES)),
        *in_hbm(pre, cotangent),
        *in_vmem(early.reshape(owners * first, LANES)),
        *in_hbm(slope, field, act),
    )
    return act, out.reshape(owners, rows, LANES)


def gradient_kernel(cos_ref, sin_ref, spec_ref, lines_ref, *refs, points, channels, unique, copies, norm, first, outputs, slots):
    last = first > 0
    if last:
        _, out_hbm, point_ref, bias_ref, sums_ref, real_ref, imag_ref, buffer, sems = refs
    else:
        out_hbm, sums_ref, real_ref, imag_ref, buffer, sems = refs
    halve_lines(lines_ref, sums_ref, points, outputs)
    half = LANES // 2
    lane = lane_index((outputs, LANES))
    scale = jnp.where(lane % MZ == 0, norm, 2.0 * norm)

    def writes(at, slot):
        return [
            pltpu.make_async_copy(
                buffer.at[slot, c],
                out_hbm.at[c, at + r * unique, :, pl.ds(first, outputs), :],
                sems.at[slot, c, r],
            )
            for r in range(copies)
            for c in range(2)
        ]

    @pl.loop(0, unique // slots)
    def _(turn):
        for slot in range(slots):
            at = slots * turn + slot

            @pl.when(turn > 0)
            def _():
                for copy in writes(at - slots, slot):
                    copy.wait()

            slope = scale * spectrum_row(cos_ref, sin_ref, sums_ref, at, slot % 2, points // 2)
            other = roll(slope, 64)
            flipped = jnp.where(lane < half, other, -other)
            real_ref[slot], imag_ref[slot] = doubled(spec_ref[at])
            for i in range(channels):
                both = real_ref[slot, pl.ds(i, 1), :] * slope + imag_ref[slot, pl.ds(i, 1), :] * flipped
                buffer[slot, 0, i] = both[:, :half]
                buffer[slot, 1, i] = both[:, half:]
            for copy in writes(at, slot):
                copy.start()

    if last:
        packed = lines_ref[0, outputs : outputs + 16, :]
        for x in range(1, points):
            packed += lines_ref[x, outputs : outputs + 16, :]
        packed = norm * packed
        for q in range(channels // 8):
            point_ref[8 * q : 8 * q + 8, :] = packed[:8, q * channels : (q + 1) * channels]
        bias_ref[...] = packed[8:9, :channels]

    for at in range(unique - slots, unique):
        for copy in writes(at, at % slots):
            copy.wait()


def gradient(cos_x, sin_x, spectrum, lines, norm, kept_x, before=()):
    points, rows, _ = lines.shape
    unique, channels, _ = spectrum.shape
    half = LANES // 2
    copies = kept_x // unique
    first = early_count(channels) if before else 0
    outputs = channels - first if before else early_count(channels)
    slots = unique
    anywhere = pl.BlockSpec(memory_space=pl.ANY)
    shape = jax.ShapeDtypeStruct((2, kept_x, channels, channels, half), F32)
    sums = [(channels, channels), (1, channels)] if before else []
    return pl.pallas_call(
        functools.partial(
            gradient_kernel, points=points, channels=channels, unique=unique, copies=copies, norm=norm,
            first=first, outputs=outputs, slots=slots,
        ),
        in_specs=[smem(), smem(), full(spectrum.shape), full(lines.shape)] + [anywhere] * len(before),
        out_specs=[anywhere] + [full(each) for each in sums],
        out_shape=[shape] + [jax.ShapeDtypeStruct(each, F32) for each in sums],
        scratch_shapes=[
            pltpu.VMEM((2, 2, points // 2, outputs, LANES), F32),
            pltpu.VMEM((slots, channels, LANES), F32),
            pltpu.VMEM((slots, channels, LANES), F32),
            pltpu.VMEM((slots, 2, channels, outputs, half), F32),
            pltpu.SemaphoreType.DMA((slots, 2, copies)),
        ],
        input_output_aliases={4: 0} if before else {},
        compiler_params=params(LIMIT),
        cost_estimate=pl.CostEstimate(flops=5 * 10**6, bytes_accessed=32 * MIB, transcendentals=0),
        name="weight_gradient",
    )(cos_x, sin_x, *in_vmem(spectrum, lines), *before)


def swap(lines):
    return lax.all_to_all(lines, "space", split_axis=0, concat_axis=0, tiled=True)


def suits(width_x, length_x, devices, channels, weights):
    held = weights.shape[2]
    even = np.array_equal(kept(MX, length_x) % length_x, np.arange(MX) % length_x)
    return (
        width_x == 1
        and held == 2 * MZ
        and devices * 2 == MY
        and 2 * held == LANES
        and MX % length_x == 0
        and length_x % 8 == 0
        and even
        and channels == MZ
    )


def body(lifted_field, cotangent, spectral_weights, point_weights, point_bias):
    devices = lax.axis_size("space")
    channels, width_x = lifted_field.shape[:2]
    length_x = width_x * devices
    if not suits(width_x, length_x, devices, channels, spectral_weights):
        return general_body(lifted_field, cotangent, spectral_weights, point_weights, point_bias)
    norm = float(length_x * NY * NZ) ** -0.5
    theta = angles(np.arange(length_x), np.arange(length_x), length_x)
    cos_x, sin_x = jnp.asarray(np.cos(theta), F32), jnp.asarray(np.sin(theta), F32)
    forward = forward_tables()
    inverse = inverse_tables(norm)
    summing = jnp.asarray(np.repeat(np.eye(channels), 8, axis=0), F32)

    field = lifted_field.reshape(channels, NY, NZ)
    slopes_in = cotangent.reshape(channels, NY, NZ)
    weights = jnp.transpose(spectral_weights, (0, 1, 3, 4, 2))

    lines, some = forward_modes(field, forward, weights, length_x)
    lines = swap(lines)
    folded = fold_rest(weights, some, length_x)
    spectrum, mixed = mix(cos_x, sin_x, lines, folded, norm)
    field_late, mixed = lax.optimization_barrier((field, mixed))
    modes = swap(mixed)
    pre = pointwise(field_late, summing, point_weights, point_bias)
    act, slope, early = early_cells(inverse, forward, modes, pre, slopes_in)
    early_lines = swap(early)
    activated, late = late_cells(inverse, forward, summing, modes, pre, slopes_in, field, early, slope, act)
    late_lines = swap(late)
    (grad,) = gradient(cos_x, sin_x, spectrum, early_lines, norm, MX)
    grad, grad_point, grad_bias = gradient(cos_x, sin_x, spectrum, late_lines, norm, MX, (grad,))
    return (
        activated.reshape(cotangent.shape),
        jnp.transpose(grad, (0, 1, 4, 2, 3)),
        grad_point,
        grad_bias.reshape(channels),
    )


HIGHEST = lax.Precision.HIGHEST


def trig_tables(positions, frequency, length):
    product = positions[:, None] * frequency[None, :] % length
    phase_angle = 2.0 * jnp.pi / length * product.astype(jnp.float32)
    return (jnp.cos(phase_angle), jnp.sin(phase_angle))


def kept_frequencies(kept_count, length):
    mode_index = jnp.arange(kept_count, dtype=jnp.int32)
    return jnp.where(mode_index < kept_count // 2, mode_index, length - kept_count + mode_index)


def forward_local(field_in):
    channels = field_in.shape[0]
    width_x = field_in.shape[1]
    cos_z, sin_z = trig_tables(jnp.arange(NZ, dtype=jnp.int32), jnp.arange(MZ, dtype=jnp.int32), NZ)
    table_z = jnp.concatenate([cos_z, -sin_z], axis=1)
    along_z = jnp.einsum("cxyz,zk->cxyk", field_in, table_z, precision=HIGHEST)
    z_real = along_z[..., :MZ]
    z_imag = along_z[..., MZ:]
    cos_y, sin_y = trig_tables(jnp.arange(NY, dtype=jnp.int32), kept_frequencies(MY, NY), NY)
    y_real = jnp.einsum("cxyk,yj->xcjk", z_real, cos_y, precision=HIGHEST) + jnp.einsum(
        "cxyk,yj->xcjk", z_imag, sin_y, precision=HIGHEST
    )
    y_imag = jnp.einsum("cxyk,yj->xcjk", z_imag, cos_y, precision=HIGHEST) - jnp.einsum(
        "cxyk,yj->xcjk", z_real, sin_y, precision=HIGHEST
    )
    stacked = jnp.stack([y_real, y_imag], axis=1)
    return stacked.reshape(width_x, 2, channels, MY * MZ)


def transform_x(x_lines):
    length_x = x_lines.shape[0]
    cos_x, sin_x = trig_tables(
        jnp.arange(length_x, dtype=jnp.int32), kept_frequencies(MX, length_x), length_x
    )
    norm_scale = 1.0 / float(length_x * NY * NZ) ** 0.5
    part_real = x_lines[:, 0]
    part_imag = x_lines[:, 1]
    x_real = jnp.einsum("xcm,xk->kcm", part_real, cos_x, precision=HIGHEST) + jnp.einsum(
        "xcm,xk->kcm", part_imag, sin_x, precision=HIGHEST
    )
    x_imag = jnp.einsum("xcm,xk->kcm", part_imag, cos_x, precision=HIGHEST) - jnp.einsum(
        "xcm,xk->kcm", part_real, sin_x, precision=HIGHEST
    )
    return norm_scale * jnp.stack([x_real, x_imag], axis=1)


def mix_modes(spectrum, weights):
    spec_real = spectrum[:, 0]
    spec_imag = spectrum[:, 1]
    out_real = jnp.einsum("kim,kmio->kom", spec_real, weights[0], precision=HIGHEST) - jnp.einsum(
        "kim,kmio->kom", spec_imag, weights[1], precision=HIGHEST
    )
    out_imag = jnp.einsum("kim,kmio->kom", spec_real, weights[1], precision=HIGHEST) + jnp.einsum(
        "kim,kmio->kom", spec_imag, weights[0], precision=HIGHEST
    )
    return jnp.stack([out_real, out_imag], axis=1)


def inverse_x(spectrum, positions, length_x):
    cos_x, sin_x = trig_tables(positions, kept_frequencies(MX, length_x), length_x)
    spec_real = spectrum[:, 0]
    spec_imag = spectrum[:, 1]
    a_real = jnp.einsum("kcm,xk->xcm", spec_real, cos_x, precision=HIGHEST) - jnp.einsum(
        "kcm,xk->xcm", spec_imag, sin_x, precision=HIGHEST
    )
    a_imag = jnp.einsum("kcm,xk->xcm", spec_imag, cos_x, precision=HIGHEST) + jnp.einsum(
        "kcm,xk->xcm", spec_real, sin_x, precision=HIGHEST
    )
    return jnp.stack([a_real, a_imag], axis=1)


def inverse_yz(x_lines, length_x):
    width_x = x_lines.shape[0]
    channels = x_lines.shape[2]
    mode_grid = x_lines.reshape(width_x, 2, channels, MY, MZ)
    cos_y, sin_y = trig_tables(jnp.arange(NY, dtype=jnp.int32), kept_frequencies(MY, NY), NY)
    b_real = jnp.einsum("xcjk,yj->cxyk", mode_grid[:, 0], cos_y, precision=HIGHEST) - jnp.einsum(
        "xcjk,yj->cxyk", mode_grid[:, 1], sin_y, precision=HIGHEST
    )
    b_imag = jnp.einsum("xcjk,yj->cxyk", mode_grid[:, 1], cos_y, precision=HIGHEST) + jnp.einsum(
        "xcjk,yj->cxyk", mode_grid[:, 0], sin_y, precision=HIGHEST
    )
    cos_z, sin_z = trig_tables(jnp.arange(NZ, dtype=jnp.int32), jnp.arange(MZ, dtype=jnp.int32), NZ)
    weight_z = jnp.where(jnp.arange(MZ, dtype=jnp.int32) == 0, 1.0, 2.0).astype(jnp.float32)
    table_z = jnp.concatenate([cos_z * weight_z[None, :], -sin_z * weight_z[None, :]], axis=1)
    stacked = jnp.concatenate([b_real, b_imag], axis=-1)
    result = jnp.einsum("cxyk,zk->cxyz", stacked, table_z, precision=HIGHEST)
    return result * (1.0 / float(length_x * NY * NZ) ** 0.5)


def gelu_slope(values):
    return (
        0.5 * (1.0 + lax.erf(values * INV_SQRT_TWO))
        + values * jnp.exp(-0.5 * values * values) * INV_SQRT_TWO_PI
    )


def weight_gradient(spectrum, slope_modes, first_mode):
    mode_ids = first_mode + jnp.arange(spectrum.shape[3], dtype=jnp.int32)
    weight_modes = jnp.where(mode_ids % MZ == 0, 1.0, 2.0).astype(jnp.float32)
    grad_real = jnp.einsum(
        "kim,kom->kmio", spectrum[:, 0], slope_modes[:, 0], precision=HIGHEST
    ) + jnp.einsum("kim,kom->kmio", spectrum[:, 1], slope_modes[:, 1], precision=HIGHEST)
    grad_imag = jnp.einsum(
        "kim,kom->kmio", spectrum[:, 0], slope_modes[:, 1], precision=HIGHEST
    ) - jnp.einsum("kim,kom->kmio", spectrum[:, 1], slope_modes[:, 0], precision=HIGHEST)
    stacked = jnp.stack([grad_real, grad_imag], axis=0)
    return stacked * weight_modes[None, None, :, None, None]


def to_modes(field_in):
    return transform_x(
        lax.all_to_all(forward_local(field_in), "space", split_axis=3, concat_axis=0, tiled=True)
    )


def general_body(lifted_field, cotangent, spectral_weights, point_weights, point_bias):
    devices = lax.axis_size("space")
    width_x = lifted_field.shape[1]
    length_x = width_x * devices
    spectrum = to_modes(lifted_field)
    mixed_modes = mix_modes(spectrum, spectral_weights)
    full_lines = inverse_x(mixed_modes, jnp.arange(length_x, dtype=jnp.int32), length_x)
    spectral = inverse_yz(
        lax.all_to_all(full_lines, "space", split_axis=0, concat_axis=3, tiled=True), length_x
    )
    pointwise = (
        jnp.einsum("ixyz,io->oxyz", lifted_field, point_weights, precision=HIGHEST)
        + point_bias[:, None, None, None]
    )
    before = spectral + pointwise
    activated = jax.nn.gelu(before, approximate=False).astype(jnp.bfloat16)
    slope_field = cotangent.astype(jnp.float32) * gelu_slope(before)
    local_point = jnp.einsum("ixyz,oxyz->io", lifted_field, slope_field, precision=HIGHEST)
    local_bias = jnp.sum(slope_field, axis=(1, 2, 3))
    partial = jnp.concatenate([local_point, local_bias[None, :]], axis=0)
    gathered = lax.all_gather(partial, "space", axis=0, tiled=False)
    summed = jnp.sum(gathered, axis=0)
    summed_point, summed_bias = summed[:-1], summed[-1]
    root_cells = float(length_x * NY * NZ) ** 0.5
    slope_spectrum = to_modes(slope_field)
    first_mode = lax.axis_index("space") * spectrum.shape[3]
    grad_spectral = weight_gradient(spectrum, slope_spectrum, first_mode)
    return (activated, grad_spectral, summed_point / root_cells, summed_bias / root_cells)


def solution(mesh):
    placed = (
        P("groups", "space", None, None),
        P("groups", "space", None, None),
        P(None, None, "space", None, None),
        P(),
        P(),
    )
    return jax.shard_map(
        body,
        mesh=mesh,
        in_specs=placed,
        out_specs=(
            P("groups", "space", None, None),
            P("groups", None, "space", None, None),
            P("groups", None),
            P("groups"),
        ),
        check_vma=False,
    )
```
